32 devices in a mesh: wide: 8 (over z, y), narrow: 4 (over x, core).
Axes of the slice: x: 2, y: 2, z: 4, core: 2. Of those that a mesh axis runs over, the one named last changes fastest.
Arguments:
- tokens: bfloat16 [32768, 768], P(('wide', 'narrow')), may hold values from -6 to 6
- cotangent: bfloat16 [32768, 768], P(('wide', 'narrow')), may hold values from -6 to 6
- w_attn_in: bfloat16 [768, 2304], P(('wide', 'narrow')), may hold values from -0.21875 to 0.21875
- w_attn_out: bfloat16 [768, 768], P(('wide', 'narrow')), may hold values from -0.21875 to 0.21875
- w_fc_in: bfloat16 [768, 3072], P(('wide', 'narrow')), may hold values from -0.21875 to 0.21875
- w_fc_out: bfloat16 [3072, 768], P(('wide', 'narrow')), may hold values from -0.109375 to 0.109375
- gains_d: bfloat16 [3, 768], P(None, ('wide', 'narrow')), may hold values from 0.099609375 to 1.8984375
- biases_d: bfloat16 [7, 768], P(None, ('wide', 'narrow')), may hold values from -3 to 3
- gains_ff: bfloat16 [3072], P(('wide', 'narrow')), may hold values from 0.099609375 to 1.8984375
- biases_ff: bfloat16 [2, 3072], P(None, ('wide', 'narrow')), may hold values from -3 to 3
- rel_table: bfloat16 [12, 1024], P(None, ('wide', 'narrow')), may hold values from -4 to 4
- head_scale: bfloat16 [12], replicated, may hold values from 0.5 to 2
- bucket: int32 [512], P(('wide', 'narrow')), may hold values from 0 to 2, as said below
- lengths: int32 [512], P(('wide', 'narrow')), may hold values from 0 to 225, as said below
Outputs:
- out_tokens: bfloat16 [32768, 768], P(('wide', 'narrow'))
- grad_tokens: bfloat16 [32768, 768], P(('wide', 'narrow'))
- grad_attn_in: float32 [768, 2304], P(('wide', 'narrow'))
- grad_attn_out: float32 [768, 768], P(('wide', 'narrow'))
- grad_fc_in: float32 [768, 3072], P(('wide', 'narrow'))
- grad_fc_out: float32 [3072, 768], P(('wide', 'narrow'))
- grad_gains_d: float32 [3, 768], P(None, ('wide', 'narrow'))
- grad_biases_d: float32 [7, 768], P(None, ('wide', 'narrow'))
- grad_gains_ff: float32 [3072], P(('wide', 'narrow'))
- grad_biases_ff: float32 [2, 3072], P(None, ('wide', 'narrow'))
- grad_rel_table: float32 [12, 1024], P(None, ('wide', 'narrow'))
- grad_head_scale: float32 [12], replicated
The draws below stay inside these ranges and needn't reach their ends.
Inputs may be any that keep to these rules, and one draw needn't show every extreme that they name: On each device's 16 slots in order: between 1 and 3 images of bucket 1 (a 15 x 15 patch grid in 256 token places), then images of bucket 0 (a 8 x 8 grid in 64 places) that fill the device's 1024 places exactly, then empty slots with id 2. `lengths`: live tokens of each image, in row-major patch order from its first place: at least half of its grid and at most all of it; 0 for empty slots. Each device's first bucket 1 image and first bucket 0 image are whole.
All inputs are finite; a program needn't handle non-finite values.
Results may differ from the reference program's by a relative error of at most 0.013.
Values may be sent and summed in bfloat16 or wider, within the bound.
No kernel may reach another device: no remote copies, remote signals or barrier semaphores. Data moves between devices by JAX's collectives and lax.ppermute only.
A program may use at most 256 MiB of HBM per device.

```python
import math
import jax
import jax.numpy as jnp
from jax import lax

HEADS = 12
HEAD_DIM = 64
FF = 3072
D = 768
TOK_DEV = 1024
GRID_L = 15
GRID_S = 8
SLOT_L = 256
SLOT_S = 64
BLOCK = 512
STRIDE = 32
RELS = 1024
SLOTS_DEV = 16
TOKENS = 32768
IMAGES = 512


def image_plan(key):
    device_count = IMAGES // SLOTS_DEV
    count_key = jax.random.fold_in(key, 37)
    large_key = jax.random.fold_in(key, 11)
    small_key = jax.random.fold_in(key, 23)
    large_count = jax.random.randint(count_key, (device_count, 1), 1, TOK_DEV // SLOT_L, dtype=jnp.int32)
    small_count = (TOK_DEV - SLOT_L * large_count) // SLOT_S
    slot_place = jnp.arange(SLOTS_DEV, dtype=jnp.int32)[None, :]
    bucket_ids = jnp.where(slot_place < large_count, 1, jnp.where(slot_place < large_count + small_count, 0, 2)).astype(jnp.int32)
    large_len = jax.random.randint(large_key, (device_count, SLOTS_DEV), (GRID_L * GRID_L + 1) // 2, GRID_L * GRID_L + 1, dtype=jnp.int32)
    small_len = jax.random.randint(small_key, (device_count, SLOTS_DEV), (GRID_S * GRID_S + 1) // 2, GRID_S * GRID_S + 1, dtype=jnp.int32)
    large_len = jnp.where(slot_place == 0, GRID_L * GRID_L, large_len)
    small_len = jnp.where(slot_place == large_count, GRID_S * GRID_S, small_len)
    live_counts = jnp.where(bucket_ids == 1, large_len, jnp.where(bucket_ids == 0, small_len, 0)).astype(jnp.int32)
    return (bucket_ids.reshape(-1), live_counts.reshape(-1))


def draw_bucket(key, part):
    return image_plan(key)[0]


def draw_lengths(key, part):
    return image_plan(key)[1]


def strengthened(entries, key, source, target, parts, factor):
    owner, partner = [(jnp.arange(entries.shape[position]) // (entries.shape[position] // parts)).reshape([-1 if axis == position else 1 for axis in range(entries.ndim)]) for position in (source, target)]
    chosen = jax.random.permutation(key, parts)[partner]
    strong = (owner == chosen) | (owner == (partner + parts // 2) % parts)
    return jnp.where(strong, factor * entries, entries)


def level_of(key, shape, cuts, low, top_value):
    loudness = 1.0
    for dim, blocks in cuts:
        draws = jax.random.uniform(jax.random.fold_in(jax.random.fold_in(key, 6), dim), (blocks,), jnp.float32, low / len(cuts), top_value / len(cuts))
        loudness = loudness * jnp.repeat(jnp.exp(draws), shape[dim] // blocks).reshape((-1,) + (1,) * (len(shape) - 1 - dim))
    return loudness


def normal_values(rng, extent, scale, limit, cuts=(), kind=jnp.bfloat16):
    values = scale * jax.random.normal(rng, extent, jnp.float32)
    if cuts:
        values = values * level_of(rng, extent, cuts, -0.22, 0.18)
    return jnp.clip(values, -limit, limit).astype(kind)


def gaussian_with(rng, extent, width, reach, shards, heavy, kind=jnp.bfloat16):
    values = width * jax.random.normal(rng, extent, jnp.float32)
    if shards:
        values = values * level_of(rng, extent, shards, -0.22, 0.18)
    return jnp.clip(strengthened(values, jax.random.fold_in(rng, 3), *heavy), -reach, reach).astype(kind)


def setup_inputs(seed: int = 0) -> dict:
    splits = jax.random.split(jax.random.key(seed), 15)
    return {
        "tokens": normal_values(splits[0], (TOKENS, D), 1.0, 6.0, ((0, 32),)),
        "cotangent": gaussian_with(splits[1], (TOKENS, D), 1.0, 6.0, ((0, 32),), (0, 1, 32, 2.75)),
        "w_attn_in": normal_values(splits[2], (D, 3 * D), D ** -0.5, 0.21875, ((0, 32),)),
        "w_attn_out": normal_values(splits[3], (D, D), D ** -0.5, 0.21875, ((0, 32),)),
        "w_fc_in": normal_values(splits[4], (D, FF), D ** -0.5, 0.21875, ((0, 32),)),
        "w_fc_out": normal_values(splits[5], (FF, D), FF ** -0.5, 0.109375, ((0, 32),)),
        "gains_d": jnp.clip(1.0 + 0.18 * jax.random.normal(splits[6], (3, D), jnp.float32), 0.099609375, 1.8984375).astype(jnp.bfloat16),
        "biases_d": normal_values(splits[7], (7, D), 0.3, 3.0, ((1, 32),)),
        "gains_ff": jnp.clip(1.0 + 0.18 * jax.random.normal(splits[8], (FF,), jnp.float32), 0.099609375, 1.8984375).astype(jnp.bfloat16),
        "biases_ff": normal_values(splits[9], (2, FF), 0.3, 3.0, ((1, 32),)),
        "rel_table": normal_values(splits[10], (HEADS, RELS), 1.0, 4.0, ((1, 32),)),
        "head_scale": jnp.clip(jnp.exp(jax.random.uniform(splits[11], (HEADS,), jnp.float32, math.log(0.5), math.log(2.0))), 0.5, 2.0).astype(jnp.bfloat16),
        "bucket": draw_bucket(jax.random.fold_in(splits[14], 71), 0),
        "lengths": draw_lengths(jax.random.fold_in(splits[14], 71), 0),
    }


PRECISE = lax.Precision.HIGHEST
NEG_FILL = -1e+30
NORM_EPS = 1e-05
QUERY_SCALE = 0.125

@jax.custom_vjp
def low(v):
    return lax.optimization_barrier(v.astype(jnp.bfloat16)).astype(jnp.float32)

@jax.custom_vjp
def low_back(v):
    return v

def low_keep(v):
    return (low(v), None)

def low_pass(kept, grad):
    return (grad,)

def back_keep(v):
    return (v, None)

def back_low(kept, grad):
    return (low(grad),)
low.defvjp(low_keep, low_pass)
low_back.defvjp(back_keep, back_low)

def matmul(left_side, right_side):
    return jnp.dot(left_side, right_side, precision=PRECISE, preferred_element_type=jnp.float32)

def normalize(values, scale_by, shift_by):
    center = values - lax.optimization_barrier(jnp.mean(values, axis=-1, keepdims=True))
    spread = lax.rsqrt(lax.optimization_barrier(jnp.mean(center * center, axis=-1, keepdims=True)) + NORM_EPS)
    return center * spread * scale_by + shift_by

def token_layout(bucket, lengths, row_count):
    slot_size = jnp.where(bucket == 1, SLOT_L, jnp.where(bucket == 0, SLOT_S, 0)).astype(jnp.int32)
    slot_end = jnp.cumsum(slot_size, dtype=jnp.int32)
    slot_start = slot_end - slot_size
    places = jnp.arange(row_count, dtype=jnp.int32)
    picture = lax.optimization_barrier(jnp.sum((slot_end[None, :] <= places[:, None]).astype(jnp.int32), axis=1, dtype=jnp.int32))
    picked = picture[:, None] == jnp.arange(bucket.shape[0], dtype=jnp.int32)[None, :]
    first_place = lax.optimization_barrier(jnp.sum(jnp.where(picked, slot_start[None, :], 0), axis=1, dtype=jnp.int32))
    live_count = lax.optimization_barrier(jnp.sum(jnp.where(picked, lengths[None, :], 0), axis=1, dtype=jnp.int32))
    slot_kind = lax.optimization_barrier(jnp.sum(jnp.where(picked, bucket[None, :], 0), axis=1, dtype=jnp.int32))
    offset = places - first_place
    grid_width = jnp.where(slot_kind == 1, GRID_L, GRID_S).astype(jnp.int32)
    row_at = jnp.minimum(offset // grid_width, GRID_L - 1).astype(jnp.int32)
    col_at = (offset % grid_width).astype(jnp.int32)
    return (picture, row_at, col_at, offset < live_count)

def attention(queries, key_rows, value_rows, bias_table, picture, row_at, col_at, live_mask):
    block_count = queries.shape[0] // BLOCK
    head_shape = (block_count, BLOCK, HEADS, HEAD_DIM)

    def attend_block(pieces):
        query_block, key_block, value_block, pic_block, row_block, col_block, live_block = pieces
        usable = (pic_block[:, None] == pic_block[None, :]) & live_block[None, :]
        table_index = (row_block[:, None] - row_block[None, :] + GRID_L) * STRIDE + (col_block[:, None] - col_block[None, :] + GRID_L)
        scores = jnp.einsum('qhd,khd->hqk', query_block, key_block, precision=PRECISE)
        scores = scores + jnp.take(bias_table, table_index, axis=1)
        scores = low_back(jnp.where(usable[None], scores, NEG_FILL))
        attn_probs = low(jax.nn.softmax(scores, axis=-1))
        return jnp.einsum('hqk,khd->qhd', attn_probs, value_block, precision=PRECISE)
    mixed = lax.map(jax.checkpoint(attend_block), (queries.reshape(head_shape), key_rows.reshape(head_shape), value_rows.reshape(head_shape), picture.reshape(block_count, BLOCK), row_at.reshape(block_count, BLOCK), col_at.reshape(block_count, BLOCK), live_mask.reshape(block_count, BLOCK)))
    return mixed.reshape(queries.shape[0], HEADS * HEAD_DIM)

def layer(inputs, w_attn_in, w_attn_out, w_fc_in, w_fc_out, gains_d, biases_d, gains_ff, biases_ff, rel_table, head_scale, picture, row_at, col_at, live_mask):
    hidden_in = low(normalize(inputs, gains_d[0], biases_d[0]))
    projected = matmul(hidden_in, w_attn_in)
    queries = low(low_back((projected[:, :D] + biases_d[1]) * QUERY_SCALE))
    key_rows = low(low_back(projected[:, D:2 * D]))
    value_rows = low(low_back(projected[:, 2 * D:] + biases_d[2]))
    attn_mixed = low_back(attention(queries, key_rows, value_rows, rel_table, picture, row_at, col_at, live_mask))
    scaled_heads = attn_mixed * jnp.repeat(head_scale, HEAD_DIM)
    attn_low = low(normalize(scaled_heads, gains_d[1], biases_d[3]))
    residual_mid = inputs + low_back(matmul(attn_low, w_attn_out) + biases_d[4])
    hidden_mid = low(normalize(residual_mid, gains_d[2], biases_d[5]))
    pre_act = low_back(matmul(hidden_mid, w_fc_in) + biases_ff[0])
    activated = jax.nn.gelu(pre_act, approximate=False)
    hidden_ff = low(normalize(activated, gains_ff, biases_ff[1]))
    branch_out = low_back(matmul(hidden_ff, w_fc_out) + biases_d[6])
    return (residual_mid + branch_out) * live_mask.astype(inputs.dtype)[:, None]

def reference(tokens, cotangent, w_attn_in, w_attn_out, w_fc_in, w_fc_out, gains_d, biases_d, gains_ff, biases_ff, rel_table, head_scale, bucket, lengths):
    params = tuple((weight_arg.astype(jnp.float32) for weight_arg in (w_attn_in, w_attn_out, w_fc_in, w_fc_out, gains_d, biases_d, gains_ff, biases_ff, rel_table, head_scale)))
    zero_grads = tuple((jnp.zeros(weight_arg.shape, jnp.float32) for weight_arg in params))

    def device_pass(carried, pieces):
        tok_rows, cot_rows, bucket_rows, length_rows = pieces
        picture, row_at, col_at, live_mask = token_layout(bucket_rows, length_rows, TOK_DEV)

        def forward(inputs, *weights):
            return layer(inputs, *weights, picture, row_at, col_at, live_mask)
        result, pull = jax.vjp(forward, tok_rows.astype(jnp.float32), *params)
        pulled = pull(cot_rows.astype(jnp.float32))
        summed = tuple((old_sum + new_term for old_sum, new_term in zip(carried, pulled[1:])))
        return (summed, (result.astype(jnp.bfloat16), pulled[0].astype(jnp.bfloat16)))
    sums, outputs = lax.scan(device_pass, zero_grads, (tokens.reshape(-1, TOK_DEV, D), cotangent.reshape(-1, TOK_DEV, D), bucket.reshape(-1, SLOTS_DEV), lengths.reshape(-1, SLOTS_DEV)))
    out_tokens = outputs[0].reshape(-1, D)
    grad_tokens = outputs[1].reshape(-1, D)
    return (out_tokens, grad_tokens, sums[0], sums[1], sums[2], sums[3], sums[4], sums[5], sums[6], sums[7], sums[8], sums[9])
```

```python
import functools

import jax
import jax.numpy as jnp
import numpy as np
from jax import lax
from jax.experimental import pallas as pl
from jax.experimental.pallas import tpu as pltpu
from jax.sharding import PartitionSpec as P

HEADS = 12
HEAD_DIM = 64
D = 768
FF = 3072
GRID_L = 15
GRID_S = 8
SLOT_L = 256
SLOT_S = 64
STRIDE = 32
RELS = 1024
CHUNK = 256
PIECES = 16
ROWS_D = D // PIECES
ROWS_F = FF // (2 * PIECES)

NEG_FILL = -1e30
NORM_EPS = 1e-05
HALF_ROOT = 0.7071067811865476
DENSITY_SCALE = 0.3989422804014327
QUERY_SCALE = 0.125
AXES = ("wide", "narrow")
F32 = jnp.float32
BF16 = jnp.bfloat16
VMEM_BIG = 60 * 2**20

NN = (((1,), (0,)), ((), ()))
NT = (((1,), (1,)), ((), ()))
TN = (((0,), (0,)), ((), ()))


def dot(left, right, dims=NN):
    return lax.dot_general(left, right, dims, preferred_element_type=F32)


def unit_rows(values):
    center = values - jnp.mean(values, axis=-1, keepdims=True)
    spread = lax.rsqrt(jnp.mean(center * center, axis=-1, keepdims=True) + NORM_EPS)
    return center * spread, spread


def unit_rows_back(inner, scaled, spread):
    return spread * (
        inner
        - jnp.mean(inner, axis=-1, keepdims=True)
        - scaled * jnp.mean(inner * scaled, axis=-1, keepdims=True)
    )


def col_sum(values):
    return jnp.sum(values, axis=0, keepdims=True)


def unit_position(kind):
    place = np.arange(CHUNK)
    if kind == 0:
        return np.minimum(place // GRID_L, GRID_L - 1), place % GRID_L
    inner = place % SLOT_S
    return inner // GRID_S, inner % GRID_S


def pick_tables():
    keys = np.zeros((2, CHUNK, 512), np.float32)
    keys_back = np.zeros((2, CHUNK, 512), np.float32)
    queries = np.zeros((2, CHUNK, CHUNK), np.float32)
    for kind in range(2):
        row, col = unit_position(kind)
        line = STRIDE * row + col
        keys[kind, np.arange(CHUNK), line] = 1
        keys_back[kind, np.arange(CHUNK), 511 - line] = 1
        queries[kind, 16 * row + col, np.arange(CHUNK)] = 1
    return keys.astype(BF16), keys_back.astype(BF16), queries.astype(BF16)


def bias_kernel(table_ref, keys_ref, queries_ref, out_ref):
    line = jnp.broadcast_to(table_ref[0], (16, RELS))
    base = pltpu.roll(line, RELS - 511, 1, stride=1, stride_axis=0)
    groups = [base[:, :512]]
    for r in range(1, 16):
        groups.append(pltpu.roll(base, STRIDE * r, 1)[:, :512])
    spread_rows = jnp.concatenate(groups, axis=0).astype(BF16)
    for kind in range(2):
        by_key = dot(keys_ref[kind], spread_rows, NT).astype(BF16)
        tile = dot(by_key, queries_ref[kind])
        if kind == 1:
            left = lax.broadcasted_iota(jnp.int32, (CHUNK, CHUNK), 0) // SLOT_S
            right = lax.broadcasted_iota(jnp.int32, (CHUNK, CHUNK), 1) // SLOT_S
            tile = jnp.where(left == right, tile, NEG_FILL)
        out_ref[kind, 0] = tile.astype(BF16)


def build_bias(flipped, keys, queries):
    return pl.pallas_call(
        bias_kernel,
        grid=(HEADS,),
        in_specs=[
            pl.BlockSpec((1, 1, RELS), lambda h: (h, 0, 0)),
            pl.BlockSpec((2, CHUNK, 512), lambda h: (0, 0, 0)),
            pl.BlockSpec((2, CHUNK, CHUNK), lambda h: (0, 0, 0)),
        ],
        out_specs=pl.BlockSpec((2, 1, CHUNK, CHUNK), lambda h: (0, h, 0, 0)),
        out_shape=jax.ShapeDtypeStruct((2, HEADS, CHUNK, CHUNK), BF16),
        compiler_params=pltpu.CompilerParams(vmem_limit_bytes=VMEM_BIG),
        name="bias_tiles",
    )(flipped, keys, queries)


def halves(values):
    high = values.astype(BF16)
    return high, (values - high.astype(F32)).astype(BF16)


def table_kernel(tiles_ref, keys_ref, queries_ref, out_ref):
    total = jnp.zeros((CHUNK, 512), F32)
    for kind in range(2):
        high, rest = halves(tiles_ref[kind, 0])
        by_query = dot(queries_ref[kind], high, NT) + dot(queries_ref[kind], rest, NT)
        high, rest = halves(by_query)
        total = total + dot(high, keys_ref[kind]) + dot(rest, keys_ref[kind])
    wide = jnp.concatenate([total, jnp.zeros((CHUNK, 512), F32)], axis=1)
    line = wide[:16]
    for r in range(1, 15):
        line = line + pltpu.roll(wide[16 * r : 16 * r + 16], STRIDE * r, 1)
    line = pltpu.roll(line, 0, 1, stride=1, stride_axis=0)
    out_ref[0] = pltpu.roll(jnp.broadcast_to(col_sum(line), (8, RELS)), RELS - 16, 1)


def table_grads(tiles, keys_back, queries):
    return pl.pallas_call(
        table_kernel,
        grid=(HEADS,),
        in_specs=[
            pl.BlockSpec((2, 1, CHUNK, CHUNK), lambda h: (0, h, 0, 0)),
            pl.BlockSpec((2, CHUNK, 512), lambda h: (0, 0, 0)),
            pl.BlockSpec((2, CHUNK, CHUNK), lambda h: (0, 0, 0)),
        ],
        out_specs=pl.BlockSpec((1, 8, RELS), lambda h: (h, 0, 0)),
        out_shape=jax.ShapeDtypeStruct((HEADS, 8, RELS), F32),
        compiler_params=pltpu.CompilerParams(vmem_limit_bytes=VMEM_BIG),
        name="table_grads",
    )(tiles, keys_back, queries)[:, 0]


META_KIND = 1
META_FROM = {"a": 8, "b": 24}
META_TO = {"a": 40, "b": 56}


class Load:
    def __init__(self, meta, sem, scratch):
        self.meta, self.sem, self.scratch = meta, sem, scratch

    def cols(self, order, own, other, start):
        core, rows = self.meta[0], own.shape[1]
        for k in range(PIECES):
            place = pl.multiple_of(self.meta[META_FROM[order] + k] * rows, 16)
            for half, source in ((core, own), (1 - core, other)):
                pltpu.make_async_copy(
                    source.at[k],
                    self.scratch.at[half, pl.ds(place, rows), pl.ds(start, own.shape[2])],
                    self.sem,
                ).start()

    def rows(self, order, own, other):
        core, rows = self.meta[0], own.shape[1]
        for k in range(PIECES):
            chip = self.meta[META_FROM[order] + k]
            for half, source in ((core, own), (1 - core, other)):
                place = pl.multiple_of((2 * chip + half) * rows, 16)
                pltpu.make_async_copy(
                    source.at[k], self.scratch.at[pl.ds(place, rows)], self.sem
                ).start()

    def wait(self):
        pltpu.make_async_copy(self.scratch, self.scratch, self.sem).wait()


ANY = pl.BlockSpec(memory_space=pl.ANY)


def full(*shape):
    return pl.BlockSpec(shape, lambda *_: (0,) * len(shape))


def attend_kernel(
    meta, x_ref, vec_ref, a0, a1, b0, b1, bias_ref, mask_ref,
    low_ref, q_ref, k_ref, v_ref, mixed_ref, turned_ref, lse_ref, w_scr, sem,
):
    @pl.when(pl.program_id(0) == 0)
    def _():
        load = Load(meta, sem, w_scr)
        load.cols("a", a0, a1, 0)
        load.cols("b", b0, b1, a0.shape[2])
        load.wait()

    scaled, _ = unit_rows(x_ref[...].astype(F32))
    low = (scaled * vec_ref[0:1] + vec_ref[3:4]).astype(BF16)
    low_ref[...] = low
    first = dot(low, w_scr[0])
    second = dot(low, w_scr[1])
    query = (first[:, :D] + vec_ref[4:5]) * QUERY_SCALE
    query_turned = query.T.astype(BF16)
    q_ref[...] = query.astype(BF16)
    k_ref[...] = jnp.concatenate([first[:, D:], second[:, : D // 2]], axis=1).astype(BF16)
    value = second[:, D // 2 :] + vec_ref[5:6]
    value_turned = value.T.astype(BF16)
    v_ref[...] = value.astype(BF16)
    mask = jnp.broadcast_to(mask_ref[...], (CHUNK, CHUNK))
    sums = []
    for h in range(HEADS):
        part = slice(h * HEAD_DIM, (h + 1) * HEAD_DIM)
        scores = dot(k_ref[:, part], query_turned[part]) + bias_ref[0, h].astype(F32) + mask
        largest = jnp.max(scores, axis=0, keepdims=True)
        exponent = jnp.exp(scores - largest)
        row_total = jnp.sum(exponent, axis=0, keepdims=True)
        out = dot(value_turned[part], exponent.astype(BF16))
        turned_ref[0, part] = out * (1.0 / row_total)
        sums.append(largest + jnp.log(row_total))
    lse_ref[0] = jnp.concatenate(sums + [jnp.zeros((16 - HEADS, CHUNK), F32)], axis=0)
    mixed_ref[...] = turned_ref[0].T


def attend(meta, tokens, vec, w_in, bias, mask):
    rows = tokens.shape[0]
    chunks = rows // CHUNK
    tile = pl.BlockSpec((CHUNK, D), lambda c, m: (c, 0))
    return pl.pallas_call(
        attend_kernel,
        grid_spec=pltpu.PrefetchScalarGridSpec(
            num_scalar_prefetch=1,
            grid=(chunks,),
            in_specs=[
                tile,
                full(16, D),
                ANY, ANY, ANY, ANY,
                pl.BlockSpec((1, HEADS, CHUNK, CHUNK), lambda c, m: (m[META_KIND + c], 0, 0, 0)),
                pl.BlockSpec((CHUNK, 1), lambda c, m: (c, 0)),
            ],
            out_specs=[
                tile, tile, tile, tile, tile,
                pl.BlockSpec((1, D, CHUNK), lambda c, m: (c, 0, 0)),
                pl.BlockSpec((1, 16, CHUNK), lambda c, m: (c, 0, 0)),
            ],
            scratch_shapes=[pltpu.VMEM((2, D, 3 * D // 2), BF16), pltpu.SemaphoreType.DMA],
        ),
        out_shape=[jax.ShapeDtypeStruct((rows, D), BF16)] * 4
        + [
            jax.ShapeDtypeStruct((rows, D), F32),
            jax.ShapeDtypeStruct((chunks, D, CHUNK), F32),
            jax.ShapeDtypeStruct((chunks, 16, CHUNK), F32),
        ],
        compiler_params=pltpu.CompilerParams(vmem_limit_bytes=VMEM_BIG),
        cost_estimate=pl.CostEstimate(
            flops=2 * rows * D * 3 * D, bytes_accessed=24 * rows * D, transcendentals=0
        ),
        name="attend",
    )(meta, tokens, vec, *w_in, bias, mask)


SUB = 16


def feed_kernel(
    meta, x_ref, mixed_ref, cot_ref, live_ref, vec_ref, wide_ref,
    o0, o1, i0, i1, f0, f1,
    out_ref, mid_ref, aln_ref, low_ref, m_ref, dz_ref, df_ref, sums_ref, sums_ff_ref,
    wo_scr, wi_scr, wf_scr, z_scr, unit_scr, dm_scr, spread_scr, acc_scr, sems,
):
    step = pl.program_id(0)

    @pl.when(step == 0)
    def _():
        loads = [Load(meta, sems.at[i], s) for i, s in enumerate((wo_scr, wi_scr, wf_scr))]
        loads[0].cols("a", o0, o1, 0)
        loads[1].cols("a", i0, i1, 0)
        loads[2].rows("b", f0, f1)
        for load in loads:
            load.wait()
        acc_scr[...] = jnp.zeros_like(acc_scr)
        sums_ref[...] = jnp.zeros_like(sums_ref)

    live = live_ref[...]
    scaled, _ = unit_rows(mixed_ref[...] * vec_ref[10:11])
    aln = (scaled * vec_ref[1:2] + vec_ref[6:7]).astype(BF16)
    aln_ref[...] = aln
    branch = jnp.concatenate([dot(aln, wo_scr[0]), dot(aln, wo_scr[1])], axis=1)
    mid = x_ref[...].astype(F32) + branch + vec_ref[7:8]
    mid_ref[...] = mid
    scaled, _ = unit_rows(mid)
    low = (scaled * vec_ref[2:3] + vec_ref[8:9]).astype(BF16)
    low_ref[...] = low
    for half in range(2):
        part = slice(half * FF // 2, (half + 1) * FF // 2)
        z_scr[:, part] = dot(low, wi_scr[half]) + wide_ref[1:2, part]

    def forward(i, carry):
        rows = pl.ds(i * SUB, SUB)
        z = z_scr[rows]
        cumulative = 0.5 * (1.0 + lax.erf(z * HALF_ROOT))
        unit, spread = unit_rows(z * cumulative)
        z_scr[rows] = cumulative + z * (DENSITY_SCALE * jnp.exp(-0.5 * z * z))
        unit_scr[rows] = unit
        spread_scr[rows] = jnp.broadcast_to(spread, (SUB, 128))
        m_ref[rows] = (unit * wide_ref[0:1] + wide_ref[2:3]).astype(BF16)
        return carry

    lax.fori_loop(0, CHUNK // SUB, forward, 0)
    out = mid + dot(m_ref[...], wf_scr[...]) + vec_ref[9:10]
    out_ref[...] = (out * live).astype(BF16)
    df_full = cot_ref[...].astype(F32) * live
    df = df_full.astype(BF16)
    df_ref[...] = df
    sums_ref[0:1] += col_sum(df_full)
    dm_scr[...] = dot(df, wf_scr[...], NT)

    def backward(i, carry):
        rows = pl.ds(i * SUB, SUB)
        dm = dm_scr[rows]
        unit = unit_scr[rows]
        acc_scr[0] += dm * unit
        acc_scr[1] += dm
        du = unit_rows_back(dm * wide_ref[0:1], unit, spread_scr[rows, 0:1])
        dz_full = du * z_scr[rows]
        dz = dz_full.astype(BF16)
        acc_scr[2] += dz_full
        dz_ref[0, rows] = dz[:, : FF // 2]
        dz_ref[1, rows] = dz[:, FF // 2 :]
        return carry

    lax.fori_loop(0, CHUNK // SUB, backward, 0)

    @pl.when(step == pl.num_programs(0) - 1)
    def _():
        sums_ff_ref[...] = jnp.sum(acc_scr[...], axis=1)


def feed(meta, tokens, mixed, cot, live, vec, wide, w_out, w_in, w_down):
    rows = tokens.shape[0]
    tile = pl.BlockSpec((CHUNK, D), lambda c, m: (c, 0))
    return pl.pallas_call(
        feed_kernel,
        grid_spec=pltpu.PrefetchScalarGridSpec(
            num_scalar_prefetch=1,
            grid=(rows // CHUNK,),
            in_specs=[
                tile, tile, tile,
                pl.BlockSpec((CHUNK, 1), lambda c, m: (c, 0)),
                full(16, D), full(8, FF),
                ANY, ANY, ANY, ANY, ANY, ANY,
            ],
            out_specs=[
                tile, tile, tile, tile,
                pl.BlockSpec((CHUNK, FF), lambda c, m: (c, 0)),
                pl.BlockSpec((2, CHUNK, FF // 2), lambda c, m: (0, c, 0)),
                tile,
                full(8, D),
                full(3, FF),
            ],
            scratch_shapes=[
                pltpu.VMEM((2, D, D // 2), BF16),
                pltpu.VMEM((2, D, FF // 2), BF16),
                pltpu.VMEM((FF, D), BF16),
                pltpu.VMEM((CHUNK, FF), F32),
                pltpu.VMEM((CHUNK, FF), F32),
                pltpu.VMEM((CHUNK, FF), F32),
                pltpu.VMEM((CHUNK, 128), F32),
                pltpu.VMEM((3, SUB, FF), F32),
                pltpu.SemaphoreType.DMA((3,)),
            ],
        ),
        out_shape=[
            jax.ShapeDtypeStruct((rows, D), BF16),
            jax.ShapeDtypeStruct((rows, D), F32),
            jax.ShapeDtypeStruct((rows, D), BF16),
            jax.ShapeDtypeStruct((rows, D), BF16),
            jax.ShapeDtypeStruct((rows, FF), BF16),
            jax.ShapeDtypeStruct((2, rows, FF // 2), BF16),
            jax.ShapeDtypeStruct((rows, D), BF16),
            jax.ShapeDtypeStruct((8, D), F32),
            jax.ShapeDtypeStruct((3, FF), F32),
        ],
        compiler_params=pltpu.CompilerParams(vmem_limit_bytes=VMEM_BIG),
        cost_estimate=pl.CostEstimate(
            flops=2 * rows * D * (D + 3 * FF), bytes_accessed=40 * rows * D, transcendentals=0
        ),
        name="feed",
    )(meta, tokens, mixed, cot, live, vec, wide, *w_out, *w_in, *w_down)


def middle_kernel(
    meta, dz_ref, mid_ref, mixed_ref, cot_ref, live_ref, vec_ref, i0, i1, o0, o1,
    da_ref, dx_ref, do_ref, sums_ref, wi_scr, wo_scr, sems,
):
    @pl.when(pl.program_id(0) == 0)
    def _():
        loads = [Load(meta, sems.at[i], s) for i, s in enumerate((wi_scr, wo_scr))]
        loads[0].cols("a", i0, i1, 0)
        loads[1].cols("a", o0, o1, 0)
        for load in loads:
            load.wait()
        sums_ref[...] = jnp.zeros_like(sums_ref)

    dh = dot(dz_ref[0], wi_scr[0], NT) + dot(dz_ref[1], wi_scr[1], NT)
    scaled, spread = unit_rows(mid_ref[...])
    sums_ref[0:1] += col_sum(dh * scaled)
    sums_ref[1:2] += col_sum(dh)
    dx = cot_ref[...].astype(F32) * live_ref[...] + unit_rows_back(dh * vec_ref[2:3], scaled, spread)
    dx_ref[...] = dx
    sums_ref[2:3] += col_sum(dx)
    da = dx.astype(BF16)
    da_ref[0] = da[:, : D // 2]
    da_ref[1] = da[:, D // 2 :]
    dn = dot(da[:, : D // 2], wo_scr[0], NT) + dot(da[:, D // 2 :], wo_scr[1], NT)
    mixed = mixed_ref[...]
    scaled, spread = unit_rows(mixed * vec_ref[10:11])
    sums_ref[3:4] += col_sum(dn * scaled)
    sums_ref[4:5] += col_sum(dn)
    heads = unit_rows_back(dn * vec_ref[1:2], scaled, spread)
    sums_ref[5:6] += col_sum(heads * mixed)
    do_ref[...] = (heads * vec_ref[10:11]).astype(BF16)


def middle(meta, dz, mid, mixed, cot, live, vec, w_in, w_out):
    rows = mid.shape[0]
    tile = pl.BlockSpec((CHUNK, D), lambda c, m: (c, 0))
    return pl.pallas_call(
        middle_kernel,
        grid_spec=pltpu.PrefetchScalarGridSpec(
            num_scalar_prefetch=1,
            grid=(rows // CHUNK,),
            in_specs=[
                pl.BlockSpec((2, CHUNK, FF // 2), lambda c, m: (0, c, 0)),
                tile, tile, tile,
                pl.BlockSpec((CHUNK, 1), lambda c, m: (c, 0)),
                full(16, D),
                ANY, ANY, ANY, ANY,
            ],
            out_specs=[
                pl.BlockSpec((2, CHUNK, D // 2), lambda c, m: (0, c, 0)),
                tile, tile,
                full(8, D),
            ],
            scratch_shapes=[
                pltpu.VMEM((2, D, FF // 2), BF16),
                pltpu.VMEM((2, D, D // 2), BF16),
                pltpu.SemaphoreType.DMA((2,)),
            ],
        ),
        out_shape=[
            jax.ShapeDtypeStruct((2, rows, D // 2), BF16),
            jax.ShapeDtypeStruct((rows, D), F32),
            jax.ShapeDtypeStruct((rows, D), BF16),
            jax.ShapeDtypeStruct((8, D), F32),
        ],
        compiler_params=pltpu.CompilerParams(vmem_limit_bytes=VMEM_BIG),
        cost_estimate=pl.CostEstimate(
            flops=2 * rows * D * (D + FF), bytes_accessed=30 * rows * D, transcendentals=0
        ),
        name="middle",
    )(meta, dz, mid, mixed, cot, live, vec, *w_in, *w_out)


def attend_back_kernel(
    meta, q_ref, k_ref, v_ref, do_ref, turned_ref, lse_ref, bias_ref, mask_ref,
    dqkv_ref, tiles_ref, dq_scr, do_scr,
):
    step = pl.program_id(0)
    kind = meta[META_KIND + step]

    @pl.when(step == 0)
    def _():
        tiles_ref[...] = jnp.zeros_like(tiles_ref)

    query = q_ref[...]
    query_turned = query.astype(F32).T.astype(BF16)
    key_turned = k_ref[...].astype(F32).T.astype(BF16)
    do_scr[...] = do_ref[...].astype(F32).T
    mask = jnp.broadcast_to(mask_ref[...], (CHUNK, CHUNK))
    dk, dv = [], []
    for h in range(HEADS):
        part = slice(h * HEAD_DIM, (h + 1) * HEAD_DIM)
        key, value = k_ref[:, part], v_ref[:, part]
        do_turned = do_scr[part]
        scores = dot(key, query_turned[part]) + bias_ref[0, h].astype(F32) + mask
        probs = jnp.exp(scores - lse_ref[0, h : h + 1])
        centre = jnp.sum(do_turned * turned_ref[0, part], axis=0, keepdims=True)
        ds_full = probs * (dot(value, do_turned.astype(BF16)) - centre)
        ds = ds_full.astype(BF16)
        tiles_ref[kind, h] += ds_full
        dv.append(dot(probs.astype(BF16), do_ref[:, part]))
        dk.append(dot(ds, q_ref[:, part]))
        dq_scr[part] = dot(key_turned[part], ds)
    dq = (dq_scr[...].T * QUERY_SCALE).astype(BF16)
    dk = jnp.concatenate(dk, axis=1).astype(BF16)
    dv = jnp.concatenate(dv, axis=1).astype(BF16)
    dqkv_ref[0, :, :D] = dq
    dqkv_ref[0, :, D:] = dk[:, : D // 2]
    dqkv_ref[1, :, : D // 2] = dk[:, D // 2 :]
    dqkv_ref[1, :, D // 2 :] = dv


def attend_back(meta, query, key, value, do, turned, lse, bias, mask):
    rows = query.shape[0]
    chunks = rows // CHUNK
    tile = pl.BlockSpec((CHUNK, D), lambda c, m: (c, 0))
    return pl.pallas_call(
        attend_back_kernel,
        grid_spec=pltpu.PrefetchScalarGridSpec(
            num_scalar_prefetch=1,
            grid=(chunks,),
            in_specs=[
                tile, tile, tile, tile,
                pl.BlockSpec((1, D, CHUNK), lambda c, m: (c, 0, 0)),
                pl.BlockSpec((1, 16, CHUNK), lambda c, m: (c, 0, 0)),
                pl.BlockSpec((1, HEADS, CHUNK, CHUNK), lambda c, m: (m[META_KIND + c], 0, 0, 0)),
                pl.BlockSpec((CHUNK, 1), lambda c, m: (c, 0)),
            ],
            out_specs=[
                pl.BlockSpec((2, CHUNK, 3 * D // 2), lambda c, m: (0, c, 0)),
                full(2, HEADS, CHUNK, CHUNK),
            ],
            scratch_shapes=[pltpu.VMEM((D, CHUNK), F32), pltpu.VMEM((D, CHUNK), F32)],
        ),
        out_shape=[
            jax.ShapeDtypeStruct((2, rows, 3 * D // 2), BF16),
            jax.ShapeDtypeStruct((2, HEADS, CHUNK, CHUNK), F32),
        ],
        compiler_params=pltpu.CompilerParams(vmem_limit_bytes=VMEM_BIG),
        cost_estimate=pl.CostEstimate(
            flops=10 * rows * CHUNK * D * 3, bytes_accessed=30 * rows * D, transcendentals=0
        ),
        name="attend_back",
    )(meta, query, key, value, do, turned, lse, bias, mask)


def last_kernel(
    meta, dqkv_ref, x_ref, dx_ref, vec_ref, a0, a1, b0, b1,
    out_ref, sums_ref, sums_p_ref, w_scr, sem,
):
    @pl.when(pl.program_id(0) == 0)
    def _():
        load = Load(meta, sem, w_scr)
        load.cols("a", a0, a1, 0)
        load.cols("b", b0, b1, a0.shape[2])
        load.wait()
        sums_ref[...] = jnp.zeros_like(sums_ref)
        sums_p_ref[...] = jnp.zeros_like(sums_p_ref)

    dh = dot(dqkv_ref[0], w_scr[0], NT) + dot(dqkv_ref[1], w_scr[1], NT)
    for half in range(2):
        sums_p_ref[half : half + 1] += col_sum(dqkv_ref[half].astype(F32))
    scaled, spread = unit_rows(x_ref[...].astype(F32))
    sums_ref[0:1] += col_sum(dh * scaled)
    sums_ref[1:2] += col_sum(dh)
    out_ref[...] = (dx_ref[...] + unit_rows_back(dh * vec_ref[0:1], scaled, spread)).astype(BF16)


def last(meta, dqkv, tokens, dx, vec, w_in):
    rows = tokens.shape[0]
    tile = pl.BlockSpec((CHUNK, D), lambda c, m: (c, 0))
    return pl.pallas_call(
        last_kernel,
        grid_spec=pltpu.PrefetchScalarGridSpec(
            num_scalar_prefetch=1,
            grid=(rows // CHUNK,),
            in_specs=[
                pl.BlockSpec((2, CHUNK, 3 * D // 2), lambda c, m: (0, c, 0)),
                tile, tile,
                full(16, D),
                ANY, ANY, ANY, ANY,
            ],
            out_specs=[tile, full(8, D), full(2, 3 * D // 2)],
            scratch_shapes=[pltpu.VMEM((2, D, 3 * D // 2), BF16), pltpu.SemaphoreType.DMA],
        ),
        out_shape=[
            jax.ShapeDtypeStruct((rows, D), BF16),
            jax.ShapeDtypeStruct((8, D), F32),
            jax.ShapeDtypeStruct((2, 3 * D // 2), F32),
        ],
        compiler_params=pltpu.CompilerParams(vmem_limit_bytes=VMEM_BIG),
        cost_estimate=pl.CostEstimate(
            flops=2 * rows * D * 3 * D, bytes_accessed=16 * rows * D, transcendentals=0
        ),
        name="last",
    )(meta, dqkv, tokens, dx, vec, *w_in)


BAND = 384


def cols_grad_kernel(meta, left_ref, right_ref, *out_refs, parts):
    step = pl.program_id(0)
    band = dot(left_ref[...], right_ref[0], TN).astype(BF16)
    at = 0
    for (order, width), out_ref in zip(parts, out_refs):
        for i in range(BAND // ROWS_D):
            piece = meta[META_TO[order] + step * (BAND // ROWS_D) + i]
            out_ref[piece] = band[i * ROWS_D : (i + 1) * ROWS_D, at : at + width]
        at += width


def cols_grad(meta, left, right, parts, own):
    rows, width = left.shape[0], right.shape[2]
    half = (lambda i, m: (m[0], 0, 0)) if own else (lambda i, m: (1 - m[0], 0, 0))
    return pl.pallas_call(
        functools.partial(cols_grad_kernel, parts=parts),
        grid_spec=pltpu.PrefetchScalarGridSpec(
            num_scalar_prefetch=1,
            grid=(D // BAND,),
            in_specs=[
                pl.BlockSpec((rows, BAND), lambda i, m: (0, i)),
                pl.BlockSpec((1, rows, width), half),
            ],
            out_specs=[full(PIECES, ROWS_D, w) for _, w in parts],
        ),
        out_shape=[jax.ShapeDtypeStruct((PIECES, ROWS_D, w), BF16) for _, w in parts],
        compiler_params=pltpu.CompilerParams(vmem_limit_bytes=VMEM_BIG),
        cost_estimate=pl.CostEstimate(
            flops=2 * rows * D * width, bytes_accessed=2 * rows * (D + width), transcendentals=0
        ),
        name="cols_grad_own" if own else "cols_grad_other",
    )(meta, left, right)


def rows_grad_kernel(meta, left_ref, right_ref, own_ref, other_ref, *, order):
    step = pl.program_id(0)
    band = dot(left_ref[...], right_ref[...], TN).astype(BF16)
    low_core = meta[0] == 0
    for i in range(BAND // (2 * ROWS_F)):
        piece = meta[META_TO[order] + step * (BAND // (2 * ROWS_F)) + i]
        even = band[2 * i * ROWS_F : (2 * i + 1) * ROWS_F]
        odd = band[(2 * i + 1) * ROWS_F : (2 * i + 2) * ROWS_F]
        own_ref[piece] = jnp.where(low_core, even, odd)
        other_ref[piece] = jnp.where(low_core, odd, even)


def rows_grad(meta, left, right, order):
    rows = left.shape[0]
    return pl.pallas_call(
        functools.partial(rows_grad_kernel, order=order),
        grid_spec=pltpu.PrefetchScalarGridSpec(
            num_scalar_prefetch=1,
            grid=(FF // BAND,),
            in_specs=[
                pl.BlockSpec((rows, BAND), lambda i, m: (0, i)),
                pl.BlockSpec((rows, D), lambda i, m: (0, 0)),
            ],
            out_specs=[full(PIECES, ROWS_F, D)] * 2,
        ),
        out_shape=[jax.ShapeDtypeStruct((PIECES, ROWS_F, D), BF16)] * 2,
        compiler_params=pltpu.CompilerParams(vmem_limit_bytes=VMEM_BIG),
        cost_estimate=pl.CostEstimate(
            flops=2 * rows * D * FF, bytes_accessed=2 * rows * (D + FF), transcendentals=0
        ),
        name="rows_grad",
    )(meta, left, right)


def swap(values, mask, count):
    return lax.ppermute(values, AXES, [(i, i ^ mask) for i in range(count)])


class Cube:
    SIDES = {"a": (2, 4), "b": (4, 2)}

    def __init__(self):
        self.me = lax.axis_index(AXES).astype(jnp.int32)

    def swap(self, values, mask):
        return swap(values, mask, 32)

    def masks(self, order):
        shift = self.SIDES[order]
        return np.array(
            [8 * (k & 3) + shift[0] * (k >> 2 & 1) + shift[1] * (k >> 3) for k in range(PIECES)]
        )

    def meta(self):
        chip = self.me >> 1
        place = jnp.arange(PIECES, dtype=jnp.int32)
        start = [chip ^ jnp.asarray(self.masks(o) >> 1, jnp.int32) for o in "ab"]
        mask = chip ^ place
        x, y = mask & 1, mask >> 1 & 1
        to = [(mask >> 2) + 4 * x + 8 * y, (mask >> 2) + 4 * y + 8 * x]
        return self.me & 1, start + to

    def spread(self, piece, order):
        held = jnp.stack([piece] + [self.swap(piece, 8 * z) for z in (1, 2, 3)])
        for side in self.SIDES[order]:
            held = jnp.concatenate([held, self.swap(held, side)])
        return held

    def gather_cols(self, shard, parts):
        half = shard.shape[1] // 2
        left, right = shard[:, :half], shard[:, half:]
        odd = (self.me & 1) == 1
        got = self.swap(jnp.where(odd, left, right), 1)
        mine = jnp.where(odd, right, left)
        block = jnp.where(odd, jnp.concatenate([got, mine]), jnp.concatenate([mine, got]))
        out, at = [], 0
        for order, width in parts:
            own = self.spread(block[:, at : at + width], order)
            out += [own, self.swap(own, 1)]
            at += width
        return out

    def gather_rows(self, shard, order):
        own = self.spread(shard, order)
        return [own, self.swap(own, 1)]

    def gather_small(self, pack):
        held = jnp.stack([pack] + [self.swap(pack, 8 * z) for z in (1, 2, 3)])
        held = jnp.stack([held] + [self.swap(held, s) for s in (2, 4, 6)])
        held = jnp.stack([held, self.swap(held, 1)]).reshape(32, -1)
        k = np.arange(32)
        masks = jnp.asarray(8 * (k & 3) + 2 * (k >> 2 & 3) + (k >> 4), jnp.int32)
        device = jnp.arange(32, dtype=jnp.int32)
        pick = (device[:, None] ^ masks[None, :]) == self.me
        return dot(pick.astype(BF16), held)

    def reduce_pieces(self, own, other, order):
        total = own.astype(F32) + self.swap(other, 1).astype(F32)
        for side in self.SIDES[order][::-1]:
            count = total.shape[0] // 2
            total = total[:count] + self.swap(total[count:].astype(BF16), side).astype(F32)
        out = total[0]
        for z in (1, 2, 3):
            out = out + self.swap(total[z].astype(BF16), 8 * z).astype(F32)
        return out

    def reduce_cols(self, own, other, parts):
        sums = [self.reduce_pieces(*pair, order) for *pair, (order, _) in zip(own, other, parts)]
        block = sums[0] if len(sums) == 1 else jnp.concatenate(sums, axis=1)
        rows = block.shape[0] // 2
        low, high = block[:rows], block[rows:]
        odd = (self.me & 1) == 1
        got = self.swap(jnp.where(odd, low, high), 1)
        mine = jnp.where(odd, high, low)
        return jnp.where(
            odd, jnp.concatenate([got, mine], axis=1), jnp.concatenate([mine, got], axis=1)
        )

    def reduce_rows(self, own, other, order):
        return self.reduce_pieces(own, other, order)

    def reduce_small(self, pack):
        k = np.arange(32)
        masks = jnp.asarray(8 * (k & 3) + 2 * (k >> 2 & 3) + (k >> 4), jnp.int32)
        device = jnp.arange(32, dtype=jnp.int32)
        pick = (device[None, :] ^ masks[:, None]) == self.me
        total = jnp.dot(pick.astype(F32), pack, precision=lax.Precision.HIGHEST)
        total = total[:16] + self.swap(total[16:], 1)
        total = total[:4] + sum(self.swap(total[4 * s : 4 * s + 4], 2 * s) for s in (1, 2, 3))
        return total[0] + sum(self.swap(total[z], 8 * z) for z in (1, 2, 3))


class Plain:
    def __init__(self, count):
        self.count = count
        self.me = lax.axis_index(AXES)

    def meta(self):
        place = jnp.arange(PIECES, dtype=jnp.int32)
        return jnp.int32(0), [place] * 4

    def gather_cols(self, shard, parts):
        whole = lax.all_gather(shard, AXES, axis=0, tiled=True)
        out, at, half = [], 0, shard.shape[1] // 2
        for _, width in parts:
            for start in (at, at + half):
                out.append(whole[:, start : start + width].reshape(PIECES, -1, width))
            at += width
        return out

    def gather_rows(self, shard, order):
        whole = lax.all_gather(shard, AXES, axis=0, tiled=True)
        whole = whole.reshape(PIECES, 2, -1, whole.shape[1])
        return [whole[:, 0], whole[:, 1]]

    def gather_small(self, pack):
        return lax.all_gather(pack, AXES).reshape(self.count, -1).astype(F32)

    def reduce_cols(self, own, other, parts):
        whole = jnp.concatenate([p.reshape(-1, p.shape[2]) for p in (*own, *other)], axis=1)
        return lax.psum_scatter(whole.astype(F32), AXES, scatter_dimension=0, tiled=True)

    def reduce_rows(self, own, other, order):
        whole = jnp.stack([own, other], axis=1).reshape(-1, own.shape[2])
        return lax.psum_scatter(whole.astype(F32), AXES, scatter_dimension=0, tiled=True)

    def reduce_small(self, pack):
        return lax.psum_scatter(pack, AXES, scatter_dimension=0, tiled=False)


PARTS_IN = (("a", 640), ("b", 512))
PARTS_OUT = (("a", D // 2),)
PARTS_FF = (("a", FF // 2),)


def layout(bucket, lengths, row_count):
    large = jnp.sum((bucket == 1).astype(jnp.int32), dtype=jnp.int32)
    place = jnp.arange(row_count, dtype=jnp.int32)
    is_large = place < large * SLOT_L
    slot = jnp.where(is_large, place // SLOT_L, large + (place - large * SLOT_L) // SLOT_S)
    offset = jnp.where(is_large, place % SLOT_L, place % SLOT_S)
    picked = slot[:, None] == jnp.arange(bucket.shape[0], dtype=jnp.int32)[None, :]
    live_count = jnp.sum(jnp.where(picked, lengths[None, :], 0), axis=1, dtype=jnp.int32)
    live = (offset < live_count).astype(F32)[:, None]
    chunk = jnp.arange(row_count // CHUNK, dtype=jnp.int32)
    return live, (chunk >= large).astype(jnp.int32)


def body(
    tokens,
    cotangent,
    w_attn_in,
    w_attn_out,
    w_fc_in,
    w_fc_out,
    gains_d,
    biases_d,
    gains_ff,
    biases_ff,
    rel_table,
    head_scale,
    bucket,
    lengths,
    *,
    count,
    cube,
):
    net = Cube() if cube else Plain(count)
    rows = tokens.shape[0]

    small = (gains_d, biases_d, gains_ff[None], biases_ff, rel_table)
    sizes = [v.size for v in small]
    ends = np.cumsum(sizes)
    width = -(-int(ends[-1] + HEADS) // 1024) * 1024
    pack = jnp.concatenate([v.reshape(-1) for v in small] + [jnp.zeros(width - ends[-1], BF16)])
    whole = net.gather_small(pack)
    gain_rows, bias_rows, gain_mid, bias_mid, table = (
        whole[:, end - size : end]
        .reshape(count, v.shape[0], v.shape[1])
        .transpose(1, 0, 2)
        .reshape(v.shape[0], -1)
        for v, size, end in zip(small, sizes, ends)
    )
    in_pieces = net.gather_cols(w_attn_in, PARTS_IN)
    out_pieces = net.gather_cols(w_attn_out, PARTS_OUT)
    ff_pieces = net.gather_cols(w_fc_in, PARTS_FF)
    down_pieces = net.gather_rows(w_fc_out, "b")

    head_wide = jnp.repeat(head_scale.astype(F32), HEAD_DIM)[None]
    vec = jnp.concatenate([gain_rows, bias_rows, head_wide, jnp.zeros((5, D), F32)])
    wide = jnp.concatenate([gain_mid, bias_mid, jnp.zeros((5, FF), F32)])
    live, kinds = layout(bucket, lengths, rows)
    mask = (1.0 - live) * NEG_FILL
    core, tables = net.meta()
    meta = jnp.concatenate(
        [core.astype(jnp.int32)[None], kinds, jnp.zeros(7 - kinds.shape[0], jnp.int32), *tables]
    )
    keys, keys_back, queries = (jnp.asarray(t) for t in pick_tables())
    flipped = jnp.pad(table[:, 1006::-1], ((0, 0), (0, RELS - 1007)))[:, None]
    bias = build_bias(flipped, keys, queries)

    low_in, query, key, value, mixed, turned, lse = attend(
        meta, tokens, vec, in_pieces, bias, mask
    )
    out_tokens, mid, low_attn, low_mid, low_ff, dz, df, sums_a, sums_ff = feed(
        meta, tokens, mixed, cotangent, live, vec, wide, out_pieces, ff_pieces, down_pieces
    )
    own, other = rows_grad(meta, low_ff, df, "b")
    grad_fc_out = net.reduce_rows(own, other, "b")

    da, dx, do, sums_b = middle(
        meta, dz, mid, mixed, cotangent, live, vec, ff_pieces, out_pieces
    )
    other, own = (cols_grad(meta, low_mid, dz, PARTS_FF, side) for side in (False, True))
    grad_fc_in = net.reduce_cols(own, other, PARTS_FF)
    other, own = (cols_grad(meta, low_attn, da, PARTS_OUT, side) for side in (False, True))
    grad_attn_out = net.reduce_cols(own, other, PARTS_OUT)

    dqkv, tiles = attend_back(meta, query, key, value, do, turned, lse, bias, mask)
    other, own = (cols_grad(meta, low_in, dqkv, PARTS_IN, side) for side in (False, True))
    grad_attn_in = net.reduce_cols(own, other, PARTS_IN)
    grad_table = table_grads(tiles, keys_back, queries)
    grad_tokens, sums_c, sums_p = last(meta, dqkv, tokens, dx, vec, in_pieces)

    sums_p = sums_p.reshape(3, D)
    d_terms = jnp.concatenate(
        [
            sums_c[0:1], sums_b[3:4], sums_b[0:1],
            sums_c[1:2], sums_p[0:1], sums_p[2:3], sums_b[4:5], sums_b[2:3], sums_b[1:2], sums_a[0:1],
        ]
    )
    head_terms = jnp.sum(sums_b[5].reshape(HEADS, HEAD_DIM), axis=1)
    terms = (d_terms[:3], d_terms[3:], sums_ff[0:1], sums_ff[2:0:-1], grad_table)
    terms = [
        t.reshape(t.shape[0], count, -1).transpose(1, 0, 2).reshape(count, -1) for t in terms
    ]
    terms += [jnp.broadcast_to(head_terms, (count, HEADS)), jnp.zeros((count, width - ends[-1] - HEADS), F32)]
    mine = net.reduce_small(jnp.concatenate(terms, axis=1))
    grads = [
        mine[end - size : end].reshape(v.shape) for v, size, end in zip(small, sizes, ends)
    ]
    grad_head_scale = mine[ends[-1] : ends[-1] + HEADS]
    return (
        out_tokens,
        grad_tokens,
        grad_attn_in,
        grad_attn_out,
        grad_fc_in,
        grad_fc_out,
        grads[0],
        grads[1],
        grads[2][0],
        grads[3],
        grads[4],
        grad_head_scale,
    )


def solution(mesh):
    rows = P(AXES, None)
    columns = P(None, AXES)
    line = P(AXES)
    count = mesh.shape["wide"] * mesh.shape["narrow"]
    cube = (mesh.shape["wide"], mesh.shape["narrow"]) == (8, 4)
    return jax.shard_map(
        functools.partial(body, count=count, cube=cube),
        mesh=mesh,
        in_specs=(
            rows, rows, rows, rows, rows, rows,
            columns, columns, line, columns, columns, P(), line, line,
        ),
        out_specs=(
            rows, rows, rows, rows, rows, rows,
            columns, columns, line, columns, columns, P(),
        ),
        check_vma=False,
    )
```

```python
import functools

import jax
import jax.numpy as jnp
import numpy as np
from jax import lax
from jax.experimental import pallas as pl
from jax.experimental.pallas import tpu as pltpu
from jax.sharding import PartitionSpec as P

HEADS = 12
HEAD_DIM = 64
D = 768
FF = 3072
GRID_L = 15
GRID_S = 8
SLOT_L = 256
SLOT_S = 64
STRIDE = 32
RELS = 1024
CHUNK = 256
PIECES = 16
ROWS_D = D // PIECES
ROWS_F = FF // (2 * PIECES)

NEG_FILL = -1e30
NORM_EPS = 1e-05
HALF_ROOT = 0.7071067811865476
DENSITY_SCALE = 0.3989422804014327
QUERY_SCALE = 0.125
AXES = ("wide", "narrow")
F32 = jnp.float32
BF16 = jnp.bfloat16
VMEM_BIG = 60 * 2**20

NN = (((1,), (0,)), ((), ()))
NT = (((1,), (1,)), ((), ()))
TN = (((0,), (0,)), ((), ()))


ANY = pl.BlockSpec(memory_space=pl.ANY)


def full(*shape):
    return pl.BlockSpec(shape, lambda *_: (0,) * len(shape))


def dot(left, right, dims=NN):
    return lax.dot_general(left, right, dims, preferred_element_type=F32)


def unit_rows(values):
    center = values - jnp.mean(values, axis=-1, keepdims=True)
    spread = lax.rsqrt(jnp.mean(center * center, axis=-1, keepdims=True) + NORM_EPS)
    return center * spread, spread


def unit_rows_back(inner, scaled, spread):
    return spread * (
        inner
        - jnp.mean(inner, axis=-1, keepdims=True)
        - scaled * jnp.mean(inner * scaled, axis=-1, keepdims=True)
    )


def col_sum(values):
    return jnp.sum(values, axis=0, keepdims=True)


def unit_position(kind):
    place = np.arange(CHUNK)
    if kind == 0:
        return np.minimum(place // GRID_L, GRID_L - 1), place % GRID_L
    inner = place % SLOT_S
    return inner // GRID_S, inner % GRID_S


def pick_tables():
    keys = np.zeros((2, CHUNK, 512), np.float32)
    keys_back = np.zeros((2, CHUNK, 512), np.float32)
    queries = np.zeros((2, CHUNK, CHUNK), np.float32)
    for kind in range(2):
        row, col = unit_position(kind)
        line = STRIDE * row + col
        keys[kind, np.arange(CHUNK), line] = 1
        keys_back[kind, np.arange(CHUNK), 511 - line] = 1
        queries[kind, 16 * row + col, np.arange(CHUNK)] = 1
    return keys.astype(BF16), keys_back.astype(BF16), queries.astype(BF16)


def owner_of_lane(lanes, each, last=None):
    lane = lax.broadcasted_iota(jnp.int32, lanes, 1)
    entry = lane if last is None else last - lane
    device = lax.broadcasted_iota(jnp.int32, lanes, 0)
    return ((entry >= device * each) & (entry < device * each + each)).astype(BF16)


def place_in_part(lanes, each, last=None):
    lane = lax.broadcasted_iota(jnp.int32, lanes, 1)
    entry = lane if last is None else last - lane
    row = lax.broadcasted_iota(jnp.int32, lanes, 0)
    return ((entry >= 0) & (lax.rem(entry + each, each) == row)).astype(F32)


def prepare_kernel(pack_ref, scale_ref, keys_ref, queries_ref, vec_ref, wide_ref, out_ref, line_scr, *, count):
    head = pl.program_id(0)
    each_d, each_f, each_t = D // count, FF // count, RELS // count

    @pl.when(head == 0)
    def _():
        pack = pack_ref[...]

        def rows(start, amount, each, lanes, last=None):
            owner = owner_of_lane((count, lanes), each, last)
            place = place_in_part((each, lanes), each, last)
            part = pack[:, start : start + amount * each]
            spread = dot(part, owner, TN)
            return [col_sum(spread[r * each : r * each + each] * place) for r in range(amount)]

        d_rows = rows(0, 10, each_d, D)
        start = 10 * each_d
        ff_rows = rows(start, 3, each_f, FF)
        start += 3 * each_f
        lines = rows(start, HEADS, each_t, RELS, 1006)
        lane = lax.broadcasted_iota(jnp.int32, (HEADS, D), 1)
        row = lax.broadcasted_iota(jnp.int32, (HEADS, D), 0)
        heads = dot(scale_ref[...], (lane // HEAD_DIM == row).astype(BF16))
        vec_ref[...] = jnp.concatenate(d_rows + [heads, jnp.zeros((5, D), F32)], axis=0)
        wide_ref[...] = jnp.concatenate(ff_rows + [jnp.zeros((5, FF), F32)], axis=0)
        for h in range(HEADS):
            line_scr[h] = jnp.broadcast_to(lines[h], (16, RELS))

    base = pltpu.roll(line_scr[head], RELS - 511, 1, stride=1, stride_axis=0)
    groups = [base[:, :512]]
    for r in range(1, 16):
        groups.append(pltpu.roll(base, STRIDE * r, 1)[:, :512])
    spread_rows = jnp.concatenate(groups, axis=0).astype(BF16)
    for kind in range(2):
        by_key = dot(keys_ref[kind], spread_rows, NT).astype(BF16)
        tile = dot(by_key, queries_ref[kind])
        if kind == 1:
            left = lax.broadcasted_iota(jnp.int32, (CHUNK, CHUNK), 0) // SLOT_S
            right = lax.broadcasted_iota(jnp.int32, (CHUNK, CHUNK), 1) // SLOT_S
            tile = jnp.where(left == right, tile, NEG_FILL)
        out_ref[kind, 0] = tile.astype(BF16)


def prepare(pack, scale, keys, queries, count):
    return pl.pallas_call(
        functools.partial(prepare_kernel, count=count),
        grid=(HEADS,),
        in_specs=[
            full(*pack.shape),
            full(1, HEADS),
            full(2, CHUNK, 512),
            full(2, CHUNK, CHUNK),
        ],
        out_specs=[
            full(16, D),
            full(8, FF),
            pl.BlockSpec((2, 1, CHUNK, CHUNK), lambda h: (0, h, 0, 0)),
        ],
        out_shape=[
            jax.ShapeDtypeStruct((16, D), F32),
            jax.ShapeDtypeStruct((8, FF), F32),
            jax.ShapeDtypeStruct((2, HEADS, CHUNK, CHUNK), BF16),
        ],
        scratch_shapes=[pltpu.VMEM((HEADS, 16, RELS), F32)],
        compiler_params=pltpu.CompilerParams(vmem_limit_bytes=VMEM_BIG),
        cost_estimate=pl.CostEstimate(flops=8 * 10**9, bytes_accessed=4 * 10**6, transcendentals=0),
        name="prepare",
    )(pack, scale, keys, queries)


def pack_kernel(a_ref, b_ref, c_ref, p_ref, ff_ref, table_ref, out_ref, *, count):
    each_d, each_f, each_t = D // count, FF // count, RELS // count

    def columns(rows, each, lanes):
        owner = owner_of_lane((count, lanes), each)
        place = place_in_part((each, lanes), each)
        parts = []
        for row in rows:
            high, rest = halves(row * place)
            parts.append(dot(high, owner, NT) + dot(rest, owner, NT))
        return jnp.concatenate(parts, axis=0)

    a, b, c = a_ref[...], b_ref[...], c_ref[...]
    p = p_ref[...]
    d_rows = [
        c[0:1], b[3:4], b[0:1],
        c[1:2], p[0:1, :D], p[1:2, D // 2 :], b[4:5], b[2:3], b[1:2], a[0:1],
    ]
    ff = ff_ref[...]
    lane = lax.broadcasted_iota(jnp.int32, (16, D), 1)
    row = lax.broadcasted_iota(jnp.int32, (16, D), 0)
    high, rest = halves(jnp.broadcast_to(b[5:6], (16, D)) * (lane // HEAD_DIM == row).astype(F32))
    ones = jnp.ones((count, D), BF16)
    out = [
        columns(d_rows, each_d, D),
        columns([ff[0:1], ff[2:3], ff[1:2]], each_f, FF),
        columns([table_ref[h, 0:1] for h in range(HEADS)], each_t, RELS),
        dot(high, ones, NT) + dot(rest, ones, NT),
    ]
    used = sum(o.shape[0] for o in out)
    out.append(jnp.zeros((out_ref.shape[1] - used, count), F32))
    out_ref[...] = jnp.concatenate(out, axis=0).T


def pack_terms(sums_a, sums_b, sums_c, sums_p, sums_ff, table, count, width):
    return pl.pallas_call(
        functools.partial(pack_kernel, count=count),
        out_shape=jax.ShapeDtypeStruct((count, width), F32),
        compiler_params=pltpu.CompilerParams(vmem_limit_bytes=VMEM_BIG),
        cost_estimate=pl.CostEstimate(flops=10**9, bytes_accessed=10**6, transcendentals=0),
        name="pack_terms",
    )(sums_a, sums_b, sums_c, sums_p, sums_ff, table)


def halves(values):
    high = values.astype(BF16)
    return high, (values - high.astype(F32)).astype(BF16)


def table_kernel(tiles_ref, keys_ref, queries_ref, out_ref):
    total = jnp.zeros((CHUNK, 512), F32)
    for kind in range(2):
        high, rest = halves(tiles_ref[kind, 0])
        by_query = dot(queries_ref[kind], high, NT) + dot(queries_ref[kind], rest, NT)
        high, rest = halves(by_query)
        total = total + dot(high, keys_ref[kind]) + dot(rest, keys_ref[kind])
    wide = jnp.concatenate([total, jnp.zeros((CHUNK, 512), F32)], axis=1)
    line = wide[:16]
    for r in range(1, 15):
        line = line + pltpu.roll(wide[16 * r : 16 * r + 16], STRIDE * r, 1)
    line = pltpu.roll(line, 0, 1, stride=1, stride_axis=0)
    out_ref[0] = pltpu.roll(jnp.broadcast_to(col_sum(line), (8, RELS)), RELS - 16, 1)


def table_grads(tiles, keys_back, queries):
    return pl.pallas_call(
        table_kernel,
        grid=(HEADS,),
        in_specs=[
            pl.BlockSpec((2, 1, CHUNK, CHUNK), lambda h: (0, h, 0, 0)),
            pl.BlockSpec((2, CHUNK, 512), lambda h: (0, 0, 0)),
            pl.BlockSpec((2, CHUNK, CHUNK), lambda h: (0, 0, 0)),
        ],
        out_specs=pl.BlockSpec((1, 8, RELS), lambda h: (h, 0, 0)),
        out_shape=jax.ShapeDtypeStruct((HEADS, 8, RELS), F32),
        compiler_params=pltpu.CompilerParams(vmem_limit_bytes=VMEM_BIG),
        cost_estimate=pl.CostEstimate(flops=8 * 10**9, bytes_accessed=6 * 10**6, transcendentals=0),
        name="table_grads",
    )(tiles, keys_back, queries)


META_KIND = 1
META_LARGE = 5
META_LENGTH = 72
META_FROM = {"a": 8, "b": 24}
META_TO = {"a": 40, "b": 56}


def live_rows(meta, chunk):
    place = lax.broadcasted_iota(jnp.int32, (CHUNK, 1), 0)
    large = meta[META_LARGE]
    first = large + (chunk - large) * (SLOT_L // SLOT_S)
    is_large = chunk < large
    end = jnp.zeros((CHUNK, 1), jnp.int32)
    for part in range(SLOT_L // SLOT_S):
        slot = jnp.where(is_large, chunk, first + part)
        start = jnp.where(is_large, 0, part * SLOT_S)
        end = jnp.where(place >= part * SLOT_S, start + meta[META_LENGTH + slot], end)
    return (place < end).astype(F32)


class Load:
    def __init__(self, meta, sem, scratch):
        self.meta, self.sem, self.scratch = meta, sem, scratch

    def cols(self, order, own, other, start, source_start, width):
        core, rows = self.meta[0], own.shape[1]
        for k in range(PIECES):
            place = pl.multiple_of(self.meta[META_FROM[order] + k] * rows, 16)
            for half, source in ((core, own), (1 - core, other)):
                pltpu.make_async_copy(
                    source.at[k, :, pl.ds(source_start, width)],
                    self.scratch.at[half, pl.ds(place, rows), pl.ds(start, width)],
                    self.sem,
                ).start()

    def rows(self, order, own, other):
        core, rows = self.meta[0], own.shape[1]
        for k in range(PIECES):
            chip = self.meta[META_FROM[order] + k]
            for half, source in ((core, own), (1 - core, other)):
                place = pl.multiple_of((2 * chip + half) * rows, 16)
                pltpu.make_async_copy(
                    source.at[k], self.scratch.at[pl.ds(place, rows)], self.sem
                ).start()

    def wait(self):
        pltpu.make_async_copy(self.scratch, self.scratch, self.sem).wait()


def attend_kernel(
    meta, x_ref, vec_ref, a0, a1, b0, b1, bias_ref,
    low_ref, q_ref, k_ref, v_ref, mixed_ref, turned_ref, lse_ref, w_scr, sem,
):
    @pl.when(pl.program_id(0) == 0)
    def _():
        load = Load(meta, sem, w_scr)
        load.cols("a", a0, a1, 0, 0, D)
        load.cols("b", b0, b1, D, 0, D // 2)
        load.wait()

    scaled, _ = unit_rows(x_ref[...].astype(F32))
    low = (scaled * vec_ref[0:1] + vec_ref[3:4]).astype(BF16)
    low_ref[...] = low
    first = dot(low, w_scr[0])
    second = dot(low, w_scr[1])
    query = (first[:, :D] + vec_ref[4:5]) * QUERY_SCALE
    query_turned = query.T.astype(BF16)
    q_ref[...] = query.astype(BF16)
    k_ref[...] = jnp.concatenate([first[:, D:], second[:, : D // 2]], axis=1).astype(BF16)
    value = second[:, D // 2 :] + vec_ref[5:6]
    value_turned = value.T.astype(BF16)
    v_ref[...] = value.astype(BF16)
    mask = jnp.broadcast_to((1.0 - live_rows(meta, pl.program_id(0))) * NEG_FILL, (CHUNK, CHUNK))
    sums = []
    for h in range(HEADS):
        part = slice(h * HEAD_DIM, (h + 1) * HEAD_DIM)
        scores = dot(k_ref[:, part], query_turned[part]) + bias_ref[0, h].astype(F32) + mask
        largest = jnp.max(scores, axis=0, keepdims=True)
        exponent = jnp.exp(scores - largest)
        row_total = jnp.sum(exponent, axis=0, keepdims=True)
        out = dot(value_turned[part], exponent.astype(BF16))
        turned_ref[0, part] = out * (1.0 / row_total)
        sums.append(largest + jnp.log(row_total))
    lse_ref[0] = jnp.concatenate(sums + [jnp.zeros((16 - HEADS, CHUNK), F32)], axis=0)
    mixed_ref[...] = turned_ref[0].T


def attend(meta, tokens, vec, w_in, bias):
    rows = tokens.shape[0]
    chunks = rows // CHUNK
    tile = pl.BlockSpec((CHUNK, D), lambda c, m: (c, 0))
    return pl.pallas_call(
        attend_kernel,
        grid_spec=pltpu.PrefetchScalarGridSpec(
            num_scalar_prefetch=1,
            grid=(chunks,),
            in_specs=[
                tile,
                full(16, D),
                ANY, ANY, ANY, ANY,
                pl.BlockSpec((1, HEADS, CHUNK, CHUNK), lambda c, m: (m[META_KIND + c], 0, 0, 0)),
            ],
            out_specs=[
                tile, tile, tile, tile, tile,
                pl.BlockSpec((1, D, CHUNK), lambda c, m: (c, 0, 0)),
                pl.BlockSpec((1, 16, CHUNK), lambda c, m: (c, 0, 0)),
            ],
            scratch_shapes=[pltpu.VMEM((2, D, 3 * D // 2), BF16), pltpu.SemaphoreType.DMA],
        ),
        out_shape=[jax.ShapeDtypeStruct((rows, D), BF16)] * 4
        + [
            jax.ShapeDtypeStruct((rows, D), F32),
            jax.ShapeDtypeStruct((chunks, D, CHUNK), F32),
            jax.ShapeDtypeStruct((chunks, 16, CHUNK), F32),
        ],
        compiler_params=pltpu.CompilerParams(vmem_limit_bytes=VMEM_BIG),
        cost_estimate=pl.CostEstimate(
            flops=2 * rows * D * 3 * D, bytes_accessed=24 * rows * D, transcendentals=0
        ),
        name="attend",
    )(meta, tokens, vec, *w_in, bias)


SUB = 16


def feed_kernel(
    meta, x_ref, mixed_ref, cot_ref, vec_ref, wide_ref,
    o0, o1, i0, i1, f0, f1,
    out_ref, mid_ref, aln_ref, low_ref, m_ref, dz_ref, df_ref, sums_ref, sums_ff_ref,
    wo_scr, wi_scr, wf_scr, z_scr, unit_scr, dm_scr, spread_scr, acc_scr, sems,
):
    step = pl.program_id(0)

    @pl.when(step == 0)
    def _():
        loads = [Load(meta, sems.at[i], s) for i, s in enumerate((wo_scr, wi_scr, wf_scr))]
        loads[0].cols("b", o0, o1, 0, D // 2, D // 2)
        loads[1].cols("a", i0, i1, 0, 0, FF // 2)
        loads[2].rows("b", f0, f1)
        for load in loads:
            load.wait()
        acc_scr[...] = jnp.zeros_like(acc_scr)
        sums_ref[...] = jnp.zeros_like(sums_ref)

    live = live_rows(meta, step)
    scaled, _ = unit_rows(mixed_ref[...] * vec_ref[10:11])
    aln = (scaled * vec_ref[1:2] + vec_ref[6:7]).astype(BF16)
    aln_ref[...] = aln
    branch = jnp.concatenate([dot(aln, wo_scr[0]), dot(aln, wo_scr[1])], axis=1)
    mid = x_ref[...].astype(F32) + branch + vec_ref[7:8]
    mid_ref[...] = mid
    scaled, _ = unit_rows(mid)
    low = (scaled * vec_ref[2:3] + vec_ref[8:9]).astype(BF16)
    low_ref[...] = low
    for half in range(2):
        part = slice(half * FF // 2, (half + 1) * FF // 2)
        z_scr[:, part] = dot(low, wi_scr[half]) + wide_ref[1:2, part]

    def forward(i, carry):
        rows = pl.ds(i * SUB, SUB)
        z = z_scr[rows]
        cumulative = 0.5 * (1.0 + lax.erf(z * HALF_ROOT))
        unit, spread = unit_rows(z * cumulative)
        z_scr[rows] = cumulative + z * (DENSITY_SCALE * jnp.exp(-0.5 * z * z))
        unit_scr[rows] = unit
        spread_scr[rows] = jnp.broadcast_to(spread, (SUB, 128))
        m_ref[rows] = (unit * wide_ref[0:1] + wide_ref[2:3]).astype(BF16)
        return carry

    lax.fori_loop(0, CHUNK // SUB, forward, 0)
    out = mid + dot(m_ref[...], wf_scr[...]) + vec_ref[9:10]
    out_ref[...] = (out * live).astype(BF16)
    df_full = cot_ref[...].astype(F32) * live
    df = df_full.astype(BF16)
    df_ref[...] = df
    sums_ref[0:1] += col_sum(df_full)
    dm_scr[...] = dot(df, wf_scr[...], NT)

    def backward(i, carry):
        rows = pl.ds(i * SUB, SUB)
        dm = dm_scr[rows]
        unit = unit_scr[rows]
        acc_scr[0] += dm * unit
        acc_scr[1] += dm
        du = unit_rows_back(dm * wide_ref[0:1], unit, spread_scr[rows, 0:1])
        dz_full = du * z_scr[rows]
        dz = dz_full.astype(BF16)
        acc_scr[2] += dz_full
        dz_ref[0, rows] = dz[:, : FF // 2]
        dz_ref[1, rows] = dz[:, FF // 2 :]
        return carry

    lax.fori_loop(0, CHUNK // SUB, backward, 0)

    @pl.when(step == pl.num_programs(0) - 1)
    def _():
        sums_ff_ref[...] = jnp.sum(acc_scr[...], axis=1)


def feed(meta, tokens, mixed, cot, vec, wide, w_out, w_in, w_down):
    rows = tokens.shape[0]
    tile = pl.BlockSpec((CHUNK, D), lambda c, m: (c, 0))
    return pl.pallas_call(
        feed_kernel,
        grid_spec=pltpu.PrefetchScalarGridSpec(
            num_scalar_prefetch=1,
            grid=(rows // CHUNK,),
            in_specs=[
                tile, tile, tile,
                full(16, D), full(8, FF),
                ANY, ANY, ANY, ANY, ANY, ANY,
            ],
            out_specs=[
                tile, tile, tile, tile,
                pl.BlockSpec((CHUNK, FF), lambda c, m: (c, 0)),
                pl.BlockSpec((2, CHUNK, FF // 2), lambda c, m: (0, c, 0)),
                tile,
                full(8, D),
                full(3, FF),
            ],
            scratch_shapes=[
                pltpu.VMEM((2, D, D // 2), BF16),
                pltpu.VMEM((2, D, FF // 2), BF16),
                pltpu.VMEM((FF, D), BF16),
                pltpu.VMEM((CHUNK, FF), F32),
                pltpu.VMEM((CHUNK, FF), F32),
                pltpu.VMEM((CHUNK, FF), F32),
                pltpu.VMEM((CHUNK, 128), F32),
                pltpu.VMEM((3, SUB, FF), F32),
                pltpu.SemaphoreType.DMA((3,)),
            ],
        ),
        out_shape=[
            jax.ShapeDtypeStruct((rows, D), BF16),
            jax.ShapeDtypeStruct((rows, D), F32),
            jax.ShapeDtypeStruct((rows, D), BF16),
            jax.ShapeDtypeStruct((rows, D), BF16),
            jax.ShapeDtypeStruct((rows, FF), BF16),
            jax.ShapeDtypeStruct((2, rows, FF // 2), BF16),
            jax.ShapeDtypeStruct((rows, D), BF16),
            jax.ShapeDtypeStruct((8, D), F32),
            jax.ShapeDtypeStruct((3, FF), F32),
        ],
        compiler_params=pltpu.CompilerParams(vmem_limit_bytes=VMEM_BIG),
        cost_estimate=pl.CostEstimate(
            flops=2 * rows * D * (D + 3 * FF), bytes_accessed=40 * rows * D, transcendentals=0
        ),
        name="feed",
    )(meta, tokens, mixed, cot, vec, wide, *w_out, *w_in, *w_down)


def middle_kernel(
    meta, dz_ref, mid_ref, mixed_ref, cot_ref, vec_ref, i0, i1, o0, o1,
    da_ref, dx_ref, do_ref, sums_ref, wi_scr, wo_scr, sems,
):
    @pl.when(pl.program_id(0) == 0)
    def _():
        loads = [Load(meta, sems.at[i], s) for i, s in enumerate((wi_scr, wo_scr))]
        loads[0].cols("a", i0, i1, 0, 0, FF // 2)
        loads[1].cols("b", o0, o1, 0, D // 2, D // 2)
        for load in loads:
            load.wait()
        sums_ref[...] = jnp.zeros_like(sums_ref)

    dh = dot(dz_ref[0], wi_scr[0], NT) + dot(dz_ref[1], wi_scr[1], NT)
    scaled, spread = unit_rows(mid_ref[...])
    sums_ref[0:1] += col_sum(dh * scaled)
    sums_ref[1:2] += col_sum(dh)
    dx = cot_ref[...].astype(F32) * live_rows(meta, pl.program_id(0)) + unit_rows_back(dh * vec_ref[2:3], scaled, spread)
    dx_ref[...] = dx
    sums_ref[2:3] += col_sum(dx)
    da = dx.astype(BF16)
    da_ref[0] = da[:, : D // 2]
    da_ref[1] = da[:, D // 2 :]
    dn = dot(da[:, : D // 2], wo_scr[0], NT) + dot(da[:, D // 2 :], wo_scr[1], NT)
    mixed = mixed_ref[...]
    scaled, spread = unit_rows(mixed * vec_ref[10:11])
    sums_ref[3:4] += col_sum(dn * scaled)
    sums_ref[4:5] += col_sum(dn)
    heads = unit_rows_back(dn * vec_ref[1:2], scaled, spread)
    sums_ref[5:6] += col_sum(heads * mixed)
    do_ref[...] = (heads * vec_ref[10:11]).astype(BF16)


def middle(meta, dz, mid, mixed, cot, vec, w_in, w_out):
    rows = mid.shape[0]
    tile = pl.BlockSpec((CHUNK, D), lambda c, m: (c, 0))
    return pl.pallas_call(
        middle_kernel,
        grid_spec=pltpu.PrefetchScalarGridSpec(
            num_scalar_prefetch=1,
            grid=(rows // CHUNK,),
            in_specs=[
                pl.BlockSpec((2, CHUNK, FF // 2), lambda c, m: (0, c, 0)),
                tile, tile, tile,
                full(16, D),
                ANY, ANY, ANY, ANY,
            ],
            out_specs=[
                pl.BlockSpec((2, CHUNK, D // 2), lambda c, m: (0, c, 0)),
                tile, tile,
                full(8, D),
            ],
            scratch_shapes=[
                pltpu.VMEM((2, D, FF // 2), BF16),
                pltpu.VMEM((2, D, D // 2), BF16),
                pltpu.SemaphoreType.DMA((2,)),
            ],
        ),
        out_shape=[
            jax.ShapeDtypeStruct((2, rows, D // 2), BF16),
            jax.ShapeDtypeStruct((rows, D), F32),
            jax.ShapeDtypeStruct((rows, D), BF16),
            jax.ShapeDtypeStruct((8, D), F32),
        ],
        compiler_params=pltpu.CompilerParams(vmem_limit_bytes=VMEM_BIG),
        cost_estimate=pl.CostEstimate(
            flops=2 * rows * D * (D + FF), bytes_accessed=30 * rows * D, transcendentals=0
        ),
        name="middle",
    )(meta, dz, mid, mixed, cot, vec, *w_in, *w_out)


def attend_back_kernel(
    meta, q_ref, k_ref, v_ref, do_ref, turned_ref, lse_ref, bias_ref,
    dqkv_ref, tiles_ref, dq_scr, do_scr,
):
    step = pl.program_id(0)
    kind = meta[META_KIND + step]

    @pl.when(step == 0)
    def _():
        tiles_ref[...] = jnp.zeros_like(tiles_ref)

    query = q_ref[...]
    query_turned = query.astype(F32).T.astype(BF16)
    key_turned = k_ref[...].astype(F32).T.astype(BF16)
    do_scr[...] = do_ref[...].astype(F32).T
    mask = jnp.broadcast_to((1.0 - live_rows(meta, pl.program_id(0))) * NEG_FILL, (CHUNK, CHUNK))
    dk, dv = [], []
    for h in range(HEADS):
        part = slice(h * HEAD_DIM, (h + 1) * HEAD_DIM)
        key, value = k_ref[:, part], v_ref[:, part]
        do_turned = do_scr[part]
        scores = dot(key, query_turned[part]) + bias_ref[0, h].astype(F32) + mask
        probs = jnp.exp(scores - lse_ref[0, h : h + 1])
        centre = jnp.sum(do_turned * turned_ref[0, part], axis=0, keepdims=True)
        ds_full = probs * (dot(value, do_turned.astype(BF16)) - centre)
        ds = ds_full.astype(BF16)
        tiles_ref[kind, h] += ds_full
        dv.append(dot(probs.astype(BF16), do_ref[:, part]))
        dk.append(dot(ds, q_ref[:, part]))
        dq_scr[part] = dot(key_turned[part], ds)
    dq = (dq_scr[...].T * QUERY_SCALE).astype(BF16)
    dk = jnp.concatenate(dk, axis=1).astype(BF16)
    dv = jnp.concatenate(dv, axis=1).astype(BF16)
    dqkv_ref[0, :, :D] = dq
    dqkv_ref[0, :, D:] = dk[:, : D // 2]
    dqkv_ref[1, :, : D // 2] = dk[:, D // 2 :]
    dqkv_ref[1, :, D // 2 :] = dv


def attend_back(meta, query, key, value, do, turned, lse, bias):
    rows = query.shape[0]
    chunks = rows // CHUNK
    tile = pl.BlockSpec((CHUNK, D), lambda c, m: (c, 0))
    return pl.pallas_call(
        attend_back_kernel,
        grid_spec=pltpu.PrefetchScalarGridSpec(
            num_scalar_prefetch=1,
            grid=(chunks,),
            in_specs=[
                tile, tile, tile, tile,
                pl.BlockSpec((1, D, CHUNK), lambda c, m: (c, 0, 0)),
                pl.BlockSpec((1, 16, CHUNK), lambda c, m: (c, 0, 0)),
                pl.BlockSpec((1, HEADS, CHUNK, CHUNK), lambda c, m: (m[META_KIND + c], 0, 0, 0)),
            ],
            out_specs=[
                pl.BlockSpec((2, CHUNK, 3 * D // 2), lambda c, m: (0, c, 0)),
                full(2, HEADS, CHUNK, CHUNK),
            ],
            scratch_shapes=[pltpu.VMEM((D, CHUNK), F32), pltpu.VMEM((D, CHUNK), F32)],
        ),
        out_shape=[
            jax.ShapeDtypeStruct((2, rows, 3 * D // 2), BF16),
            jax.ShapeDtypeStruct((2, HEADS, CHUNK, CHUNK), F32),
        ],
        compiler_params=pltpu.CompilerParams(vmem_limit_bytes=VMEM_BIG),
        cost_estimate=pl.CostEstimate(
            flops=10 * rows * CHUNK * D * 3, bytes_accessed=30 * rows * D, transcendentals=0
        ),
        name="attend_back",
    )(meta, query, key, value, do, turned, lse, bias)


def last_kernel(
    meta, dqkv_ref, x_ref, dx_ref, vec_ref, a0, a1, b0, b1,
    out_ref, sums_ref, sums_p_ref, w_scr, sem,
):
    @pl.when(pl.program_id(0) == 0)
    def _():
        load = Load(meta, sem, w_scr)
        load.cols("a", a0, a1, 0, 0, D)
        load.cols("b", b0, b1, D, 0, D // 2)
        load.wait()
        sums_ref[...] = jnp.zeros_like(sums_ref)
        sums_p_ref[...] = jnp.zeros_like(sums_p_ref)

    dh = dot(dqkv_ref[0], w_scr[0], NT) + dot(dqkv_ref[1], w_scr[1], NT)
    for half in range(2):
        sums_p_ref[half : half + 1] += col_sum(dqkv_ref[half].astype(F32))
    scaled, spread = unit_rows(x_ref[...].astype(F32))
    sums_ref[0:1] += col_sum(dh * scaled)
    sums_ref[1:2] += col_sum(dh)
    out_ref[...] = (dx_ref[...] + unit_rows_back(dh * vec_ref[0:1], scaled, spread)).astype(BF16)


def last(meta, dqkv, tokens, dx, vec, w_in):
    rows = tokens.shape[0]
    tile = pl.BlockSpec((CHUNK, D), lambda c, m: (c, 0))
    return pl.pallas_call(
        last_kernel,
        grid_spec=pltpu.PrefetchScalarGridSpec(
            num_scalar_prefetch=1,
            grid=(rows // CHUNK,),
            in_specs=[
                pl.BlockSpec((2, CHUNK, 3 * D // 2), lambda c, m: (0, c, 0)),
                tile, tile,
                full(16, D),
                ANY, ANY, ANY, ANY,
            ],
            out_specs=[tile, full(8, D), full(2, 3 * D // 2)],
            scratch_shapes=[pltpu.VMEM((2, D, 3 * D // 2), BF16), pltpu.SemaphoreType.DMA],
        ),
        out_shape=[
            jax.ShapeDtypeStruct((rows, D), BF16),
            jax.ShapeDtypeStruct((8, D), F32),
            jax.ShapeDtypeStruct((2, 3 * D // 2), F32),
        ],
        compiler_params=pltpu.CompilerParams(vmem_limit_bytes=VMEM_BIG),
        cost_estimate=pl.CostEstimate(
            flops=2 * rows * D * 3 * D, bytes_accessed=16 * rows * D, transcendentals=0
        ),
        name="last",
    )(meta, dqkv, tokens, dx, vec, *w_in)


BAND = 384


def cols_grad_kernel(meta, left_ref, right_ref, *out_refs, parts):
    step = pl.program_id(0)
    band = dot(left_ref[...], right_ref[0], TN).astype(BF16)
    at = 0
    for (order, width), out_ref in zip(parts, out_refs):
        for i in range(BAND // ROWS_D):
            piece = meta[META_TO[order] + step * (BAND // ROWS_D) + i]
            out_ref[piece] = band[i * ROWS_D : (i + 1) * ROWS_D, at : at + width]
        at += width


def cols_grad(meta, left, right, parts, own):
    rows, width = left.shape[0], right.shape[2]
    half = (lambda i, m: (m[0], 0, 0)) if own else (lambda i, m: (1 - m[0], 0, 0))
    return pl.pallas_call(
        functools.partial(cols_grad_kernel, parts=parts),
        grid_spec=pltpu.PrefetchScalarGridSpec(
            num_scalar_prefetch=1,
            grid=(D // BAND,),
            in_specs=[
                pl.BlockSpec((rows, BAND), lambda i, m: (0, i)),
                pl.BlockSpec((1, rows, width), half),
            ],
            out_specs=[full(PIECES, ROWS_D, w) for _, w in parts],
        ),
        out_shape=[jax.ShapeDtypeStruct((PIECES, ROWS_D, w), BF16) for _, w in parts],
        compiler_params=pltpu.CompilerParams(vmem_limit_bytes=VMEM_BIG),
        cost_estimate=pl.CostEstimate(
            flops=2 * rows * D * width, bytes_accessed=2 * rows * (D + width), transcendentals=0
        ),
        name="cols_grad_own" if own else "cols_grad_other",
    )(meta, left, right)


def rows_grad_kernel(meta, left_ref, right_ref, own_ref, other_ref, *, order):
    step = pl.program_id(0)
    band = dot(left_ref[...], right_ref[...], TN).astype(BF16)
    low_core = meta[0] == 0
    for i in range(BAND // (2 * ROWS_F)):
        piece = meta[META_TO[order] + step * (BAND // (2 * ROWS_F)) + i]
        even = band[2 * i * ROWS_F : (2 * i + 1) * ROWS_F]
        odd = band[(2 * i + 1) * ROWS_F : (2 * i + 2) * ROWS_F]
        own_ref[piece] = jnp.where(low_core, even, odd)
        other_ref[piece] = jnp.where(low_core, odd, even)


def rows_grad(meta, left, right, order):
    rows = left.shape[0]
    return pl.pallas_call(
        functools.partial(rows_grad_kernel, order=order),
        grid_spec=pltpu.PrefetchScalarGridSpec(
            num_scalar_prefetch=1,
            grid=(FF // BAND,),
            in_specs=[
                pl.BlockSpec((rows, BAND), lambda i, m: (0, i)),
                pl.BlockSpec((rows, D), lambda i, m: (0, 0)),
            ],
            out_specs=[full(PIECES, ROWS_F, D)] * 2,
        ),
        out_shape=[jax.ShapeDtypeStruct((PIECES, ROWS_F, D), BF16)] * 2,
        compiler_params=pltpu.CompilerParams(vmem_limit_bytes=VMEM_BIG),
        cost_estimate=pl.CostEstimate(
            flops=2 * rows * D * FF, bytes_accessed=2 * rows * (D + FF), transcendentals=0
        ),
        name="rows_grad",
    )(meta, left, right)


def swap(values, mask, count):
    return lax.ppermute(values, AXES, [(i, i ^ mask) for i in range(count)])


def tie(values, after):
    values, after = list(values), list(after)
    if not after:
        return values
    return list(lax.optimization_barrier(tuple(values + after))[: len(values)])


class Chain:
    def __init__(self, net, steps, finish):
        self.net, self.steps, self.finish = net, list(steps), finish
        self.got = [None] * len(self.steps)
        self.sends = [[] for _ in self.steps]
        self.results = [None] * len(self.steps)

    def go(self, *after):
        for i, step in enumerate(self.steps):
            if self.results[i] is not None:
                continue
            try:
                got = self.got[i] if self.got[i] is None else tie(self.got[i], after)
                sends = step.send(got)
                values = [v for v, _ in sends]
                if got is None:
                    values = tie(values, after)
                self.sends[i] = values
                self.got[i] = [self.net.swap(v, m) for v, (_, m) in zip(values, sends)]
            except StopIteration as end:
                self.results[i] = end.value
                self.sends[i] = []
        return self

    @property
    def sent(self):
        return [v for part in self.sends for v in part]

    @property
    def received(self):
        return [v for part in self.got for v in part or []]

    def done(self, *after):
        while any(r is None for r in self.results):
            self.go(*after)
            after = ()
        return self.finish(self.results)


class Ready:
    def __init__(self, value):
        self.value, self.sent, self.received = value, [], []

    def go(self, *after):
        return self

    def done(self, *after):
        return self.value


class Cube:
    SIDES = {"a": (2, 4), "b": (4, 2)}

    def __init__(self):
        self.me = lax.axis_index(AXES).astype(jnp.int32)

    def swap(self, values, mask):
        return swap(values, mask, 32)

    def masks(self, order):
        shift = self.SIDES[order]
        return np.array(
            [8 * (k & 3) + shift[0] * (k >> 2 & 1) + shift[1] * (k >> 3) for k in range(PIECES)]
        )

    def meta(self):
        chip = self.me >> 1
        place = jnp.arange(PIECES, dtype=jnp.int32)
        start = [chip ^ jnp.asarray(self.masks(o) >> 1, jnp.int32) for o in "ab"]
        mask = chip ^ place
        x, y = mask & 1, mask >> 1 & 1
        to = [(mask >> 2) + 4 * x + 8 * y, (mask >> 2) + 4 * y + 8 * x]
        return self.me & 1, start + to

    def spread(self, piece, order):
        got = yield [(piece, 8 * z) for z in (1, 2, 3)]
        held = jnp.stack([piece] + got)
        for side in self.SIDES[order]:
            (got,) = yield [(held, side)]
            held = jnp.concatenate([held, got])
        (got,) = yield [(held, 1)]
        return [held, got]

    def gather_cols(self, shards, parts):
        left, right = (
            jnp.concatenate([h[side] for h in (jnp.split(s, 2, axis=1) for s in shards)], axis=1)
            for side in (0, 1)
        )
        odd = (self.me & 1) == 1
        got = self.swap(jnp.where(odd, left, right), 1)
        mine = jnp.where(odd, right, left)
        block = jnp.where(odd, jnp.concatenate([got, mine]), jnp.concatenate([mine, got]))
        steps, at = [], 0
        for order, width in parts:
            steps.append(self.spread(block[:, at : at + width], order))
            at += width
        return Chain(self, steps, lambda parts: [v for pair in parts for v in pair])

    def gather_small(self, pack):
        every = jnp.broadcast_to(pack, (32, pack.shape[0]))
        return lax.all_to_all(every, AXES, 0, 0, tiled=True)

    def reduce_small(self, pack):
        return jnp.sum(lax.all_to_all(pack, AXES, 0, 0, tiled=True), axis=0)

    def gather_rows(self, shard, order):
        return Chain(self, [self.spread(shard, order)], lambda parts: parts[0])

    def reduce_pieces(self, own, other, order):
        (got,) = yield [(other, 1)]
        total = own.astype(F32) + got.astype(F32)
        for side in self.SIDES[order][::-1]:
            count = total.shape[0] // 2
            (got,) = yield [(total[count:].astype(BF16), side)]
            total = total[:count] + got.astype(F32)
        got = yield [(total[z].astype(BF16), 8 * z) for z in (1, 2, 3)]
        return total[0] + sum(g.astype(F32) for g in got)

    def join_cols(self, sums):
        block = sums[0] if len(sums) == 1 else jnp.concatenate(sums, axis=1)
        rows = block.shape[0] // 2
        low, high = block[:rows], block[rows:]
        odd = (self.me & 1) == 1
        got = self.swap(jnp.where(odd, low, high), 1)
        mine = jnp.where(odd, high, low)
        return jnp.where(
            odd, jnp.concatenate([got, mine], axis=1), jnp.concatenate([mine, got], axis=1)
        )

    def reduce_cols(self, own, other, parts):
        steps = [self.reduce_pieces(*pair, order) for *pair, (order, _) in zip(own, other, parts)]
        return Chain(self, steps, self.join_cols)

    def reduce_rows(self, own, other, order):
        return Chain(self, [self.reduce_pieces(own, other, order)], lambda sums: sums[0])


class Plain:
    def __init__(self, count):
        self.count = count
        self.me = lax.axis_index(AXES)

    def meta(self):
        place = jnp.arange(PIECES, dtype=jnp.int32)
        return jnp.int32(0), [place] * 4

    def gather_cols(self, shards, parts):
        whole = [lax.all_gather(s, AXES, axis=0, tiled=True) for s in shards]
        left, right = (
            jnp.concatenate([h[side] for h in (jnp.split(w, 2, axis=1) for w in whole)], axis=1)
            for side in (0, 1)
        )
        out, at = [], 0
        for _, width in parts:
            for half in (left, right):
                out.append(half[:, at : at + width].reshape(PIECES, -1, width))
            at += width
        return Ready(out)

    def gather_small(self, pack):
        return lax.all_gather(pack, AXES)

    def reduce_small(self, pack):
        return lax.psum_scatter(pack, AXES, scatter_dimension=0, tiled=False)

    def gather_rows(self, shard, order):
        whole = lax.all_gather(shard, AXES, axis=0, tiled=True)
        whole = whole.reshape(PIECES, 2, -1, whole.shape[1])
        return Ready([whole[:, 0], whole[:, 1]])

    def reduce_cols(self, own, other, parts):
        whole = jnp.concatenate([p.reshape(-1, p.shape[2]) for p in (*own, *other)], axis=1)
        return Ready(lax.psum_scatter(whole.astype(F32), AXES, scatter_dimension=0, tiled=True))

    def reduce_rows(self, own, other, order):
        whole = jnp.stack([own, other], axis=1).reshape(-1, own.shape[2])
        return Ready(lax.psum_scatter(whole.astype(F32), AXES, scatter_dimension=0, tiled=True))


PARTS_ATTN = (("a", D), ("b", D))
PARTS_IN = (("a", 640), ("b", 512))
PARTS_OUT = (("a", D // 2),)
PARTS_FF = (("a", FF // 2),)


def body(
    tokens,
    cotangent,
    w_attn_in,
    w_attn_out,
    w_fc_in,
    w_fc_out,
    gains_d,
    biases_d,
    gains_ff,
    biases_ff,
    rel_table,
    head_scale,
    bucket,
    lengths,
    *,
    count,
    cube,
):
    net = Cube() if cube else Plain(count)
    rows = tokens.shape[0]
    chunks = rows // CHUNK

    gather_attn = net.gather_cols([w_attn_in, w_attn_out], PARTS_ATTN).go()
    small = (gains_d, biases_d, gains_ff[None], biases_ff, rel_table)
    sizes = [v.size for v in small]
    ends = np.cumsum(sizes)
    width = -(-int(ends[-1] + 16) // 1024) * 1024
    pack = jnp.concatenate([v.reshape(-1) for v in small] + [jnp.zeros(width - ends[-1], BF16)])
    (pack,) = tie([pack], gather_attn.sent)
    packs = net.gather_small(pack)

    large = jnp.sum((bucket == 1).astype(jnp.int32), dtype=jnp.int32)
    kinds = (jnp.arange(chunks, dtype=jnp.int32) >= large).astype(jnp.int32)
    core, tables = net.meta()
    meta = jnp.concatenate(
        [core.astype(jnp.int32)[None], kinds, large[None], jnp.zeros(2, jnp.int32), *tables, lengths]
    )
    keys, keys_back, queries = (jnp.asarray(t) for t in pick_tables())

    arrived = gather_attn.received
    gather_attn.go()
    gather_ff = net.gather_cols([w_fc_in], PARTS_FF)
    gather_down = net.gather_rows(w_fc_out, "b")
    rest = (gather_ff, gather_down)
    (packs,) = tie([packs], gather_attn.sent)
    vec, wide, bias = prepare(packs, head_scale[None], keys, queries, count)
    gather_ff.go(*arrived)
    gather_down.go(vec)
    gather_attn.go(vec)
    a0, a1, b0, b1 = gather_attn.done()
    attn_pieces = (a0, a1, b0, b1)

    for chain in rest:
        chain.go()
    (tokens_in,) = tie([tokens], [v for chain in rest for v in chain.sent])
    low_in, query, key, value, mixed, turned, lse = attend(meta, tokens_in, vec, attn_pieces, bias)
    ff_pieces, down_pieces = (chain.done(lse) for chain in rest)
    out_tokens, mid, low_attn, low_mid, low_ff, dz, df, sums_a, sums_ff = feed(
        meta, tokens, mixed, cotangent, vec, wide, (b0, b1), ff_pieces, down_pieces
    )

    other = cols_grad(meta, low_mid, dz, PARTS_FF, False)
    (left,) = tie([low_mid], other)
    own = cols_grad(meta, left, dz, PARTS_FF, True)
    reduce_ff = net.reduce_cols(own, other, PARTS_FF).go()
    (left,) = tie([low_ff], own)
    own, other = rows_grad(meta, left, df, "b")
    reduce_down = net.reduce_rows(own, other, "b").go()
    reduce_ff.go(own)

    (dz,) = tie([dz], reduce_ff.sent + reduce_down.sent)
    da, dx, do, sums_b = middle(meta, dz, mid, mixed, cotangent, vec, ff_pieces, (b0, b1))
    reduce_down.go(sums_b)
    reduce_ff.go(sums_b)
    (left,) = tie([low_attn], reduce_ff.sent + reduce_down.sent)
    other, own = (cols_grad(meta, left, da, PARTS_OUT, side) for side in (False, True))
    reduce_out = net.reduce_cols(own, other, PARTS_OUT).go()
    (do,) = tie([do], reduce_out.sent)
    dqkv, tiles = attend_back(meta, query, key, value, do, turned, lse, bias)
    for chain in (reduce_out, reduce_down, reduce_ff):
        chain.go(tiles)
    (left,) = tie([low_in], reduce_out.sent + reduce_down.sent + reduce_ff.sent)
    other = cols_grad(meta, left, dqkv, PARTS_IN, False)
    (left,) = tie([low_in], other)
    own = cols_grad(meta, left, dqkv, PARTS_IN, True)
    reduce_in = net.reduce_cols(own, other, PARTS_IN).go()
    for chain in (reduce_out, reduce_down):
        chain.go(*own)
    (tiles,) = tie([tiles], reduce_in.sent + reduce_out.sent + reduce_down.sent)
    grad_table = table_grads(tiles, keys_back, queries)
    for chain in (reduce_in, reduce_out):
        chain.go(grad_table)
    (dqkv,) = tie([dqkv], reduce_in.sent + reduce_out.sent)
    grad_tokens, sums_c, sums_p = last(meta, dqkv, tokens, dx, vec, attn_pieces)
    reduce_in.go(sums_c)
    terms = (sums_a, sums_b, sums_c, sums_p, sums_ff, grad_table)
    terms = pack_terms(*tie(terms, reduce_in.sent), count, width)
    reduce_in.go(terms)
    (terms,) = tie([terms], reduce_in.sent)
    mine = net.reduce_small(terms)
    grad_fc_out = reduce_down.done()
    grad_fc_in = reduce_ff.done()
    grad_attn_out = reduce_out.done()
    grad_attn_in = reduce_in.done(mine)

    grads = [mine[end - size : end].reshape(v.shape) for v, size, end in zip(small, sizes, ends)]
    return (
        out_tokens,
        grad_tokens,
        grad_attn_in,
        grad_attn_out,
        grad_fc_in,
        grad_fc_out,
        grads[0],
        grads[1],
        grads[2][0],
        grads[3],
        grads[4],
        mine[ends[-1] : ends[-1] + HEADS],
    )


def solution(mesh):
    rows = P(AXES, None)
    columns = P(None, AXES)
    line = P(AXES)
    count = mesh.shape["wide"] * mesh.shape["narrow"]
    cube = (mesh.shape["wide"], mesh.shape["narrow"]) == (8, 4)
    return jax.shard_map(
        functools.partial(body, count=count, cube=cube),
        mesh=mesh,
        in_specs=(
            rows, rows, rows, rows, rows, rows,
            columns, columns, line, columns, columns, P(), line, line,
        ),
        out_specs=(
            rows, rows, rows, rows, rows, rows,
            columns, columns, line, columns, columns, P(),
        ),
        check_vma=False,
    )
```

```python
import functools

import jax
import jax.numpy as jnp
import numpy as np
from jax import lax
from jax.experimental import pallas as pl
from jax.experimental.pallas import tpu as pltpu
from jax.sharding import PartitionSpec as P

HEADS = 12
HEAD_DIM = 64
D = 768
FF = 3072
GRID_L = 15
GRID_S = 8
SLOT_L = 256
SLOT_S = 64
STRIDE = 32
RELS = 1024
CHUNK = 256
PIECES = 16
ROWS_D = D // PIECES
ROWS_F = FF // (2 * PIECES)

NEG_FILL = -1e30
NORM_EPS = 1e-05
HALF_ROOT = 0.7071067811865476
DENSITY_SCALE = 0.3989422804014327
QUERY_SCALE = 0.125
AXES = ("wide", "narrow")
F32 = jnp.float32
BF16 = jnp.bfloat16
VMEM_BIG = 60 * 2**20

NN = (((1,), (0,)), ((), ()))
NT = (((1,), (1,)), ((), ()))
TN = (((0,), (0,)), ((), ()))


ANY = pl.BlockSpec(memory_space=pl.ANY)


def full(*shape):
    return pl.BlockSpec(shape, lambda *_: (0,) * len(shape))


def dot(left, right, dims=NN):
    return lax.dot_general(left, right, dims, preferred_element_type=F32)


def unit_rows(values):
    center = values - jnp.mean(values, axis=-1, keepdims=True)
    spread = lax.rsqrt(jnp.mean(center * center, axis=-1, keepdims=True) + NORM_EPS)
    return center * spread, spread


def unit_rows_back(inner, scaled, spread):
    return spread * (
        inner
        - jnp.mean(inner, axis=-1, keepdims=True)
        - scaled * jnp.mean(inner * scaled, axis=-1, keepdims=True)
    )


def col_sum(values):
    return jnp.sum(values, axis=0, keepdims=True)


def unit_position(kind):
    place = np.arange(CHUNK)
    if kind == 0:
        return np.minimum(place // GRID_L, GRID_L - 1), place % GRID_L
    inner = place % SLOT_S
    return inner // GRID_S, inner % GRID_S


def pick_tables():
    keys = np.zeros((2, CHUNK, 512), np.float32)
    keys_back = np.zeros((2, CHUNK, 512), np.float32)
    queries = np.zeros((2, CHUNK, CHUNK), np.float32)
    for kind in range(2):
        row, col = unit_position(kind)
        line = STRIDE * row + col
        keys[kind, np.arange(CHUNK), line] = 1
        keys_back[kind, np.arange(CHUNK), 511 - line] = 1
        queries[kind, 16 * row + col, np.arange(CHUNK)] = 1
    return keys.astype(BF16), keys_back.astype(BF16), queries.astype(BF16)


def owner_of_lane(lanes, each, last=None):
    lane = lax.broadcasted_iota(jnp.int32, lanes, 1)
    entry = lane if last is None else last - lane
    device = lax.broadcasted_iota(jnp.int32, lanes, 0)
    return ((entry >= device * each) & (entry < device * each + each)).astype(BF16)


def place_in_part(lanes, each, last=None):
    lane = lax.broadcasted_iota(jnp.int32, lanes, 1)
    entry = lane if last is None else last - lane
    row = lax.broadcasted_iota(jnp.int32, lanes, 0)
    return ((entry >= 0) & (lax.rem(entry + each, each) == row)).astype(F32)


def unpack_kernel(pack_ref, scale_ref, vec_ref, wide_ref, line_ref, *, count):
    each_d, each_f, each_t = D // count, FF // count, RELS // count
    pack = pack_ref[...]

    def rows(start, amount, each, lanes, last=None):
        owner = owner_of_lane((count, lanes), each, last)
        place = place_in_part((each, lanes), each, last)
        part = pack[:, start : start + amount * each]
        spread = dot(part, owner, TN)
        return [col_sum(spread[r * each : r * each + each] * place) for r in range(amount)]

    d_rows = rows(0, 10, each_d, D)
    ff_rows = rows(10 * each_d, 3, each_f, FF)
    lines = rows(10 * each_d + 3 * each_f, HEADS, each_t, RELS, 1006)
    lane = lax.broadcasted_iota(jnp.int32, (HEADS, D), 1)
    row = lax.broadcasted_iota(jnp.int32, (HEADS, D), 0)
    heads = dot(scale_ref[...], (lane // HEAD_DIM == row).astype(BF16))
    vec_ref[...] = jnp.concatenate(d_rows + [heads, jnp.zeros((5, D), F32)], axis=0)
    wide_ref[...] = jnp.concatenate(ff_rows + [jnp.zeros((5, FF), F32)], axis=0)
    for h in range(HEADS):
        line_ref[h] = jnp.broadcast_to(lines[h], (16, RELS))


def unpack(pack, scale, count):
    return pl.pallas_call(
        functools.partial(unpack_kernel, count=count),
        out_shape=[
            jax.ShapeDtypeStruct((16, D), F32),
            jax.ShapeDtypeStruct((8, FF), F32),
            jax.ShapeDtypeStruct((HEADS, 16, RELS), F32),
        ],
        compiler_params=pltpu.CompilerParams(vmem_limit_bytes=VMEM_BIG),
        cost_estimate=pl.CostEstimate(flops=2 * 10**9, bytes_accessed=4 * 10**6, transcendentals=0),
        name="unpack",
    )(pack, scale)


TURN = 4


def bias_kernel(line_ref, keys_ref, queries_ref, out_ref):
    left = lax.broadcasted_iota(jnp.int32, (CHUNK, CHUNK), 0) // SLOT_S
    right = lax.broadcasted_iota(jnp.int32, (CHUNK, CHUNK), 1) // SLOT_S
    spread_rows = []
    for h in range(TURN):
        base = pltpu.roll(line_ref[h], RELS - 511, 1, stride=1, stride_axis=0)
        turns = [base] + [pltpu.roll(base, STRIDE * m, 1) for m in (1, 2, 3)]
        twice = [jnp.concatenate([t, t[:, :512]], axis=1) for t in turns]
        groups = []
        for r in range(16):
            start = (RELS - 128 * (r // 4)) % RELS
            groups.append(twice[r % 4][:, start : start + 512])
        spread_rows.append(jnp.concatenate(groups, axis=0).astype(BF16))
    by_key = [
        (dot(keys_ref[0], g, NT).astype(BF16), dot(keys_ref[1, :SLOT_S], g, NT).astype(BF16))
        for g in spread_rows
    ]
    for h in range(TURN):
        out_ref[0, h] = dot(by_key[h][0], queries_ref[0]).astype(BF16)
        tile = dot(by_key[h][1], queries_ref[1])
        tile = jnp.concatenate([tile] * (CHUNK // SLOT_S), axis=0)
        out_ref[1, h] = jnp.where(left == right, tile, NEG_FILL).astype(BF16)


def build_bias(lines, keys, queries):
    return pl.pallas_call(
        bias_kernel,
        grid=(HEADS // TURN,),
        in_specs=[
            pl.BlockSpec((TURN, 16, RELS), lambda h: (h, 0, 0)),
            full(2, CHUNK, 512),
            full(2, CHUNK, CHUNK),
        ],
        out_specs=pl.BlockSpec((2, TURN, CHUNK, CHUNK), lambda h: (0, h, 0, 0)),
        out_shape=jax.ShapeDtypeStruct((2, HEADS, CHUNK, CHUNK), BF16),
        compiler_params=pltpu.CompilerParams(vmem_limit_bytes=VMEM_BIG),
        cost_estimate=pl.CostEstimate(flops=8 * 10**9, bytes_accessed=4 * 10**6, transcendentals=0),
        name="bias_tiles",
    )(lines, keys, queries)


def pack_kernel(a_ref, b_ref, c_ref, p_ref, ff_ref, table_ref, out_ref, *, count):
    each_d, each_f, each_t = D // count, FF // count, RELS // count

    def columns(rows, each, lanes):
        owner = owner_of_lane((count, lanes), each)
        place = place_in_part((each, lanes), each)
        parts = []
        for row in rows:
            high, rest = halves(row * place)
            parts.append(dot(high, owner, NT) + dot(rest, owner, NT))
        return jnp.concatenate(parts, axis=0)

    a, b, c = a_ref[...], b_ref[...], c_ref[...]
    p = p_ref[...]
    d_rows = [
        c[0:1], b[3:4], b[0:1],
        c[1:2], p[0:1, :D], p[1:2, D // 2 :], b[4:5], b[2:3], b[1:2], a[0:1],
    ]
    ff = ff_ref[...]
    lane = lax.broadcasted_iota(jnp.int32, (16, D), 1)
    row = lax.broadcasted_iota(jnp.int32, (16, D), 0)
    high, rest = halves(jnp.broadcast_to(b[5:6], (16, D)) * (lane // HEAD_DIM == row).astype(F32))
    ones = jnp.ones((count, D), BF16)
    out = [
        columns(d_rows, each_d, D),
        columns([ff[0:1], ff[2:3], ff[1:2]], each_f, FF),
        columns([table_ref[h, 0:1] for h in range(HEADS)], each_t, RELS),
        dot(high, ones, NT) + dot(rest, ones, NT),
    ]
    used = sum(o.shape[0] for o in out)
    out.append(jnp.zeros((out_ref.shape[1] - used, count), F32))
    out_ref[...] = jnp.concatenate(out, axis=0).T


def pack_terms(sums_a, sums_b, sums_c, sums_p, sums_ff, table, count, width):
    return pl.pallas_call(
        functools.partial(pack_kernel, count=count),
        out_shape=jax.ShapeDtypeStruct((count, width), F32),
        compiler_params=pltpu.CompilerParams(vmem_limit_bytes=VMEM_BIG),
        cost_estimate=pl.CostEstimate(flops=10**9, bytes_accessed=10**6, transcendentals=0),
        name="pack_terms",
    )(sums_a, sums_b, sums_c, sums_p, sums_ff, table)


def halves(values):
    high = values.astype(BF16)
    return high, (values - high.astype(F32)).astype(BF16)


def table_kernel(tiles_ref, keys_ref, queries_ref, out_ref):
    by_query = []
    for h in range(TURN):
        small = tiles_ref[1, h, :SLOT_S]
        for part in range(1, CHUNK // SLOT_S):
            small = small + tiles_ref[1, h, part * SLOT_S : (part + 1) * SLOT_S]
        by_query.append(
            (
                dot(queries_ref[0], tiles_ref[0, h].astype(BF16), NT).astype(BF16),
                dot(queries_ref[1], small.astype(BF16), NT).astype(BF16),
            )
        )
    totals = [
        dot(large, keys_ref[0]) + dot(small, keys_ref[1, :SLOT_S]) for large, small in by_query
    ]
    for h, total in enumerate(totals):
        line = jnp.zeros((16, RELS), F32)
        for m in range(4):
            part = jnp.zeros((16, RELS), F32)
            for k in range(4):
                group = total[16 * (4 * k + m) : 16 * (4 * k + m) + 16]
                pieces = [group, jnp.zeros((16, 512 - 128 * k), F32)]
                if k:
                    pieces = [jnp.zeros((16, 128 * k), F32)] + pieces
                part += jnp.concatenate(pieces, axis=1)
            line += pltpu.roll(part, STRIDE * m, 1) if m else part
        line = pltpu.roll(line, 0, 1, stride=1, stride_axis=0)
        out_ref[h] = pltpu.roll(jnp.broadcast_to(col_sum(line), (8, RELS)), RELS - 16, 1)


def table_grads(tiles, keys_back, queries):
    return pl.pallas_call(
        table_kernel,
        grid=(HEADS // TURN,),
        in_specs=[
            pl.BlockSpec((2, TURN, CHUNK, CHUNK), lambda h: (0, h, 0, 0)),
            full(2, CHUNK, 512),
            full(2, CHUNK, CHUNK),
        ],
        out_specs=pl.BlockSpec((TURN, 8, RELS), lambda h: (h, 0, 0)),
        out_shape=jax.ShapeDtypeStruct((HEADS, 8, RELS), F32),
        compiler_params=pltpu.CompilerParams(vmem_limit_bytes=VMEM_BIG),
        cost_estimate=pl.CostEstimate(flops=8 * 10**9, bytes_accessed=6 * 10**6, transcendentals=0),
        name="table_grads",
    )(tiles, keys_back, queries)


META_KIND = 1
META_LARGE = 5
META_LENGTH = 72
META_FROM = {"a": 8, "b": 24}
META_TO = {"a": 40, "b": 56}


def live_rows(meta, chunk):
    place = lax.broadcasted_iota(jnp.int32, (CHUNK, 1), 0)
    large = meta[META_LARGE]
    first = large + (chunk - large) * (SLOT_L // SLOT_S)
    is_large = chunk < large
    end = jnp.zeros((CHUNK, 1), jnp.int32)
    for part in range(SLOT_L // SLOT_S):
        slot = jnp.where(is_large, chunk, first + part)
        start = jnp.where(is_large, 0, part * SLOT_S)
        end = jnp.where(place >= part * SLOT_S, start + meta[META_LENGTH + slot], end)
    return (place < end).astype(F32)


class Load:
    def __init__(self, meta, sem, scratch):
        self.meta, self.sem, self.scratch = meta, sem, scratch

    def cols(self, order, own, other, start, source_start, width):
        core, rows = self.meta[0], own.shape[1]
        for k in range(PIECES):
            place = pl.multiple_of(self.meta[META_FROM[order] + k] * rows, 16)
            for half, source in ((core, own), (1 - core, other)):
                pltpu.make_async_copy(
                    source.at[k, :, pl.ds(source_start, width)],
                    self.scratch.at[half, pl.ds(place, rows), pl.ds(start, width)],
                    self.sem,
                ).start()

    def rows(self, order, own, other, start):
        core, rows, width = self.meta[0], own.shape[1], own.shape[2]
        for k in range(PIECES):
            chip = self.meta[META_FROM[order] + k]
            for half, source in ((core, own), (1 - core, other)):
                place = pl.multiple_of((2 * chip + half) * rows, 16)
                pltpu.make_async_copy(
                    source.at[k],
                    self.scratch.at[pl.ds(place, rows), pl.ds(start, width)],
                    self.sem,
                ).start()

    def wait(self):
        pltpu.make_async_copy(self.scratch, self.scratch, self.sem).wait()


def project_kernel(meta, x_ref, vec_ref, a0, a1, b0, b1, low_ref, q_ref, k_ref, v_ref, w_scr, sem):
    @pl.when(pl.program_id(0) == 0)
    def _():
        load = Load(meta, sem, w_scr)
        load.cols("a", a0, a1, 0, 0, D)
        load.cols("b", b0, b1, D, 0, D // 2)
        load.wait()

    scaled, _ = unit_rows(x_ref[...].astype(F32))
    low = (scaled * vec_ref[0:1] + vec_ref[3:4]).astype(BF16)
    low_ref[...] = low
    first = dot(low, w_scr[0])
    second = dot(low, w_scr[1])
    q_ref[...] = ((first[:, :D] + vec_ref[4:5]) * QUERY_SCALE).astype(BF16)
    k_ref[:, : D // 2] = first[:, D:].astype(BF16)
    k_ref[:, D // 2 :] = second[:, : D // 2].astype(BF16)
    v_ref[...] = (second[:, D // 2 :] + vec_ref[5:6]).astype(BF16)


def project(meta, tokens, vec, pieces):
    rows = tokens.shape[0]
    tile = pl.BlockSpec((CHUNK, D), lambda c, m: (c, 0))
    return pl.pallas_call(
        project_kernel,
        grid_spec=pltpu.PrefetchScalarGridSpec(
            num_scalar_prefetch=1,
            grid=(rows // CHUNK,),
            in_specs=[tile, full(16, D), ANY, ANY, ANY, ANY],
            out_specs=[tile] * 4,
            scratch_shapes=[pltpu.VMEM((2, D, 3 * D // 2), BF16), pltpu.SemaphoreType.DMA],
        ),
        out_shape=[jax.ShapeDtypeStruct((rows, D), BF16)] * 4,
        compiler_params=pltpu.CompilerParams(vmem_limit_bytes=VMEM_BIG),
        cost_estimate=pl.CostEstimate(
            flops=2 * rows * D * 3 * D, bytes_accessed=16 * rows * D, transcendentals=0
        ),
        name="project",
    )(meta, tokens, vec, *pieces)


def attend_kernel(meta, q_ref, k_ref, v_ref, bias_ref, *refs, first):
    mixed_ref, turned_ref, lse_ref = refs[-3:]
    mask = (1.0 - live_rows(meta, pl.program_id(0) + first)) * NEG_FILL
    mask = jnp.broadcast_to(mask, (CHUNK, CHUNK))
    query_turned = q_ref[...].astype(F32).T.astype(BF16)
    value_turned = v_ref[...].astype(F32).T.astype(BF16)
    sums = []
    for h in range(HEADS):
        part = slice(h * HEAD_DIM, (h + 1) * HEAD_DIM)
        scores = dot(k_ref[:, part], query_turned[part]) + bias_ref[0, h].astype(F32) + mask
        largest = jnp.max(scores, axis=0, keepdims=True)
        exponent = jnp.exp(scores - largest)
        row_total = jnp.sum(exponent, axis=0, keepdims=True)
        out = dot(value_turned[part], exponent.astype(BF16))
        turned_ref[0, part] = out * (1.0 / row_total)
        sums.append(largest + jnp.log(row_total))
    lse_ref[0] = jnp.concatenate(sums + [jnp.zeros((16 - HEADS, CHUNK), F32)], axis=0)
    mixed_ref[...] = turned_ref[0].T


def attend(meta, query, key, value, bias, first, chunks, before=()):
    rows = query.shape[0]
    tile = pl.BlockSpec((CHUNK, D), lambda c, m: (c + first, 0))
    return pl.pallas_call(
        functools.partial(attend_kernel, first=first),
        grid_spec=pltpu.PrefetchScalarGridSpec(
            num_scalar_prefetch=1,
            grid=(chunks,),
            in_specs=[
                tile, tile, tile,
                pl.BlockSpec(
                    (1, HEADS, CHUNK, CHUNK), lambda c, m: (m[META_KIND + c + first], 0, 0, 0)
                ),
            ]
            + [ANY] * len(before),
            out_specs=[
                tile,
                pl.BlockSpec((1, D, CHUNK), lambda c, m: (c + first, 0, 0)),
                pl.BlockSpec((1, 16, CHUNK), lambda c, m: (c + first, 0, 0)),
            ],
        ),
        out_shape=[
            jax.ShapeDtypeStruct((rows, D), F32),
            jax.ShapeDtypeStruct((rows // CHUNK, D, CHUNK), F32),
            jax.ShapeDtypeStruct((rows // CHUNK, 16, CHUNK), F32),
        ],
        input_output_aliases={5 + i: i for i in range(len(before))},
        compiler_params=pltpu.CompilerParams(vmem_limit_bytes=VMEM_BIG),
        cost_estimate=pl.CostEstimate(
            flops=10 * 10**9, bytes_accessed=16 * rows * D, transcendentals=0
        ),
        name="attend",
    )(meta, query, key, value, bias, *before)


CUT = 512
ROOT_PART = 0.3275911 * HALF_ROOT
TAIL = (0.127414796, -0.142248368, 0.7107068705, -0.7265760135, 0.5307027145)


def normal_parts(z):
    density = jnp.exp(-0.5 * z * z)
    t = 1.0 / (1.0 + ROOT_PART * jnp.abs(z))
    tail = TAIL[4] * t + TAIL[3]
    for c in (TAIL[2], TAIL[1], TAIL[0]):
        tail = tail * t + c
    tail = tail * t * density
    return jnp.where(z >= 0.0, 1.0 - tail, tail), z * (DENSITY_SCALE * density)


def lane_sum(values):
    return jnp.sum(values, axis=-1, keepdims=True)


def feed_kernel(
    meta, x_ref, mixed_ref, cot_ref, vec_ref, wide_ref,
    o0, o1, i0, i1, i2, i3, f0, f1, f2, f3,
    out_ref, mid_ref, aln_ref, low_ref, m_ref, dz_ref, df_ref, sums_ref, sums_ff_ref,
    wo_scr, wi_scr, wf_scr, unit_scr, slope_scr, dm_scr, sems,
):
    step = pl.program_id(0)

    def feed_loads():
        return [Load(meta, sems.at[i], s) for i, s in enumerate((wo_scr, wi_scr, wf_scr))]

    def arrived(which):
        @pl.when(step == 0)
        def _():
            feed_loads()[which].wait()

    @pl.when(step == 0)
    def _():
        loads = feed_loads()
        loads[0].cols("b", o0, o1, 0, D // 2, D // 2)
        loads[1].cols("a", i0, i1, 0, 0, FF // 4)
        loads[1].cols("b", i2, i3, FF // 4, 0, FF // 4)
        loads[2].rows("a", f0, f1, 0)
        loads[2].rows("b", f2, f3, D // 2)
        sums_ref[...] = jnp.zeros_like(sums_ref)
        sums_ff_ref[...] = jnp.zeros_like(sums_ff_ref)

    live = live_rows(meta, step)
    df_full = cot_ref[...].astype(F32) * live
    df = df_full.astype(BF16)
    df_ref[...] = df
    sums_ref[0:1] += col_sum(df_full)
    scaled, _ = unit_rows(mixed_ref[...] * vec_ref[10:11])
    aln = (scaled * vec_ref[1:2] + vec_ref[6:7]).astype(BF16)
    aln_ref[...] = aln
    arrived(0)
    branch = jnp.concatenate([dot(aln, wo_scr[0]), dot(aln, wo_scr[1])], axis=1)
    mid = x_ref[...].astype(F32) + branch + vec_ref[7:8]
    mid_ref[...] = mid
    scaled, _ = unit_rows(mid)
    low = (scaled * vec_ref[2:3] + vec_ref[8:9]).astype(BF16)
    low_ref[...] = low
    arrived(1)

    cuts = [slice(a, a + CUT) for a in range(0, FF, CUT)]
    inner = [(a * CUT // (FF // 2), slice(a * CUT % (FF // 2), a * CUT % (FF // 2) + CUT)) for a in range(FF // CUT)]
    total = jnp.zeros((CHUNK, 1), F32)
    for cut, (half, part) in zip(cuts, inner):
        z = dot(low, wi_scr[half, :, part]) + wide_ref[1:2, cut]
        cumulative, rest = normal_parts(z)
        act = z * cumulative
        unit_scr[:, cut] = act
        slope_scr[:, cut] = cumulative + rest
        total += lane_sum(act)
    mean = total * (1.0 / FF)
    square = jnp.zeros((CHUNK, 1), F32)
    arrived(2)
    for cut in cuts:
        dm_scr[:, cut] = dot(df, wf_scr[cut], NT)
        center = unit_scr[:, cut] - mean
        square += lane_sum(center * center)
    spread = lax.rsqrt(square * (1.0 / FF) + NORM_EPS)
    out = mid + vec_ref[9:10]
    first = jnp.zeros((CHUNK, 1), F32)
    second = jnp.zeros((CHUNK, 1), F32)
    for cut in cuts:
        unit = (unit_scr[:, cut] - mean) * spread
        unit_scr[:, cut] = unit
        m = (unit * wide_ref[0:1, cut] + wide_ref[2:3, cut]).astype(BF16)
        m_ref[:, cut] = m
        out += dot(m, wf_scr[cut])
        dm = dm_scr[:, cut]
        sums_ff_ref[0:1, cut] += col_sum(dm * unit)
        sums_ff_ref[1:2, cut] += col_sum(dm)
        inside = dm * wide_ref[0:1, cut]
        first += lane_sum(inside)
        second += lane_sum(inside * unit)
    out_ref[...] = (out * live).astype(BF16)
    first = first * (1.0 / FF)
    second = second * (1.0 / FF)
    for cut, (half, part) in zip(cuts, inner):
        inside = dm_scr[:, cut] * wide_ref[0:1, cut]
        du = spread * (inside - first - unit_scr[:, cut] * second)
        dz_full = du * slope_scr[:, cut]
        sums_ff_ref[2:3, cut] += col_sum(dz_full)
        dz_ref[half, :, part] = dz_full.astype(BF16)


def feed(meta, tokens, mixed, cot, vec, wide, w_out, w_in, w_down):
    rows = tokens.shape[0]
    tile = pl.BlockSpec((CHUNK, D), lambda c, m: (c, 0))
    return pl.pallas_call(
        feed_kernel,
        grid_spec=pltpu.PrefetchScalarGridSpec(
            num_scalar_prefetch=1,
            grid=(rows // CHUNK,),
            in_specs=[
                tile, tile, tile,
                full(16, D), full(8, FF),
                *[ANY] * 10,
            ],
            out_specs=[
                tile, tile, tile, tile,
                pl.BlockSpec((CHUNK, FF), lambda c, m: (c, 0)),
                pl.BlockSpec((2, CHUNK, FF // 2), lambda c, m: (0, c, 0)),
                tile,
                full(8, D),
                full(3, FF),
            ],
            scratch_shapes=[
                pltpu.VMEM((2, D, D // 2), BF16),
                pltpu.VMEM((2, D, FF // 2), BF16),
                pltpu.VMEM((FF, D), BF16),
                pltpu.VMEM((CHUNK, FF), F32),
                pltpu.VMEM((CHUNK, FF), F32),
                pltpu.VMEM((CHUNK, FF), F32),
                pltpu.SemaphoreType.DMA((3,)),
            ],
        ),
        out_shape=[
            jax.ShapeDtypeStruct((rows, D), BF16),
            jax.ShapeDtypeStruct((rows, D), F32),
            jax.ShapeDtypeStruct((rows, D), BF16),
            jax.ShapeDtypeStruct((rows, D), BF16),
            jax.ShapeDtypeStruct((rows, FF), BF16),
            jax.ShapeDtypeStruct((2, rows, FF // 2), BF16),
            jax.ShapeDtypeStruct((rows, D), BF16),
            jax.ShapeDtypeStruct((8, D), F32),
            jax.ShapeDtypeStruct((3, FF), F32),
        ],
        compiler_params=pltpu.CompilerParams(vmem_limit_bytes=VMEM_BIG),
        cost_estimate=pl.CostEstimate(
            flops=2 * rows * D * (D + 3 * FF), bytes_accessed=40 * rows * D, transcendentals=0
        ),
        name="feed",
    )(meta, tokens, mixed, cot, vec, wide, *w_out, *w_in, *w_down)


PART = 256


def middle_kernel(
    meta, dz_ref, mid_ref, mixed_ref, cot_ref, vec_ref, i0, i1, i2, i3, o0, o1,
    da_ref, dx_ref, do_ref, sums_ref, wi_scr, wo_scr, sems,
):
    @pl.when(pl.program_id(0) == 0)
    def _():
        loads = [Load(meta, sems.at[i], s) for i, s in enumerate((wi_scr, wo_scr))]
        loads[0].cols("a", i0, i1, 0, 0, FF // 4)
        loads[0].cols("b", i2, i3, FF // 4, 0, FF // 4)
        loads[1].cols("b", o0, o1, 0, D // 2, D // 2)
        for load in loads:
            load.wait()
        sums_ref[...] = jnp.zeros_like(sums_ref)

    parts = [slice(a, a + PART) for a in range(0, CHUNK, PART)]
    live = live_rows(meta, pl.program_id(0))
    dhs = [dot(dz_ref[0, p], wi_scr[0], NT) + dot(dz_ref[1, p], wi_scr[1], NT) for p in parts]
    sums = [jnp.zeros((1, D), F32)] * 6
    dns = []
    for p, dh in zip(parts, dhs):
        scaled, spread = unit_rows(mid_ref[p])
        sums[0] += col_sum(dh * scaled)
        sums[1] += col_sum(dh)
        dx = cot_ref[p].astype(F32) * live[p] + unit_rows_back(dh * vec_ref[2:3], scaled, spread)
        dx_ref[p] = dx
        sums[2] += col_sum(dx)
        da = dx.astype(BF16)
        da_ref[0, p] = da[:, : D // 2]
        da_ref[1, p] = da[:, D // 2 :]
        dns.append(dot(da[:, : D // 2], wo_scr[0], NT) + dot(da[:, D // 2 :], wo_scr[1], NT))
    for p, dn in zip(parts, dns):
        mixed = mixed_ref[p]
        scaled, spread = unit_rows(mixed * vec_ref[10:11])
        sums[3] += col_sum(dn * scaled)
        sums[4] += col_sum(dn)
        heads = unit_rows_back(dn * vec_ref[1:2], scaled, spread)
        sums[5] += col_sum(heads * mixed)
        do_ref[p] = (heads * vec_ref[10:11]).astype(BF16)
    sums_ref[...] += jnp.concatenate(sums + [jnp.zeros((2, D), F32)], axis=0)


def middle(meta, dz, mid, mixed, cot, vec, w_in, w_out):
    rows = mid.shape[0]
    tile = pl.BlockSpec((CHUNK, D), lambda c, m: (c, 0))
    return pl.pallas_call(
        middle_kernel,
        grid_spec=pltpu.PrefetchScalarGridSpec(
            num_scalar_prefetch=1,
            grid=(rows // CHUNK,),
            in_specs=[
                pl.BlockSpec((2, CHUNK, FF // 2), lambda c, m: (0, c, 0)),
                tile, tile, tile,
                full(16, D),
                *[ANY] * 6,
            ],
            out_specs=[
                pl.BlockSpec((2, CHUNK, D // 2), lambda c, m: (0, c, 0)),
                tile, tile,
                full(8, D),
            ],
            scratch_shapes=[
                pltpu.VMEM((2, D, FF // 2), BF16),
                pltpu.VMEM((2, D, D // 2), BF16),
                pltpu.SemaphoreType.DMA((2,)),
            ],
        ),
        out_shape=[
            jax.ShapeDtypeStruct((2, rows, D // 2), BF16),
            jax.ShapeDtypeStruct((rows, D), F32),
            jax.ShapeDtypeStruct((rows, D), BF16),
            jax.ShapeDtypeStruct((8, D), F32),
        ],
        compiler_params=pltpu.CompilerParams(vmem_limit_bytes=VMEM_BIG),
        cost_estimate=pl.CostEstimate(
            flops=2 * rows * D * (D + FF), bytes_accessed=30 * rows * D, transcendentals=0
        ),
        name="middle",
    )(meta, dz, mid, mixed, cot, vec, *w_in, *w_out)


def attend_back_kernel(
    meta, q_ref, k_ref, v_ref, do_ref, turned_ref, lse_ref, bias_ref,
    dqkv_ref, tiles_ref, dq_scr, do_scr,
):
    step = pl.program_id(0)
    kind = meta[META_KIND + step]

    @pl.when(step == 0)
    def _():
        tiles_ref[...] = jnp.zeros_like(tiles_ref)

    query = q_ref[...]
    query_turned = query.astype(F32).T.astype(BF16)
    key_turned = k_ref[...].astype(F32).T.astype(BF16)
    do_scr[...] = do_ref[...].astype(F32).T
    mask = jnp.broadcast_to((1.0 - live_rows(meta, pl.program_id(0))) * NEG_FILL, (CHUNK, CHUNK))
    dk, dv = [], []
    for h in range(HEADS):
        part = slice(h * HEAD_DIM, (h + 1) * HEAD_DIM)
        key, value = k_ref[:, part], v_ref[:, part]
        do_turned = do_scr[part]
        scores = dot(key, query_turned[part]) + bias_ref[0, h].astype(F32) + mask
        probs = jnp.exp(scores - lse_ref[0, h : h + 1])
        centre = jnp.sum(do_turned * turned_ref[0, part], axis=0, keepdims=True)
        ds_full = probs * (dot(value, do_turned.astype(BF16)) - centre)
        ds = ds_full.astype(BF16)
        tiles_ref[kind, h] += ds_full
        dv.append(dot(probs.astype(BF16), do_ref[:, part]))
        dk.append(dot(ds, q_ref[:, part]))
        dq_scr[part] = dot(key_turned[part], ds)
    dq = (dq_scr[...].T * QUERY_SCALE).astype(BF16)
    dk = jnp.concatenate(dk, axis=1).astype(BF16)
    dv = jnp.concatenate(dv, axis=1).astype(BF16)
    dqkv_ref[0, :, :D] = dq
    dqkv_ref[0, :, D:] = dk[:, : D // 2]
    dqkv_ref[1, :, : D // 2] = dk[:, D // 2 :]
    dqkv_ref[1, :, D // 2 :] = dv


def attend_back(meta, query, key, value, do, turned, lse, bias):
    rows = query.shape[0]
    chunks = rows // CHUNK
    tile = pl.BlockSpec((CHUNK, D), lambda c, m: (c, 0))
    return pl.pallas_call(
        attend_back_kernel,
        grid_spec=pltpu.PrefetchScalarGridSpec(
            num_scalar_prefetch=1,
            grid=(chunks,),
            in_specs=[
                tile, tile, tile, tile,
                pl.BlockSpec((1, D, CHUNK), lambda c, m: (c, 0, 0)),
                pl.BlockSpec((1, 16, CHUNK), lambda c, m: (c, 0, 0)),
                pl.BlockSpec((1, HEADS, CHUNK, CHUNK), lambda c, m: (m[META_KIND + c], 0, 0, 0)),
            ],
            out_specs=[
                pl.BlockSpec((2, CHUNK, 3 * D // 2), lambda c, m: (0, c, 0)),
                full(2, HEADS, CHUNK, CHUNK),
            ],
            scratch_shapes=[pltpu.VMEM((D, CHUNK), F32), pltpu.VMEM((D, CHUNK), F32)],
        ),
        out_shape=[
            jax.ShapeDtypeStruct((2, rows, 3 * D // 2), BF16),
            jax.ShapeDtypeStruct((2, HEADS, CHUNK, CHUNK), F32),
        ],
        compiler_params=pltpu.CompilerParams(vmem_limit_bytes=VMEM_BIG),
        cost_estimate=pl.CostEstimate(
            flops=10 * rows * CHUNK * D * 3, bytes_accessed=30 * rows * D, transcendentals=0
        ),
        name="attend_back",
    )(meta, query, key, value, do, turned, lse, bias)


def last_kernel(
    meta, dqkv_ref, x_ref, dx_ref, vec_ref, a0, a1, b0, b1,
    out_ref, sums_ref, sums_p_ref, w_scr, sem,
):
    @pl.when(pl.program_id(0) == 0)
    def _():
        load = Load(meta, sem, w_scr)
        load.cols("a", a0, a1, 0, 0, D)
        load.cols("b", b0, b1, D, 0, D // 2)
        load.wait()
        sums_ref[...] = jnp.zeros_like(sums_ref)
        sums_p_ref[...] = jnp.zeros_like(sums_p_ref)

    parts = [slice(a, a + PART) for a in range(0, CHUNK, PART)]
    dhs = [dot(dqkv_ref[0, p], w_scr[0], NT) + dot(dqkv_ref[1, p], w_scr[1], NT) for p in parts]
    for half in range(2):
        sums_p_ref[half : half + 1] += col_sum(dqkv_ref[half].astype(F32))
    sums = [jnp.zeros((1, D), F32)] * 2
    for p, dh in zip(parts, dhs):
        scaled, spread = unit_rows(x_ref[p].astype(F32))
        sums[0] += col_sum(dh * scaled)
        sums[1] += col_sum(dh)
        back = unit_rows_back(dh * vec_ref[0:1], scaled, spread)
        out_ref[p] = (dx_ref[p] + back).astype(BF16)
    sums_ref[...] += jnp.concatenate(sums + [jnp.zeros((6, D), F32)], axis=0)


def last(meta, dqkv, tokens, dx, vec, w_in):
    rows = tokens.shape[0]
    tile = pl.BlockSpec((CHUNK, D), lambda c, m: (c, 0))
    return pl.pallas_call(
        last_kernel,
        grid_spec=pltpu.PrefetchScalarGridSpec(
            num_scalar_prefetch=1,
            grid=(rows // CHUNK,),
            in_specs=[
                pl.BlockSpec((2, CHUNK, 3 * D // 2), lambda c, m: (0, c, 0)),
                tile, tile,
                full(16, D),
                ANY, ANY, ANY, ANY,
            ],
            out_specs=[tile, full(8, D), full(2, 3 * D // 2)],
            scratch_shapes=[pltpu.VMEM((2, D, 3 * D // 2), BF16), pltpu.SemaphoreType.DMA],
        ),
        out_shape=[
            jax.ShapeDtypeStruct((rows, D), BF16),
            jax.ShapeDtypeStruct((8, D), F32),
            jax.ShapeDtypeStruct((2, 3 * D // 2), F32),
        ],
        compiler_params=pltpu.CompilerParams(vmem_limit_bytes=VMEM_BIG),
        cost_estimate=pl.CostEstimate(
            flops=2 * rows * D * 3 * D, bytes_accessed=16 * rows * D, transcendentals=0
        ),
        name="last",
    )(meta, dqkv, tokens, dx, vec, *w_in)


BAND = 384


class Place:
    def __init__(self, order, rows, width, block, runs):
        self.order, self.runs = order, runs
        self.spec = pl.BlockSpec((PIECES, rows, width), lambda *_: (0, 0, block))
        self.shape = jax.ShapeDtypeStruct((PIECES, rows, D), BF16)


TO_FF = (Place("a", 2 * ROWS_D, D, 0, ((0, 0, D), (ROWS_D, D, 2 * D))),)
TO_OUT = (Place("b", ROWS_D, D // 2, 1, ((0, 0, D // 2),)),)
TO_IN = (
    Place("a", ROWS_D, D, 0, ((0, 0, D),)),
    Place("b", ROWS_D, D // 2, 0, ((0, D, 3 * D // 2),)),
)


def cols_grad_kernel(meta, left_ref, right_ref, *refs, places):
    side, step = pl.program_id(0), pl.program_id(1)
    out_refs = refs[-2 * len(places) :]
    band = dot(left_ref[...], right_ref[0], TN).astype(BF16)
    for which in range(2):

        @pl.when(side == which)
        def _():
            for place, out_ref in zip(places, out_refs[which * len(places) :]):
                for i in range(BAND // ROWS_D):
                    piece = meta[META_TO[place.order] + step * (BAND // ROWS_D) + i]
                    for row, start, end in place.runs:
                        part = band[i * ROWS_D : (i + 1) * ROWS_D, start:end]
                        out_ref[piece, row : row + ROWS_D] = part


def cols_grad(meta, left, right, places, before=()):
    rows, width = left.shape[0], right.shape[2]
    count = len(places)
    return pl.pallas_call(
        functools.partial(cols_grad_kernel, places=places),
        grid_spec=pltpu.PrefetchScalarGridSpec(
            num_scalar_prefetch=1,
            grid=(2, D // BAND),
            in_specs=[
                pl.BlockSpec((rows, BAND), lambda s, i, m: (0, i)),
                pl.BlockSpec((1, rows, width), lambda s, i, m: (m[0] + (1 - s) * (1 - 2 * m[0]), 0, 0)),
            ]
            + [ANY] * len(before),
            out_specs=[p.spec for p in places] * 2,
        ),
        out_shape=[p.shape for p in places] * 2,
        input_output_aliases={3 + i: (i + 1) * count - 1 for i in range(len(before))},
        compiler_params=pltpu.CompilerParams(vmem_limit_bytes=VMEM_BIG),
        cost_estimate=pl.CostEstimate(
            flops=4 * rows * D * width, bytes_accessed=4 * rows * (D + width), transcendentals=0
        ),
        name="cols_grad",
    )(meta, left, right, *before)


def rows_grad_kernel(meta, left_ref, right_ref, own_ref, other_ref, *, order):
    step = pl.program_id(0)
    band = dot(left_ref[...], right_ref[...], TN).astype(BF16)
    low_core = meta[0] == 0
    for i in range(BAND // (2 * ROWS_F)):
        piece = meta[META_TO[order] + step * (BAND // (2 * ROWS_F)) + i]
        even = band[2 * i * ROWS_F : (2 * i + 1) * ROWS_F]
        odd = band[(2 * i + 1) * ROWS_F : (2 * i + 2) * ROWS_F]
        own_ref[piece] = jnp.where(low_core, even, odd)
        other_ref[piece] = jnp.where(low_core, odd, even)


def rows_grad(meta, left, right, order):
    rows = left.shape[0]
    return pl.pallas_call(
        functools.partial(rows_grad_kernel, order=order),
        grid_spec=pltpu.PrefetchScalarGridSpec(
            num_scalar_prefetch=1,
            grid=(FF // BAND,),
            in_specs=[
                pl.BlockSpec((rows, BAND), lambda i, m: (0, i)),
                pl.BlockSpec((rows, D), lambda i, m: (0, 0)),
            ],
            out_specs=[full(PIECES, ROWS_F, D)] * 2,
        ),
        out_shape=[jax.ShapeDtypeStruct((PIECES, ROWS_F, D), BF16)] * 2,
        compiler_params=pltpu.CompilerParams(vmem_limit_bytes=VMEM_BIG),
        cost_estimate=pl.CostEstimate(
            flops=2 * rows * D * FF, bytes_accessed=2 * rows * (D + FF), transcendentals=0
        ),
        name="rows_grad",
    )(meta, left, right)


def swap(values, mask, count):
    return lax.ppermute(values, AXES, [(i, i ^ mask) for i in range(count)])


def tie(values, after):
    values, after = list(values), list(after)
    if not after:
        return values
    return list(lax.optimization_barrier(tuple(values + after))[: len(values)])


class Chain:
    def __init__(self, net, steps, finish):
        self.net, self.steps, self.finish = net, list(steps), finish
        self.got = [None] * len(self.steps)
        self.sends = [[] for _ in self.steps]
        self.results = [None] * len(self.steps)

    def go(self, *after):
        for i, step in enumerate(self.steps):
            if self.results[i] is not None:
                continue
            try:
                got = self.got[i] if self.got[i] is None else tie(self.got[i], after)
                sends = step.send(got)
                values = [v for v, _ in sends]
                if got is None:
                    values = tie(values, after)
                self.sends[i] = values
                self.got[i] = [self.net.swap(v, m) for v, (_, m) in zip(values, sends)]
            except StopIteration as end:
                self.results[i] = end.value
                self.sends[i] = []
        return self

    @property
    def sent(self):
        return [v for part in self.sends for v in part]

    @property
    def received(self):
        return [v for part in self.got for v in part or []]

    def done(self, *after):
        while any(r is None for r in self.results):
            self.go(*after)
            after = ()
        return self.finish(self.results)


class Ready:
    def __init__(self, value):
        self.value, self.sent, self.received = value, [], []

    def go(self, *after):
        return self

    def done(self, *after):
        return self.value


class Cube:
    SIDES = {"a": (2, 4), "b": (4, 2)}

    def __init__(self):
        self.me = lax.axis_index(AXES).astype(jnp.int32)

    def swap(self, values, mask):
        return swap(values, mask, 32)

    def masks(self, order):
        shift = self.SIDES[order]
        return np.array(
            [8 * (k & 3) + shift[0] * (k >> 2 & 1) + shift[1] * (k >> 3) for k in range(PIECES)]
        )

    def meta(self):
        chip = self.me >> 1
        place = jnp.arange(PIECES, dtype=jnp.int32)
        start = [chip ^ jnp.asarray(self.masks(o) >> 1, jnp.int32) for o in "ab"]
        mask = chip ^ place
        x, y = mask & 1, mask >> 1 & 1
        to = [(mask >> 2) + 4 * x + 8 * y, (mask >> 2) + 4 * y + 8 * x]
        return self.me & 1, start + to

    def spread(self, piece, parts):
        got = yield [(piece, 8 * z) for z in (1, 2, 3)]
        held = jnp.stack([piece] + got)
        ends = np.cumsum([0] + [w for _, w in parts])
        cuts = [held[..., a:b] for a, b in zip(ends[:-1], ends[1:])]
        for stage in (0, 1):
            got = yield [(c, self.SIDES[order][stage]) for c, (order, _) in zip(cuts, parts)]
            cuts = [jnp.concatenate(pair) for pair in zip(cuts, got)]
        got = yield [(c, 1) for c in cuts]
        return [v for pair in zip(cuts, got) for v in pair]

    def gather_cols(self, shards, parts):
        left, right = (
            jnp.concatenate([h[side] for h in (jnp.split(s, 2, axis=1) for s in shards)], axis=1)
            for side in (0, 1)
        )
        odd = (self.me & 1) == 1
        got = self.swap(jnp.where(odd, left, right), 1)
        mine = jnp.where(odd, right, left)
        block = jnp.where(odd, jnp.concatenate([got, mine]), jnp.concatenate([mine, got]))
        return Chain(self, [self.spread(block, parts)], lambda results: results[0])

    def gather_rows(self, shard, parts):
        return Chain(self, [self.spread(shard, parts)], lambda results: results[0])

    def gather_small(self, pack):
        every = jnp.broadcast_to(pack, (32, pack.shape[0]))
        return lax.all_to_all(every, AXES, 0, 0, tiled=True)

    def reduce_small(self, pack):
        return jnp.sum(lax.all_to_all(pack, AXES, 0, 0, tiled=True), axis=0)

    def gather_rows(self, shard, order):
        return Chain(self, [self.spread(shard, order)], lambda parts: parts[0])

    def collect(self, owns, others, orders):
        got = yield [(o, 1) for o in others]
        totals = [a.astype(F32) + b.astype(F32) for a, b in zip(owns, got)]
        for stage in (1, 0):
            count = totals[0].shape[0] // 2
            got = yield [
                (t[count:].astype(BF16), self.SIDES[o][stage]) for t, o in zip(totals, orders)
            ]
            totals = [t[:count] + g.astype(F32) for t, g in zip(totals, got)]
        total = jnp.concatenate(totals, axis=1)
        got = yield [(total[z].astype(BF16), 8 * z) for z in (1, 2, 3)]
        return total[0] + sum(g.astype(F32) for g in got)

    def reduce_ff(self, others, owns):
        def finish(results):
            (total,) = results
            block = jnp.concatenate([total[:ROWS_D], total[ROWS_D : 2 * ROWS_D]], axis=1)
            return jnp.concatenate(self.join(block), axis=1), total[2 * ROWS_D :]

        return Chain(self, [self.collect(owns, others, "ab")], finish)

    def reduce_attn(self, others, owns):
        def finish(results):
            (total,) = results
            block = jnp.concatenate([total[:ROWS_D], total[ROWS_D:]], axis=1)
            sides = self.join(block)
            cut = 3 * D // 2
            return tuple(
                jnp.concatenate([s[:, part] for s in sides], axis=1)
                for part in (slice(0, cut), slice(cut, None))
            )

        return Chain(self, [self.collect(owns, others, "ab")], finish)

    def join(self, block):
        rows = block.shape[0] // 2
        low, high = block[:rows], block[rows:]
        odd = (self.me & 1) == 1
        got = self.swap(jnp.where(odd, low, high), 1)
        mine = jnp.where(odd, high, low)
        return jnp.where(odd, got, mine), jnp.where(odd, mine, got)


class Plain:
    def __init__(self, count):
        self.count = count
        self.me = lax.axis_index(AXES)

    def meta(self):
        place = jnp.arange(PIECES, dtype=jnp.int32)
        return jnp.int32(0), [place] * 4

    def gather_cols(self, shards, parts):
        whole = [lax.all_gather(s, AXES, axis=0, tiled=True) for s in shards]
        left, right = (
            jnp.concatenate([h[side] for h in (jnp.split(w, 2, axis=1) for w in whole)], axis=1)
            for side in (0, 1)
        )
        out, at = [], 0
        for _, width in parts:
            for half in (left, right):
                out.append(half[:, at : at + width].reshape(PIECES, -1, width))
            at += width
        return Ready(out)

    def gather_small(self, pack):
        return lax.all_gather(pack, AXES)

    def reduce_small(self, pack):
        return lax.psum_scatter(pack, AXES, scatter_dimension=0, tiled=False)

    def gather_rows(self, shard, parts):
        whole = lax.all_gather(shard, AXES, axis=0, tiled=True)
        whole = whole.reshape(PIECES, 2, -1, whole.shape[1])
        out, at = [], 0
        for _, width in parts:
            out += [whole[:, side, :, at : at + width] for side in (0, 1)]
            at += width
        return Ready(out)

    def scatter(self, whole):
        return lax.psum_scatter(whole.astype(F32), AXES, scatter_dimension=0, tiled=True)

    def reduce_ff(self, others, owns):
        runs = [
            a[:, row : row + ROWS_D].reshape(D, D)
            for a in (owns[0], others[0])
            for row in (0, ROWS_D)
        ]
        rows = jnp.stack([owns[1], others[1]], axis=1).reshape(FF, D)
        return Ready((self.scatter(jnp.concatenate(runs, axis=1)), self.scatter(rows)))

    def reduce_attn(self, others, owns):
        halves_in, halves_out = [], []
        for a, b in (owns, others):
            a, b = a.reshape(D, D), b.reshape(D, D)
            halves_in += [a, b[:, : D // 2]]
            halves_out.append(b[:, D // 2 :])
        return Ready(tuple(self.scatter(jnp.concatenate(h, axis=1)) for h in (halves_in, halves_out)))


PARTS_ATTN = (("a", D), ("b", D))
PARTS_HALVES = (("a", FF // 4), ("b", FF // 4))
PARTS_ROWS = (("a", D // 2), ("b", D // 2))


def body(
    tokens,
    cotangent,
    w_attn_in,
    w_attn_out,
    w_fc_in,
    w_fc_out,
    gains_d,
    biases_d,
    gains_ff,
    biases_ff,
    rel_table,
    head_scale,
    bucket,
    lengths,
    *,
    count,
    cube,
):
    net = Cube() if cube else Plain(count)
    rows = tokens.shape[0]
    chunks = rows // CHUNK

    gather_attn = net.gather_cols([w_attn_in, w_attn_out], PARTS_ATTN).go()
    small = (gains_d, biases_d, gains_ff[None], biases_ff, rel_table)
    sizes = [v.size for v in small]
    ends = np.cumsum(sizes)
    width = -(-int(ends[-1] + 16) // 1024) * 1024
    pack = jnp.concatenate([v.reshape(-1) for v in small] + [jnp.zeros(width - ends[-1], BF16)])
    (pack,) = tie([pack], gather_attn.sent)
    packs = net.gather_small(pack)
    gather_ff = net.gather_cols([w_fc_in], PARTS_HALVES)
    gather_down = net.gather_rows(w_fc_out, PARTS_ROWS)

    large = jnp.sum((bucket == 1).astype(jnp.int32), dtype=jnp.int32)
    kinds = (jnp.arange(chunks, dtype=jnp.int32) >= large).astype(jnp.int32)
    core, tables = net.meta()
    meta = jnp.concatenate(
        [core.astype(jnp.int32)[None], kinds, large[None], jnp.zeros(2, jnp.int32), *tables, lengths]
    )
    keys, keys_back, queries = (jnp.asarray(t) for t in pick_tables())

    arrived = gather_attn.received
    gather_attn.go()
    gather_ff.go(*arrived)
    (packs,) = tie([packs], gather_attn.sent)
    vec, wide, lines = unpack(packs, head_scale[None], count)
    gather_attn.go(vec)
    (lines,) = tie([lines], gather_attn.sent)
    bias = build_bias(lines, keys, queries)
    arrived = gather_attn.received
    gather_attn.go(bias)
    gather_ff.go(*arrived, bias)
    gather_down.go(*gather_ff.sent)
    attn_pieces = gather_attn.done()
    out_pieces = attn_pieces[2:]

    gather_ff.go()
    (tokens_in,) = tie([tokens], gather_ff.sent)
    low_in, query, key, value = project(meta, tokens_in, vec, attn_pieces)
    gather_down.go(low_in)
    (query_in,) = tie([query], gather_down.sent)
    heads = attend(meta, query_in, key, value, bias, 0, chunks // 2)
    gather_ff.go(heads[2])
    gather_down.go(heads[2])
    (query_in,) = tie([query], gather_down.sent + gather_ff.sent)
    mixed, turned, lse = attend(
        meta, query_in, key, value, bias, chunks // 2, chunks - chunks // 2, heads
    )
    ff_pieces = gather_ff.done()
    gather_down.go(lse)
    down_pieces = gather_down.done()
    out_tokens, mid, low_attn, low_mid, low_ff, dz, df, sums_a, sums_ff = feed(
        meta, tokens, mixed, cotangent, vec, wide, out_pieces, ff_pieces, down_pieces
    )

    other_in, own_in = cols_grad(meta, low_mid, dz, TO_FF)
    (left,) = tie([low_ff], [other_in])
    own, other = rows_grad(meta, left, df, "b")
    reduce_ff = net.reduce_ff((other_in, other), (own_in, own)).go()
    (dz,) = tie([dz], reduce_ff.sent)
    da, dx, do, sums_b = middle(meta, dz, mid, mixed, cotangent, vec, ff_pieces, out_pieces)
    reduce_ff.go(sums_b)
    (left,) = tie([low_attn], reduce_ff.sent)
    out_grads = cols_grad(meta, left, da, TO_OUT)
    (do,) = tie([do], out_grads)
    dqkv, tiles = attend_back(meta, query, key, value, do, turned, lse, bias)
    reduce_ff.go(tiles)
    (left,) = tie([low_in], reduce_ff.sent)
    other_a, other_b, own_a, own_b = cols_grad(meta, left, dqkv, TO_IN, out_grads)
    reduce_attn = net.reduce_attn((other_a, other_b), (own_a, own_b)).go()
    (tiles,) = tie([tiles], reduce_attn.sent)
    grad_table = table_grads(tiles, keys_back, queries)
    reduce_attn.go(grad_table)
    reduce_ff.go(grad_table)
    (dqkv,) = tie([dqkv], reduce_attn.sent + reduce_ff.sent)
    grad_tokens, sums_c, sums_p = last(meta, dqkv, tokens, dx, vec, attn_pieces)
    reduce_attn.go(sums_c)
    terms = (sums_a, sums_b, sums_c, sums_p, sums_ff, grad_table)
    terms = pack_terms(*tie(terms, reduce_attn.sent), count, width)
    reduce_attn.go(terms)
    (terms,) = tie([terms], reduce_attn.sent)
    mine = net.reduce_small(terms)
    grad_fc_in, grad_fc_out = reduce_ff.done(sums_c)
    grad_attn_in, grad_attn_out = reduce_attn.done()

    grads = [mine[end - size : end].reshape(v.shape) for v, size, end in zip(small, sizes, ends)]
    return (
        out_tokens,
        grad_tokens,
        grad_attn_in,
        grad_attn_out,
        grad_fc_in,
        grad_fc_out,
        grads[0],
        grads[1],
        grads[2][0],
        grads[3],
        grads[4],
        mine[ends[-1] : ends[-1] + HEADS],
    )


def solution(mesh):
    rows = P(AXES, None)
    columns = P(None, AXES)
    line = P(AXES)
    count = mesh.shape["wide"] * mesh.shape["narrow"]
    cube = (mesh.shape["wide"], mesh.shape["narrow"]) == (8, 4)
    return jax.shard_map(
        functools.partial(body, count=count, cube=cube),
        mesh=mesh,
        in_specs=(
            rows, rows, rows, rows, rows, rows,
            columns, columns, line, columns, columns, P(), line, line,
        ),
        out_specs=(
            rows, rows, rows, rows, rows, rows,
            columns, columns, line, columns, columns, P(),
        ),
        check_vma=False,
    )
```

```python
import functools

import jax
import jax.numpy as jnp
import numpy as np
from jax import lax
from jax.experimental import pallas as pl
from jax.experimental.pallas import tpu as pltpu
from jax.sharding import PartitionSpec as P

HEADS = 12
HEAD_DIM = 64
D = 768
FF = 3072
GRID_L = 15
GRID_S = 8
SLOT_L = 256
SLOT_S = 64
STRIDE = 32
RELS = 1024
CHUNK = 256
PIECES = 16
ROWS_D = D // PIECES
ROWS_F = FF // (2 * PIECES)

NEG_FILL = -1e30
NORM_EPS = 1e-05
HALF_ROOT = 0.7071067811865476
DENSITY_SCALE = 0.3989422804014327
QUERY_SCALE = 0.125
AXES = ("wide", "narrow")
F32 = jnp.float32
BF16 = jnp.bfloat16
VMEM_BIG = 60 * 2**20

NN = (((1,), (0,)), ((), ()))
NT = (((1,), (1,)), ((), ()))
TN = (((0,), (0,)), ((), ()))


ANY = pl.BlockSpec(memory_space=pl.ANY)


def full(*shape):
    return pl.BlockSpec(shape, lambda *_: (0,) * len(shape))


def dot(left, right, dims=NN):
    return lax.dot_general(left, right, dims, preferred_element_type=F32)


def unit_rows(values):
    center = values - jnp.mean(values, axis=-1, keepdims=True)
    spread = lax.rsqrt(jnp.mean(center * center, axis=-1, keepdims=True) + NORM_EPS)
    return center * spread, spread


def unit_rows_back(inner, scaled, spread):
    return spread * (
        inner
        - jnp.mean(inner, axis=-1, keepdims=True)
        - scaled * jnp.mean(inner * scaled, axis=-1, keepdims=True)
    )


def col_sum(values):
    return jnp.sum(values, axis=0, keepdims=True)


def unit_position(kind):
    place = np.arange(CHUNK)
    if kind == 0:
        return np.minimum(place // GRID_L, GRID_L - 1), place % GRID_L
    inner = place % SLOT_S
    return inner // GRID_S, inner % GRID_S


def pick_tables():
    keys = np.zeros((2, CHUNK, 512), np.float32)
    keys_back = np.zeros((2, CHUNK, 512), np.float32)
    queries = np.zeros((2, CHUNK, CHUNK), np.float32)
    for kind in range(2):
        row, col = unit_position(kind)
        line = STRIDE * row + col
        keys[kind, np.arange(CHUNK), line] = 1
        keys_back[kind, np.arange(CHUNK), 511 - line] = 1
        queries[kind, 16 * row + col, np.arange(CHUNK)] = 1
    return keys.astype(BF16), keys_back.astype(BF16), queries.astype(BF16)


def owner_of_lane(lanes, each, last=None):
    lane = lax.broadcasted_iota(jnp.int32, lanes, 1)
    entry = lane if last is None else last - lane
    device = lax.broadcasted_iota(jnp.int32, lanes, 0)
    return ((entry >= device * each) & (entry < device * each + each)).astype(BF16)


def place_in_part(lanes, each, last=None):
    lane = lax.broadcasted_iota(jnp.int32, lanes, 1)
    entry = lane if last is None else last - lane
    row = lax.broadcasted_iota(jnp.int32, lanes, 0)
    return ((entry >= 0) & (lax.rem(entry + each, each) == row)).astype(F32)


def unpack_kernel(pack_ref, scale_ref, vec_ref, wide_ref, line_ref, *, count):
    each_d, each_f, each_t = D // count, FF // count, RELS // count
    pack = pack_ref[...]

    def rows(start, amount, each, lanes, last=None):
        owner = owner_of_lane((count, lanes), each, last)
        place = place_in_part((each, lanes), each, last)
        part = pack[:, start : start + amount * each]
        spread = dot(part, owner, TN)
        return [col_sum(spread[r * each : r * each + each] * place) for r in range(amount)]

    d_rows = rows(0, 10, each_d, D)
    ff_rows = rows(10 * each_d, 3, each_f, FF)
    lines = rows(10 * each_d + 3 * each_f, HEADS, each_t, RELS, 1006)
    lane = lax.broadcasted_iota(jnp.int32, (HEADS, D), 1)
    row = lax.broadcasted_iota(jnp.int32, (HEADS, D), 0)
    heads = dot(scale_ref[...], (lane // HEAD_DIM == row).astype(BF16))
    vec_ref[...] = jnp.concatenate(d_rows + [heads, jnp.zeros((5, D), F32)], axis=0)
    wide_ref[...] = jnp.concatenate(ff_rows + [jnp.zeros((5, FF), F32)], axis=0)
    for h in range(HEADS):
        line_ref[h] = jnp.broadcast_to(lines[h], (16, RELS))


def unpack(pack, scale, count):
    return pl.pallas_call(
        functools.partial(unpack_kernel, count=count),
        out_shape=[
            jax.ShapeDtypeStruct((16, D), F32),
            jax.ShapeDtypeStruct((8, FF), F32),
            jax.ShapeDtypeStruct((HEADS, 16, RELS), F32),
        ],
        compiler_params=pltpu.CompilerParams(vmem_limit_bytes=VMEM_BIG),
        cost_estimate=pl.CostEstimate(flops=2 * 10**9, bytes_accessed=4 * 10**6, transcendentals=0),
        name="unpack",
    )(pack, scale)


TURN = 4


def bias_kernel(line_ref, keys_ref, queries_ref, out_ref):
    left = lax.broadcasted_iota(jnp.int32, (CHUNK, CHUNK), 0) // SLOT_S
    right = lax.broadcasted_iota(jnp.int32, (CHUNK, CHUNK), 1) // SLOT_S
    spread_rows = []
    for h in range(TURN):
        base = pltpu.roll(line_ref[h], RELS - 511, 1, stride=1, stride_axis=0)
        turns = [base] + [pltpu.roll(base, STRIDE * m, 1) for m in (1, 2, 3)]
        twice = [jnp.concatenate([t, t[:, :512]], axis=1) for t in turns]
        groups = []
        for r in range(16):
            start = (RELS - 128 * (r // 4)) % RELS
            groups.append(twice[r % 4][:, start : start + 512])
        spread_rows.append(jnp.concatenate(groups, axis=0).astype(BF16))
    by_key = [
        (dot(keys_ref[0], g, NT).astype(BF16), dot(keys_ref[1, :SLOT_S], g, NT).astype(BF16))
        for g in spread_rows
    ]
    for h in range(TURN):
        out_ref[0, h] = dot(by_key[h][0], queries_ref[0]).astype(BF16)
        tile = dot(by_key[h][1], queries_ref[1])
        tile = jnp.concatenate([tile] * (CHUNK // SLOT_S), axis=0)
        out_ref[1, h] = jnp.where(left == right, tile, NEG_FILL).astype(BF16)


def build_bias(lines, keys, queries):
    return pl.pallas_call(
        bias_kernel,
        grid=(HEADS // TURN,),
        in_specs=[
            pl.BlockSpec((TURN, 16, RELS), lambda h: (h, 0, 0)),
            full(2, CHUNK, 512),
            full(2, CHUNK, CHUNK),
        ],
        out_specs=pl.BlockSpec((2, TURN, CHUNK, CHUNK), lambda h: (0, h, 0, 0)),
        out_shape=jax.ShapeDtypeStruct((2, HEADS, CHUNK, CHUNK), BF16),
        compiler_params=pltpu.CompilerParams(vmem_limit_bytes=VMEM_BIG),
        cost_estimate=pl.CostEstimate(flops=8 * 10**9, bytes_accessed=4 * 10**6, transcendentals=0),
        name="bias_tiles",
    )(lines, keys, queries)


def pack_kernel(a_ref, b_ref, c_ref, p_ref, ff_ref, table_ref, out_ref, *, count):
    each_d, each_f, each_t = D // count, FF // count, RELS // count

    def columns(rows, each, lanes):
        owner = owner_of_lane((count, lanes), each)
        place = place_in_part((each, lanes), each)
        parts = []
        for row in rows:
            high, rest = halves(row * place)
            parts.append(dot(high, owner, NT) + dot(rest, owner, NT))
        return jnp.concatenate(parts, axis=0)

    a, b, c = a_ref[...], b_ref[...], c_ref[...]
    p = p_ref[...]
    d_rows = [
        c[0:1], b[3:4], b[0:1],
        c[1:2], p[0:1, :D], p[1:2, D // 2 :], b[4:5], b[2:3], b[1:2], a[0:1],
    ]
    ff = ff_ref[...]
    lane = lax.broadcasted_iota(jnp.int32, (16, D), 1)
    row = lax.broadcasted_iota(jnp.int32, (16, D), 0)
    high, rest = halves(jnp.broadcast_to(b[5:6], (16, D)) * (lane // HEAD_DIM == row).astype(F32))
    ones = jnp.ones((count, D), BF16)
    out = [
        columns(d_rows, each_d, D),
        columns([ff[0:1], ff[2:3], ff[1:2]], each_f, FF),
        columns([table_ref[h, 0:1] for h in range(HEADS)], each_t, RELS),
        dot(high, ones, NT) + dot(rest, ones, NT),
    ]
    used = sum(o.shape[0] for o in out)
    out.append(jnp.zeros((out_ref.shape[1] - used, count), F32))
    out_ref[...] = jnp.concatenate(out, axis=0).T


def pack_terms(sums_a, sums_b, sums_c, sums_p, sums_ff, table, count, width):
    return pl.pallas_call(
        functools.partial(pack_kernel, count=count),
        out_shape=jax.ShapeDtypeStruct((count, width), F32),
        compiler_params=pltpu.CompilerParams(vmem_limit_bytes=VMEM_BIG),
        cost_estimate=pl.CostEstimate(flops=10**9, bytes_accessed=10**6, transcendentals=0),
        name="pack_terms",
    )(sums_a, sums_b, sums_c, sums_p, sums_ff, table)


def halves(values):
    high = values.astype(BF16)
    return high, (values - high.astype(F32)).astype(BF16)


def table_kernel(tiles_ref, keys_ref, queries_ref, out_ref):
    by_query = []
    for h in range(TURN):
        small = tiles_ref[1, h, :SLOT_S]
        for part in range(1, CHUNK // SLOT_S):
            small = small + tiles_ref[1, h, part * SLOT_S : (part + 1) * SLOT_S]
        by_query.append(
            (
                dot(queries_ref[0], tiles_ref[0, h].astype(BF16), NT).astype(BF16),
                dot(queries_ref[1], small.astype(BF16), NT).astype(BF16),
            )
        )
    totals = [
        dot(large, keys_ref[0]) + dot(small, keys_ref[1, :SLOT_S]) for large, small in by_query
    ]
    for h, total in enumerate(totals):
        line = jnp.zeros((16, RELS), F32)
        for m in range(4):
            part = jnp.zeros((16, RELS), F32)
            for k in range(4):
                group = total[16 * (4 * k + m) : 16 * (4 * k + m) + 16]
                pieces = [group, jnp.zeros((16, 512 - 128 * k), F32)]
                if k:
                    pieces = [jnp.zeros((16, 128 * k), F32)] + pieces
                part += jnp.concatenate(pieces, axis=1)
            line += pltpu.roll(part, STRIDE * m, 1) if m else part
        line = pltpu.roll(line, 0, 1, stride=1, stride_axis=0)
        out_ref[h] = pltpu.roll(jnp.broadcast_to(col_sum(line), (8, RELS)), RELS - 16, 1)


def table_grads(tiles, keys_back, queries):
    return pl.pallas_call(
        table_kernel,
        grid=(HEADS // TURN,),
        in_specs=[
            pl.BlockSpec((2, TURN, CHUNK, CHUNK), lambda h: (0, h, 0, 0)),
            full(2, CHUNK, 512),
            full(2, CHUNK, CHUNK),
        ],
        out_specs=pl.BlockSpec((TURN, 8, RELS), lambda h: (h, 0, 0)),
        out_shape=jax.ShapeDtypeStruct((HEADS, 8, RELS), F32),
        compiler_params=pltpu.CompilerParams(vmem_limit_bytes=VMEM_BIG),
        cost_estimate=pl.CostEstimate(flops=8 * 10**9, bytes_accessed=6 * 10**6, transcendentals=0),
        name="table_grads",
    )(tiles, keys_back, queries)


META_KIND = 1
META_LARGE = 5
META_LENGTH = 72
META_FROM = {"a": 8, "b": 24}
META_TO = {"a": 40, "b": 56}


def live_rows(meta, chunk):
    place = lax.broadcasted_iota(jnp.int32, (CHUNK, 1), 0)
    large = meta[META_LARGE]
    first = large + (chunk - large) * (SLOT_L // SLOT_S)
    is_large = chunk < large
    end = jnp.zeros((CHUNK, 1), jnp.int32)
    for part in range(SLOT_L // SLOT_S):
        slot = jnp.where(is_large, chunk, first + part)
        start = jnp.where(is_large, 0, part * SLOT_S)
        end = jnp.where(place >= part * SLOT_S, start + meta[META_LENGTH + slot], end)
    return (place < end).astype(F32)


class Load:
    def __init__(self, meta, sem, scratch):
        self.meta, self.sem, self.scratch = meta, sem, scratch

    def cols(self, order, own, other, start, source_start, width):
        core, rows = self.meta[0], own.shape[1]
        for k in range(PIECES):
            place = pl.multiple_of(self.meta[META_FROM[order] + k] * rows, 16)
            for half, source in ((core, own), (1 - core, other)):
                pltpu.make_async_copy(
                    source.at[k, :, pl.ds(source_start, width)],
                    self.scratch.at[half, pl.ds(place, rows), pl.ds(start, width)],
                    self.sem,
                ).start()

    def rows(self, order, own, other, start):
        core, rows, width = self.meta[0], own.shape[1], own.shape[2]
        for k in range(PIECES):
            chip = self.meta[META_FROM[order] + k]
            for half, source in ((core, own), (1 - core, other)):
                place = pl.multiple_of((2 * chip + half) * rows, 16)
                pltpu.make_async_copy(
                    source.at[k],
                    self.scratch.at[pl.ds(place, rows), pl.ds(start, width)],
                    self.sem,
                ).start()

    def wait(self):
        pltpu.make_async_copy(self.scratch, self.scratch, self.sem).wait()


def project_kernel(meta, x_ref, vec_ref, a0, a1, b0, b1, low_ref, q_ref, k_ref, v_ref, w_scr, sem):
    @pl.when(pl.program_id(0) == 0)
    def _():
        load = Load(meta, sem, w_scr)
        load.cols("a", a0, a1, 0, 0, D)
        load.cols("b", b0, b1, D, 0, D // 2)
        load.wait()

    scaled, _ = unit_rows(x_ref[...].astype(F32))
    low = (scaled * vec_ref[0:1] + vec_ref[3:4]).astype(BF16)
    low_ref[...] = low
    first = dot(low, w_scr[0])
    second = dot(low, w_scr[1])
    q_ref[...] = ((first[:, :D] + vec_ref[4:5]) * QUERY_SCALE).astype(BF16)
    k_ref[:, : D // 2] = first[:, D:].astype(BF16)
    k_ref[:, D // 2 :] = second[:, : D // 2].astype(BF16)
    v_ref[...] = (second[:, D // 2 :] + vec_ref[5:6]).astype(BF16)


def project(meta, tokens, vec, pieces):
    rows = tokens.shape[0]
    tile = pl.BlockSpec((CHUNK, D), lambda c, m: (c, 0))
    return pl.pallas_call(
        project_kernel,
        grid_spec=pltpu.PrefetchScalarGridSpec(
            num_scalar_prefetch=1,
            grid=(rows // CHUNK,),
            in_specs=[tile, full(16, D), ANY, ANY, ANY, ANY],
            out_specs=[tile] * 4,
            scratch_shapes=[pltpu.VMEM((2, D, 3 * D // 2), BF16), pltpu.SemaphoreType.DMA],
        ),
        out_shape=[jax.ShapeDtypeStruct((rows, D), BF16)] * 4,
        compiler_params=pltpu.CompilerParams(vmem_limit_bytes=VMEM_BIG),
        cost_estimate=pl.CostEstimate(
            flops=2 * rows * D * 3 * D, bytes_accessed=16 * rows * D, transcendentals=0
        ),
        name="project",
    )(meta, tokens, vec, *pieces)


def attend_kernel(meta, q_ref, k_ref, v_ref, bias_ref, *refs, first):
    mixed_ref, turned_ref, lse_ref = refs[-3:]
    mask = (1.0 - live_rows(meta, pl.program_id(0) + first)) * NEG_FILL
    mask = jnp.broadcast_to(mask, (CHUNK, CHUNK))
    query_turned = q_ref[...].astype(F32).T.astype(BF16)
    value_turned = v_ref[...].astype(F32).T.astype(BF16)
    sums = []
    for h in range(HEADS):
        part = slice(h * HEAD_DIM, (h + 1) * HEAD_DIM)
        scores = dot(k_ref[:, part], query_turned[part]) + bias_ref[0, h].astype(F32) + mask
        largest = jnp.max(scores, axis=0, keepdims=True)
        exponent = jnp.exp(scores - largest)
        row_total = jnp.sum(exponent, axis=0, keepdims=True)
        out = dot(value_turned[part], exponent.astype(BF16))
        turned_ref[0, part] = out * (1.0 / row_total)
        sums.append(largest + jnp.log(row_total))
    lse_ref[0] = jnp.concatenate(sums + [jnp.zeros((16 - HEADS, CHUNK), F32)], axis=0)
    mixed_ref[...] = turned_ref[0].T


def attend(meta, query, key, value, bias, first, chunks, before=()):
    rows = query.shape[0]
    tile = pl.BlockSpec((CHUNK, D), lambda c, m: (c + first, 0))
    return pl.pallas_call(
        functools.partial(attend_kernel, first=first),
        grid_spec=pltpu.PrefetchScalarGridSpec(
            num_scalar_prefetch=1,
            grid=(chunks,),
            in_specs=[
                tile, tile, tile,
                pl.BlockSpec(
                    (1, HEADS, CHUNK, CHUNK), lambda c, m: (m[META_KIND + c + first], 0, 0, 0)
                ),
            ]
            + [ANY] * len(before),
            out_specs=[
                tile,
                pl.BlockSpec((1, D, CHUNK), lambda c, m: (c + first, 0, 0)),
                pl.BlockSpec((1, 16, CHUNK), lambda c, m: (c + first, 0, 0)),
            ],
        ),
        out_shape=[
            jax.ShapeDtypeStruct((rows, D), F32),
            jax.ShapeDtypeStruct((rows // CHUNK, D, CHUNK), F32),
            jax.ShapeDtypeStruct((rows // CHUNK, 16, CHUNK), F32),
        ],
        input_output_aliases={5 + i: i for i in range(len(before))},
        compiler_params=pltpu.CompilerParams(vmem_limit_bytes=VMEM_BIG),
        cost_estimate=pl.CostEstimate(
            flops=10 * 10**9, bytes_accessed=16 * rows * D, transcendentals=0
        ),
        name="attend",
    )(meta, query, key, value, bias, *before)


CUT = 512
ROOT_PART = 0.3275911 * HALF_ROOT
TAIL = (0.127414796, -0.142248368, 0.7107068705, -0.7265760135, 0.5307027145)


def normal_parts(z):
    density = jnp.exp(-0.5 * z * z)
    t = 1.0 / (1.0 + ROOT_PART * jnp.abs(z))
    tail = TAIL[4] * t + TAIL[3]
    for c in (TAIL[2], TAIL[1], TAIL[0]):
        tail = tail * t + c
    tail = tail * t * density
    return jnp.where(z >= 0.0, 1.0 - tail, tail), z * (DENSITY_SCALE * density)


def lane_sum(values):
    return jnp.sum(values, axis=-1, keepdims=True)


def feed_kernel(
    meta, x_ref, mixed_ref, cot_ref, vec_ref, wide_ref,
    o0, o1, i0, i1, i2, i3, f0, f1, f2, f3,
    out_ref, mid_ref, aln_ref, sums_ref, sums_ff_ref, dz_out, g0, g1, g2, g3,
    wo_scr, wi_scr, wf_scr, unit_scr, slope_scr, dm_scr,
    df_scr, low_scr, m_scr, dz_scr, cols_scr, rows_scr, sems, stage_sems,
):
    step = pl.program_id(0)
    mine = pl.ds(pl.multiple_of(step * CHUNK, CHUNK), CHUNK)

    def feed_loads():
        return [Load(meta, sems.at[i], s) for i, s in enumerate((wo_scr, wi_scr, wf_scr))]

    def arrived(which):
        @pl.when(step == 0)
        def _():
            feed_loads()[which].wait()

    @pl.when(step == 0)
    def _():
        loads = feed_loads()
        loads[0].cols("b", o0, o1, 0, D // 2, D // 2)
        loads[1].cols("a", i0, i1, 0, 0, FF // 4)
        loads[1].cols("b", i2, i3, FF // 4, 0, FF // 4)
        loads[2].rows("a", f0, f1, 0)
        loads[2].rows("b", f2, f3, D // 2)
        sums_ref[...] = jnp.zeros_like(sums_ref)
        sums_ff_ref[...] = jnp.zeros_like(sums_ff_ref)

    live = live_rows(meta, step)
    df_full = cot_ref[...].astype(F32) * live
    df = df_full.astype(BF16)
    df_scr[mine] = df
    sums_ref[0:1] += col_sum(df_full)
    scaled, _ = unit_rows(mixed_ref[...] * vec_ref[10:11])
    aln = (scaled * vec_ref[1:2] + vec_ref[6:7]).astype(BF16)
    aln_ref[...] = aln
    arrived(0)
    branch = jnp.concatenate([dot(aln, wo_scr[0]), dot(aln, wo_scr[1])], axis=1)
    mid = x_ref[...].astype(F32) + branch + vec_ref[7:8]
    mid_ref[...] = mid
    scaled, _ = unit_rows(mid)
    low = (scaled * vec_ref[2:3] + vec_ref[8:9]).astype(BF16)
    low_scr[mine] = low
    arrived(1)

    cuts = [slice(a, a + CUT) for a in range(0, FF, CUT)]
    inner = [(a * CUT // (FF // 2), slice(a * CUT % (FF // 2), a * CUT % (FF // 2) + CUT)) for a in range(FF // CUT)]
    total = jnp.zeros((CHUNK, 1), F32)
    for cut, (half, part) in zip(cuts, inner):
        z = dot(low, wi_scr[half, :, part]) + wide_ref[1:2, cut]
        cumulative, rest = normal_parts(z)
        act = z * cumulative
        unit_scr[:, cut] = act
        slope_scr[:, cut] = cumulative + rest
        total += lane_sum(act)
    mean = total * (1.0 / FF)
    square = jnp.zeros((CHUNK, 1), F32)
    arrived(2)
    for cut in cuts:
        dm_scr[:, cut] = dot(df, wf_scr[cut], NT)
        center = unit_scr[:, cut] - mean
        square += lane_sum(center * center)
    spread = lax.rsqrt(square * (1.0 / FF) + NORM_EPS)
    out = mid + vec_ref[9:10]
    first = jnp.zeros((CHUNK, 1), F32)
    second = jnp.zeros((CHUNK, 1), F32)
    for cut in cuts:
        unit = (unit_scr[:, cut] - mean) * spread
        unit_scr[:, cut] = unit
        m = (unit * wide_ref[0:1, cut] + wide_ref[2:3, cut]).astype(BF16)
        m_scr[mine, cut] = m
        out += dot(m, wf_scr[cut])
        dm = dm_scr[:, cut]
        sums_ff_ref[0:1, cut] += col_sum(dm * unit)
        sums_ff_ref[1:2, cut] += col_sum(dm)
        inside = dm * wide_ref[0:1, cut]
        first += lane_sum(inside)
        second += lane_sum(inside * unit)
    out_ref[...] = (out * live).astype(BF16)
    first = first * (1.0 / FF)
    second = second * (1.0 / FF)
    for cut, (half, part) in zip(cuts, inner):
        inside = dm_scr[:, cut] * wide_ref[0:1, cut]
        du = spread * (inside - first - unit_scr[:, cut] * second)
        dz_full = du * slope_scr[:, cut]
        sums_ff_ref[2:3, cut] += col_sum(dz_full)
        dz_scr[half, mine, part] = dz_full.astype(BF16)
    pltpu.make_async_copy(dz_scr.at[:, mine], dz_out.at[:, mine], sems.at[3]).start()

    @pl.when(step == pl.num_programs(0) - 1)
    def _():
        core = meta[0]
        stages = [Stage(cols_scr, stage_sems, 0), Stage(rows_scr, stage_sems, 2)]
        for side, out in ((1 - core, g0), (core, g2)):
            for b in range(D // BAND):
                band = dot(low_scr[:, b * BAND : (b + 1) * BAND], dz_scr[side], TN).astype(BF16)
                stage = stages[0].take()
                for i in range(BAND // ROWS_D):
                    rows = slice(i * ROWS_D, (i + 1) * ROWS_D)
                    stage[i, :ROWS_D] = band[rows, :D]
                    stage[i, ROWS_D:] = band[rows, D:]
                    piece = meta[META_TO["a"] + b * (BAND // ROWS_D) + i]
                    stages[0].send(stage.at[i], out.at[piece])
        for b in range(FF // BAND):
            band = dot(m_scr[:, b * BAND : (b + 1) * BAND], df_scr[...], TN).astype(BF16)
            stage = stages[1].take()
            for i in range(BAND // ROWS_F):
                stage[i] = band[i * ROWS_F : (i + 1) * ROWS_F]
            for parity in range(2):
                for own, out in ((True, g3), (False, g1)):

                    @pl.when((core == parity) == own)
                    def _():
                        for i in range(parity, BAND // ROWS_F, 2):
                            piece = meta[META_TO["b"] + (b * (BAND // ROWS_F) + i) // 2]
                            stages[1].send(stage.at[i], out.at[piece])

        for stage in stages:
            stage.end()
        pltpu.make_async_copy(dz_scr, dz_out, sems.at[3]).wait()


class Stage:
    def __init__(self, scratch, sems, first):
        self.scratch, self.sems, self.first, self.count = scratch, sems, first, 0

    def wait(self, slot):
        buffer = self.scratch.at[slot]
        pltpu.make_async_copy(buffer, buffer, self.sems.at[self.first + slot]).wait()

    def take(self):
        self.slot = self.count % 2
        if self.count >= 2:
            self.wait(self.slot)
        self.count += 1
        return self.scratch.at[self.slot]

    def send(self, source, target):
        pltpu.make_async_copy(source, target, self.sems.at[self.first + self.slot]).start()

    def end(self):
        for slot in range(min(2, self.count)):
            self.wait((self.count - 1 - slot) % 2)


BAND = 384


def feed(meta, tokens, mixed, cot, vec, wide, w_out, w_in, w_down):
    rows = tokens.shape[0]
    tile = pl.BlockSpec((CHUNK, D), lambda c, m: (c, 0))
    return pl.pallas_call(
        feed_kernel,
        grid_spec=pltpu.PrefetchScalarGridSpec(
            num_scalar_prefetch=1,
            grid=(rows // CHUNK,),
            in_specs=[
                tile, tile, tile,
                full(16, D), full(8, FF),
                *[ANY] * 10,
            ],
            out_specs=[tile, tile, tile, full(8, D), full(3, FF), *[ANY] * 5],
            scratch_shapes=[
                pltpu.VMEM((2, D, D // 2), BF16),
                pltpu.VMEM((2, D, FF // 2), BF16),
                pltpu.VMEM((FF, D), BF16),
                pltpu.VMEM((CHUNK, FF), F32),
                pltpu.VMEM((CHUNK, FF), F32),
                pltpu.VMEM((CHUNK, FF), F32),
                pltpu.VMEM((rows, D), BF16),
                pltpu.VMEM((rows, D), BF16),
                pltpu.VMEM((rows, FF), BF16),
                pltpu.VMEM((2, rows, FF // 2), BF16),
                pltpu.VMEM((2, BAND // ROWS_D, 2 * ROWS_D, D), BF16),
                pltpu.VMEM((2, BAND // ROWS_F, ROWS_F, D), BF16),
                pltpu.SemaphoreType.DMA((4,)),
                pltpu.SemaphoreType.DMA((4,)),
            ],
        ),
        out_shape=[
            jax.ShapeDtypeStruct((rows, D), BF16),
            jax.ShapeDtypeStruct((rows, D), F32),
            jax.ShapeDtypeStruct((rows, D), BF16),
            jax.ShapeDtypeStruct((8, D), F32),
            jax.ShapeDtypeStruct((3, FF), F32),
            jax.ShapeDtypeStruct((2, rows, FF // 2), BF16),
        ]
        + [jax.ShapeDtypeStruct((PIECES, ROWS_F, D), BF16)] * 4,
        compiler_params=pltpu.CompilerParams(vmem_limit_bytes=VMEM_BIG),
        cost_estimate=pl.CostEstimate(
            flops=2 * rows * D * (D + 5 * FF), bytes_accessed=40 * rows * D, transcendentals=0
        ),
        name="feed",
    )(meta, tokens, mixed, cot, vec, wide, *w_out, *w_in, *w_down)


PART = 256


def middle_kernel(
    meta, dz_ref, mid_ref, mixed_ref, cot_ref, aln_ref, vec_ref, i0, i1, i2, i3, o0, o1,
    dx_ref, do_ref, sums_ref, other_out, own_out, wi_scr, wo_scr, da_scr, stage_scr, sems,
):
    step = pl.program_id(0)
    mine = pl.ds(pl.multiple_of(step * CHUNK, CHUNK), CHUNK)

    def loads():
        return [Load(meta, sems.at[i], s) for i, s in enumerate((wi_scr, wo_scr))]

    @pl.when(step == 0)
    def _():
        first, second = loads()
        first.cols("a", i0, i1, 0, 0, FF // 4)
        first.cols("b", i2, i3, FF // 4, 0, FF // 4)
        second.cols("b", o0, o1, 0, D // 2, D // 2)
        sums_ref[...] = jnp.zeros_like(sums_ref)
        first.wait()
        second.wait()

    dh = dot(dz_ref[0], wi_scr[0], NT) + dot(dz_ref[1], wi_scr[1], NT)
    scaled, spread = unit_rows(mid_ref[...])
    sums_ref[0:1] += col_sum(dh * scaled)
    sums_ref[1:2] += col_sum(dh)
    grad = cot_ref[...].astype(F32) * live_rows(meta, step)
    dx = grad + unit_rows_back(dh * vec_ref[2:3], scaled, spread)
    dx_ref[...] = dx
    sums_ref[2:3] += col_sum(dx)
    da = dx.astype(BF16)
    da_scr[0, mine] = da[:, : D // 2]
    da_scr[1, mine] = da[:, D // 2 :]
    dn = dot(da[:, : D // 2], wo_scr[0], NT) + dot(da[:, D // 2 :], wo_scr[1], NT)
    mixed = mixed_ref[...]
    scaled, spread = unit_rows(mixed * vec_ref[10:11])
    sums_ref[3:4] += col_sum(dn * scaled)
    sums_ref[4:5] += col_sum(dn)
    heads = unit_rows_back(dn * vec_ref[1:2], scaled, spread)
    sums_ref[5:6] += col_sum(heads * mixed)
    do_ref[...] = (heads * vec_ref[10:11]).astype(BF16)

    @pl.when(step == pl.num_programs(0) - 1)
    def _():
        core = meta[0]
        stages = Stage(stage_scr, sems, 2)
        for side, out in ((1 - core, other_out), (core, own_out)):
            band = dot(aln_ref[...], da_scr[side], TN).astype(BF16)
            stage = stages.take()
            for i in range(PIECES):
                stage[i] = band[i * ROWS_D : (i + 1) * ROWS_D]
                piece = meta[META_TO["b"] + i]
                stages.send(stage.at[i], out.at[piece, :, pl.ds(D // 2, D // 2)])
        stages.end()


def middle(meta, dz, mid, mixed, cot, aln, vec, w_in, w_out):
    rows = mid.shape[0]
    tile = pl.BlockSpec((CHUNK, D), lambda c, m: (c, 0))
    return pl.pallas_call(
        middle_kernel,
        grid_spec=pltpu.PrefetchScalarGridSpec(
            num_scalar_prefetch=1,
            grid=(rows // CHUNK,),
            in_specs=[
                pl.BlockSpec((2, CHUNK, FF // 2), lambda c, m: (0, c, 0)),
                tile, tile, tile,
                full(rows, D),
                full(16, D),
                *[ANY] * 6,
            ],
            out_specs=[tile, tile, full(8, D), ANY, ANY],
            scratch_shapes=[
                pltpu.VMEM((2, D, FF // 2), BF16),
                pltpu.VMEM((2, D, D // 2), BF16),
                pltpu.VMEM((2, rows, D // 2), BF16),
                pltpu.VMEM((2, PIECES, ROWS_D, D // 2), BF16),
                pltpu.SemaphoreType.DMA((4,)),
            ],
        ),
        out_shape=[
            jax.ShapeDtypeStruct((rows, D), F32),
            jax.ShapeDtypeStruct((rows, D), BF16),
            jax.ShapeDtypeStruct((8, D), F32),
        ]
        + [jax.ShapeDtypeStruct((PIECES, ROWS_D, D), BF16)] * 2,
        compiler_params=pltpu.CompilerParams(vmem_limit_bytes=VMEM_BIG),
        cost_estimate=pl.CostEstimate(
            flops=2 * rows * D * (2 * D + FF), bytes_accessed=30 * rows * D, transcendentals=0
        ),
        name="middle",
    )(meta, dz, mid, mixed, cot, aln, vec, *w_in, *w_out)


def attend_back_kernel(
    meta, q_ref, k_ref, v_ref, do_ref, turned_ref, lse_ref, bias_ref, low_ref, before_0, before_1,
    dqkv_out, tiles_out, g0, g2, g1, g3, dq_scr, do_scr, tiles_ref, dqkv_scr, a_scr, b_scr, sems,
):
    step = pl.program_id(0)
    mine = pl.ds(pl.multiple_of(step * CHUNK, CHUNK), CHUNK)
    kind = meta[META_KIND + step]

    @pl.when(step == 0)
    def _():
        tiles_ref[...] = jnp.zeros_like(tiles_ref)

    query = q_ref[...]
    query_turned = query.astype(F32).T.astype(BF16)
    key_turned = k_ref[...].astype(F32).T.astype(BF16)
    do_scr[...] = do_ref[...].astype(F32).T
    mask = jnp.broadcast_to((1.0 - live_rows(meta, pl.program_id(0))) * NEG_FILL, (CHUNK, CHUNK))
    dk, dv = [], []
    for h in range(HEADS):
        part = slice(h * HEAD_DIM, (h + 1) * HEAD_DIM)
        key, value = k_ref[:, part], v_ref[:, part]
        do_turned = do_scr[part]
        scores = dot(key, query_turned[part]) + bias_ref[0, h].astype(F32) + mask
        probs = jnp.exp(scores - lse_ref[0, h : h + 1])
        centre = jnp.sum(do_turned * turned_ref[0, part], axis=0, keepdims=True)
        ds_full = probs * (dot(value, do_turned.astype(BF16)) - centre)
        ds = ds_full.astype(BF16)
        tiles_ref[kind, h] += ds_full
        dv.append(dot(probs.astype(BF16), do_ref[:, part]))
        dk.append(dot(ds, q_ref[:, part]))
        dq_scr[part] = dot(key_turned[part], ds)
    dq = (dq_scr[...].T * QUERY_SCALE).astype(BF16)
    dk = jnp.concatenate(dk, axis=1).astype(BF16)
    dv = jnp.concatenate(dv, axis=1).astype(BF16)
    dqkv_scr[0, mine, :D] = dq
    dqkv_scr[0, mine, D:] = dk[:, : D // 2]
    dqkv_scr[1, mine, : D // 2] = dk[:, D // 2 :]
    dqkv_scr[1, mine, D // 2 :] = dv
    pltpu.make_async_copy(dqkv_scr.at[:, mine], dqkv_out.at[:, mine], sems.at[0]).start()

    @pl.when(step == pl.num_programs(0) - 1)
    def _():
        pltpu.make_async_copy(tiles_ref, tiles_out, sems.at[1]).start()
        core = meta[0]
        stages = [Stage(a_scr, sems, 2), Stage(b_scr, sems, 4)]
        for side, out_a, out_b in ((1 - core, g0, g1), (core, g2, g3)):
            for b in range(D // BAND):
                band = dot(low_ref[:, b * BAND : (b + 1) * BAND], dqkv_scr[side], TN).astype(BF16)
                stage_a, stage_b = (stage.take() for stage in stages)
                for i in range(BAND // ROWS_D):
                    rows = slice(i * ROWS_D, (i + 1) * ROWS_D)
                    stage_a[i] = band[rows, :D]
                    stage_b[i] = band[rows, D:]
                    piece = meta[META_TO["a"] + b * (BAND // ROWS_D) + i]
                    stages[0].send(stage_a.at[i], out_a.at[piece])
                    piece = meta[META_TO["b"] + b * (BAND // ROWS_D) + i]
                    stages[1].send(stage_b.at[i], out_b.at[piece, :, pl.ds(0, D // 2)])
        for stage in stages:
            stage.end()
        pltpu.make_async_copy(dqkv_scr, dqkv_out, sems.at[0]).wait()
        pltpu.make_async_copy(tiles_ref, tiles_out, sems.at[1]).wait()


def attend_back(meta, query, key, value, do, turned, lse, bias, low, before):
    rows = query.shape[0]
    chunks = rows // CHUNK
    tile = pl.BlockSpec((CHUNK, D), lambda c, m: (c, 0))
    pieces = jax.ShapeDtypeStruct((PIECES, ROWS_D, D), BF16)
    return pl.pallas_call(
        attend_back_kernel,
        grid_spec=pltpu.PrefetchScalarGridSpec(
            num_scalar_prefetch=1,
            grid=(chunks,),
            in_specs=[
                tile, tile, tile, tile,
                pl.BlockSpec((1, D, CHUNK), lambda c, m: (c, 0, 0)),
                pl.BlockSpec((1, 16, CHUNK), lambda c, m: (c, 0, 0)),
                pl.BlockSpec((1, HEADS, CHUNK, CHUNK), lambda c, m: (m[META_KIND + c], 0, 0, 0)),
                full(rows, D),
                ANY, ANY,
            ],
            out_specs=[ANY] * 6,
            scratch_shapes=[
                pltpu.VMEM((D, CHUNK), F32),
                pltpu.VMEM((D, CHUNK), F32),
                pltpu.VMEM((2, HEADS, CHUNK, CHUNK), F32),
                pltpu.VMEM((2, rows, 3 * D // 2), BF16),
                pltpu.VMEM((2, BAND // ROWS_D, ROWS_D, D), BF16),
                pltpu.VMEM((2, BAND // ROWS_D, ROWS_D, D // 2), BF16),
                pltpu.SemaphoreType.DMA((6,)),
            ],
        ),
        out_shape=[
            jax.ShapeDtypeStruct((2, rows, 3 * D // 2), BF16),
            jax.ShapeDtypeStruct((2, HEADS, CHUNK, CHUNK), F32),
            *[pieces] * 4,
        ],
        input_output_aliases={9: 4, 10: 5},
        compiler_params=pltpu.CompilerParams(vmem_limit_bytes=VMEM_BIG),
        cost_estimate=pl.CostEstimate(
            flops=20 * 10**9, bytes_accessed=30 * rows * D, transcendentals=0
        ),
        name="attend_back",
    )(meta, query, key, value, do, turned, lse, bias, low, *before)


def last_kernel(
    meta, dqkv_ref, x_ref, dx_ref, vec_ref, a0, a1, b0, b1,
    out_ref, sums_ref, sums_p_ref, w_scr, sem,
):
    @pl.when(pl.program_id(0) == 0)
    def _():
        load = Load(meta, sem, w_scr)
        load.cols("a", a0, a1, 0, 0, D)
        load.cols("b", b0, b1, D, 0, D // 2)
        load.wait()
        sums_ref[...] = jnp.zeros_like(sums_ref)
        sums_p_ref[...] = jnp.zeros_like(sums_p_ref)

    parts = [slice(a, a + PART) for a in range(0, CHUNK, PART)]
    dhs = [dot(dqkv_ref[0, p], w_scr[0], NT) + dot(dqkv_ref[1, p], w_scr[1], NT) for p in parts]
    for half in range(2):
        sums_p_ref[half : half + 1] += col_sum(dqkv_ref[half].astype(F32))
    sums = [jnp.zeros((1, D), F32)] * 2
    for p, dh in zip(parts, dhs):
        scaled, spread = unit_rows(x_ref[p].astype(F32))
        sums[0] += col_sum(dh * scaled)
        sums[1] += col_sum(dh)
        back = unit_rows_back(dh * vec_ref[0:1], scaled, spread)
        out_ref[p] = (dx_ref[p] + back).astype(BF16)
    sums_ref[...] += jnp.concatenate(sums + [jnp.zeros((6, D), F32)], axis=0)


def last(meta, dqkv, tokens, dx, vec, w_in):
    rows = tokens.shape[0]
    tile = pl.BlockSpec((CHUNK, D), lambda c, m: (c, 0))
    return pl.pallas_call(
        last_kernel,
        grid_spec=pltpu.PrefetchScalarGridSpec(
            num_scalar_prefetch=1,
            grid=(rows // CHUNK,),
            in_specs=[
                pl.BlockSpec((2, CHUNK, 3 * D // 2), lambda c, m: (0, c, 0)),
                tile, tile,
                full(16, D),
                ANY, ANY, ANY, ANY,
            ],
            out_specs=[tile, full(8, D), full(2, 3 * D // 2)],
            scratch_shapes=[pltpu.VMEM((2, D, 3 * D // 2), BF16), pltpu.SemaphoreType.DMA],
        ),
        out_shape=[
            jax.ShapeDtypeStruct((rows, D), BF16),
            jax.ShapeDtypeStruct((8, D), F32),
            jax.ShapeDtypeStruct((2, 3 * D // 2), F32),
        ],
        compiler_params=pltpu.CompilerParams(vmem_limit_bytes=VMEM_BIG),
        cost_estimate=pl.CostEstimate(
            flops=2 * rows * D * 3 * D, bytes_accessed=16 * rows * D, transcendentals=0
        ),
        name="last",
    )(meta, dqkv, tokens, dx, vec, *w_in)


def swap(values, mask, count):
    return lax.ppermute(values, AXES, [(i, i ^ mask) for i in range(count)])


def tie(values, after):
    values, after = list(values), list(after)
    if not after:
        return values
    return list(lax.optimization_barrier(tuple(values + after))[: len(values)])


class Chain:
    def __init__(self, net, steps, finish):
        self.net, self.steps, self.finish = net, list(steps), finish
        self.got = [None] * len(self.steps)
        self.sends = [[] for _ in self.steps]
        self.results = [None] * len(self.steps)

    def go(self, *after):
        for i, step in enumerate(self.steps):
            if self.results[i] is not None:
                continue
            try:
                got = self.got[i] if self.got[i] is None else tie(self.got[i], after)
                sends = step.send(got)
                values = [v for v, _ in sends]
                if got is None:
                    values = tie(values, after)
                self.sends[i] = values
                self.got[i] = [self.net.swap(v, m) for v, (_, m) in zip(values, sends)]
            except StopIteration as end:
                self.results[i] = end.value
                self.sends[i] = []
        return self

    @property
    def sent(self):
        return [v for part in self.sends for v in part]

    @property
    def received(self):
        return [v for part in self.got for v in part or []]

    def done(self, *after):
        while any(r is None for r in self.results):
            self.go(*after)
            after = ()
        return self.finish(self.results)


class Ready:
    def __init__(self, value):
        self.value, self.sent, self.received = value, [], []

    def go(self, *after):
        return self

    def done(self, *after):
        return self.value


class Cube:
    SIDES = {"a": (2, 4), "b": (4, 2)}

    def __init__(self):
        self.me = lax.axis_index(AXES).astype(jnp.int32)

    def swap(self, values, mask):
        return swap(values, mask, 32)

    def masks(self, order):
        shift = self.SIDES[order]
        return np.array(
            [8 * (k & 3) + shift[0] * (k >> 2 & 1) + shift[1] * (k >> 3) for k in range(PIECES)]
        )

    def meta(self):
        chip = self.me >> 1
        place = jnp.arange(PIECES, dtype=jnp.int32)
        start = [chip ^ jnp.asarray(self.masks(o) >> 1, jnp.int32) for o in "ab"]
        mask = chip ^ place
        x, y = mask & 1, mask >> 1 & 1
        to = [(mask >> 2) + 4 * x + 8 * y, (mask >> 2) + 4 * y + 8 * x]
        return self.me & 1, start + to

    def spread(self, piece, parts):
        got = yield [(piece, 8 * z) for z in (1, 2, 3)]
        held = jnp.stack([piece] + got)
        ends = np.cumsum([0] + [w for _, w in parts])
        cuts = [held[..., a:b] for a, b in zip(ends[:-1], ends[1:])]
        for stage in (0, 1):
            got = yield [(c, self.SIDES[order][stage]) for c, (order, _) in zip(cuts, parts)]
            cuts = [jnp.concatenate(pair) for pair in zip(cuts, got)]
        got = yield [(c, 1) for c in cuts]
        return [v for pair in zip(cuts, got) for v in pair]

    def gather_cols(self, shards, parts):
        left, right = (
            jnp.concatenate([h[side] for h in (jnp.split(s, 2, axis=1) for s in shards)], axis=1)
            for side in (0, 1)
        )
        odd = (self.me & 1) == 1
        got = self.swap(jnp.where(odd, left, right), 1)
        mine = jnp.where(odd, right, left)
        block = jnp.where(odd, jnp.concatenate([got, mine]), jnp.concatenate([mine, got]))
        return Chain(self, [self.spread(block, parts)], lambda results: results[0])

    def gather_rows(self, shard, parts):
        return Chain(self, [self.spread(shard, parts)], lambda results: results[0])

    def gather_small(self, pack):
        every = jnp.broadcast_to(pack, (32, pack.shape[0]))
        return lax.all_to_all(every, AXES, 0, 0, tiled=True)

    def reduce_small(self, pack):
        return jnp.sum(lax.all_to_all(pack, AXES, 0, 0, tiled=True), axis=0)

    def gather_rows(self, shard, order):
        return Chain(self, [self.spread(shard, order)], lambda parts: parts[0])

    def collect(self, owns, others, orders):
        got = yield [(o, 1) for o in others]
        totals = [a.astype(F32) + b.astype(F32) for a, b in zip(owns, got)]
        for stage in (1, 0):
            count = totals[0].shape[0] // 2
            got = yield [
                (t[count:].astype(BF16), self.SIDES[o][stage]) for t, o in zip(totals, orders)
            ]
            totals = [t[:count] + g.astype(F32) for t, g in zip(totals, got)]
        total = jnp.concatenate(totals, axis=1)
        got = yield [(total[z].astype(BF16), 8 * z) for z in (1, 2, 3)]
        return total[0] + sum(g.astype(F32) for g in got)

    def reduce_ff(self, others, owns):
        def finish(results):
            (total,) = results
            block = jnp.concatenate([total[:ROWS_D], total[ROWS_D : 2 * ROWS_D]], axis=1)
            return jnp.concatenate(self.join(block), axis=1), total[2 * ROWS_D :]

        return Chain(self, [self.collect(owns, others, "ab")], finish)

    def reduce_attn(self, others, owns):
        def finish(results):
            (total,) = results
            block = jnp.concatenate([total[:ROWS_D], total[ROWS_D:]], axis=1)
            sides = self.join(block)
            cut = 3 * D // 2
            return tuple(
                jnp.concatenate([s[:, part] for s in sides], axis=1)
                for part in (slice(0, cut), slice(cut, None))
            )

        return Chain(self, [self.collect(owns, others, "ab")], finish)

    def join(self, block):
        rows = block.shape[0] // 2
        low, high = block[:rows], block[rows:]
        odd = (self.me & 1) == 1
        got = self.swap(jnp.where(odd, low, high), 1)
        mine = jnp.where(odd, high, low)
        return jnp.where(odd, got, mine), jnp.where(odd, mine, got)


class Plain:
    def __init__(self, count):
        self.count = count
        self.me = lax.axis_index(AXES)

    def meta(self):
        place = jnp.arange(PIECES, dtype=jnp.int32)
        return jnp.int32(0), [place] * 4

    def gather_cols(self, shards, parts):
        whole = [lax.all_gather(s, AXES, axis=0, tiled=True) for s in shards]
        left, right = (
            jnp.concatenate([h[side] for h in (jnp.split(w, 2, axis=1) for w in whole)], axis=1)
            for side in (0, 1)
        )
        out, at = [], 0
        for _, width in parts:
            for half in (left, right):
                out.append(half[:, at : at + width].reshape(PIECES, -1, width))
            at += width
        return Ready(out)

    def gather_small(self, pack):
        return lax.all_gather(pack, AXES)

    def reduce_small(self, pack):
        return lax.psum_scatter(pack, AXES, scatter_dimension=0, tiled=False)

    def gather_rows(self, shard, parts):
        whole = lax.all_gather(shard, AXES, axis=0, tiled=True)
        whole = whole.reshape(PIECES, 2, -1, whole.shape[1])
        out, at = [], 0
        for _, width in parts:
            out += [whole[:, side, :, at : at + width] for side in (0, 1)]
            at += width
        return Ready(out)

    def scatter(self, whole):
        return lax.psum_scatter(whole.astype(F32), AXES, scatter_dimension=0, tiled=True)

    def reduce_ff(self, others, owns):
        runs = [
            a[:, row : row + ROWS_D].reshape(D, D)
            for a in (owns[0], others[0])
            for row in (0, ROWS_D)
        ]
        rows = jnp.stack([owns[1], others[1]], axis=1).reshape(FF, D)
        return Ready((self.scatter(jnp.concatenate(runs, axis=1)), self.scatter(rows)))

    def reduce_attn(self, others, owns):
        halves_in, halves_out = [], []
        for a, b in (owns, others):
            a, b = a.reshape(D, D), b.reshape(D, D)
            halves_in += [a, b[:, : D // 2]]
            halves_out.append(b[:, D // 2 :])
        return Ready(tuple(self.scatter(jnp.concatenate(h, axis=1)) for h in (halves_in, halves_out)))


PARTS_ATTN = (("a", D), ("b", D))
PARTS_HALVES = (("a", FF // 4), ("b", FF // 4))
PARTS_ROWS = (("a", D // 2), ("b", D // 2))


def body(
    tokens,
    cotangent,
    w_attn_in,
    w_attn_out,
    w_fc_in,
    w_fc_out,
    gains_d,
    biases_d,
    gains_ff,
    biases_ff,
    rel_table,
    head_scale,
    bucket,
    lengths,
    *,
    count,
    cube,
):
    net = Cube() if cube else Plain(count)
    rows = tokens.shape[0]
    chunks = rows // CHUNK

    gather_attn = net.gather_cols([w_attn_in, w_attn_out], PARTS_ATTN).go()
    small = tie((gains_d, biases_d, gains_ff[None], biases_ff, rel_table), gather_attn.sent)
    sizes = [v.size for v in small]
    ends = np.cumsum(sizes)
    width = -(-int(ends[-1] + 16) // 1024) * 1024
    pack = jnp.concatenate([v.reshape(-1) for v in small] + [jnp.zeros(width - ends[-1], BF16)])
    packs = net.gather_small(pack)

    bucket, lengths = tie([bucket, lengths], [pack])
    large = jnp.sum((bucket == 1).astype(jnp.int32), dtype=jnp.int32)
    kinds = (jnp.arange(chunks, dtype=jnp.int32) >= large).astype(jnp.int32)
    core, tables = net.meta()
    meta = jnp.concatenate(
        [core.astype(jnp.int32)[None], kinds, large[None], jnp.zeros(2, jnp.int32), *tables, lengths]
    )
    keys, keys_back, queries = (jnp.asarray(t) for t in pick_tables())
    gather_ff = net.gather_cols([w_fc_in], PARTS_HALVES)
    gather_down = net.gather_rows(w_fc_out, PARTS_ROWS)

    arrived = gather_attn.received
    gather_attn.go(meta)
    gather_ff.go(*arrived)
    (packs,) = tie([packs], gather_attn.sent + gather_ff.sent)
    vec, wide, lines = unpack(packs, head_scale[None], count)
    gather_attn.go(vec)
    (lines,) = tie([lines], gather_attn.sent)
    bias = build_bias(lines, keys, queries)
    gather_ff.go(bias)
    gather_attn.go(*gather_ff.sent)
    gather_down.go(*gather_ff.sent)
    attn_pieces = gather_attn.done()
    out_pieces = attn_pieces[2:]

    (tokens_in,) = tie([tokens], gather_ff.sent)
    low_in, query, key, value = project(meta, tokens_in, vec, attn_pieces)
    gather_ff.go(low_in)
    gather_down.go(low_in)
    (query_in,) = tie([query], gather_ff.sent + gather_down.sent)
    heads = attend(meta, query_in, key, value, bias, 0, chunks // 2)
    gather_down.go(heads[2])
    gather_ff.go(heads[2])
    (query_in,) = tie([query], gather_down.sent + gather_ff.sent)
    mixed, turned, lse = attend(
        meta, query_in, key, value, bias, chunks // 2, chunks - chunks // 2, heads
    )
    gather_down.go(lse)
    ff_pieces = gather_ff.done(lse)
    down_pieces = gather_down.done()
    out_tokens, mid, low_attn, sums_a, sums_ff, dz, *ff_grads = feed(
        meta, tokens, mixed, cotangent, vec, wide, out_pieces, ff_pieces, down_pieces
    )

    reduce_ff = net.reduce_ff(ff_grads[:2], ff_grads[2:]).go()
    (dz,) = tie([dz], reduce_ff.sent)
    dx, do, sums_b, *out_grads = middle(
        meta, dz, mid, mixed, cotangent, low_attn, vec, ff_pieces, out_pieces
    )
    reduce_ff.go(sums_b)
    (do,) = tie([do], reduce_ff.sent)
    dqkv, tiles, other_a, own_a, other_b, own_b = attend_back(
        meta, query, key, value, do, turned, lse, bias, low_in, out_grads
    )
    reduce_attn = net.reduce_attn((other_a, other_b), (own_a, own_b)).go()
    reduce_ff.go(tiles)
    (tiles,) = tie([tiles], reduce_ff.sent)
    (tiles,) = tie([tiles], reduce_attn.sent)
    grad_table = table_grads(tiles, keys_back, queries)
    reduce_attn.go(grad_table)
    reduce_ff.go(grad_table)
    (dqkv,) = tie([dqkv], reduce_attn.sent + reduce_ff.sent)
    grad_tokens, sums_c, sums_p = last(meta, dqkv, tokens, dx, vec, attn_pieces)
    reduce_attn.go(sums_c)
    terms = (sums_a, sums_b, sums_c, sums_p, sums_ff, grad_table)
    terms = pack_terms(*tie(terms, reduce_attn.sent), count, width)
    reduce_attn.go(terms)
    (terms,) = tie([terms], reduce_attn.sent)
    mine = net.reduce_small(terms)
    grad_fc_in, grad_fc_out = reduce_ff.done(sums_c)
    grad_attn_in, grad_attn_out = reduce_attn.done()

    grads = [mine[end - size : end].reshape(v.shape) for v, size, end in zip(small, sizes, ends)]
    return (
        out_tokens,
        grad_tokens,
        grad_attn_in,
        grad_attn_out,
        grad_fc_in,
        grad_fc_out,
        grads[0],
        grads[1],
        grads[2][0],
        grads[3],
        grads[4],
        mine[ends[-1] : ends[-1] + HEADS],
    )


def solution(mesh):
    rows = P(AXES, None)
    columns = P(None, AXES)
    line = P(AXES)
    count = mesh.shape["wide"] * mesh.shape["narrow"]
    cube = (mesh.shape["wide"], mesh.shape["narrow"]) == (8, 4)
    return jax.shard_map(
        functools.partial(body, count=count, cube=cube),
        mesh=mesh,
        in_specs=(
            rows, rows, rows, rows, rows, rows,
            columns, columns, line, columns, columns, P(), line, line,
        ),
        out_specs=(
            rows, rows, rows, rows, rows, rows,
            columns, columns, line, columns, columns, P(),
        ),
        check_vma=False,
    )
```

```python
import functools

import jax
import jax.numpy as jnp
import numpy as np
from jax import lax
from jax.experimental import pallas as pl
from jax.experimental.pallas import tpu as pltpu
from jax.sharding import PartitionSpec as P

HEADS = 12
HEAD_DIM = 64
D = 768
FF = 3072
GRID_L = 15
GRID_S = 8
SLOT_L = 256
SLOT_S = 64
STRIDE = 32
RELS = 1024
CHUNK = 256
PAIR = 2 * CHUNK
PIECES = 16
ROWS_D = D // PIECES
ROWS_F = FF // (2 * PIECES)

NEG_FILL = -1e30
NORM_EPS = 1e-05
HALF_ROOT = 0.7071067811865476
DENSITY_SCALE = 0.3989422804014327
QUERY_SCALE = 0.125
AXES = ("wide", "narrow")
F32 = jnp.float32
BF16 = jnp.bfloat16
VMEM_BIG = 60 * 2**20
VMEM_ALL = 63 * 2**20

NN = (((1,), (0,)), ((), ()))
NT = (((1,), (1,)), ((), ()))
TN = (((0,), (0,)), ((), ()))


ANY = pl.BlockSpec(memory_space=pl.ANY)


def full(*shape):
    return pl.BlockSpec(shape, lambda *_: (0,) * len(shape))


def dot(left, right, dims=NN):
    return lax.dot_general(left, right, dims, preferred_element_type=F32)


def unit_rows(values):
    center = values - jnp.mean(values, axis=-1, keepdims=True)
    spread = lax.rsqrt(jnp.mean(center * center, axis=-1, keepdims=True) + NORM_EPS)
    return center * spread, spread


def unit_rows_back(inner, scaled, spread):
    return spread * (
        inner
        - jnp.mean(inner, axis=-1, keepdims=True)
        - scaled * jnp.mean(inner * scaled, axis=-1, keepdims=True)
    )


def col_sum(values):
    return jnp.sum(values, axis=0, keepdims=True)


def unit_position(kind):
    place = np.arange(CHUNK)
    if kind == 0:
        return np.minimum(place // GRID_L, GRID_L - 1), place % GRID_L
    inner = place % SLOT_S
    return inner // GRID_S, inner % GRID_S


def pick_tables():
    keys = np.zeros((2, CHUNK, 512), np.float32)
    keys_back = np.zeros((2, CHUNK, 512), np.float32)
    queries = np.zeros((2, CHUNK, CHUNK), np.float32)
    for kind in range(2):
        row, col = unit_position(kind)
        line = STRIDE * row + col
        keys[kind, np.arange(CHUNK), line] = 1
        keys_back[kind, np.arange(CHUNK), 511 - line] = 1
        queries[kind, 16 * row + col, np.arange(CHUNK)] = 1
    return keys.astype(BF16), keys_back.astype(BF16), queries.astype(BF16)


def owner_of_lane(lanes, each, last=None):
    lane = lax.broadcasted_iota(jnp.int32, lanes, 1)
    entry = lane if last is None else last - lane
    device = lax.broadcasted_iota(jnp.int32, lanes, 0)
    return ((entry >= device * each) & (entry < device * each + each)).astype(BF16)


def place_in_part(lanes, each, last=None):
    lane = lax.broadcasted_iota(jnp.int32, lanes, 1)
    entry = lane if last is None else last - lane
    row = lax.broadcasted_iota(jnp.int32, lanes, 0)
    return ((entry >= 0) & (lax.rem(entry + each, each) == row)).astype(F32)


def unpack_kernel(pack_ref, scale_ref, vec_ref, wide_ref, line_ref, *, count):
    each_d, each_f, each_t = D // count, FF // count, RELS // count
    pack = pack_ref[...]

    def rows(start, amount, each, lanes, last=None):
        owner = owner_of_lane((count, lanes), each, last)
        place = place_in_part((each, lanes), each, last)
        part = pack[:, start : start + amount * each]
        spread = dot(part, owner, TN)
        return [col_sum(spread[r * each : r * each + each] * place) for r in range(amount)]

    d_rows = rows(0, 10, each_d, D)
    ff_rows = rows(10 * each_d, 3, each_f, FF)
    lines = rows(10 * each_d + 3 * each_f, HEADS, each_t, RELS, 1006)
    lane = lax.broadcasted_iota(jnp.int32, (HEADS, D), 1)
    row = lax.broadcasted_iota(jnp.int32, (HEADS, D), 0)
    heads = dot(scale_ref[...], (lane // HEAD_DIM == row).astype(BF16))
    vec_ref[...] = jnp.concatenate(d_rows + [heads, jnp.zeros((5, D), F32)], axis=0)
    wide_ref[...] = jnp.concatenate(ff_rows + [jnp.zeros((5, FF), F32)], axis=0)
    for h in range(HEADS):
        line_ref[h] = jnp.broadcast_to(lines[h], (16, RELS))


def unpack(pack, scale, count):
    return pl.pallas_call(
        functools.partial(unpack_kernel, count=count),
        out_shape=[
            jax.ShapeDtypeStruct((16, D), F32),
            jax.ShapeDtypeStruct((8, FF), F32),
            jax.ShapeDtypeStruct((HEADS, 16, RELS), F32),
        ],
        compiler_params=pltpu.CompilerParams(vmem_limit_bytes=VMEM_BIG),
        cost_estimate=pl.CostEstimate(flops=2 * 10**9, bytes_accessed=4 * 10**6, transcendentals=0),
        name="unpack",
    )(pack, scale)


TURN = 4


def bias_kernel(line_ref, keys_ref, queries_ref, out_ref):
    left = lax.broadcasted_iota(jnp.int32, (CHUNK, CHUNK), 0) // SLOT_S
    right = lax.broadcasted_iota(jnp.int32, (CHUNK, CHUNK), 1) // SLOT_S
    spread_rows = []
    for h in range(TURN):
        base = pltpu.roll(line_ref[h], RELS - 511, 1, stride=1, stride_axis=0)
        turns = [base] + [pltpu.roll(base, STRIDE * m, 1) for m in (1, 2, 3)]
        twice = [jnp.concatenate([t, t[:, :512]], axis=1) for t in turns]
        groups = []
        for r in range(16):
            start = (RELS - 128 * (r // 4)) % RELS
            groups.append(twice[r % 4][:, start : start + 512])
        spread_rows.append(jnp.concatenate(groups, axis=0).astype(BF16))
    by_key = [
        (dot(keys_ref[0], g, NT).astype(BF16), dot(keys_ref[1, :SLOT_S], g, NT).astype(BF16))
        for g in spread_rows
    ]
    for h in range(TURN):
        out_ref[0, h] = dot(by_key[h][0], queries_ref[0]).astype(BF16)
        tile = dot(by_key[h][1], queries_ref[1])
        tile = jnp.concatenate([tile] * (CHUNK // SLOT_S), axis=0)
        out_ref[1, h] = jnp.where(left == right, tile, NEG_FILL).astype(BF16)


def build_bias(lines, keys, queries):
    return pl.pallas_call(
        bias_kernel,
        grid=(HEADS // TURN,),
        in_specs=[
            pl.BlockSpec((TURN, 16, RELS), lambda h: (h, 0, 0)),
            full(2, CHUNK, 512),
            full(2, CHUNK, CHUNK),
        ],
        out_specs=pl.BlockSpec((2, TURN, CHUNK, CHUNK), lambda h: (0, h, 0, 0)),
        out_shape=jax.ShapeDtypeStruct((2, HEADS, CHUNK, CHUNK), BF16),
        compiler_params=pltpu.CompilerParams(vmem_limit_bytes=VMEM_BIG),
        cost_estimate=pl.CostEstimate(flops=8 * 10**9, bytes_accessed=4 * 10**6, transcendentals=0),
        name="bias_tiles",
    )(lines, keys, queries)


def pack_kernel(a_ref, b_ref, c_ref, p_ref, ff_ref, table_ref, out_ref, *, count):
    each_d, each_f, each_t = D // count, FF // count, RELS // count

    def columns(rows, each, lanes):
        owner = owner_of_lane((count, lanes), each)
        place = place_in_part((each, lanes), each)
        parts = []
        for row in rows:
            high, rest = halves(row * place)
            parts.append(dot(high, owner, NT) + dot(rest, owner, NT))
        return jnp.concatenate(parts, axis=0)

    a, b, c = a_ref[...], b_ref[...], c_ref[...]
    p = p_ref[...]
    d_rows = [
        c[0:1], b[3:4], b[0:1],
        c[1:2], p[0:1, :D], p[1:2, D // 2 :], b[4:5], b[2:3], b[1:2], a[0:1],
    ]
    ff = ff_ref[...]
    lane = lax.broadcasted_iota(jnp.int32, (16, D), 1)
    row = lax.broadcasted_iota(jnp.int32, (16, D), 0)
    high, rest = halves(jnp.broadcast_to(b[5:6], (16, D)) * (lane // HEAD_DIM == row).astype(F32))
    ones = jnp.ones((count, D), BF16)
    out = [
        columns(d_rows, each_d, D),
        columns([ff[0:1], ff[2:3], ff[1:2]], each_f, FF),
        columns([table_ref[h, 0:1] for h in range(HEADS)], each_t, RELS),
        dot(high, ones, NT) + dot(rest, ones, NT),
    ]
    used = sum(o.shape[0] for o in out)
    out.append(jnp.zeros((out_ref.shape[1] - used, count), F32))
    out_ref[...] = jnp.concatenate(out, axis=0).T


def pack_terms(sums_a, sums_b, sums_c, sums_p, sums_ff, table, count, width):
    return pl.pallas_call(
        functools.partial(pack_kernel, count=count),
        out_shape=jax.ShapeDtypeStruct((count, width), F32),
        compiler_params=pltpu.CompilerParams(vmem_limit_bytes=VMEM_BIG),
        cost_estimate=pl.CostEstimate(flops=10**9, bytes_accessed=10**6, transcendentals=0),
        name="pack_terms",
    )(sums_a, sums_b, sums_c, sums_p, sums_ff, table)


def halves(values):
    high = values.astype(BF16)
    return high, (values - high.astype(F32)).astype(BF16)


def table_kernel(tiles_ref, keys_ref, queries_ref, out_ref):
    by_query = []
    for h in range(TURN):
        small = tiles_ref[1, h, :SLOT_S]
        for part in range(1, CHUNK // SLOT_S):
            small = small + tiles_ref[1, h, part * SLOT_S : (part + 1) * SLOT_S]
        by_query.append(
            (
                dot(queries_ref[0], tiles_ref[0, h].astype(BF16), NT).astype(BF16),
                dot(queries_ref[1], small.astype(BF16), NT).astype(BF16),
            )
        )
    totals = [
        dot(large, keys_ref[0]) + dot(small, keys_ref[1, :SLOT_S]) for large, small in by_query
    ]
    for h, total in enumerate(totals):
        line = jnp.zeros((16, RELS), F32)
        for m in range(4):
            part = jnp.zeros((16, RELS), F32)
            for k in range(4):
                group = total[16 * (4 * k + m) : 16 * (4 * k + m) + 16]
                pieces = [group, jnp.zeros((16, 512 - 128 * k), F32)]
                if k:
                    pieces = [jnp.zeros((16, 128 * k), F32)] + pieces
                part += jnp.concatenate(pieces, axis=1)
            line += pltpu.roll(part, STRIDE * m, 1) if m else part
        line = pltpu.roll(line, 0, 1, stride=1, stride_axis=0)
        out_ref[h] = pltpu.roll(jnp.broadcast_to(col_sum(line), (8, RELS)), RELS - 16, 1)


def table_grads(tiles, keys_back, queries):
    return pl.pallas_call(
        table_kernel,
        grid=(HEADS // TURN,),
        in_specs=[
            pl.BlockSpec((2, TURN, CHUNK, CHUNK), lambda h: (0, h, 0, 0)),
            full(2, CHUNK, 512),
            full(2, CHUNK, CHUNK),
        ],
        out_specs=pl.BlockSpec((TURN, 8, RELS), lambda h: (h, 0, 0)),
        out_shape=jax.ShapeDtypeStruct((HEADS, 8, RELS), F32),
        compiler_params=pltpu.CompilerParams(vmem_limit_bytes=VMEM_BIG),
        cost_estimate=pl.CostEstimate(flops=8 * 10**9, bytes_accessed=6 * 10**6, transcendentals=0),
        name="table_grads",
    )(tiles, keys_back, queries)


META_KIND = 1
META_LARGE = 5
META_LENGTH = 72
META_FROM = {"a": 8, "b": 24}
META_TO = {"a": 40, "b": 56}


def live_rows(meta, chunk):
    place = lax.broadcasted_iota(jnp.int32, (CHUNK, 1), 0)
    large = meta[META_LARGE]
    first = large + (chunk - large) * (SLOT_L // SLOT_S)
    is_large = chunk < large
    end = jnp.zeros((CHUNK, 1), jnp.int32)
    for part in range(SLOT_L // SLOT_S):
        slot = jnp.where(is_large, chunk, first + part)
        start = jnp.where(is_large, 0, part * SLOT_S)
        end = jnp.where(place >= part * SLOT_S, start + meta[META_LENGTH + slot], end)
    return (place < end).astype(F32)


class Load:
    def __init__(self, meta, sem, scratch):
        self.meta, self.sem, self.scratch = meta, sem, scratch

    def cols(self, order, own, other, start, source_start, width):
        core, rows = self.meta[0], own.shape[1]
        for k in range(PIECES):
            place = pl.multiple_of(self.meta[META_FROM[order] + k] * rows, 16)
            for half, source in ((core, own), (1 - core, other)):
                pltpu.make_async_copy(
                    source.at[k, :, pl.ds(source_start, width)],
                    self.scratch.at[half, pl.ds(place, rows), pl.ds(start, width)],
                    self.sem,
                ).start()

    def rows(self, order, own, other, start):
        core, rows, width = self.meta[0], own.shape[1], own.shape[2]
        for k in range(PIECES):
            chip = self.meta[META_FROM[order] + k]
            for half, source in ((core, own), (1 - core, other)):
                place = pl.multiple_of((2 * chip + half) * rows, 16)
                pltpu.make_async_copy(
                    source.at[k],
                    self.scratch.at[pl.ds(place, rows), pl.ds(start, width)],
                    self.sem,
                ).start()

    def wait(self):
        pltpu.make_async_copy(self.scratch, self.scratch, self.sem).wait()


PARTS = (slice(0, CHUNK), slice(CHUNK, PAIR))


def project_kernel(meta, x_ref, vec_ref, a0, a1, b0, b1, low_ref, q_ref, k_ref, v_ref, w_scr, sem):
    @pl.when(pl.program_id(0) == 0)
    def _():
        load = Load(meta, sem, w_scr)
        load.cols("a", a0, a1, 0, 0, D)
        load.cols("b", b0, b1, D, 0, D // 2)
        load.wait()

    products = []
    for p in PARTS:
        scaled, _ = unit_rows(x_ref[p].astype(F32))
        low = (scaled * vec_ref[0:1] + vec_ref[3:4]).astype(BF16)
        low_ref[p] = low
        products.append((dot(low, w_scr[0]), dot(low, w_scr[1])))
    for p, (first, second) in zip(PARTS, products):
        q_ref[p] = ((first[:, :D] + vec_ref[4:5]) * QUERY_SCALE).astype(BF16)
        k_ref[p, : D // 2] = first[:, D:].astype(BF16)
        k_ref[p, D // 2 :] = second[:, : D // 2].astype(BF16)
        v_ref[p] = (second[:, D // 2 :] + vec_ref[5:6]).astype(BF16)


def project(meta, tokens, vec, pieces):
    rows = tokens.shape[0]
    tile = pl.BlockSpec((PAIR, D), lambda c, m: (c, 0))
    return pl.pallas_call(
        project_kernel,
        grid_spec=pltpu.PrefetchScalarGridSpec(
            num_scalar_prefetch=1,
            grid=(rows // PAIR,),
            in_specs=[tile, full(16, D), ANY, ANY, ANY, ANY],
            out_specs=[tile] * 4,
            scratch_shapes=[pltpu.VMEM((2, D, 3 * D // 2), BF16), pltpu.SemaphoreType.DMA],
        ),
        out_shape=[jax.ShapeDtypeStruct((rows, D), BF16)] * 4,
        compiler_params=pltpu.CompilerParams(vmem_limit_bytes=VMEM_BIG),
        cost_estimate=pl.CostEstimate(
            flops=2 * rows * D * 3 * D, bytes_accessed=16 * rows * D, transcendentals=0
        ),
        name="project",
    )(meta, tokens, vec, *pieces)


def attend_kernel(meta, q_ref, k_ref, v_ref, bias_ref, x_ref, vec_ref, o0, o1, *refs, first):
    mixed_ref, turned_ref, lse_ref, mid_ref, aln_ref, low_ref, wo_scr, sem = refs[-8:]

    @pl.when(pl.program_id(0) == 0)
    def _():
        Load(meta, sem, wo_scr).cols("b", o0, o1, 0, D // 2, D // 2)

    mask = (1.0 - live_rows(meta, pl.program_id(0) + first)) * NEG_FILL
    mask = jnp.broadcast_to(mask, (CHUNK, CHUNK))
    query_turned = q_ref[...].astype(F32).T.astype(BF16)
    value_turned = v_ref[...].astype(F32).T.astype(BF16)
    parts = [slice(h * HEAD_DIM, (h + 1) * HEAD_DIM) for h in range(HEADS)]
    sums = []

    def mix(h, exponent, largest, row_total):
        out = dot(value_turned[parts[h]], exponent)
        turned_ref[0, parts[h]] = out * (1.0 / row_total)
        sums.append(largest + jnp.log(row_total))

    product, before = dot(k_ref[:, parts[0]], query_turned[parts[0]]), None
    for h in range(HEADS):
        scores = product + bias_ref[0, h].astype(F32) + mask
        if h + 1 < HEADS:
            product = dot(k_ref[:, parts[h + 1]], query_turned[parts[h + 1]])
        largest = jnp.max(scores, axis=0, keepdims=True)
        exponent = jnp.exp(scores - largest)
        row_total = jnp.sum(exponent, axis=0, keepdims=True)
        if before:
            mix(*before)
        before = (h, exponent.astype(BF16), largest, row_total)
    mix(*before)
    lse_ref[0] = jnp.concatenate(sums + [jnp.zeros((16 - HEADS, CHUNK), F32)], axis=0)
    mixed = turned_ref[0].T
    mixed_ref[...] = mixed

    @pl.when(pl.program_id(0) == 0)
    def _():
        Load(meta, sem, wo_scr).wait()

    scaled, _ = unit_rows(mixed * vec_ref[10:11])
    aln = (scaled * vec_ref[1:2] + vec_ref[6:7]).astype(BF16)
    aln_ref[...] = aln
    branch = jnp.concatenate([dot(aln, wo_scr[0]), dot(aln, wo_scr[1])], axis=1)
    mid = x_ref[...].astype(F32) + branch + vec_ref[7:8]
    mid_ref[...] = mid
    scaled, _ = unit_rows(mid)
    low_ref[...] = (scaled * vec_ref[2:3] + vec_ref[8:9]).astype(BF16)


def attend(meta, query, key, value, bias, tokens, vec, w_out, first, chunks, before=()):
    rows = query.shape[0]
    tile = pl.BlockSpec((CHUNK, D), lambda c, m: (c + first, 0))
    return pl.pallas_call(
        functools.partial(attend_kernel, first=first),
        grid_spec=pltpu.PrefetchScalarGridSpec(
            num_scalar_prefetch=1,
            grid=(chunks,),
            in_specs=[
                tile, tile, tile,
                pl.BlockSpec(
                    (1, HEADS, CHUNK, CHUNK), lambda c, m: (m[META_KIND + c + first], 0, 0, 0)
                ),
                tile,
                full(16, D),
                ANY, ANY,
            ]
            + [ANY] * len(before),
            out_specs=[
                tile,
                pl.BlockSpec((1, D, CHUNK), lambda c, m: (c + first, 0, 0)),
                pl.BlockSpec((1, 16, CHUNK), lambda c, m: (c + first, 0, 0)),
                tile, tile, tile,
            ],
            scratch_shapes=[pltpu.VMEM((2, D, D // 2), BF16), pltpu.SemaphoreType.DMA],
        ),
        out_shape=[
            jax.ShapeDtypeStruct((rows, D), F32),
            jax.ShapeDtypeStruct((rows // CHUNK, D, CHUNK), F32),
            jax.ShapeDtypeStruct((rows // CHUNK, 16, CHUNK), F32),
            jax.ShapeDtypeStruct((rows, D), F32),
            jax.ShapeDtypeStruct((rows, D), BF16),
            jax.ShapeDtypeStruct((rows, D), BF16),
        ],
        input_output_aliases={9 + i: i for i in range(len(before))},
        compiler_params=pltpu.CompilerParams(vmem_limit_bytes=VMEM_BIG),
        cost_estimate=pl.CostEstimate(
            flops=10 * 10**9, bytes_accessed=16 * rows * D, transcendentals=0
        ),
        name="attend",
    )(meta, query, key, value, bias, tokens, vec, *w_out, *before)


CUT = 512
ROOT_PART = 0.3275911 * HALF_ROOT
TAIL = (0.127414796, -0.142248368, 0.7107068705, -0.7265760135, 0.5307027145)


def normal_parts(z):
    density = jnp.exp(-0.5 * z * z)
    t = 1.0 / (1.0 + ROOT_PART * jnp.abs(z))
    tail = TAIL[4] * t + TAIL[3]
    for c in (TAIL[2], TAIL[1], TAIL[0]):
        tail = tail * t + c
    tail = tail * t * density
    return jnp.where(z >= 0.0, 1.0 - tail, tail), z * (DENSITY_SCALE * density)


def lane_sum(values):
    return jnp.sum(values, axis=-1, keepdims=True)


def feed_kernel(
    meta, mid_ref, low_ref, cot_ref, vec_ref, wide_ref,
    i0, i1, i2, i3, f0, f1, f2, f3,
    out_ref, sums_ref, sums_ff_ref, dz_out, g0, g1, g2, g3,
    wi_scr, wf_scr, unit_scr, slope_scr, dm_scr,
    df_scr, low_scr, m_scr, dz_scr, cols_scr, rows_scr, sems, stage_sems,
):
    step = pl.program_id(0)
    mine = pl.ds(pl.multiple_of(step * CHUNK, CHUNK), CHUNK)

    def feed_loads():
        return [Load(meta, sems.at[i], s) for i, s in enumerate((wi_scr, wf_scr))]

    def arrived(which):
        @pl.when(step == 0)
        def _():
            feed_loads()[which].wait()

    @pl.when(step == 0)
    def _():
        loads = feed_loads()
        loads[0].cols("a", i0, i1, 0, 0, FF // 4)
        loads[0].cols("b", i2, i3, FF // 4, 0, FF // 4)
        loads[1].rows("a", f0, f1, 0)
        loads[1].rows("b", f2, f3, D // 2)
        sums_ref[...] = jnp.zeros_like(sums_ref)
        sums_ff_ref[...] = jnp.zeros_like(sums_ff_ref)

    live = live_rows(meta, step)
    df_full = cot_ref[...].astype(F32) * live
    df = df_full.astype(BF16)
    df_scr[mine] = df
    sums_ref[0:1] += col_sum(df_full)
    mid = mid_ref[...]
    low = low_ref[...]
    low_scr[mine] = low
    arrived(0)

    cuts = [slice(a, a + CUT) for a in range(0, FF, CUT)]
    inner = [(a * CUT // (FF // 2), slice(a * CUT % (FF // 2), a * CUT % (FF // 2) + CUT)) for a in range(FF // CUT)]
    total = jnp.zeros((CHUNK, 1), F32)
    for cut, (half, part) in zip(cuts, inner):
        z = dot(low, wi_scr[half, :, part]) + wide_ref[1:2, cut]
        cumulative, rest = normal_parts(z)
        act = z * cumulative
        unit_scr[:, cut] = act
        slope_scr[:, cut] = cumulative + rest
        total += lane_sum(act)
    mean = total * (1.0 / FF)
    square = jnp.zeros((CHUNK, 1), F32)
    arrived(1)
    for cut in cuts:
        dm_scr[:, cut] = dot(df, wf_scr[cut], NT)
        center = unit_scr[:, cut] - mean
        square += lane_sum(center * center)
    spread = lax.rsqrt(square * (1.0 / FF) + NORM_EPS)
    out = mid + vec_ref[9:10]
    first = jnp.zeros((CHUNK, 1), F32)
    second = jnp.zeros((CHUNK, 1), F32)
    for cut in cuts:
        unit = (unit_scr[:, cut] - mean) * spread
        unit_scr[:, cut] = unit
        m = (unit * wide_ref[0:1, cut] + wide_ref[2:3, cut]).astype(BF16)
        m_scr[mine, cut] = m
        out += dot(m, wf_scr[cut])
        dm = dm_scr[:, cut]
        sums_ff_ref[0:1, cut] += col_sum(dm * unit)
        sums_ff_ref[1:2, cut] += col_sum(dm)
        inside = dm * wide_ref[0:1, cut]
        first += lane_sum(inside)
        second += lane_sum(inside * unit)
    out_ref[...] = (out * live).astype(BF16)
    first = first * (1.0 / FF)
    second = second * (1.0 / FF)
    for cut, (half, part) in zip(cuts, inner):
        inside = dm_scr[:, cut] * wide_ref[0:1, cut]
        du = spread * (inside - first - unit_scr[:, cut] * second)
        dz_full = du * slope_scr[:, cut]
        sums_ff_ref[2:3, cut] += col_sum(dz_full)
        dz_scr[half, mine, part] = dz_full.astype(BF16)
    pltpu.make_async_copy(dz_scr.at[:, mine], dz_out.at[:, mine], sems.at[2]).start()

    @pl.when(step == pl.num_programs(0) - 1)
    def _():
        core = meta[0]
        stages = [Stage(cols_scr, stage_sems, 0), Stage(rows_scr, stage_sems, 2)]
        for side, out in ((1 - core, g0), (core, g2)):
            for b in range(D // BAND):
                band = dot(low_scr[:, b * BAND : (b + 1) * BAND], dz_scr[side], TN).astype(BF16)
                stage = stages[0].take()
                for i in range(BAND // ROWS_D):
                    rows = slice(i * ROWS_D, (i + 1) * ROWS_D)
                    stage[i, :ROWS_D] = band[rows, :D]
                    stage[i, ROWS_D:] = band[rows, D:]
                    piece = meta[META_TO["a"] + b * (BAND // ROWS_D) + i]
                    stages[0].send(stage.at[i], out.at[piece])
        for b in range(FF // BAND):
            band = dot(m_scr[:, b * BAND : (b + 1) * BAND], df_scr[...], TN).astype(BF16)
            stage = stages[1].take()
            for i in range(BAND // ROWS_F):
                stage[i] = band[i * ROWS_F : (i + 1) * ROWS_F]
            for parity in range(2):
                for own, out in ((True, g3), (False, g1)):

                    @pl.when((core == parity) == own)
                    def _():
                        for i in range(parity, BAND // ROWS_F, 2):
                            piece = meta[META_TO["b"] + (b * (BAND // ROWS_F) + i) // 2]
                            stages[1].send(stage.at[i], out.at[piece])

        for stage in stages:
            stage.end()
        pltpu.make_async_copy(dz_scr, dz_out, sems.at[2]).wait()


class Stage:
    def __init__(self, scratch, sems, first):
        self.scratch, self.sems, self.first, self.count = scratch, sems, first, 0

    def wait(self, slot):
        buffer = self.scratch.at[slot]
        pltpu.make_async_copy(buffer, buffer, self.sems.at[self.first + slot]).wait()

    def take(self):
        self.slot = self.count % 2
        if self.count >= 2:
            self.wait(self.slot)
        self.count += 1
        return self.scratch.at[self.slot]

    def send(self, source, target):
        pltpu.make_async_copy(source, target, self.sems.at[self.first + self.slot]).start()

    def end(self):
        for slot in range(min(2, self.count)):
            self.wait((self.count - 1 - slot) % 2)


BAND = 384


def feed(meta, mid, low, cot, vec, wide, w_in, w_down):
    rows = mid.shape[0]
    tile = pl.BlockSpec((CHUNK, D), lambda c, m: (c, 0))
    return pl.pallas_call(
        feed_kernel,
        grid_spec=pltpu.PrefetchScalarGridSpec(
            num_scalar_prefetch=1,
            grid=(rows // CHUNK,),
            in_specs=[
                tile, tile, tile,
                full(16, D), full(8, FF),
                *[ANY] * 8,
            ],
            out_specs=[tile, full(8, D), full(3, FF), *[ANY] * 5],
            scratch_shapes=[
                pltpu.VMEM((2, D, FF // 2), BF16),
                pltpu.VMEM((FF, D), BF16),
                pltpu.VMEM((CHUNK, FF), F32),
                pltpu.VMEM((CHUNK, FF), F32),
                pltpu.VMEM((CHUNK, FF), F32),
                pltpu.VMEM((rows, D), BF16),
                pltpu.VMEM((rows, D), BF16),
                pltpu.VMEM((rows, FF), BF16),
                pltpu.VMEM((2, rows, FF // 2), BF16),
                pltpu.VMEM((2, BAND // ROWS_D, 2 * ROWS_D, D), BF16),
                pltpu.VMEM((2, BAND // ROWS_F, ROWS_F, D), BF16),
                pltpu.SemaphoreType.DMA((4,)),
                pltpu.SemaphoreType.DMA((4,)),
            ],
        ),
        out_shape=[
            jax.ShapeDtypeStruct((rows, D), BF16),
            jax.ShapeDtypeStruct((8, D), F32),
            jax.ShapeDtypeStruct((3, FF), F32),
            jax.ShapeDtypeStruct((2, rows, FF // 2), BF16),
        ]
        + [jax.ShapeDtypeStruct((PIECES, ROWS_F, D), BF16)] * 4,
        compiler_params=pltpu.CompilerParams(vmem_limit_bytes=VMEM_ALL),
        cost_estimate=pl.CostEstimate(
            flops=2 * rows * D * 5 * FF, bytes_accessed=40 * rows * D, transcendentals=0
        ),
        name="feed",
    )(meta, mid, low, cot, vec, wide, *w_in, *w_down)


def middle_kernel(
    meta, dz_ref, mid_ref, mixed_ref, cot_ref, aln_ref, vec_ref, i0, i1, i2, i3, o0, o1,
    dx_ref, do_ref, sums_ref, other_out, own_out, wi_scr, wo_scr, da_scr, stage_scr, sems,
):
    step = pl.program_id(0)

    def loads():
        return [Load(meta, sems.at[i], s) for i, s in enumerate((wi_scr, wo_scr))]

    @pl.when(step == 0)
    def _():
        first, second = loads()
        first.cols("a", i0, i1, 0, 0, FF // 4)
        first.cols("b", i2, i3, FF // 4, 0, FF // 4)
        second.cols("b", o0, o1, 0, D // 2, D // 2)
        sums_ref[...] = jnp.zeros_like(sums_ref)
        first.wait()
        second.wait()

    dhs = [dot(dz_ref[0, p], wi_scr[0], NT) + dot(dz_ref[1, p], wi_scr[1], NT) for p in PARTS]
    dns = []
    for k, (p, dh) in enumerate(zip(PARTS, dhs)):
        scaled, spread = unit_rows(mid_ref[p])
        grad = cot_ref[p].astype(F32) * live_rows(meta, 2 * step + k)
        dx = grad + unit_rows_back(dh * vec_ref[2:3], scaled, spread)
        da = dx.astype(BF16)
        dns.append(dot(da[:, : D // 2], wo_scr[0], NT) + dot(da[:, D // 2 :], wo_scr[1], NT))
        mine = pl.ds(pl.multiple_of(step * PAIR + k * CHUNK, CHUNK), CHUNK)
        da_scr[0, mine] = da[:, : D // 2]
        da_scr[1, mine] = da[:, D // 2 :]
        dx_ref[p] = dx
        sums_ref[0:1] += col_sum(dh * scaled)
        sums_ref[1:2] += col_sum(dh)
        sums_ref[2:3] += col_sum(dx)
    for p, dn in zip(PARTS, dns):
        mixed = mixed_ref[p]
        scaled, spread = unit_rows(mixed * vec_ref[10:11])
        heads = unit_rows_back(dn * vec_ref[1:2], scaled, spread)
        do_ref[p] = (heads * vec_ref[10:11]).astype(BF16)
        sums_ref[3:4] += col_sum(dn * scaled)
        sums_ref[4:5] += col_sum(dn)
        sums_ref[5:6] += col_sum(heads * mixed)

    @pl.when(step == pl.num_programs(0) - 1)
    def _():
        core = meta[0]
        stages = Stage(stage_scr, sems, 2)
        for side, out in ((1 - core, other_out), (core, own_out)):
            band = dot(aln_ref[...], da_scr[side], TN).astype(BF16)
            stage = stages.take()
            for i in range(PIECES):
                stage[i] = band[i * ROWS_D : (i + 1) * ROWS_D]
                piece = meta[META_TO["b"] + i]
                stages.send(stage.at[i], out.at[piece, :, pl.ds(D // 2, D // 2)])
        stages.end()


def middle(meta, dz, mid, mixed, cot, aln, vec, w_in, w_out):
    rows = mid.shape[0]
    tile = pl.BlockSpec((PAIR, D), lambda c, m: (c, 0))
    return pl.pallas_call(
        middle_kernel,
        grid_spec=pltpu.PrefetchScalarGridSpec(
            num_scalar_prefetch=1,
            grid=(rows // PAIR,),
            in_specs=[
                pl.BlockSpec((2, PAIR, FF // 2), lambda c, m: (0, c, 0)),
                tile, tile, tile,
                full(rows, D),
                full(16, D),
                *[ANY] * 6,
            ],
            out_specs=[tile, tile, full(8, D), ANY, ANY],
            scratch_shapes=[
                pltpu.VMEM((2, D, FF // 2), BF16),
                pltpu.VMEM((2, D, D // 2), BF16),
                pltpu.VMEM((2, rows, D // 2), BF16),
                pltpu.VMEM((2, PIECES, ROWS_D, D // 2), BF16),
                pltpu.SemaphoreType.DMA((4,)),
            ],
        ),
        out_shape=[
            jax.ShapeDtypeStruct((rows, D), F32),
            jax.ShapeDtypeStruct((rows, D), BF16),
            jax.ShapeDtypeStruct((8, D), F32),
        ]
        + [jax.ShapeDtypeStruct((PIECES, ROWS_D, D), BF16)] * 2,
        compiler_params=pltpu.CompilerParams(vmem_limit_bytes=VMEM_BIG),
        cost_estimate=pl.CostEstimate(
            flops=2 * rows * D * (2 * D + FF), bytes_accessed=30 * rows * D, transcendentals=0
        ),
        name="middle",
    )(meta, dz, mid, mixed, cot, aln, vec, *w_in, *w_out)


def attend_back_kernel(
    meta, q_ref, k_ref, v_ref, do_ref, turned_ref, lse_ref, bias_ref, low_ref, before_0, before_1,
    dqkv_out, tiles_out, g0, g2, g1, g3, dq_scr, do_scr, tiles_ref, dqkv_scr, a_scr, b_scr, sems,
):
    step = pl.program_id(0)
    mine = pl.ds(pl.multiple_of(step * CHUNK, CHUNK), CHUNK)
    kind = meta[META_KIND + step]

    @pl.when(step == 0)
    def _():
        tiles_ref[...] = jnp.zeros_like(tiles_ref)

    query = q_ref[...]
    query_turned = query.astype(F32).T.astype(BF16)
    key_turned = k_ref[...].astype(F32).T.astype(BF16)
    do_scr[...] = do_ref[...].astype(F32).T
    mask = jnp.broadcast_to((1.0 - live_rows(meta, pl.program_id(0))) * NEG_FILL, (CHUNK, CHUNK))
    parts = [slice(h * HEAD_DIM, (h + 1) * HEAD_DIM) for h in range(HEADS)]
    dk, dv = [], []

    def products(h):
        part = parts[h]
        return (
            dot(k_ref[:, part], query_turned[part]),
            dot(v_ref[:, part], do_scr[part].astype(BF16)),
        )

    def finish(h, probs, ds):
        dv.append(dot(probs, do_ref[:, parts[h]]))
        dk.append(dot(ds, q_ref[:, parts[h]]))
        dq_scr[parts[h]] = dot(key_turned[parts[h]], ds)

    coming, before = products(0), None
    for h in range(HEADS):
        scores, dprobs = coming
        if h + 1 < HEADS:
            coming = products(h + 1)
        scores = scores + bias_ref[0, h].astype(F32) + mask
        probs = jnp.exp(scores - lse_ref[0, h : h + 1])
        centre = jnp.sum(do_scr[parts[h]] * turned_ref[0, parts[h]], axis=0, keepdims=True)
        ds = probs * (dprobs - centre)
        tiles_ref[kind, h] += ds
        if before:
            finish(*before)
        before = (h, probs.astype(BF16), ds.astype(BF16))
    finish(*before)
    dq = (dq_scr[...].T * QUERY_SCALE).astype(BF16)
    dk = jnp.concatenate(dk, axis=1).astype(BF16)
    dv = jnp.concatenate(dv, axis=1).astype(BF16)
    dqkv_scr[0, mine, :D] = dq
    dqkv_scr[0, mine, D:] = dk[:, : D // 2]
    dqkv_scr[1, mine, : D // 2] = dk[:, D // 2 :]
    dqkv_scr[1, mine, D // 2 :] = dv
    pltpu.make_async_copy(dqkv_scr.at[:, mine], dqkv_out.at[:, mine], sems.at[0]).start()

    @pl.when(step == pl.num_programs(0) - 1)
    def _():
        pltpu.make_async_copy(tiles_ref, tiles_out, sems.at[1]).start()
        core = meta[0]
        stages = [Stage(a_scr, sems, 2), Stage(b_scr, sems, 4)]
        for side, out_a, out_b in ((1 - core, g0, g1), (core, g2, g3)):
            for b in range(D // BAND):
                band = dot(low_ref[:, b * BAND : (b + 1) * BAND], dqkv_scr[side], TN).astype(BF16)
                stage_a, stage_b = (stage.take() for stage in stages)
                for i in range(BAND // ROWS_D):
                    rows = slice(i * ROWS_D, (i + 1) * ROWS_D)
                    stage_a[i] = band[rows, :D]
                    stage_b[i] = band[rows, D:]
                    piece = meta[META_TO["a"] + b * (BAND // ROWS_D) + i]
                    stages[0].send(stage_a.at[i], out_a.at[piece])
                    piece = meta[META_TO["b"] + b * (BAND // ROWS_D) + i]
                    stages[1].send(stage_b.at[i], out_b.at[piece, :, pl.ds(0, D // 2)])
        for stage in stages:
            stage.end()
        pltpu.make_async_copy(dqkv_scr, dqkv_out, sems.at[0]).wait()
        pltpu.make_async_copy(tiles_ref, tiles_out, sems.at[1]).wait()


def attend_back(meta, query, key, value, do, turned, lse, bias, low, before):
    rows = query.shape[0]
    chunks = rows // CHUNK
    tile = pl.BlockSpec((CHUNK, D), lambda c, m: (c, 0))
    pieces = jax.ShapeDtypeStruct((PIECES, ROWS_D, D), BF16)
    return pl.pallas_call(
        attend_back_kernel,
        grid_spec=pltpu.PrefetchScalarGridSpec(
            num_scalar_prefetch=1,
            grid=(chunks,),
            in_specs=[
                tile, tile, tile, tile,
                pl.BlockSpec((1, D, CHUNK), lambda c, m: (c, 0, 0)),
                pl.BlockSpec((1, 16, CHUNK), lambda c, m: (c, 0, 0)),
                pl.BlockSpec((1, HEADS, CHUNK, CHUNK), lambda c, m: (m[META_KIND + c], 0, 0, 0)),
                full(rows, D),
                ANY, ANY,
            ],
            out_specs=[ANY] * 6,
            scratch_shapes=[
                pltpu.VMEM((D, CHUNK), F32),
                pltpu.VMEM((D, CHUNK), F32),
                pltpu.VMEM((2, HEADS, CHUNK, CHUNK), F32),
                pltpu.VMEM((2, rows, 3 * D // 2), BF16),
                pltpu.VMEM((2, BAND // ROWS_D, ROWS_D, D), BF16),
                pltpu.VMEM((2, BAND // ROWS_D, ROWS_D, D // 2), BF16),
                pltpu.SemaphoreType.DMA((6,)),
            ],
        ),
        out_shape=[
            jax.ShapeDtypeStruct((2, rows, 3 * D // 2), BF16),
            jax.ShapeDtypeStruct((2, HEADS, CHUNK, CHUNK), F32),
            *[pieces] * 4,
        ],
        input_output_aliases={9: 4, 10: 5},
        compiler_params=pltpu.CompilerParams(vmem_limit_bytes=VMEM_BIG),
        cost_estimate=pl.CostEstimate(
            flops=20 * 10**9, bytes_accessed=30 * rows * D, transcendentals=0
        ),
        name="attend_back",
    )(meta, query, key, value, do, turned, lse, bias, low, *before)


def last_kernel(
    meta, dqkv_ref, x_ref, dx_ref, vec_ref, a0, a1, b0, b1,
    out_ref, sums_ref, sums_p_ref, w_scr, sem,
):
    @pl.when(pl.program_id(0) == 0)
    def _():
        load = Load(meta, sem, w_scr)
        load.cols("a", a0, a1, 0, 0, D)
        load.cols("b", b0, b1, D, 0, D // 2)
        load.wait()
        sums_ref[...] = jnp.zeros_like(sums_ref)
        sums_p_ref[...] = jnp.zeros_like(sums_p_ref)

    dh = dot(dqkv_ref[0], w_scr[0], NT) + dot(dqkv_ref[1], w_scr[1], NT)
    for half in range(2):
        sums_p_ref[half : half + 1] += col_sum(dqkv_ref[half].astype(F32))
    scaled, spread = unit_rows(x_ref[...].astype(F32))
    sums_ref[0:1] += col_sum(dh * scaled)
    sums_ref[1:2] += col_sum(dh)
    out_ref[...] = (dx_ref[...] + unit_rows_back(dh * vec_ref[0:1], scaled, spread)).astype(BF16)


def last(meta, dqkv, tokens, dx, vec, w_in):
    rows = tokens.shape[0]
    tile = pl.BlockSpec((CHUNK, D), lambda c, m: (c, 0))
    return pl.pallas_call(
        last_kernel,
        grid_spec=pltpu.PrefetchScalarGridSpec(
            num_scalar_prefetch=1,
            grid=(rows // CHUNK,),
            in_specs=[
                pl.BlockSpec((2, CHUNK, 3 * D // 2), lambda c, m: (0, c, 0)),
                tile, tile,
                full(16, D),
                ANY, ANY, ANY, ANY,
            ],
            out_specs=[tile, full(8, D), full(2, 3 * D // 2)],
            scratch_shapes=[pltpu.VMEM((2, D, 3 * D // 2), BF16), pltpu.SemaphoreType.DMA],
        ),
        out_shape=[
            jax.ShapeDtypeStruct((rows, D), BF16),
            jax.ShapeDtypeStruct((8, D), F32),
            jax.ShapeDtypeStruct((2, 3 * D // 2), F32),
        ],
        compiler_params=pltpu.CompilerParams(vmem_limit_bytes=VMEM_BIG),
        cost_estimate=pl.CostEstimate(
            flops=2 * rows * D * 3 * D, bytes_accessed=16 * rows * D, transcendentals=0
        ),
        name="last",
    )(meta, dqkv, tokens, dx, vec, *w_in)


def swap(values, mask, count):
    return lax.ppermute(values, AXES, [(i, i ^ mask) for i in range(count)])


def tie(values, after):
    values, after = list(values), list(after)
    if not after:
        return values
    return list(lax.optimization_barrier(tuple(values + after))[: len(values)])


class Chain:
    def __init__(self, net, steps, finish):
        self.net, self.steps, self.finish = net, list(steps), finish
        self.got = [None] * len(self.steps)
        self.sends = [[] for _ in self.steps]
        self.results = [None] * len(self.steps)

    def go(self, *after):
        for i, step in enumerate(self.steps):
            if self.results[i] is not None:
                continue
            try:
                got = self.got[i] if self.got[i] is None else tie(self.got[i], after)
                sends = step.send(got)
                values = [v for v, _ in sends]
                if got is None:
                    values = tie(values, after)
                self.sends[i] = values
                self.got[i] = [self.net.swap(v, m) for v, (_, m) in zip(values, sends)]
            except StopIteration as end:
                self.results[i] = end.value
                self.sends[i] = []
        return self

    @property
    def sent(self):
        return [v for part in self.sends for v in part]

    @property
    def received(self):
        return [v for part in self.got for v in part or []]

    def done(self, *after):
        while any(r is None for r in self.results):
            self.go(*after)
            after = ()
        return self.finish(self.results)


class Ready:
    def __init__(self, value):
        self.value, self.sent, self.received = value, [], []

    def go(self, *after):
        return self

    def done(self, *after):
        return self.value


def add_kernel(*refs, sizes):
    outs = refs[sum(sizes) :]
    at = 0
    for size, out in zip(sizes, outs):
        total = refs[at][...].astype(F32)
        for ref in refs[at + 1 : at + size]:
            total += ref[...].astype(F32)
        out[...] = total.astype(BF16)
        at += size


def add_pieces(parts, count):
    rows = parts[0][0].shape[1]
    step = min(count, 4)
    return pl.pallas_call(
        functools.partial(add_kernel, sizes=[len(p) for p in parts]),
        grid=(count // step,),
        in_specs=[
            pl.BlockSpec((step, rows, D), lambda i: (count // step + i, 0, 0)) for p in parts for _ in p
        ],
        out_specs=[pl.BlockSpec((step, rows, D), lambda i: (i, 0, 0))] * len(parts),
        out_shape=[jax.ShapeDtypeStruct((count, rows, D), BF16)] * len(parts),
        compiler_params=pltpu.CompilerParams(vmem_limit_bytes=32 * 2**20),
        cost_estimate=pl.CostEstimate(
            flops=count * rows * D * 4, bytes_accessed=16 * count * rows * D, transcendentals=0
        ),
        name="add_pieces",
    )(*(a for p in parts for a in p))


def add_last_kernel(*refs, sizes):
    outs = refs[sum(sizes) :]
    rows = refs[0].shape[1]
    for z, out in enumerate(outs, 1):
        at = 0
        for k, size in enumerate(sizes):
            total = refs[at][z].astype(F32)
            for ref in refs[at + 1 : at + size]:
                total += ref[z].astype(F32)
            out[k * rows : (k + 1) * rows] = total.astype(BF16)
            at += size


def add_last_pieces(parts):
    rows = parts[0][0].shape[1]
    out = jax.ShapeDtypeStruct((len(parts) * rows, D), BF16)
    return pl.pallas_call(
        functools.partial(add_last_kernel, sizes=[len(p) for p in parts]),
        grid=(1,),
        in_specs=[pl.BlockSpec((4, rows, D), lambda i: (0, 0, 0)) for p in parts for _ in p],
        out_specs=[full(len(parts) * rows, D)] * 3,
        out_shape=[out] * 3,
        compiler_params=pltpu.CompilerParams(vmem_limit_bytes=32 * 2**20),
        cost_estimate=pl.CostEstimate(
            flops=rows * D * 24, bytes_accessed=80 * rows * D, transcendentals=0
        ),
        name="add_last_pieces",
    )(*(a for p in parts for a in p))


class Cube:
    SIDES = {"a": (2, 4), "b": (4, 2)}

    def __init__(self):
        self.me = lax.axis_index(AXES).astype(jnp.int32)

    def swap(self, values, mask):
        return swap(values, mask, 32)

    def masks(self, order):
        shift = self.SIDES[order]
        return np.array(
            [8 * (k & 3) + shift[0] * (k >> 2 & 1) + shift[1] * (k >> 3) for k in range(PIECES)]
        )

    def meta(self):
        chip = self.me >> 1
        place = jnp.arange(PIECES, dtype=jnp.int32)
        start = [chip ^ jnp.asarray(self.masks(o) >> 1, jnp.int32) for o in "ab"]
        mask = chip ^ place
        x, y = mask & 1, mask >> 1 & 1
        to = [(mask >> 2) + 4 * x + 8 * y, (mask >> 2) + 4 * y + 8 * x]
        return self.me & 1, start + to

    def spread(self, piece, parts):
        got = yield [(piece, 8 * z) for z in (1, 2, 3)]
        held = jnp.stack([piece] + got)
        ends = np.cumsum([0] + [w for _, w in parts])
        cuts = [held[..., a:b] for a, b in zip(ends[:-1], ends[1:])]
        for stage in (0, 1):
            got = yield [(c, self.SIDES[order][stage]) for c, (order, _) in zip(cuts, parts)]
            cuts = [jnp.concatenate(pair) for pair in zip(cuts, got)]
        got = yield [(c, 1) for c in cuts]
        return [v for pair in zip(cuts, got) for v in pair]

    def gather_cols(self, shards, parts):
        left, right = (
            jnp.concatenate([h[side] for h in (jnp.split(s, 2, axis=1) for s in shards)], axis=1)
            for side in (0, 1)
        )
        odd = (self.me & 1) == 1
        got = self.swap(jnp.where(odd, left, right), 1)
        mine = jnp.where(odd, right, left)
        block = jnp.where(odd, jnp.concatenate([got, mine]), jnp.concatenate([mine, got]))
        return Chain(self, [self.spread(block, parts)], lambda results: results[0])

    def gather_rows(self, shard, parts):
        return Chain(self, [self.spread(shard, parts)], lambda results: results[0])

    def gather_small(self, pack):
        every = jnp.broadcast_to(pack, (32, pack.shape[0]))
        return lax.all_to_all(every, AXES, 0, 0, tiled=True)

    def reduce_small(self, pack):
        return jnp.sum(lax.all_to_all(pack, AXES, 0, 0, tiled=True), axis=0)

    def gather_rows(self, shard, order):
        return Chain(self, [self.spread(shard, order)], lambda parts: parts[0])

    def collect(self, owns, others, orders):
        got = yield [(o, 1) for o in others]
        terms = [[a, b] for a, b in zip(owns, got)]
        count = PIECES
        for stage in (1, 0):
            count //= 2
            sends = add_pieces(terms, count)
            got = yield [(v, self.SIDES[o][stage]) for v, o in zip(sends, orders)]
            terms = [part + [g] for part, g in zip(terms, got)]
        sends = add_last_pieces(terms)
        got = yield [(v, 8 * z) for z, v in zip((1, 2, 3), sends)]
        mine = [sum((t[0].astype(F32) for t in part[1:]), part[0][0].astype(F32)) for part in terms]
        return jnp.concatenate(mine) + sum(g.astype(F32) for g in got)

    def reduce_ff(self, others, owns):
        def finish(results):
            (total,) = results
            block = jnp.concatenate([total[:ROWS_D], total[ROWS_D : 2 * ROWS_D]], axis=1)
            return jnp.concatenate(self.join(block), axis=1), total[2 * ROWS_D :]

        return Chain(self, [self.collect(owns, others, "ab")], finish)

    def reduce_attn(self, others, owns):
        def finish(results):
            (total,) = results
            block = jnp.concatenate([total[:ROWS_D], total[ROWS_D:]], axis=1)
            sides = self.join(block)
            cut = 3 * D // 2
            return tuple(
                jnp.concatenate([s[:, part] for s in sides], axis=1)
                for part in (slice(0, cut), slice(cut, None))
            )

        return Chain(self, [self.collect(owns, others, "ab")], finish)

    def join(self, block):
        rows = block.shape[0] // 2
        low, high = block[:rows], block[rows:]
        odd = (self.me & 1) == 1
        got = self.swap(jnp.where(odd, low, high), 1)
        mine = jnp.where(odd, high, low)
        return jnp.where(odd, got, mine), jnp.where(odd, mine, got)


class Plain:
    def __init__(self, count):
        self.count = count
        self.me = lax.axis_index(AXES)

    def meta(self):
        place = jnp.arange(PIECES, dtype=jnp.int32)
        return jnp.int32(0), [place] * 4

    def gather_cols(self, shards, parts):
        whole = [lax.all_gather(s, AXES, axis=0, tiled=True) for s in shards]
        left, right = (
            jnp.concatenate([h[side] for h in (jnp.split(w, 2, axis=1) for w in whole)], axis=1)
            for side in (0, 1)
        )
        out, at = [], 0
        for _, width in parts:
            for half in (left, right):
                out.append(half[:, at : at + width].reshape(PIECES, -1, width))
            at += width
        return Ready(out)

    def gather_small(self, pack):
        return lax.all_gather(pack, AXES)

    def reduce_small(self, pack):
        return lax.psum_scatter(pack, AXES, scatter_dimension=0, tiled=False)

    def gather_rows(self, shard, parts):
        whole = lax.all_gather(shard, AXES, axis=0, tiled=True)
        whole = whole.reshape(PIECES, 2, -1, whole.shape[1])
        out, at = [], 0
        for _, width in parts:
            out += [whole[:, side, :, at : at + width] for side in (0, 1)]
            at += width
        return Ready(out)

    def scatter(self, whole):
        return lax.psum_scatter(whole.astype(F32), AXES, scatter_dimension=0, tiled=True)

    def reduce_ff(self, others, owns):
        runs = [
            a[:, row : row + ROWS_D].reshape(D, D)
            for a in (owns[0], others[0])
            for row in (0, ROWS_D)
        ]
        rows = jnp.stack([owns[1], others[1]], axis=1).reshape(FF, D)
        return Ready((self.scatter(jnp.concatenate(runs, axis=1)), self.scatter(rows)))

    def reduce_attn(self, others, owns):
        halves_in, halves_out = [], []
        for a, b in (owns, others):
            a, b = a.reshape(D, D), b.reshape(D, D)
            halves_in += [a, b[:, : D // 2]]
            halves_out.append(b[:, D // 2 :])
        return Ready(tuple(self.scatter(jnp.concatenate(h, axis=1)) for h in (halves_in, halves_out)))


PARTS_ATTN = (("a", D), ("b", D))
PARTS_HALVES = (("a", FF // 4), ("b", FF // 4))
PARTS_ROWS = (("a", D // 2), ("b", D // 2))


def body(
    tokens,
    cotangent,
    w_attn_in,
    w_attn_out,
    w_fc_in,
    w_fc_out,
    gains_d,
    biases_d,
    gains_ff,
    biases_ff,
    rel_table,
    head_scale,
    bucket,
    lengths,
    *,
    count,
    cube,
):
    net = Cube() if cube else Plain(count)
    rows = tokens.shape[0]
    chunks = rows // CHUNK

    gather_attn = net.gather_cols([w_attn_in, w_attn_out], PARTS_ATTN).go()
    small = tie((gains_d, biases_d, gains_ff[None], biases_ff, rel_table), gather_attn.sent)
    sizes = [v.size for v in small]
    ends = np.cumsum(sizes)
    width = -(-int(ends[-1] + 16) // 1024) * 1024
    pack = jnp.concatenate([v.reshape(-1) for v in small] + [jnp.zeros(width - ends[-1], BF16)])
    packs = net.gather_small(pack)

    bucket, lengths = tie([bucket, lengths], [pack])
    large = jnp.sum((bucket == 1).astype(jnp.int32), dtype=jnp.int32)
    kinds = (jnp.arange(chunks, dtype=jnp.int32) >= large).astype(jnp.int32)
    core, tables = net.meta()
    meta = jnp.concatenate(
        [core.astype(jnp.int32)[None], kinds, large[None], jnp.zeros(2, jnp.int32), *tables, lengths]
    )
    keys, keys_back, queries = (jnp.asarray(t) for t in pick_tables())
    gather_ff = net.gather_cols([w_fc_in], PARTS_HALVES)
    gather_down = net.gather_rows(w_fc_out, PARTS_ROWS)

    arrived = gather_attn.received
    gather_attn.go(meta)
    gather_ff.go(*arrived)
    (packs,) = tie([packs], gather_attn.sent + gather_ff.sent)
    vec, wide, lines = unpack(packs, head_scale[None], count)
    gather_attn.go(vec)
    (lines,) = tie([lines], gather_attn.sent)
    bias = build_bias(lines, keys, queries)
    gather_ff.go(bias)
    gather_attn.go(*gather_ff.sent)
    gather_down.go(*gather_ff.sent)
    attn_pieces = gather_attn.done()
    out_pieces = attn_pieces[2:]

    (tokens_in,) = tie([tokens], gather_ff.sent)
    low_in, query, key, value = project(meta, tokens_in, vec, attn_pieces)
    gather_ff.go(low_in)
    gather_down.go(low_in)
    (query_in,) = tie([query], gather_ff.sent + gather_down.sent)
    heads = attend(
        meta, query_in, key, value, bias, tokens, vec, out_pieces, 0, chunks // 2
    )
    gather_down.go(heads[2])
    gather_ff.go(heads[2])
    (query_in,) = tie([query], gather_down.sent + gather_ff.sent)
    mixed, turned, lse, mid, low_attn, low_mid = attend(
        meta, query_in, key, value, bias, tokens, vec, out_pieces, chunks // 2,
        chunks - chunks // 2, heads,
    )
    gather_down.go(lse)
    ff_pieces = gather_ff.done(lse)
    down_pieces = gather_down.done()
    out_tokens, sums_a, sums_ff, dz, *ff_grads = feed(
        meta, mid, low_mid, cotangent, vec, wide, ff_pieces, down_pieces
    )

    reduce_ff = net.reduce_ff(ff_grads[:2], ff_grads[2:]).go()
    (dz,) = tie([dz], reduce_ff.sent)
    dx, do, sums_b, *out_grads = middle(
        meta, dz, mid, mixed, cotangent, low_attn, vec, ff_pieces, out_pieces
    )
    reduce_ff.go(sums_b)
    (do,) = tie([do], reduce_ff.sent)
    dqkv, tiles, other_a, own_a, other_b, own_b = attend_back(
        meta, query, key, value, do, turned, lse, bias, low_in, out_grads
    )
    reduce_attn = net.reduce_attn((other_a, other_b), (own_a, own_b)).go()
    reduce_ff.go(tiles)
    (tiles,) = tie([tiles], reduce_ff.sent)
    (tiles,) = tie([tiles], reduce_attn.sent)
    grad_table = table_grads(tiles, keys_back, queries)
    reduce_attn.go(grad_table)
    reduce_ff.go(grad_table)
    (dqkv,) = tie([dqkv], reduce_attn.sent + reduce_ff.sent)
    grad_tokens, sums_c, sums_p = last(meta, dqkv, tokens, dx, vec, attn_pieces)
    reduce_attn.go(sums_c)
    terms = (sums_a, sums_b, sums_c, sums_p, sums_ff, grad_table)
    terms = pack_terms(*tie(terms, reduce_attn.sent + reduce_ff.received), count, width)
    reduce_attn.go(terms)
    (terms,) = tie([terms], reduce_attn.sent)
    mine = net.reduce_small(terms)
    grad_fc_in, grad_fc_out = reduce_ff.done(*reduce_attn.sent)
    grad_attn_in, grad_attn_out = reduce_attn.done(grad_fc_out)

    grads = [mine[end - size : end].reshape(v.shape) for v, size, end in zip(small, sizes, ends)]
    return (
        out_tokens,
        grad_tokens,
        grad_attn_in,
        grad_attn_out,
        grad_fc_in,
        grad_fc_out,
        grads[0],
        grads[1],
        grads[2][0],
        grads[3],
        grads[4],
        mine[ends[-1] : ends[-1] + HEADS],
    )


def solution(mesh):
    rows = P(AXES, None)
    columns = P(None, AXES)
    line = P(AXES)
    count = mesh.shape["wide"] * mesh.shape["narrow"]
    cube = (mesh.shape["wide"], mesh.shape["narrow"]) == (8, 4)
    return jax.shard_map(
        functools.partial(body, count=count, cube=cube),
        mesh=mesh,
        in_specs=(
            rows, rows, rows, rows, rows, rows,
            columns, columns, line, columns, columns, P(), line, line,
        ),
        out_specs=(
            rows, rows, rows, rows, rows, rows,
            columns, columns, line, columns, columns, P(),
        ),
        check_vma=False,
    )
```

```python
import functools

import jax
import jax.numpy as jnp
import numpy as np
from jax import lax
from jax.experimental import pallas as pl
from jax.experimental.pallas import tpu as pltpu
from jax.sharding import PartitionSpec as P

HEADS = 12
HEAD_DIM = 64
D = 768
FF = 3072
GRID_L = 15
GRID_S = 8
SLOT_L = 256
SLOT_S = 64
STRIDE = 32
RELS = 1024
CHUNK = 256
PAIR = 2 * CHUNK
PIECES = 16
ROWS_D = D // PIECES
ROWS_F = FF // (2 * PIECES)

NEG_FILL = -1e30
NORM_EPS = 1e-05
HALF_ROOT = 0.7071067811865476
DENSITY_SCALE = 0.3989422804014327
QUERY_SCALE = 0.125
AXES = ("wide", "narrow")
F32 = jnp.float32
BF16 = jnp.bfloat16
VMEM_BIG = 60 * 2**20
VMEM_ALL = 63 * 2**20

NN = (((1,), (0,)), ((), ()))
NT = (((1,), (1,)), ((), ()))
TN = (((0,), (0,)), ((), ()))


ANY = pl.BlockSpec(memory_space=pl.ANY)


def full(*shape):
    return pl.BlockSpec(shape, lambda *_: (0,) * len(shape))


def dot(left, right, dims=NN):
    return lax.dot_general(left, right, dims, preferred_element_type=F32)


def unit_rows(values):
    center = values - jnp.mean(values, axis=-1, keepdims=True)
    spread = lax.rsqrt(jnp.mean(center * center, axis=-1, keepdims=True) + NORM_EPS)
    return center * spread, spread


def unit_rows_back(inner, scaled, spread):
    return spread * (
        inner
        - jnp.mean(inner, axis=-1, keepdims=True)
        - scaled * jnp.mean(inner * scaled, axis=-1, keepdims=True)
    )


def col_sum(values):
    return jnp.sum(values, axis=0, keepdims=True)


def unit_position(kind):
    place = np.arange(CHUNK)
    if kind == 0:
        return np.minimum(place // GRID_L, GRID_L - 1), place % GRID_L
    inner = place % SLOT_S
    return inner // GRID_S, inner % GRID_S


def pick_tables():
    keys = np.zeros((2, CHUNK, 512), np.float32)
    keys_back = np.zeros((2, CHUNK, 512), np.float32)
    queries = np.zeros((2, CHUNK, CHUNK), np.float32)
    for kind in range(2):
        row, col = unit_position(kind)
        line = STRIDE * row + col
        keys[kind, np.arange(CHUNK), line] = 1
        keys_back[kind, np.arange(CHUNK), 511 - line] = 1
        queries[kind, 16 * row + col, np.arange(CHUNK)] = 1
    return keys.astype(BF16), keys_back.astype(BF16), queries.astype(BF16)


def owner_of_lane(lanes, each, last=None):
    lane = lax.broadcasted_iota(jnp.int32, lanes, 1)
    entry = lane if last is None else last - lane
    device = lax.broadcasted_iota(jnp.int32, lanes, 0)
    return ((entry >= device * each) & (entry < device * each + each)).astype(BF16)


def place_in_part(lanes, each, last=None):
    lane = lax.broadcasted_iota(jnp.int32, lanes, 1)
    entry = lane if last is None else last - lane
    row = lax.broadcasted_iota(jnp.int32, lanes, 0)
    return ((entry >= 0) & (lax.rem(entry + each, each) == row)).astype(F32)


def unpack_kernel(pack_ref, scale_ref, vec_ref, wide_ref, line_ref, *, count):
    each_d, each_f, each_t = D // count, FF // count, RELS // count
    pack = pack_ref[...]

    def rows(start, amount, each, lanes, last=None):
        owner = owner_of_lane((count, lanes), each, last)
        place = place_in_part((each, lanes), each, last)
        part = pack[:, start : start + amount * each]
        spread = dot(part, owner, TN)
        return [col_sum(spread[r * each : r * each + each] * place) for r in range(amount)]

    d_rows = rows(0, 10, each_d, D)
    ff_rows = rows(10 * each_d, 3, each_f, FF)
    lines = rows(10 * each_d + 3 * each_f, HEADS, each_t, RELS, 1006)
    lane = lax.broadcasted_iota(jnp.int32, (HEADS, D), 1)
    row = lax.broadcasted_iota(jnp.int32, (HEADS, D), 0)
    heads = dot(scale_ref[...], (lane // HEAD_DIM == row).astype(BF16))
    vec_ref[...] = jnp.concatenate(d_rows + [heads, jnp.zeros((5, D), F32)], axis=0)
    wide_ref[...] = jnp.concatenate(ff_rows + [jnp.zeros((5, FF), F32)], axis=0)
    for h in range(HEADS):
        line_ref[h] = jnp.broadcast_to(lines[h], (16, RELS))


def unpack(pack, scale, count):
    return pl.pallas_call(
        functools.partial(unpack_kernel, count=count),
        out_shape=[
            jax.ShapeDtypeStruct((16, D), F32),
            jax.ShapeDtypeStruct((8, FF), F32),
            jax.ShapeDtypeStruct((HEADS, 16, RELS), F32),
        ],
        compiler_params=pltpu.CompilerParams(vmem_limit_bytes=VMEM_BIG),
        cost_estimate=pl.CostEstimate(flops=2 * 10**9, bytes_accessed=4 * 10**6, transcendentals=0),
        name="unpack",
    )(pack, scale)


TURN = 4


def bias_kernel(line_ref, keys_ref, queries_ref, out_ref):
    left = lax.broadcasted_iota(jnp.int32, (CHUNK, CHUNK), 0) // SLOT_S
    right = lax.broadcasted_iota(jnp.int32, (CHUNK, CHUNK), 1) // SLOT_S
    spread_rows = []
    for h in range(TURN):
        base = pltpu.roll(line_ref[h], RELS - 511, 1, stride=1, stride_axis=0)
        turns = [base] + [pltpu.roll(base, STRIDE * m, 1) for m in (1, 2, 3)]
        twice = [jnp.concatenate([t, t[:, :512]], axis=1) for t in turns]
        groups = []
        for r in range(16):
            start = (RELS - 128 * (r // 4)) % RELS
            groups.append(twice[r % 4][:, start : start + 512])
        spread_rows.append(jnp.concatenate(groups, axis=0).astype(BF16))
    by_key = [
        (dot(keys_ref[0], g, NT).astype(BF16), dot(keys_ref[1, :SLOT_S], g, NT).astype(BF16))
        for g in spread_rows
    ]
    for h in range(TURN):
        out_ref[0, h] = dot(by_key[h][0], queries_ref[0]).astype(BF16)
        tile = dot(by_key[h][1], queries_ref[1])
        tile = jnp.concatenate([tile] * (CHUNK // SLOT_S), axis=0)
        out_ref[1, h] = jnp.where(left == right, tile, NEG_FILL).astype(BF16)


def build_bias(lines, keys, queries):
    return pl.pallas_call(
        bias_kernel,
        grid=(HEADS // TURN,),
        in_specs=[
            pl.BlockSpec((TURN, 16, RELS), lambda h: (h, 0, 0)),
            full(2, CHUNK, 512),
            full(2, CHUNK, CHUNK),
        ],
        out_specs=pl.BlockSpec((2, TURN, CHUNK, CHUNK), lambda h: (0, h, 0, 0)),
        out_shape=jax.ShapeDtypeStruct((2, HEADS, CHUNK, CHUNK), BF16),
        compiler_params=pltpu.CompilerParams(vmem_limit_bytes=VMEM_BIG),
        cost_estimate=pl.CostEstimate(flops=8 * 10**9, bytes_accessed=4 * 10**6, transcendentals=0),
        name="bias_tiles",
    )(lines, keys, queries)


def pack_kernel(a_ref, b_ref, c_ref, p_ref, ff_ref, table_ref, out_ref, *, count):
    each_d, each_f, each_t = D // count, FF // count, RELS // count

    def columns(rows, each, lanes):
        owner = owner_of_lane((count, lanes), each)
        place = place_in_part((each, lanes), each)
        parts = []
        for row in rows:
            high, rest = halves(row * place)
            parts.append(dot(high, owner, NT) + dot(rest, owner, NT))
        return jnp.concatenate(parts, axis=0)

    a, b, c = a_ref[...], b_ref[...], c_ref[...]
    p = p_ref[...]
    d_rows = [
        c[0:1], b[3:4], b[0:1],
        c[1:2], p[0:1, :D], p[1:2, D // 2 :], b[4:5], b[2:3], b[1:2], a[0:1],
    ]
    ff = ff_ref[...]
    lane = lax.broadcasted_iota(jnp.int32, (16, D), 1)
    row = lax.broadcasted_iota(jnp.int32, (16, D), 0)
    high, rest = halves(jnp.broadcast_to(b[5:6], (16, D)) * (lane // HEAD_DIM == row).astype(F32))
    ones = jnp.ones((count, D), BF16)
    out = [
        columns(d_rows, each_d, D),
        columns([ff[0:1], ff[2:3], ff[1:2]], each_f, FF),
        columns([table_ref[h, 0:1] for h in range(HEADS)], each_t, RELS),
        dot(high, ones, NT) + dot(rest, ones, NT),
    ]
    used = sum(o.shape[0] for o in out)
    out.append(jnp.zeros((out_ref.shape[1] - used, count), F32))
    out_ref[...] = jnp.concatenate(out, axis=0).T


def pack_terms(sums_a, sums_b, sums_c, sums_p, sums_ff, table, count, width):
    return pl.pallas_call(
        functools.partial(pack_kernel, count=count),
        out_shape=jax.ShapeDtypeStruct((count, width), F32),
        compiler_params=pltpu.CompilerParams(vmem_limit_bytes=VMEM_BIG),
        cost_estimate=pl.CostEstimate(flops=10**9, bytes_accessed=10**6, transcendentals=0),
        name="pack_terms",
    )(sums_a, sums_b, sums_c, sums_p, sums_ff, table)


def halves(values):
    high = values.astype(BF16)
    return high, (values - high.astype(F32)).astype(BF16)


def table_kernel(tiles_ref, keys_ref, queries_ref, out_ref):
    by_query = []
    for h in range(TURN):
        small = tiles_ref[1, h, :SLOT_S]
        for part in range(1, CHUNK // SLOT_S):
            small = small + tiles_ref[1, h, part * SLOT_S : (part + 1) * SLOT_S]
        by_query.append(
            (
                dot(queries_ref[0], tiles_ref[0, h].astype(BF16), NT).astype(BF16),
                dot(queries_ref[1], small.astype(BF16), NT).astype(BF16),
            )
        )
    totals = [
        dot(large, keys_ref[0]) + dot(small, keys_ref[1, :SLOT_S]) for large, small in by_query
    ]
    for h, total in enumerate(totals):
        line = jnp.zeros((16, RELS), F32)
        for m in range(4):
            part = jnp.zeros((16, RELS), F32)
            for k in range(4):
                group = total[16 * (4 * k + m) : 16 * (4 * k + m) + 16]
                pieces = [group, jnp.zeros((16, 512 - 128 * k), F32)]
                if k:
                    pieces = [jnp.zeros((16, 128 * k), F32)] + pieces
                part += jnp.concatenate(pieces, axis=1)
            line += pltpu.roll(part, STRIDE * m, 1) if m else part
        line = pltpu.roll(line, 0, 1, stride=1, stride_axis=0)
        out_ref[h] = pltpu.roll(jnp.broadcast_to(col_sum(line), (8, RELS)), RELS - 16, 1)


def table_grads(tiles, keys_back, queries):
    return pl.pallas_call(
        table_kernel,
        grid=(HEADS // TURN,),
        in_specs=[
            pl.BlockSpec((2, TURN, CHUNK, CHUNK), lambda h: (0, h, 0, 0)),
            full(2, CHUNK, 512),
            full(2, CHUNK, CHUNK),
        ],
        out_specs=pl.BlockSpec((TURN, 8, RELS), lambda h: (h, 0, 0)),
        out_shape=jax.ShapeDtypeStruct((HEADS, 8, RELS), F32),
        compiler_params=pltpu.CompilerParams(vmem_limit_bytes=VMEM_BIG),
        cost_estimate=pl.CostEstimate(flops=8 * 10**9, bytes_accessed=6 * 10**6, transcendentals=0),
        name="table_grads",
    )(tiles, keys_back, queries)


META_KIND = 1
META_LARGE = 5
META_LENGTH = 72
META_FROM = {"a": 8, "b": 24}
META_TO = {"a": 40, "b": 56}


def live_rows(meta, chunk):
    place = lax.broadcasted_iota(jnp.int32, (CHUNK, 1), 0)
    large = meta[META_LARGE]
    first = large + (chunk - large) * (SLOT_L // SLOT_S)
    is_large = chunk < large
    end = jnp.zeros((CHUNK, 1), jnp.int32)
    for part in range(SLOT_L // SLOT_S):
        slot = jnp.where(is_large, chunk, first + part)
        start = jnp.where(is_large, 0, part * SLOT_S)
        end = jnp.where(place >= part * SLOT_S, start + meta[META_LENGTH + slot], end)
    return (place < end).astype(F32)


class Load:
    def __init__(self, meta, sem, scratch):
        self.meta, self.sem, self.scratch = meta, sem, scratch

    def cols(self, order, own, other, start, source_start, width):
        core, rows = self.meta[0], own.shape[1]
        for k in range(PIECES):
            place = pl.multiple_of(self.meta[META_FROM[order] + k] * rows, 16)
            for half, source in ((core, own), (1 - core, other)):
                pltpu.make_async_copy(
                    source.at[k, :, pl.ds(source_start, width)],
                    self.scratch.at[half, pl.ds(place, rows), pl.ds(start, width)],
                    self.sem,
                ).start()

    def rows(self, order, own, other, start):
        core, rows, width = self.meta[0], own.shape[1], own.shape[2]
        for k in range(PIECES):
            chip = self.meta[META_FROM[order] + k]
            for half, source in ((core, own), (1 - core, other)):
                place = pl.multiple_of((2 * chip + half) * rows, 16)
                pltpu.make_async_copy(
                    source.at[k],
                    self.scratch.at[pl.ds(place, rows), pl.ds(start, width)],
                    self.sem,
                ).start()

    def wait(self):
        pltpu.make_async_copy(self.scratch, self.scratch, self.sem).wait()


PARTS = (slice(0, CHUNK), slice(CHUNK, PAIR))


def project_kernel(meta, x_ref, vec_ref, a0, a1, b0, b1, low_ref, q_ref, k_ref, v_ref, w_scr, sem):
    @pl.when(pl.program_id(0) == 0)
    def _():
        load = Load(meta, sem, w_scr)
        load.cols("a", a0, a1, 0, 0, D)
        load.cols("b", b0, b1, D, 0, D // 2)
        load.wait()

    products = []
    for p in PARTS:
        scaled, _ = unit_rows(x_ref[p].astype(F32))
        low = (scaled * vec_ref[0:1] + vec_ref[3:4]).astype(BF16)
        low_ref[p] = low
        products.append((dot(low, w_scr[0]), dot(low, w_scr[1])))
    for p, (first, second) in zip(PARTS, products):
        q_ref[p] = ((first[:, :D] + vec_ref[4:5]) * QUERY_SCALE).astype(BF16)
        k_ref[p, : D // 2] = first[:, D:].astype(BF16)
        k_ref[p, D // 2 :] = second[:, : D // 2].astype(BF16)
        v_ref[p] = (second[:, D // 2 :] + vec_ref[5:6]).astype(BF16)


def project(meta, tokens, vec, pieces):
    rows = tokens.shape[0]
    tile = pl.BlockSpec((PAIR, D), lambda c, m: (c, 0))
    return pl.pallas_call(
        project_kernel,
        grid_spec=pltpu.PrefetchScalarGridSpec(
            num_scalar_prefetch=1,
            grid=(rows // PAIR,),
            in_specs=[tile, full(16, D), ANY, ANY, ANY, ANY],
            out_specs=[tile] * 4,
            scratch_shapes=[pltpu.VMEM((2, D, 3 * D // 2), BF16), pltpu.SemaphoreType.DMA],
        ),
        out_shape=[jax.ShapeDtypeStruct((rows, D), BF16)] * 4,
        compiler_params=pltpu.CompilerParams(vmem_limit_bytes=VMEM_BIG),
        cost_estimate=pl.CostEstimate(
            flops=2 * rows * D * 3 * D, bytes_accessed=16 * rows * D, transcendentals=0
        ),
        name="project",
    )(meta, tokens, vec, *pieces)


def attend_kernel(meta, q_ref, k_ref, v_ref, bias_ref, x_ref, vec_ref, o0, o1, *refs, first):
    mixed_ref, turned_ref, lse_ref, mid_ref, aln_ref, low_ref, wo_scr, sem = refs[-8:]

    @pl.when(pl.program_id(0) == 0)
    def _():
        Load(meta, sem, wo_scr).cols("b", o0, o1, 0, D // 2, D // 2)

    mask = (1.0 - live_rows(meta, pl.program_id(0) + first)) * NEG_FILL
    mask = jnp.broadcast_to(mask, (CHUNK, CHUNK))
    query_turned = q_ref[...].astype(F32).T.astype(BF16)
    value_turned = v_ref[...].astype(F32).T.astype(BF16)
    parts = [slice(h * HEAD_DIM, (h + 1) * HEAD_DIM) for h in range(HEADS)]
    sums = []

    def mix(h, exponent, largest, row_total):
        out = dot(value_turned[parts[h]], exponent)
        turned_ref[0, parts[h]] = out * (1.0 / row_total)
        sums.append(largest + jnp.log(row_total))

    product, before = dot(k_ref[:, parts[0]], query_turned[parts[0]]), None
    for h in range(HEADS):
        scores = product + bias_ref[0, h].astype(F32) + mask
        if h + 1 < HEADS:
            product = dot(k_ref[:, parts[h + 1]], query_turned[parts[h + 1]])
        largest = jnp.max(scores, axis=0, keepdims=True)
        exponent = jnp.exp(scores - largest)
        row_total = jnp.sum(exponent, axis=0, keepdims=True)
        if before:
            mix(*before)
        before = (h, exponent.astype(BF16), largest, row_total)
    mix(*before)
    lse_ref[0] = jnp.concatenate(sums + [jnp.zeros((16 - HEADS, CHUNK), F32)], axis=0)
    mixed = turned_ref[0].T
    mixed_ref[...] = mixed

    @pl.when(pl.program_id(0) == 0)
    def _():
        Load(meta, sem, wo_scr).wait()

    scaled, _ = unit_rows(mixed * vec_ref[10:11])
    aln = (scaled * vec_ref[1:2] + vec_ref[6:7]).astype(BF16)
    aln_ref[...] = aln
    branch = jnp.concatenate([dot(aln, wo_scr[0]), dot(aln, wo_scr[1])], axis=1)
    mid = x_ref[...].astype(F32) + branch + vec_ref[7:8]
    mid_ref[...] = mid
    scaled, _ = unit_rows(mid)
    low_ref[...] = (scaled * vec_ref[2:3] + vec_ref[8:9]).astype(BF16)


def attend(meta, query, key, value, bias, tokens, vec, w_out, first, chunks, before=()):
    rows = query.shape[0]
    tile = pl.BlockSpec((CHUNK, D), lambda c, m: (c + first, 0))
    return pl.pallas_call(
        functools.partial(attend_kernel, first=first),
        grid_spec=pltpu.PrefetchScalarGridSpec(
            num_scalar_prefetch=1,
            grid=(chunks,),
            in_specs=[
                tile, tile, tile,
                pl.BlockSpec(
                    (1, HEADS, CHUNK, CHUNK), lambda c, m: (m[META_KIND + c + first], 0, 0, 0)
                ),
                tile,
                full(16, D),
                ANY, ANY,
            ]
            + [ANY] * len(before),
            out_specs=[
                tile,
                pl.BlockSpec((1, D, CHUNK), lambda c, m: (c + first, 0, 0)),
                pl.BlockSpec((1, 16, CHUNK), lambda c, m: (c + first, 0, 0)),
                tile, tile, tile,
            ],
            scratch_shapes=[pltpu.VMEM((2, D, D // 2), BF16), pltpu.SemaphoreType.DMA],
        ),
        out_shape=[
            jax.ShapeDtypeStruct((rows, D), F32),
            jax.ShapeDtypeStruct((rows // CHUNK, D, CHUNK), F32),
            jax.ShapeDtypeStruct((rows // CHUNK, 16, CHUNK), F32),
            jax.ShapeDtypeStruct((rows, D), F32),
            jax.ShapeDtypeStruct((rows, D), BF16),
            jax.ShapeDtypeStruct((rows, D), BF16),
        ],
        input_output_aliases={9 + i: i for i in range(len(before))},
        compiler_params=pltpu.CompilerParams(vmem_limit_bytes=VMEM_BIG),
        cost_estimate=pl.CostEstimate(
            flops=10 * 10**9, bytes_accessed=16 * rows * D, transcendentals=0
        ),
        name="attend",
    )(meta, query, key, value, bias, tokens, vec, *w_out, *before)


CUT = 512
ROOT_PART = 0.3275911 * HALF_ROOT
TAIL = (0.127414796, -0.142248368, 0.7107068705, -0.7265760135, 0.5307027145)


def normal_parts(z):
    density = jnp.exp(-0.5 * z * z)
    t = 1.0 / (1.0 + ROOT_PART * jnp.abs(z))
    tail = TAIL[4] * t + TAIL[3]
    for c in (TAIL[2], TAIL[1], TAIL[0]):
        tail = tail * t + c
    tail = tail * t * density
    return jnp.where(z >= 0.0, 1.0 - tail, tail), z * (DENSITY_SCALE * density)


def lane_sum(values):
    return jnp.sum(values, axis=-1, keepdims=True)


def feed_kernel(
    meta, mid_ref, low_ref, cot_ref, vec_ref, wide_ref,
    i0, i1, i2, i3, f0, f1, f2, f3,
    out_ref, sums_ref, sums_ff_ref, dz_out, g0, g1, g2, g3,
    wi_scr, wf_scr, unit_scr, slope_scr, dm_scr,
    df_scr, low_scr, m_scr, dz_scr, cols_scr, rows_scr, sems, stage_sems,
):
    step = pl.program_id(0)
    mine = pl.ds(pl.multiple_of(step * CHUNK, CHUNK), CHUNK)

    def feed_loads():
        return [Load(meta, sems.at[i], s) for i, s in enumerate((wi_scr, wf_scr))]

    def arrived(which):
        @pl.when(step == 0)
        def _():
            feed_loads()[which].wait()

    @pl.when(step == 0)
    def _():
        loads = feed_loads()
        loads[0].cols("a", i0, i1, 0, 0, FF // 4)
        loads[0].cols("b", i2, i3, FF // 4, 0, FF // 4)
        loads[1].rows("a", f0, f1, 0)
        loads[1].rows("b", f2, f3, D // 2)
        sums_ref[...] = jnp.zeros_like(sums_ref)
        sums_ff_ref[...] = jnp.zeros_like(sums_ff_ref)

    live = live_rows(meta, step)
    df_full = cot_ref[...].astype(F32) * live
    df = df_full.astype(BF16)
    df_scr[mine] = df
    sums_ref[0:1] += col_sum(df_full)
    mid = mid_ref[...]
    low = low_ref[...]
    low_scr[mine] = low
    arrived(0)

    cuts = [slice(a, a + CUT) for a in range(0, FF, CUT)]
    inner = [(a * CUT // (FF // 2), slice(a * CUT % (FF // 2), a * CUT % (FF // 2) + CUT)) for a in range(FF // CUT)]
    total = jnp.zeros((CHUNK, 1), F32)
    for cut, (half, part) in zip(cuts, inner):
        z = dot(low, wi_scr[half, :, part]) + wide_ref[1:2, cut]
        cumulative, rest = normal_parts(z)
        act = z * cumulative
        unit_scr[:, cut] = act
        slope_scr[:, cut] = cumulative + rest
        total += lane_sum(act)
    mean = total * (1.0 / FF)
    square = jnp.zeros((CHUNK, 1), F32)
    arrived(1)
    for cut in cuts:
        dm_scr[:, cut] = dot(df, wf_scr[cut], NT)
        center = unit_scr[:, cut] - mean
        square += lane_sum(center * center)
    spread = lax.rsqrt(square * (1.0 / FF) + NORM_EPS)
    out = mid + vec_ref[9:10]
    first = jnp.zeros((CHUNK, 1), F32)
    second = jnp.zeros((CHUNK, 1), F32)
    for cut in cuts:
        unit = (unit_scr[:, cut] - mean) * spread
        unit_scr[:, cut] = unit
        m = (unit * wide_ref[0:1, cut] + wide_ref[2:3, cut]).astype(BF16)
        m_scr[mine, cut] = m
        out += dot(m, wf_scr[cut])
        dm = dm_scr[:, cut]
        sums_ff_ref[0:1, cut] += col_sum(dm * unit)
        sums_ff_ref[1:2, cut] += col_sum(dm)
        inside = dm * wide_ref[0:1, cut]
        first += lane_sum(inside)
        second += lane_sum(inside * unit)
    out_ref[...] = (out * live).astype(BF16)
    first = first * (1.0 / FF)
    second = second * (1.0 / FF)
    for cut, (half, part) in zip(cuts, inner):
        inside = dm_scr[:, cut] * wide_ref[0:1, cut]
        du = spread * (inside - first - unit_scr[:, cut] * second)
        dz_full = du * slope_scr[:, cut]
        sums_ff_ref[2:3, cut] += col_sum(dz_full)
        dz_scr[half, mine, part] = dz_full.astype(BF16)
    pltpu.make_async_copy(dz_scr.at[:, mine], dz_out.at[:, mine], sems.at[2]).start()

    @pl.when(step == pl.num_programs(0) - 1)
    def _():
        core = meta[0]
        stages = [Stage(cols_scr, stage_sems, 0), Stage(rows_scr, stage_sems, 2)]
        for side, out in ((1 - core, g0), (core, g2)):
            for b in range(D // BAND):
                band = dot(low_scr[:, b * BAND : (b + 1) * BAND], dz_scr[side], TN).astype(BF16)
                stage = stages[0].take()
                for i in range(BAND // ROWS_D):
                    rows = slice(i * ROWS_D, (i + 1) * ROWS_D)
                    stage[i, :ROWS_D] = band[rows, :D]
                    stage[i, ROWS_D:] = band[rows, D:]
                    piece = meta[META_TO["a"] + b * (BAND // ROWS_D) + i]
                    stages[0].send(stage.at[i], out.at[piece])
        for b in range(FF // BAND):
            band = dot(m_scr[:, b * BAND : (b + 1) * BAND], df_scr[...], TN).astype(BF16)
            stage = stages[1].take()
            for i in range(BAND // ROWS_F):
                stage[i] = band[i * ROWS_F : (i + 1) * ROWS_F]
            for parity in range(2):
                for own, out in ((True, g3), (False, g1)):

                    @pl.when((core == parity) == own)
                    def _():
                        for i in range(parity, BAND // ROWS_F, 2):
                            piece = meta[META_TO["b"] + (b * (BAND // ROWS_F) + i) // 2]
                            stages[1].send(stage.at[i], out.at[piece])

        for stage in stages:
            stage.end()
        pltpu.make_async_copy(dz_scr, dz_out, sems.at[2]).wait()


class Stage:
    def __init__(self, scratch, sems, first):
        self.scratch, self.sems, self.first, self.count = scratch, sems, first, 0

    def wait(self, slot):
        buffer = self.scratch.at[slot]
        pltpu.make_async_copy(buffer, buffer, self.sems.at[self.first + slot]).wait()

    def take(self):
        self.slot = self.count % 2
        if self.count >= 2:
            self.wait(self.slot)
        self.count += 1
        return self.scratch.at[self.slot]

    def send(self, source, target):
        pltpu.make_async_copy(source, target, self.sems.at[self.first + self.slot]).start()

    def end(self):
        for slot in range(min(2, self.count)):
            self.wait((self.count - 1 - slot) % 2)


BAND = 384


def feed(meta, mid, low, cot, vec, wide, w_in, w_down):
    rows = mid.shape[0]
    tile = pl.BlockSpec((CHUNK, D), lambda c, m: (c, 0))
    return pl.pallas_call(
        feed_kernel,
        grid_spec=pltpu.PrefetchScalarGridSpec(
            num_scalar_prefetch=1,
            grid=(rows // CHUNK,),
            in_specs=[
                tile, tile, tile,
                full(16, D), full(8, FF),
                *[ANY] * 8,
            ],
            out_specs=[tile, full(8, D), full(3, FF), *[ANY] * 5],
            scratch_shapes=[
                pltpu.VMEM((2, D, FF // 2), BF16),
                pltpu.VMEM((FF, D), BF16),
                pltpu.VMEM((CHUNK, FF), F32),
                pltpu.VMEM((CHUNK, FF), F32),
                pltpu.VMEM((CHUNK, FF), F32),
                pltpu.VMEM((rows, D), BF16),
                pltpu.VMEM((rows, D), BF16),
                pltpu.VMEM((rows, FF), BF16),
                pltpu.VMEM((2, rows, FF // 2), BF16),
                pltpu.VMEM((2, BAND // ROWS_D, 2 * ROWS_D, D), BF16),
                pltpu.VMEM((2, BAND // ROWS_F, ROWS_F, D), BF16),
                pltpu.SemaphoreType.DMA((4,)),
                pltpu.SemaphoreType.DMA((4,)),
            ],
        ),
        out_shape=[
            jax.ShapeDtypeStruct((rows, D), BF16),
            jax.ShapeDtypeStruct((8, D), F32),
            jax.ShapeDtypeStruct((3, FF), F32),
            jax.ShapeDtypeStruct((2, rows, FF // 2), BF16),
        ]
        + [jax.ShapeDtypeStruct((PIECES, ROWS_F, D), BF16)] * 4,
        compiler_params=pltpu.CompilerParams(vmem_limit_bytes=VMEM_ALL),
        cost_estimate=pl.CostEstimate(
            flops=2 * rows * D * 5 * FF, bytes_accessed=40 * rows * D, transcendentals=0
        ),
        name="feed",
    )(meta, mid, low, cot, vec, wide, *w_in, *w_down)


def middle_kernel(
    meta, dz_ref, mid_ref, mixed_ref, cot_ref, aln_ref, vec_ref, i0, i1, i2, i3, o0, o1,
    dx_ref, do_ref, sums_ref, other_out, own_out, wi_scr, wo_scr, da_scr, stage_scr, sems,
):
    step = pl.program_id(0)

    def loads():
        return [Load(meta, sems.at[i], s) for i, s in enumerate((wi_scr, wo_scr))]

    @pl.when(step == 0)
    def _():
        first, second = loads()
        first.cols("a", i0, i1, 0, 0, FF // 4)
        first.cols("b", i2, i3, FF // 4, 0, FF // 4)
        second.cols("b", o0, o1, 0, D // 2, D // 2)
        sums_ref[...] = jnp.zeros_like(sums_ref)
        first.wait()
        second.wait()

    dhs = [dot(dz_ref[0, p], wi_scr[0], NT) + dot(dz_ref[1, p], wi_scr[1], NT) for p in PARTS]
    dns = []
    for k, (p, dh) in enumerate(zip(PARTS, dhs)):
        scaled, spread = unit_rows(mid_ref[p])
        grad = cot_ref[p].astype(F32) * live_rows(meta, 2 * step + k)
        dx = grad + unit_rows_back(dh * vec_ref[2:3], scaled, spread)
        da = dx.astype(BF16)
        dns.append(dot(da[:, : D // 2], wo_scr[0], NT) + dot(da[:, D // 2 :], wo_scr[1], NT))
        mine = pl.ds(pl.multiple_of(step * PAIR + k * CHUNK, CHUNK), CHUNK)
        da_scr[0, mine] = da[:, : D // 2]
        da_scr[1, mine] = da[:, D // 2 :]
        dx_ref[p] = dx
        sums_ref[0:1] += col_sum(dh * scaled)
        sums_ref[1:2] += col_sum(dh)
        sums_ref[2:3] += col_sum(dx)
    for p, dn in zip(PARTS, dns):
        mixed = mixed_ref[p]
        scaled, spread = unit_rows(mixed * vec_ref[10:11])
        heads = unit_rows_back(dn * vec_ref[1:2], scaled, spread)
        do_ref[p] = (heads * vec_ref[10:11]).astype(BF16)
        sums_ref[3:4] += col_sum(dn * scaled)
        sums_ref[4:5] += col_sum(dn)
        sums_ref[5:6] += col_sum(heads * mixed)

    @pl.when(step == pl.num_programs(0) - 1)
    def _():
        core = meta[0]
        stages = Stage(stage_scr, sems, 2)
        for side, out in ((1 - core, other_out), (core, own_out)):
            band = dot(aln_ref[...], da_scr[side], TN).astype(BF16)
            stage = stages.take()
            for i in range(PIECES):
                stage[i] = band[i * ROWS_D : (i + 1) * ROWS_D]
                piece = meta[META_TO["b"] + i]
                stages.send(stage.at[i], out.at[piece, :, pl.ds(D // 2, D // 2)])
        stages.end()


def middle(meta, dz, mid, mixed, cot, aln, vec, w_in, w_out):
    rows = mid.shape[0]
    tile = pl.BlockSpec((PAIR, D), lambda c, m: (c, 0))
    return pl.pallas_call(
        middle_kernel,
        grid_spec=pltpu.PrefetchScalarGridSpec(
            num_scalar_prefetch=1,
            grid=(rows // PAIR,),
            in_specs=[
                pl.BlockSpec((2, PAIR, FF // 2), lambda c, m: (0, c, 0)),
                tile, tile, tile,
                full(rows, D),
                full(16, D),
                *[ANY] * 6,
            ],
            out_specs=[tile, tile, full(8, D), ANY, ANY],
            scratch_shapes=[
                pltpu.VMEM((2, D, FF // 2), BF16),
                pltpu.VMEM((2, D, D // 2), BF16),
                pltpu.VMEM((2, rows, D // 2), BF16),
                pltpu.VMEM((2, PIECES, ROWS_D, D // 2), BF16),
                pltpu.SemaphoreType.DMA((4,)),
            ],
        ),
        out_shape=[
            jax.ShapeDtypeStruct((rows, D), F32),
            jax.ShapeDtypeStruct((rows, D), BF16),
            jax.ShapeDtypeStruct((8, D), F32),
        ]
        + [jax.ShapeDtypeStruct((PIECES, ROWS_D, D), BF16)] * 2,
        compiler_params=pltpu.CompilerParams(vmem_limit_bytes=VMEM_BIG),
        cost_estimate=pl.CostEstimate(
            flops=2 * rows * D * (2 * D + FF), bytes_accessed=30 * rows * D, transcendentals=0
        ),
        name="middle",
    )(meta, dz, mid, mixed, cot, aln, vec, *w_in, *w_out)


def attend_back_kernel(
    meta, q_ref, k_ref, v_ref, do_ref, turned_ref, lse_ref, bias_ref, low_ref, before_0, before_1,
    dqkv_out, tiles_out, g0, g2, g1, g3, dq_scr, do_scr, tiles_ref, dqkv_scr, a_scr, b_scr, sems,
):
    step = pl.program_id(0)
    mine = pl.ds(pl.multiple_of(step * CHUNK, CHUNK), CHUNK)
    kind = meta[META_KIND + step]

    @pl.when(step == 0)
    def _():
        tiles_ref[...] = jnp.zeros_like(tiles_ref)

    query = q_ref[...]
    query_turned = query.astype(F32).T.astype(BF16)
    key_turned = k_ref[...].astype(F32).T.astype(BF16)
    do_scr[...] = do_ref[...].astype(F32).T
    mask = jnp.broadcast_to((1.0 - live_rows(meta, pl.program_id(0))) * NEG_FILL, (CHUNK, CHUNK))
    parts = [slice(h * HEAD_DIM, (h + 1) * HEAD_DIM) for h in range(HEADS)]
    dk, dv = [], []

    def products(h):
        part = parts[h]
        return (
            dot(k_ref[:, part], query_turned[part]),
            dot(v_ref[:, part], do_scr[part].astype(BF16)),
        )

    def finish(h, probs, ds):
        dv.append(dot(probs, do_ref[:, parts[h]]))
        dk.append(dot(ds, q_ref[:, parts[h]]))
        dq_scr[parts[h]] = dot(key_turned[parts[h]], ds)

    coming, before = products(0), None
    for h in range(HEADS):
        scores, dprobs = coming
        if h + 1 < HEADS:
            coming = products(h + 1)
        scores = scores + bias_ref[0, h].astype(F32) + mask
        probs = jnp.exp(scores - lse_ref[0, h : h + 1])
        centre = jnp.sum(do_scr[parts[h]] * turned_ref[0, parts[h]], axis=0, keepdims=True)
        ds = probs * (dprobs - centre)
        tiles_ref[kind, h] += ds
        if before:
            finish(*before)
        before = (h, probs.astype(BF16), ds.astype(BF16))
    finish(*before)
    dq = (dq_scr[...].T * QUERY_SCALE).astype(BF16)
    dk = jnp.concatenate(dk, axis=1).astype(BF16)
    dv = jnp.concatenate(dv, axis=1).astype(BF16)
    dqkv_scr[0, mine, :D] = dq
    dqkv_scr[0, mine, D:] = dk[:, : D // 2]
    dqkv_scr[1, mine, : D // 2] = dk[:, D // 2 :]
    dqkv_scr[1, mine, D // 2 :] = dv
    pltpu.make_async_copy(dqkv_scr.at[:, mine], dqkv_out.at[:, mine], sems.at[0]).start()

    @pl.when(step == pl.num_programs(0) - 1)
    def _():
        pltpu.make_async_copy(tiles_ref, tiles_out, sems.at[1]).start()
        core = meta[0]
        stages = [Stage(a_scr, sems, 2), Stage(b_scr, sems, 4)]
        for side, out_a, out_b in ((1 - core, g0, g1), (core, g2, g3)):
            for b in range(D // BAND):
                band = dot(low_ref[:, b * BAND : (b + 1) * BAND], dqkv_scr[side], TN).astype(BF16)
                stage_a, stage_b = (stage.take() for stage in stages)
                for i in range(BAND // ROWS_D):
                    rows = slice(i * ROWS_D, (i + 1) * ROWS_D)
                    stage_a[i] = band[rows, :D]
                    stage_b[i] = band[rows, D:]
                    piece = meta[META_TO["a"] + b * (BAND // ROWS_D) + i]
                    stages[0].send(stage_a.at[i], out_a.at[piece])
                    piece = meta[META_TO["b"] + b * (BAND // ROWS_D) + i]
                    stages[1].send(stage_b.at[i], out_b.at[piece, :, pl.ds(0, D // 2)])
        for stage in stages:
            stage.end()
        pltpu.make_async_copy(dqkv_scr, dqkv_out, sems.at[0]).wait()
        pltpu.make_async_copy(tiles_ref, tiles_out, sems.at[1]).wait()


def attend_back(meta, query, key, value, do, turned, lse, bias, low, before):
    rows = query.shape[0]
    chunks = rows // CHUNK
    tile = pl.BlockSpec((CHUNK, D), lambda c, m: (c, 0))
    pieces = jax.ShapeDtypeStruct((PIECES, ROWS_D, D), BF16)
    return pl.pallas_call(
        attend_back_kernel,
        grid_spec=pltpu.PrefetchScalarGridSpec(
            num_scalar_prefetch=1,
            grid=(chunks,),
            in_specs=[
                tile, tile, tile, tile,
                pl.BlockSpec((1, D, CHUNK), lambda c, m: (c, 0, 0)),
                pl.BlockSpec((1, 16, CHUNK), lambda c, m: (c, 0, 0)),
                pl.BlockSpec((1, HEADS, CHUNK, CHUNK), lambda c, m: (m[META_KIND + c], 0, 0, 0)),
                full(rows, D),
                ANY, ANY,
            ],
            out_specs=[ANY] * 6,
            scratch_shapes=[
                pltpu.VMEM((D, CHUNK), F32),
                pltpu.VMEM((D, CHUNK), F32),
                pltpu.VMEM((2, HEADS, CHUNK, CHUNK), F32),
                pltpu.VMEM((2, rows, 3 * D // 2), BF16),
                pltpu.VMEM((2, BAND // ROWS_D, ROWS_D, D), BF16),
                pltpu.VMEM((2, BAND // ROWS_D, ROWS_D, D // 2), BF16),
                pltpu.SemaphoreType.DMA((6,)),
            ],
        ),
        out_shape=[
            jax.ShapeDtypeStruct((2, rows, 3 * D // 2), BF16),
            jax.ShapeDtypeStruct((2, HEADS, CHUNK, CHUNK), F32),
            *[pieces] * 4,
        ],
        input_output_aliases={9: 4, 10: 5},
        compiler_params=pltpu.CompilerParams(vmem_limit_bytes=VMEM_BIG),
        cost_estimate=pl.CostEstimate(
            flops=20 * 10**9, bytes_accessed=30 * rows * D, transcendentals=0
        ),
        name="attend_back",
    )(meta, query, key, value, do, turned, lse, bias, low, *before)


def last_kernel(
    meta, dqkv_ref, x_ref, dx_ref, vec_ref, a0, a1, b0, b1,
    out_ref, sums_ref, sums_p_ref, w_scr, sem,
):
    @pl.when(pl.program_id(0) == 0)
    def _():
        load = Load(meta, sem, w_scr)
        load.cols("a", a0, a1, 0, 0, D)
        load.cols("b", b0, b1, D, 0, D // 2)
        load.wait()
        sums_ref[...] = jnp.zeros_like(sums_ref)
        sums_p_ref[...] = jnp.zeros_like(sums_p_ref)

    dh = dot(dqkv_ref[0], w_scr[0], NT) + dot(dqkv_ref[1], w_scr[1], NT)
    for half in range(2):
        sums_p_ref[half : half + 1] += col_sum(dqkv_ref[half].astype(F32))
    scaled, spread = unit_rows(x_ref[...].astype(F32))
    sums_ref[0:1] += col_sum(dh * scaled)
    sums_ref[1:2] += col_sum(dh)
    out_ref[...] = (dx_ref[...] + unit_rows_back(dh * vec_ref[0:1], scaled, spread)).astype(BF16)


def last(meta, dqkv, tokens, dx, vec, w_in):
    rows = tokens.shape[0]
    tile = pl.BlockSpec((CHUNK, D), lambda c, m: (c, 0))
    return pl.pallas_call(
        last_kernel,
        grid_spec=pltpu.PrefetchScalarGridSpec(
            num_scalar_prefetch=1,
            grid=(rows // CHUNK,),
            in_specs=[
                pl.BlockSpec((2, CHUNK, 3 * D // 2), lambda c, m: (0, c, 0)),
                tile, tile,
                full(16, D),
                ANY, ANY, ANY, ANY,
            ],
            out_specs=[tile, full(8, D), full(2, 3 * D // 2)],
            scratch_shapes=[pltpu.VMEM((2, D, 3 * D // 2), BF16), pltpu.SemaphoreType.DMA],
        ),
        out_shape=[
            jax.ShapeDtypeStruct((rows, D), BF16),
            jax.ShapeDtypeStruct((8, D), F32),
            jax.ShapeDtypeStruct((2, 3 * D // 2), F32),
        ],
        compiler_params=pltpu.CompilerParams(vmem_limit_bytes=VMEM_BIG),
        cost_estimate=pl.CostEstimate(
            flops=2 * rows * D * 3 * D, bytes_accessed=16 * rows * D, transcendentals=0
        ),
        name="last",
    )(meta, dqkv, tokens, dx, vec, *w_in)


def swap(values, mask, count):
    return lax.ppermute(values, AXES, [(i, i ^ mask) for i in range(count)])


def tie(values, after):
    values, after = list(values), list(after)
    if not after:
        return values
    return list(lax.optimization_barrier(tuple(values + after))[: len(values)])


class Chain:
    def __init__(self, net, steps, finish):
        self.net, self.steps, self.finish = net, list(steps), finish
        self.got = [None] * len(self.steps)
        self.sends = [[] for _ in self.steps]
        self.results = [None] * len(self.steps)

    def go(self, *after):
        for i, step in enumerate(self.steps):
            if self.results[i] is not None:
                continue
            try:
                got = self.got[i] if self.got[i] is None else tie(self.got[i], after)
                sends = step.send(got)
                values = [v for v, _ in sends]
                if got is None:
                    values = tie(values, after)
                self.sends[i] = values
                self.got[i] = [self.net.swap(v, m) for v, (_, m) in zip(values, sends)]
            except StopIteration as end:
                self.results[i] = end.value
                self.sends[i] = []
        return self

    @property
    def sent(self):
        return [v for part in self.sends for v in part]

    @property
    def received(self):
        return [v for part in self.got for v in part or []]

    def done(self, *after):
        while any(r is None for r in self.results):
            self.go(*after)
            after = ()
        return self.finish(self.results)


class Ready:
    def __init__(self, value):
        self.value, self.sent, self.received = value, [], []

    def go(self, *after):
        return self

    def done(self, *after):
        return self.value


def add_kernel(*refs, sizes):
    outs = refs[sum(sizes) :]
    at = 0
    for size, out in zip(sizes, outs):
        total = refs[at][...].astype(F32)
        for ref in refs[at + 1 : at + size]:
            total += ref[...].astype(F32)
        out[...] = total.astype(BF16)
        at += size


def add_pieces(parts, count):
    rows = parts[0][0].shape[1]
    step = min(count, 4)
    return pl.pallas_call(
        functools.partial(add_kernel, sizes=[len(p) for p in parts]),
        grid=(count // step,),
        in_specs=[
            pl.BlockSpec((step, rows, D), lambda i: (count // step + i, 0, 0)) for p in parts for _ in p
        ],
        out_specs=[pl.BlockSpec((step, rows, D), lambda i: (i, 0, 0))] * len(parts),
        out_shape=[jax.ShapeDtypeStruct((count, rows, D), BF16)] * len(parts),
        compiler_params=pltpu.CompilerParams(vmem_limit_bytes=32 * 2**20),
        cost_estimate=pl.CostEstimate(
            flops=count * rows * D * 4, bytes_accessed=16 * count * rows * D, transcendentals=0
        ),
        name="add_pieces",
    )(*(a for p in parts for a in p))


def add_last_kernel(*refs, sizes):
    outs = refs[sum(sizes) :]
    rows = refs[0].shape[1]
    for z, out in enumerate(outs):
        at = 0
        for k, size in enumerate(sizes):
            total = refs[at][z].astype(F32)
            for ref in refs[at + 1 : at + size]:
                total += ref[z].astype(F32)
            out[k * rows : (k + 1) * rows] = total.astype(out.dtype)
            at += size


def add_last_pieces(parts):
    rows = parts[0][0].shape[1]
    shape = (len(parts) * rows, D)
    return pl.pallas_call(
        functools.partial(add_last_kernel, sizes=[len(p) for p in parts]),
        grid=(1,),
        in_specs=[pl.BlockSpec((4, rows, D), lambda i: (0, 0, 0)) for p in parts for _ in p],
        out_specs=[full(*shape)] * 4,
        out_shape=[jax.ShapeDtypeStruct(shape, F32)] + [jax.ShapeDtypeStruct(shape, BF16)] * 3,
        compiler_params=pltpu.CompilerParams(vmem_limit_bytes=32 * 2**20),
        cost_estimate=pl.CostEstimate(
            flops=rows * D * 24, bytes_accessed=80 * rows * D, transcendentals=0
        ),
        name="add_last_pieces",
    )(*(a for p in parts for a in p))


class Cube:
    SIDES = {"a": (2, 4), "b": (4, 2)}

    def __init__(self):
        self.me = lax.axis_index(AXES).astype(jnp.int32)

    def swap(self, values, mask):
        return swap(values, mask, 32)

    def masks(self, order):
        shift = self.SIDES[order]
        return np.array(
            [8 * (k & 3) + shift[0] * (k >> 2 & 1) + shift[1] * (k >> 3) for k in range(PIECES)]
        )

    def meta(self):
        chip = self.me >> 1
        place = jnp.arange(PIECES, dtype=jnp.int32)
        start = [chip ^ jnp.asarray(self.masks(o) >> 1, jnp.int32) for o in "ab"]
        mask = chip ^ place
        x, y = mask & 1, mask >> 1 & 1
        to = [(mask >> 2) + 4 * x + 8 * y, (mask >> 2) + 4 * y + 8 * x]
        return self.me & 1, start + to

    def spread(self, piece, parts):
        got = yield [(piece, 8 * z) for z in (1, 2, 3)]
        held = jnp.stack([piece] + got)
        ends = np.cumsum([0] + [w for _, w in parts])
        cuts = [held[..., a:b] for a, b in zip(ends[:-1], ends[1:])]
        for stage in (0, 1):
            got = yield [(c, self.SIDES[order][stage]) for c, (order, _) in zip(cuts, parts)]
            cuts = [jnp.concatenate(pair) for pair in zip(cuts, got)]
        got = yield [(c, 1) for c in cuts]
        return [v for pair in zip(cuts, got) for v in pair]

    def gather_cols(self, shards, parts):
        left, right = (
            jnp.concatenate([h[side] for h in (jnp.split(s, 2, axis=1) for s in shards)], axis=1)
            for side in (0, 1)
        )
        odd = (self.me & 1) == 1
        got = self.swap(jnp.where(odd, left, right), 1)
        mine = jnp.where(odd, right, left)
        block = jnp.where(odd, jnp.concatenate([got, mine]), jnp.concatenate([mine, got]))
        return Chain(self, [self.spread(block, parts)], lambda results: results[0])

    def gather_rows(self, shard, parts):
        return Chain(self, [self.spread(shard, parts)], lambda results: results[0])

    def gather_small(self, pack):
        every = jnp.broadcast_to(pack, (32, pack.shape[0]))
        return lax.all_to_all(every, AXES, 0, 0, tiled=True)

    def reduce_small(self, pack):
        return jnp.sum(lax.all_to_all(pack, AXES, 0, 0, tiled=True), axis=0)

    def gather_rows(self, shard, order):
        return Chain(self, [self.spread(shard, order)], lambda parts: parts[0])

    def collect(self, owns, others, orders):
        got = yield [(o, 1) for o in others]
        terms = [[a, b] for a, b in zip(owns, got)]
        count = PIECES
        for stage in (1, 0):
            count //= 2
            sends = add_pieces(terms, count)
            got = yield [(v, self.SIDES[o][stage]) for v, o in zip(sends, orders)]
            terms = [part + [g] for part, g in zip(terms, got)]
        mine, *sends = add_last_pieces(terms)
        got = yield [(v, 8 * z) for z, v in zip((1, 2, 3), sends)]
        return mine + sum(g.astype(F32) for g in got)

    def reduce_ff(self, others, owns):
        def finish(results):
            (total,) = results
            block = jnp.concatenate([total[:ROWS_D], total[ROWS_D : 2 * ROWS_D]], axis=1)
            return jnp.concatenate(self.join(block), axis=1), total[2 * ROWS_D :]

        return Chain(self, [self.collect(owns, others, "ab")], finish)

    def reduce_attn(self, others, owns):
        def finish(results):
            (total,) = results
            block = jnp.concatenate([total[:ROWS_D], total[ROWS_D:]], axis=1)
            sides = self.join(block)
            cut = 3 * D // 2
            return tuple(
                jnp.concatenate([s[:, part] for s in sides], axis=1)
                for part in (slice(0, cut), slice(cut, None))
            )

        return Chain(self, [self.collect(owns, others, "ab")], finish)

    def join(self, block):
        rows = block.shape[0] // 2
        low, high = block[:rows], block[rows:]
        odd = (self.me & 1) == 1
        got = self.swap(jnp.where(odd, low, high), 1)
        mine = jnp.where(odd, high, low)
        return jnp.where(odd, got, mine), jnp.where(odd, mine, got)


class Plain:
    def __init__(self, count):
        self.count = count
        self.me = lax.axis_index(AXES)

    def meta(self):
        place = jnp.arange(PIECES, dtype=jnp.int32)
        return jnp.int32(0), [place] * 4

    def gather_cols(self, shards, parts):
        whole = [lax.all_gather(s, AXES, axis=0, tiled=True) for s in shards]
        left, right = (
            jnp.concatenate([h[side] for h in (jnp.split(w, 2, axis=1) for w in whole)], axis=1)
            for side in (0, 1)
        )
        out, at = [], 0
        for _, width in parts:
            for half in (left, right):
                out.append(half[:, at : at + width].reshape(PIECES, -1, width))
            at += width
        return Ready(out)

    def gather_small(self, pack):
        return lax.all_gather(pack, AXES)

    def reduce_small(self, pack):
        return lax.psum_scatter(pack, AXES, scatter_dimension=0, tiled=False)

    def gather_rows(self, shard, parts):
        whole = lax.all_gather(shard, AXES, axis=0, tiled=True)
        whole = whole.reshape(PIECES, 2, -1, whole.shape[1])
        out, at = [], 0
        for _, width in parts:
            out += [whole[:, side, :, at : at + width] for side in (0, 1)]
            at += width
        return Ready(out)

    def scatter(self, whole):
        return lax.psum_scatter(whole.astype(F32), AXES, scatter_dimension=0, tiled=True)

    def reduce_ff(self, others, owns):
        runs = [
            a[:, row : row + ROWS_D].reshape(D, D)
            for a in (owns[0], others[0])
            for row in (0, ROWS_D)
        ]
        rows = jnp.stack([owns[1], others[1]], axis=1).reshape(FF, D)
        return Ready((self.scatter(jnp.concatenate(runs, axis=1)), self.scatter(rows)))

    def reduce_attn(self, others, owns):
        halves_in, halves_out = [], []
        for a, b in (owns, others):
            a, b = a.reshape(D, D), b.reshape(D, D)
            halves_in += [a, b[:, : D // 2]]
            halves_out.append(b[:, D // 2 :])
        return Ready(tuple(self.scatter(jnp.concatenate(h, axis=1)) for h in (halves_in, halves_out)))


PARTS_ATTN = (("a", D), ("b", D))
PARTS_HALVES = (("a", FF // 4), ("b", FF // 4))
PARTS_ROWS = (("a", D // 2), ("b", D // 2))


def body(
    tokens,
    cotangent,
    w_attn_in,
    w_attn_out,
    w_fc_in,
    w_fc_out,
    gains_d,
    biases_d,
    gains_ff,
    biases_ff,
    rel_table,
    head_scale,
    bucket,
    lengths,
    *,
    count,
    cube,
):
    net = Cube() if cube else Plain(count)
    rows = tokens.shape[0]
    chunks = rows // CHUNK

    gather_attn = net.gather_cols([w_attn_in, w_attn_out], PARTS_ATTN).go()
    small = tie((gains_d, biases_d, gains_ff[None], biases_ff, rel_table), gather_attn.sent)
    sizes = [v.size for v in small]
    ends = np.cumsum(sizes)
    width = -(-int(ends[-1] + 16) // 1024) * 1024
    pack = jnp.concatenate([v.reshape(-1) for v in small] + [jnp.zeros(width - ends[-1], BF16)])
    packs = net.gather_small(pack)

    bucket, lengths = tie([bucket, lengths], [pack])
    large = jnp.sum((bucket == 1).astype(jnp.int32), dtype=jnp.int32)
    kinds = (jnp.arange(chunks, dtype=jnp.int32) >= large).astype(jnp.int32)
    core, tables = net.meta()
    meta = jnp.concatenate(
        [core.astype(jnp.int32)[None], kinds, large[None], jnp.zeros(2, jnp.int32), *tables, lengths]
    )
    keys, keys_back, queries = (jnp.asarray(t) for t in pick_tables())
    gather_ff = net.gather_cols([w_fc_in], PARTS_HALVES)
    gather_down = net.gather_rows(w_fc_out, PARTS_ROWS)

    arrived = gather_attn.received
    gather_attn.go(meta)
    gather_ff.go(*arrived)
    (packs,) = tie([packs], gather_attn.sent + gather_ff.sent)
    vec, wide, lines = unpack(packs, head_scale[None], count)
    gather_attn.go(vec)
    (lines,) = tie([lines], gather_attn.sent)
    bias = build_bias(lines, keys, queries)
    gather_ff.go(bias)
    gather_attn.go(*gather_ff.sent)
    gather_down.go(*gather_ff.sent)
    attn_pieces = gather_attn.done()
    out_pieces = attn_pieces[2:]

    (tokens_in,) = tie([tokens], gather_ff.sent)
    low_in, query, key, value = project(meta, tokens_in, vec, attn_pieces)
    gather_ff.go(low_in)
    gather_down.go(low_in)
    (query_in,) = tie([query], gather_ff.sent + gather_down.sent)
    heads = attend(
        meta, query_in, key, value, bias, tokens, vec, out_pieces, 0, chunks // 2
    )
    gather_down.go(heads[2])
    gather_ff.go(heads[2])
    (query_in,) = tie([query], gather_down.sent + gather_ff.sent)
    mixed, turned, lse, mid, low_attn, low_mid = attend(
        meta, query_in, key, value, bias, tokens, vec, out_pieces, chunks // 2,
        chunks - chunks // 2, heads,
    )
    gather_down.go(lse)
    ff_pieces = gather_ff.done(lse)
    down_pieces = gather_down.done()
    out_tokens, sums_a, sums_ff, dz, *ff_grads = feed(
        meta, mid, low_mid, cotangent, vec, wide, ff_pieces, down_pieces
    )

    reduce_ff = net.reduce_ff(ff_grads[:2], ff_grads[2:]).go()
    (dz,) = tie([dz], reduce_ff.sent)
    dx, do, sums_b, *out_grads = middle(
        meta, dz, mid, mixed, cotangent, low_attn, vec, ff_pieces, out_pieces
    )
    reduce_ff.go(sums_b)
    (do,) = tie([do], reduce_ff.sent)
    dqkv, tiles, other_a, own_a, other_b, own_b = attend_back(
        meta, query, key, value, do, turned, lse, bias, low_in, out_grads
    )
    reduce_attn = net.reduce_attn((other_a, other_b), (own_a, own_b)).go()
    reduce_ff.go(tiles)
    (tiles,) = tie([tiles], reduce_ff.sent)
    (tiles,) = tie([tiles], reduce_attn.sent)
    grad_table = table_grads(tiles, keys_back, queries)
    reduce_attn.go(grad_table)
    reduce_ff.go(grad_table)
    (dqkv,) = tie([dqkv], reduce_attn.sent + reduce_ff.sent)
    grad_tokens, sums_c, sums_p = last(meta, dqkv, tokens, dx, vec, attn_pieces)
    reduce_attn.go(sums_c)
    terms = (sums_a, sums_b, sums_c, sums_p, sums_ff, grad_table)
    terms = pack_terms(*tie(terms, reduce_attn.sent + reduce_ff.received), count, width)
    reduce_attn.go(terms)
    mine = net.reduce_small(terms)
    grad_fc_in, grad_fc_out = reduce_ff.done(*reduce_attn.received)
    grad_attn_in, grad_attn_out = reduce_attn.done()

    grads = [mine[end - size : end].reshape(v.shape) for v, size, end in zip(small, sizes, ends)]
    return (
        out_tokens,
        grad_tokens,
        grad_attn_in,
        grad_attn_out,
        grad_fc_in,
        grad_fc_out,
        grads[0],
        grads[1],
        grads[2][0],
        grads[3],
        grads[4],
        mine[ends[-1] : ends[-1] + HEADS],
    )


def solution(mesh):
    rows = P(AXES, None)
    columns = P(None, AXES)
    line = P(AXES)
    count = mesh.shape["wide"] * mesh.shape["narrow"]
    cube = (mesh.shape["wide"], mesh.shape["narrow"]) == (8, 4)
    return jax.shard_map(
        functools.partial(body, count=count, cube=cube),
        mesh=mesh,
        in_specs=(
            rows, rows, rows, rows, rows, rows,
            columns, columns, line, columns, columns, P(), line, line,
        ),
        out_specs=(
            rows, rows, rows, rows, rows, rows,
            columns, columns, line, columns, columns, P(),
        ),
        check_vma=False,
    )
```

```python
import functools

import jax
import jax.numpy as jnp
import numpy as np
from jax import lax
from jax.experimental import pallas as pl
from jax.experimental.pallas import tpu as pltpu
from jax.sharding import PartitionSpec as P

HEADS = 12
HEAD_DIM = 64
D = 768
FF = 3072
GRID_L = 15
GRID_S = 8
SLOT_L = 256
SLOT_S = 64
STRIDE = 32
RELS = 1024
CHUNK = 256
PAIR = 2 * CHUNK
PIECES = 16
ROWS_D = D // PIECES
ROWS_F = FF // (2 * PIECES)

NEG_FILL = -1e30
NORM_EPS = 1e-05
HALF_ROOT = 0.7071067811865476
DENSITY_SCALE = 0.3989422804014327
QUERY_SCALE = 0.125
AXES = ("wide", "narrow")
F32 = jnp.float32
BF16 = jnp.bfloat16
VMEM_BIG = 60 * 2**20
VMEM_ALL = 63 * 2**20

NN = (((1,), (0,)), ((), ()))
NT = (((1,), (1,)), ((), ()))
TN = (((0,), (0,)), ((), ()))


ANY = pl.BlockSpec(memory_space=pl.ANY)


def full(*shape):
    return pl.BlockSpec(shape, lambda *_: (0,) * len(shape))


def dot(left, right, dims=NN):
    return lax.dot_general(left, right, dims, preferred_element_type=F32)


def unit_rows(values):
    center = values - jnp.mean(values, axis=-1, keepdims=True)
    spread = lax.rsqrt(jnp.mean(center * center, axis=-1, keepdims=True) + NORM_EPS)
    return center * spread, spread


def unit_rows_back(inner, scaled, spread):
    return spread * (
        inner
        - jnp.mean(inner, axis=-1, keepdims=True)
        - scaled * jnp.mean(inner * scaled, axis=-1, keepdims=True)
    )


def col_sum(values):
    return jnp.sum(values, axis=0, keepdims=True)


def unit_position(kind):
    place = np.arange(CHUNK)
    if kind == 0:
        return np.minimum(place // GRID_L, GRID_L - 1), place % GRID_L
    inner = place % SLOT_S
    return inner // GRID_S, inner % GRID_S


def pick_tables():
    keys = np.zeros((2, CHUNK, 512), np.float32)
    keys_back = np.zeros((2, CHUNK, 512), np.float32)
    queries = np.zeros((2, CHUNK, CHUNK), np.float32)
    for kind in range(2):
        row, col = unit_position(kind)
        line = STRIDE * row + col
        keys[kind, np.arange(CHUNK), line] = 1
        keys_back[kind, np.arange(CHUNK), 511 - line] = 1
        queries[kind, 16 * row + col, np.arange(CHUNK)] = 1
    return keys.astype(BF16), keys_back.astype(BF16), queries.astype(BF16)


def owner_of_lane(lanes, each, last=None):
    lane = lax.broadcasted_iota(jnp.int32, lanes, 1)
    entry = lane if last is None else last - lane
    device = lax.broadcasted_iota(jnp.int32, lanes, 0)
    return ((entry >= device * each) & (entry < device * each + each)).astype(BF16)


def place_in_part(lanes, each, last=None):
    lane = lax.broadcasted_iota(jnp.int32, lanes, 1)
    entry = lane if last is None else last - lane
    row = lax.broadcasted_iota(jnp.int32, lanes, 0)
    return ((entry >= 0) & (lax.rem(entry + each, each) == row)).astype(F32)


def unpack_kernel(pack_ref, scale_ref, vec_ref, wide_ref, line_ref, *, count):
    each_d, each_f, each_t = D // count, FF // count, RELS // count
    pack = pack_ref[...]

    def rows(start, amount, each, lanes, last=None):
        owner = owner_of_lane((count, lanes), each, last)
        place = place_in_part((each, lanes), each, last)
        part = pack[:, start : start + amount * each]
        spread = dot(part, owner, TN)
        return [col_sum(spread[r * each : r * each + each] * place) for r in range(amount)]

    d_rows = rows(0, 10, each_d, D)
    ff_rows = rows(10 * each_d, 3, each_f, FF)
    lines = rows(10 * each_d + 3 * each_f, HEADS, each_t, RELS, 1006)
    lane = lax.broadcasted_iota(jnp.int32, (HEADS, D), 1)
    row = lax.broadcasted_iota(jnp.int32, (HEADS, D), 0)
    heads = dot(scale_ref[...], (lane // HEAD_DIM == row).astype(BF16))
    vec_ref[...] = jnp.concatenate(d_rows + [heads, jnp.zeros((5, D), F32)], axis=0)
    wide_ref[...] = jnp.concatenate(ff_rows + [jnp.zeros((5, FF), F32)], axis=0)
    for h in range(HEADS):
        line_ref[h] = jnp.broadcast_to(lines[h], (16, RELS))


def unpack(pack, scale, count):
    return pl.pallas_call(
        functools.partial(unpack_kernel, count=count),
        out_shape=[
            jax.ShapeDtypeStruct((16, D), F32),
            jax.ShapeDtypeStruct((8, FF), F32),
            jax.ShapeDtypeStruct((HEADS, 16, RELS), F32),
        ],
        compiler_params=pltpu.CompilerParams(vmem_limit_bytes=VMEM_BIG),
        cost_estimate=pl.CostEstimate(flops=2 * 10**9, bytes_accessed=4 * 10**6, transcendentals=0),
        name="unpack",
    )(pack, scale)


TURN = 4


def bias_kernel(line_ref, keys_ref, queries_ref, out_ref):
    left = lax.broadcasted_iota(jnp.int32, (CHUNK, CHUNK), 0) // SLOT_S
    right = lax.broadcasted_iota(jnp.int32, (CHUNK, CHUNK), 1) // SLOT_S
    spread_rows = []
    for h in range(TURN):
        base = pltpu.roll(line_ref[h], RELS - 511, 1, stride=1, stride_axis=0)
        turns = [base] + [pltpu.roll(base, STRIDE * m, 1) for m in (1, 2, 3)]
        twice = [jnp.concatenate([t, t[:, :512]], axis=1) for t in turns]
        groups = []
        for r in range(16):
            start = (RELS - 128 * (r // 4)) % RELS
            groups.append(twice[r % 4][:, start : start + 512])
        spread_rows.append(jnp.concatenate(groups, axis=0).astype(BF16))
    by_key = [
        (dot(keys_ref[0], g, NT).astype(BF16), dot(keys_ref[1, :SLOT_S], g, NT).astype(BF16))
        for g in spread_rows
    ]
    for h in range(TURN):
        out_ref[0, h] = dot(by_key[h][0], queries_ref[0]).astype(BF16)
        tile = dot(by_key[h][1], queries_ref[1])
        tile = jnp.concatenate([tile] * (CHUNK // SLOT_S), axis=0)
        out_ref[1, h] = jnp.where(left == right, tile, NEG_FILL).astype(BF16)


def build_bias(lines, keys, queries):
    return pl.pallas_call(
        bias_kernel,
        grid=(HEADS // TURN,),
        in_specs=[
            pl.BlockSpec((TURN, 16, RELS), lambda h: (h, 0, 0)),
            full(2, CHUNK, 512),
            full(2, CHUNK, CHUNK),
        ],
        out_specs=pl.BlockSpec((2, TURN, CHUNK, CHUNK), lambda h: (0, h, 0, 0)),
        out_shape=jax.ShapeDtypeStruct((2, HEADS, CHUNK, CHUNK), BF16),
        compiler_params=pltpu.CompilerParams(vmem_limit_bytes=VMEM_BIG),
        cost_estimate=pl.CostEstimate(flops=8 * 10**9, bytes_accessed=4 * 10**6, transcendentals=0),
        name="bias_tiles",
    )(lines, keys, queries)


def pack_kernel(a_ref, b_ref, c_ref, p_ref, ff_ref, table_ref, out_ref, *, count):
    each_d, each_f, each_t = D // count, FF // count, RELS // count

    def columns(rows, each, lanes):
        owner = owner_of_lane((count, lanes), each)
        place = place_in_part((each, lanes), each)
        parts = []
        for row in rows:
            high, rest = halves(row * place)
            parts.append(dot(high, owner, NT) + dot(rest, owner, NT))
        return jnp.concatenate(parts, axis=0)

    a, b, c = a_ref[...], b_ref[...], c_ref[...]
    p = p_ref[...]
    d_rows = [
        c[0:1], b[3:4], b[0:1],
        c[1:2], p[0:1, :D], p[1:2, D // 2 :], b[4:5], b[2:3], b[1:2], a[0:1],
    ]
    ff = ff_ref[...]
    lane = lax.broadcasted_iota(jnp.int32, (16, D), 1)
    row = lax.broadcasted_iota(jnp.int32, (16, D), 0)
    high, rest = halves(jnp.broadcast_to(b[5:6], (16, D)) * (lane // HEAD_DIM == row).astype(F32))
    ones = jnp.ones((count, D), BF16)
    out = [
        columns(d_rows, each_d, D),
        columns([ff[0:1], ff[2:3], ff[1:2]], each_f, FF),
        columns([table_ref[h, 0:1] for h in range(HEADS)], each_t, RELS),
        dot(high, ones, NT) + dot(rest, ones, NT),
    ]
    used = sum(o.shape[0] for o in out)
    out.append(jnp.zeros((out_ref.shape[1] - used, count), F32))
    out_ref[...] = jnp.concatenate(out, axis=0).T


def pack_terms(sums_a, sums_b, sums_c, sums_p, sums_ff, table, count, width):
    return pl.pallas_call(
        functools.partial(pack_kernel, count=count),
        out_shape=jax.ShapeDtypeStruct((count, width), F32),
        compiler_params=pltpu.CompilerParams(vmem_limit_bytes=VMEM_BIG),
        cost_estimate=pl.CostEstimate(flops=10**9, bytes_accessed=10**6, transcendentals=0),
        name="pack_terms",
    )(sums_a, sums_b, sums_c, sums_p, sums_ff, table)


def small_kernel(terms_ref, *out_refs):
    total = col_sum(terms_ref[...])
    at = 0
    for out_ref in out_refs:
        rows, width = out_ref.shape
        for r in range(rows):
            out_ref[r : r + 1] = total[:, at : at + width]
            at += width


def small_grads(terms, shapes):
    return pl.pallas_call(
        small_kernel,
        out_shape=[jax.ShapeDtypeStruct(s, F32) for s in shapes],
        cost_estimate=pl.CostEstimate(flops=10**6, bytes_accessed=4 * 10**5, transcendentals=0),
        name="small_grads",
    )(terms)


def halves(values):
    high = values.astype(BF16)
    return high, (values - high.astype(F32)).astype(BF16)


def table_kernel(tiles_ref, keys_ref, queries_ref, out_ref):
    by_query = []
    for h in range(TURN):
        small = tiles_ref[1, h, :SLOT_S]
        for part in range(1, CHUNK // SLOT_S):
            small = small + tiles_ref[1, h, part * SLOT_S : (part + 1) * SLOT_S]
        by_query.append(
            (
                dot(queries_ref[0], tiles_ref[0, h].astype(BF16), NT).astype(BF16),
                dot(queries_ref[1], small.astype(BF16), NT).astype(BF16),
            )
        )
    totals = [
        dot(large, keys_ref[0]) + dot(small, keys_ref[1, :SLOT_S]) for large, small in by_query
    ]
    for h, total in enumerate(totals):
        line = jnp.zeros((16, RELS), F32)
        for m in range(4):
            part = jnp.zeros((16, RELS), F32)
            for k in range(4):
                group = total[16 * (4 * k + m) : 16 * (4 * k + m) + 16]
                pieces = [group, jnp.zeros((16, 512 - 128 * k), F32)]
                if k:
                    pieces = [jnp.zeros((16, 128 * k), F32)] + pieces
                part += jnp.concatenate(pieces, axis=1)
            line += pltpu.roll(part, STRIDE * m, 1) if m else part
        line = pltpu.roll(line, 0, 1, stride=1, stride_axis=0)
        out_ref[h] = pltpu.roll(jnp.broadcast_to(col_sum(line), (8, RELS)), RELS - 16, 1)


def table_grads(tiles, keys_back, queries):
    return pl.pallas_call(
        table_kernel,
        grid=(HEADS // TURN,),
        in_specs=[
            pl.BlockSpec((2, TURN, CHUNK, CHUNK), lambda h: (0, h, 0, 0)),
            full(2, CHUNK, 512),
            full(2, CHUNK, CHUNK),
        ],
        out_specs=pl.BlockSpec((TURN, 8, RELS), lambda h: (h, 0, 0)),
        out_shape=jax.ShapeDtypeStruct((HEADS, 8, RELS), F32),
        compiler_params=pltpu.CompilerParams(vmem_limit_bytes=VMEM_BIG),
        cost_estimate=pl.CostEstimate(flops=8 * 10**9, bytes_accessed=6 * 10**6, transcendentals=0),
        name="table_grads",
    )(tiles, keys_back, queries)


META_KIND = 1
META_LARGE = 5
META_LENGTH = 72
META_FROM = {"a": 8, "b": 24}
META_TO = {"a": 40, "b": 56}


def live_rows(meta, chunk):
    place = lax.broadcasted_iota(jnp.int32, (CHUNK, 1), 0)
    large = meta[META_LARGE]
    first = large + (chunk - large) * (SLOT_L // SLOT_S)
    is_large = chunk < large
    end = jnp.zeros((CHUNK, 1), jnp.int32)
    for part in range(SLOT_L // SLOT_S):
        slot = jnp.where(is_large, chunk, first + part)
        start = jnp.where(is_large, 0, part * SLOT_S)
        end = jnp.where(place >= part * SLOT_S, start + meta[META_LENGTH + slot], end)
    return (place < end).astype(F32)


class Load:
    def __init__(self, meta, sem, scratch):
        self.meta, self.sem, self.scratch = meta, sem, scratch

    def cols(self, order, own, other, start, source_start, width):
        core, rows = self.meta[0], own.shape[1]
        for k in range(PIECES):
            place = pl.multiple_of(self.meta[META_FROM[order] + k] * rows, 16)
            for half, source in ((core, own), (1 - core, other)):
                pltpu.make_async_copy(
                    source.at[k, :, pl.ds(source_start, width)],
                    self.scratch.at[half, pl.ds(place, rows), pl.ds(start, width)],
                    self.sem,
                ).start()

    def rows(self, order, own, other, start):
        core, rows, width = self.meta[0], own.shape[1], own.shape[2]
        for k in range(PIECES):
            chip = self.meta[META_FROM[order] + k]
            for half, source in ((core, own), (1 - core, other)):
                place = pl.multiple_of((2 * chip + half) * rows, 16)
                pltpu.make_async_copy(
                    source.at[k],
                    self.scratch.at[pl.ds(place, rows), pl.ds(start, width)],
                    self.sem,
                ).start()

    def wait(self):
        pltpu.make_async_copy(self.scratch, self.scratch, self.sem).wait()


PARTS = (slice(0, CHUNK), slice(CHUNK, PAIR))


def project_kernel(meta, x_ref, vec_ref, a0, a1, b0, b1, low_ref, q_ref, k_ref, v_ref, w_scr, sem):
    @pl.when(pl.program_id(0) == 0)
    def _():
        load = Load(meta, sem, w_scr)
        load.cols("a", a0, a1, 0, 0, D)
        load.cols("b", b0, b1, D, 0, D // 2)
        load.wait()

    products = []
    for p in PARTS:
        scaled, _ = unit_rows(x_ref[p].astype(F32))
        low = (scaled * vec_ref[0:1] + vec_ref[3:4]).astype(BF16)
        low_ref[p] = low
        products.append((dot(low, w_scr[0]), dot(low, w_scr[1])))
    for p, (first, second) in zip(PARTS, products):
        q_ref[p] = ((first[:, :D] + vec_ref[4:5]) * QUERY_SCALE).astype(BF16)
        k_ref[p, : D // 2] = first[:, D:].astype(BF16)
        k_ref[p, D // 2 :] = second[:, : D // 2].astype(BF16)
        v_ref[p] = (second[:, D // 2 :] + vec_ref[5:6]).astype(BF16)


def project(meta, tokens, vec, pieces):
    rows = tokens.shape[0]
    tile = pl.BlockSpec((PAIR, D), lambda c, m: (c, 0))
    return pl.pallas_call(
        project_kernel,
        grid_spec=pltpu.PrefetchScalarGridSpec(
            num_scalar_prefetch=1,
            grid=(rows // PAIR,),
            in_specs=[tile, full(16, D), ANY, ANY, ANY, ANY],
            out_specs=[tile] * 4,
            scratch_shapes=[pltpu.VMEM((2, D, 3 * D // 2), BF16), pltpu.SemaphoreType.DMA],
        ),
        out_shape=[jax.ShapeDtypeStruct((rows, D), BF16)] * 4,
        compiler_params=pltpu.CompilerParams(vmem_limit_bytes=VMEM_BIG),
        cost_estimate=pl.CostEstimate(
            flops=2 * rows * D * 3 * D, bytes_accessed=16 * rows * D, transcendentals=0
        ),
        name="project",
    )(meta, tokens, vec, *pieces)


def attend_kernel(meta, q_ref, k_ref, v_ref, bias_ref, x_ref, vec_ref, o0, o1, *refs, first):
    mixed_ref, turned_ref, lse_ref, mid_ref, aln_ref, low_ref, wo_scr, sem = refs[-8:]

    @pl.when(pl.program_id(0) == 0)
    def _():
        Load(meta, sem, wo_scr).cols("b", o0, o1, 0, D // 2, D // 2)

    mask = (1.0 - live_rows(meta, pl.program_id(0) + first)) * NEG_FILL
    mask = jnp.broadcast_to(mask, (CHUNK, CHUNK))
    query_turned = q_ref[...].astype(F32).T.astype(BF16)
    value_turned = v_ref[...].astype(F32).T.astype(BF16)
    parts = [slice(h * HEAD_DIM, (h + 1) * HEAD_DIM) for h in range(HEADS)]
    sums = []

    def mix(h, exponent, largest, row_total):
        out = dot(value_turned[parts[h]], exponent)
        turned_ref[0, parts[h]] = out * (1.0 / row_total)
        sums.append(largest + jnp.log(row_total))

    product, before = dot(k_ref[:, parts[0]], query_turned[parts[0]]), None
    for h in range(HEADS):
        scores = product + bias_ref[0, h].astype(F32) + mask
        if h + 1 < HEADS:
            product = dot(k_ref[:, parts[h + 1]], query_turned[parts[h + 1]])
        largest = jnp.max(scores, axis=0, keepdims=True)
        exponent = jnp.exp(scores - largest)
        row_total = jnp.sum(exponent, axis=0, keepdims=True)
        if before:
            mix(*before)
        before = (h, exponent.astype(BF16), largest, row_total)
    mix(*before)
    lse_ref[0] = jnp.concatenate(sums + [jnp.zeros((16 - HEADS, CHUNK), F32)], axis=0)
    mixed = turned_ref[0].T
    mixed_ref[...] = mixed

    @pl.when(pl.program_id(0) == 0)
    def _():
        Load(meta, sem, wo_scr).wait()

    scaled, _ = unit_rows(mixed * vec_ref[10:11])
    aln = (scaled * vec_ref[1:2] + vec_ref[6:7]).astype(BF16)
    aln_ref[...] = aln
    branch = jnp.concatenate([dot(aln, wo_scr[0]), dot(aln, wo_scr[1])], axis=1)
    mid = x_ref[...].astype(F32) + branch + vec_ref[7:8]
    mid_ref[...] = mid
    scaled, _ = unit_rows(mid)
    low_ref[...] = (scaled * vec_ref[2:3] + vec_ref[8:9]).astype(BF16)


def attend(meta, query, key, value, bias, tokens, vec, w_out, first, chunks, before=()):
    rows = query.shape[0]
    tile = pl.BlockSpec((CHUNK, D), lambda c, m: (c + first, 0))
    return pl.pallas_call(
        functools.partial(attend_kernel, first=first),
        grid_spec=pltpu.PrefetchScalarGridSpec(
            num_scalar_prefetch=1,
            grid=(chunks,),
            in_specs=[
                tile, tile, tile,
                pl.BlockSpec(
                    (1, HEADS, CHUNK, CHUNK), lambda c, m: (m[META_KIND + c + first], 0, 0, 0)
                ),
                tile,
                full(16, D),
                ANY, ANY,
            ]
            + [ANY] * len(before),
            out_specs=[
                tile,
                pl.BlockSpec((1, D, CHUNK), lambda c, m: (c + first, 0, 0)),
                pl.BlockSpec((1, 16, CHUNK), lambda c, m: (c + first, 0, 0)),
                tile, tile, tile,
            ],
            scratch_shapes=[pltpu.VMEM((2, D, D // 2), BF16), pltpu.SemaphoreType.DMA],
        ),
        out_shape=[
            jax.ShapeDtypeStruct((rows, D), F32),
            jax.ShapeDtypeStruct((rows // CHUNK, D, CHUNK), F32),
            jax.ShapeDtypeStruct((rows // CHUNK, 16, CHUNK), F32),
            jax.ShapeDtypeStruct((rows, D), F32),
            jax.ShapeDtypeStruct((rows, D), BF16),
            jax.ShapeDtypeStruct((rows, D), BF16),
        ],
        input_output_aliases={9 + i: i for i in range(len(before))},
        compiler_params=pltpu.CompilerParams(vmem_limit_bytes=VMEM_BIG),
        cost_estimate=pl.CostEstimate(
            flops=10 * 10**9, bytes_accessed=16 * rows * D, transcendentals=0
        ),
        name="attend",
    )(meta, query, key, value, bias, tokens, vec, *w_out, *before)


CUT = 512
ROOT_PART = 0.3275911 * HALF_ROOT
TAIL = (0.127414796, -0.142248368, 0.7107068705, -0.7265760135, 0.5307027145)


def normal_parts(z):
    density = jnp.exp(-0.5 * z * z)
    t = 1.0 / (1.0 + ROOT_PART * jnp.abs(z))
    tail = TAIL[4] * t + TAIL[3]
    for c in (TAIL[2], TAIL[1], TAIL[0]):
        tail = tail * t + c
    tail = tail * t * density
    return jnp.where(z >= 0.0, 1.0 - tail, tail), z * (DENSITY_SCALE * density)


def lane_sum(values):
    return jnp.sum(values, axis=-1, keepdims=True)


def feed_kernel(
    meta, mid_ref, low_ref, cot_ref, vec_ref, wide_ref,
    i0, i1, i2, i3, f0, f1, f2, f3,
    out_ref, sums_ref, sums_ff_ref, dz_out, g0, g1, g2, g3,
    wi_scr, wf_scr, unit_scr, slope_scr, dm_scr,
    df_scr, low_scr, m_scr, dz_scr, cols_scr, rows_scr, sems, stage_sems,
):
    step = pl.program_id(0)
    mine = pl.ds(pl.multiple_of(step * CHUNK, CHUNK), CHUNK)

    def feed_loads():
        return [Load(meta, sems.at[i], s) for i, s in enumerate((wi_scr, wf_scr))]

    def arrived(which):
        @pl.when(step == 0)
        def _():
            feed_loads()[which].wait()

    @pl.when(step == 0)
    def _():
        loads = feed_loads()
        loads[0].cols("a", i0, i1, 0, 0, FF // 4)
        loads[0].cols("b", i2, i3, FF // 4, 0, FF // 4)
        loads[1].rows("a", f0, f1, 0)
        loads[1].rows("b", f2, f3, D // 2)
        sums_ref[...] = jnp.zeros_like(sums_ref)
        sums_ff_ref[...] = jnp.zeros_like(sums_ff_ref)

    live = live_rows(meta, step)
    df_full = cot_ref[...].astype(F32) * live
    df = df_full.astype(BF16)
    df_scr[mine] = df
    sums_ref[0:1] += col_sum(df_full)
    mid = mid_ref[...]
    low = low_ref[...]
    low_scr[mine] = low
    arrived(0)

    cuts = [slice(a, a + CUT) for a in range(0, FF, CUT)]
    inner = [(a * CUT // (FF // 2), slice(a * CUT % (FF // 2), a * CUT % (FF // 2) + CUT)) for a in range(FF // CUT)]
    total = jnp.zeros((CHUNK, 1), F32)
    for cut, (half, part) in zip(cuts, inner):
        z = dot(low, wi_scr[half, :, part]) + wide_ref[1:2, cut]
        cumulative, rest = normal_parts(z)
        act = z * cumulative
        unit_scr[:, cut] = act
        slope_scr[:, cut] = cumulative + rest
        total += lane_sum(act)
    mean = total * (1.0 / FF)
    square = jnp.zeros((CHUNK, 1), F32)
    arrived(1)
    for cut in cuts:
        dm_scr[:, cut] = dot(df, wf_scr[cut], NT)
        center = unit_scr[:, cut] - mean
        square += lane_sum(center * center)
    spread = lax.rsqrt(square * (1.0 / FF) + NORM_EPS)
    out = mid + vec_ref[9:10]
    first = jnp.zeros((CHUNK, 1), F32)
    second = jnp.zeros((CHUNK, 1), F32)
    for cut in cuts:
        unit = (unit_scr[:, cut] - mean) * spread
        unit_scr[:, cut] = unit
        m = (unit * wide_ref[0:1, cut] + wide_ref[2:3, cut]).astype(BF16)
        m_scr[mine, cut] = m
        out += dot(m, wf_scr[cut])
        dm = dm_scr[:, cut]
        sums_ff_ref[0:1, cut] += col_sum(dm * unit)
        sums_ff_ref[1:2, cut] += col_sum(dm)
        inside = dm * wide_ref[0:1, cut]
        first += lane_sum(inside)
        second += lane_sum(inside * unit)
    out_ref[...] = (out * live).astype(BF16)
    first = first * (1.0 / FF)
    second = second * (1.0 / FF)
    for cut, (half, part) in zip(cuts, inner):
        inside = dm_scr[:, cut] * wide_ref[0:1, cut]
        du = spread * (inside - first - unit_scr[:, cut] * second)
        dz_full = du * slope_scr[:, cut]
        sums_ff_ref[2:3, cut] += col_sum(dz_full)
        dz_scr[half, mine, part] = dz_full.astype(BF16)
    pltpu.make_async_copy(dz_scr.at[:, mine], dz_out.at[:, mine], sems.at[2]).start()

    @pl.when(step == pl.num_programs(0) - 1)
    def _():
        core = meta[0]
        stages = [Stage(cols_scr, stage_sems, 0), Stage(rows_scr, stage_sems, 2)]
        for side, out in ((1 - core, g0), (core, g2)):
            for b in range(D // BAND):
                band = dot(low_scr[:, b * BAND : (b + 1) * BAND], dz_scr[side], TN).astype(BF16)
                stage = stages[0].take()
                for i in range(BAND // ROWS_D):
                    rows = slice(i * ROWS_D, (i + 1) * ROWS_D)
                    stage[i, :ROWS_D] = band[rows, :D]
                    stage[i, ROWS_D:] = band[rows, D:]
                    piece = meta[META_TO["a"] + b * (BAND // ROWS_D) + i]
                    stages[0].send(stage.at[i], out.at[piece])
        for b in range(FF // BAND):
            band = dot(m_scr[:, b * BAND : (b + 1) * BAND], df_scr[...], TN).astype(BF16)
            stage = stages[1].take()
            for i in range(BAND // ROWS_F):
                stage[i] = band[i * ROWS_F : (i + 1) * ROWS_F]
            for parity in range(2):
                for own, out in ((True, g3), (False, g1)):

                    @pl.when((core == parity) == own)
                    def _():
                        for i in range(parity, BAND // ROWS_F, 2):
                            piece = meta[META_TO["b"] + (b * (BAND // ROWS_F) + i) // 2]
                            stages[1].send(stage.at[i], out.at[piece])

        for stage in stages:
            stage.end()
        pltpu.make_async_copy(dz_scr, dz_out, sems.at[2]).wait()


class Stage:
    def __init__(self, scratch, sems, first):
        self.scratch, self.sems, self.first, self.count = scratch, sems, first, 0

    def wait(self, slot):
        buffer = self.scratch.at[slot]
        pltpu.make_async_copy(buffer, buffer, self.sems.at[self.first + slot]).wait()

    def take(self):
        self.slot = self.count % 2
        if self.count >= 2:
            self.wait(self.slot)
        self.count += 1
        return self.scratch.at[self.slot]

    def send(self, source, target):
        pltpu.make_async_copy(source, target, self.sems.at[self.first + self.slot]).start()

    def end(self):
        for slot in range(min(2, self.count)):
            self.wait((self.count - 1 - slot) % 2)


BAND = 384


def feed(meta, mid, low, cot, vec, wide, w_in, w_down):
    rows = mid.shape[0]
    tile = pl.BlockSpec((CHUNK, D), lambda c, m: (c, 0))
    return pl.pallas_call(
        feed_kernel,
        grid_spec=pltpu.PrefetchScalarGridSpec(
            num_scalar_prefetch=1,
            grid=(rows // CHUNK,),
            in_specs=[
                tile, tile, tile,
                full(16, D), full(8, FF),
                *[ANY] * 8,
            ],
            out_specs=[tile, full(8, D), full(3, FF), *[ANY] * 5],
            scratch_shapes=[
                pltpu.VMEM((2, D, FF // 2), BF16),
                pltpu.VMEM((FF, D), BF16),
                pltpu.VMEM((CHUNK, FF), F32),
                pltpu.VMEM((CHUNK, FF), F32),
                pltpu.VMEM((CHUNK, FF), F32),
                pltpu.VMEM((rows, D), BF16),
                pltpu.VMEM((rows, D), BF16),
                pltpu.VMEM((rows, FF), BF16),
                pltpu.VMEM((2, rows, FF // 2), BF16),
                pltpu.VMEM((2, BAND // ROWS_D, 2 * ROWS_D, D), BF16),
                pltpu.VMEM((2, BAND // ROWS_F, ROWS_F, D), BF16),
                pltpu.SemaphoreType.DMA((4,)),
                pltpu.SemaphoreType.DMA((4,)),
            ],
        ),
        out_shape=[
            jax.ShapeDtypeStruct((rows, D), BF16),
            jax.ShapeDtypeStruct((8, D), F32),
            jax.ShapeDtypeStruct((3, FF), F32),
            jax.ShapeDtypeStruct((2, rows, FF // 2), BF16),
        ]
        + [jax.ShapeDtypeStruct((PIECES, ROWS_F, D), BF16)] * 4,
        compiler_params=pltpu.CompilerParams(vmem_limit_bytes=VMEM_ALL),
        cost_estimate=pl.CostEstimate(
            flops=2 * rows * D * 5 * FF, bytes_accessed=40 * rows * D, transcendentals=0
        ),
        name="feed",
    )(meta, mid, low, cot, vec, wide, *w_in, *w_down)


def middle_kernel(
    meta, dz_ref, mid_ref, mixed_ref, cot_ref, aln_ref, vec_ref, i0, i1, i2, i3, o0, o1,
    dx_ref, do_ref, sums_ref, other_out, own_out, wi_scr, wo_scr, da_scr, stage_scr, sems,
):
    step = pl.program_id(0)

    def loads():
        return [Load(meta, sems.at[i], s) for i, s in enumerate((wi_scr, wo_scr))]

    @pl.when(step == 0)
    def _():
        first, second = loads()
        first.cols("a", i0, i1, 0, 0, FF // 4)
        first.cols("b", i2, i3, FF // 4, 0, FF // 4)
        second.cols("b", o0, o1, 0, D // 2, D // 2)
        sums_ref[...] = jnp.zeros_like(sums_ref)
        first.wait()
        second.wait()

    dhs = [dot(dz_ref[0, p], wi_scr[0], NT) + dot(dz_ref[1, p], wi_scr[1], NT) for p in PARTS]
    dns = []
    for k, (p, dh) in enumerate(zip(PARTS, dhs)):
        scaled, spread = unit_rows(mid_ref[p])
        grad = cot_ref[p].astype(F32) * live_rows(meta, 2 * step + k)
        dx = grad + unit_rows_back(dh * vec_ref[2:3], scaled, spread)
        da = dx.astype(BF16)
        dns.append(dot(da[:, : D // 2], wo_scr[0], NT) + dot(da[:, D // 2 :], wo_scr[1], NT))
        mine = pl.ds(pl.multiple_of(step * PAIR + k * CHUNK, CHUNK), CHUNK)
        da_scr[0, mine] = da[:, : D // 2]
        da_scr[1, mine] = da[:, D // 2 :]
        dx_ref[p] = dx
        sums_ref[0:1] += col_sum(dh * scaled)
        sums_ref[1:2] += col_sum(dh)
        sums_ref[2:3] += col_sum(dx)
    for p, dn in zip(PARTS, dns):
        mixed = mixed_ref[p]
        scaled, spread = unit_rows(mixed * vec_ref[10:11])
        heads = unit_rows_back(dn * vec_ref[1:2], scaled, spread)
        do_ref[p] = (heads * vec_ref[10:11]).astype(BF16)
        sums_ref[3:4] += col_sum(dn * scaled)
        sums_ref[4:5] += col_sum(dn)
        sums_ref[5:6] += col_sum(heads * mixed)

    @pl.when(step == pl.num_programs(0) - 1)
    def _():
        core = meta[0]
        stages = Stage(stage_scr, sems, 2)
        for side, out in ((1 - core, other_out), (core, own_out)):
            band = dot(aln_ref[...], da_scr[side], TN).astype(BF16)
            stage = stages.take()
            for i in range(PIECES):
                stage[i] = band[i * ROWS_D : (i + 1) * ROWS_D]
                piece = meta[META_TO["b"] + i]
                stages.send(stage.at[i], out.at[piece, :, pl.ds(D // 2, D // 2)])
        stages.end()


def middle(meta, dz, mid, mixed, cot, aln, vec, w_in, w_out):
    rows = mid.shape[0]
    tile = pl.BlockSpec((PAIR, D), lambda c, m: (c, 0))
    return pl.pallas_call(
        middle_kernel,
        grid_spec=pltpu.PrefetchScalarGridSpec(
            num_scalar_prefetch=1,
            grid=(rows // PAIR,),
            in_specs=[
                pl.BlockSpec((2, PAIR, FF // 2), lambda c, m: (0, c, 0)),
                tile, tile, tile,
                full(rows, D),
                full(16, D),
                *[ANY] * 6,
            ],
            out_specs=[tile, tile, full(8, D), ANY, ANY],
            scratch_shapes=[
                pltpu.VMEM((2, D, FF // 2), BF16),
                pltpu.VMEM((2, D, D // 2), BF16),
                pltpu.VMEM((2, rows, D // 2), BF16),
                pltpu.VMEM((2, PIECES, ROWS_D, D // 2), BF16),
                pltpu.SemaphoreType.DMA((4,)),
            ],
        ),
        out_shape=[
            jax.ShapeDtypeStruct((rows, D), F32),
            jax.ShapeDtypeStruct((rows, D), BF16),
            jax.ShapeDtypeStruct((8, D), F32),
        ]
        + [jax.ShapeDtypeStruct((PIECES, ROWS_D, D), BF16)] * 2,
        compiler_params=pltpu.CompilerParams(vmem_limit_bytes=VMEM_BIG),
        cost_estimate=pl.CostEstimate(
            flops=2 * rows * D * (2 * D + FF), bytes_accessed=30 * rows * D, transcendentals=0
        ),
        name="middle",
    )(meta, dz, mid, mixed, cot, aln, vec, *w_in, *w_out)


def attend_back_kernel(
    meta, q_ref, k_ref, v_ref, do_ref, turned_ref, lse_ref, bias_ref, low_ref, before_0, before_1,
    dqkv_out, tiles_out, g0, g2, g1, g3, dq_scr, do_scr, tiles_ref, dqkv_scr, a_scr, b_scr, sems,
):
    step = pl.program_id(0)
    mine = pl.ds(pl.multiple_of(step * CHUNK, CHUNK), CHUNK)
    kind = meta[META_KIND + step]

    @pl.when(step == 0)
    def _():
        tiles_ref[...] = jnp.zeros_like(tiles_ref)

    query = q_ref[...]
    query_turned = query.astype(F32).T.astype(BF16)
    key_turned = k_ref[...].astype(F32).T.astype(BF16)
    do_scr[...] = do_ref[...].astype(F32).T
    mask = jnp.broadcast_to((1.0 - live_rows(meta, pl.program_id(0))) * NEG_FILL, (CHUNK, CHUNK))
    parts = [slice(h * HEAD_DIM, (h + 1) * HEAD_DIM) for h in range(HEADS)]
    dk, dv = [], []

    def products(h):
        part = parts[h]
        return (
            dot(k_ref[:, part], query_turned[part]),
            dot(v_ref[:, part], do_scr[part].astype(BF16)),
        )

    def finish(h, probs, ds):
        dv.append(dot(probs, do_ref[:, parts[h]]))
        dk.append(dot(ds, q_ref[:, parts[h]]))
        dq_scr[parts[h]] = dot(key_turned[parts[h]], ds)

    coming, before = products(0), None
    for h in range(HEADS):
        scores, dprobs = coming
        if h + 1 < HEADS:
            coming = products(h + 1)
        scores = scores + bias_ref[0, h].astype(F32) + mask
        probs = jnp.exp(scores - lse_ref[0, h : h + 1])
        centre = jnp.sum(do_scr[parts[h]] * turned_ref[0, parts[h]], axis=0, keepdims=True)
        ds = probs * (dprobs - centre)
        tiles_ref[kind, h] += ds
        if before:
            finish(*before)
        before = (h, probs.astype(BF16), ds.astype(BF16))
    finish(*before)
    dq = (dq_scr[...].T * QUERY_SCALE).astype(BF16)
    dk = jnp.concatenate(dk, axis=1).astype(BF16)
    dv = jnp.concatenate(dv, axis=1).astype(BF16)
    dqkv_scr[0, mine, :D] = dq
    dqkv_scr[0, mine, D:] = dk[:, : D // 2]
    dqkv_scr[1, mine, : D // 2] = dk[:, D // 2 :]
    dqkv_scr[1, mine, D // 2 :] = dv
    pltpu.make_async_copy(dqkv_scr.at[:, mine], dqkv_out.at[:, mine], sems.at[0]).start()

    @pl.when(step == pl.num_programs(0) - 1)
    def _():
        pltpu.make_async_copy(tiles_ref, tiles_out, sems.at[1]).start()
        core = meta[0]
        stages = [Stage(a_scr, sems, 2), Stage(b_scr, sems, 4)]
        for side, out_a, out_b in ((1 - core, g0, g1), (core, g2, g3)):
            for b in range(D // BAND):
                band = dot(low_ref[:, b * BAND : (b + 1) * BAND], dqkv_scr[side], TN).astype(BF16)
                stage_a, stage_b = (stage.take() for stage in stages)
                for i in range(BAND // ROWS_D):
                    rows = slice(i * ROWS_D, (i + 1) * ROWS_D)
                    stage_a[i] = band[rows, :D]
                    stage_b[i] = band[rows, D:]
                    piece = meta[META_TO["a"] + b * (BAND // ROWS_D) + i]
                    stages[0].send(stage_a.at[i], out_a.at[piece])
                    piece = meta[META_TO["b"] + b * (BAND // ROWS_D) + i]
                    stages[1].send(stage_b.at[i], out_b.at[piece, :, pl.ds(0, D // 2)])
        for stage in stages:
            stage.end()
        pltpu.make_async_copy(dqkv_scr, dqkv_out, sems.at[0]).wait()
        pltpu.make_async_copy(tiles_ref, tiles_out, sems.at[1]).wait()


def attend_back(meta, query, key, value, do, turned, lse, bias, low, before):
    rows = query.shape[0]
    chunks = rows // CHUNK
    tile = pl.BlockSpec((CHUNK, D), lambda c, m: (c, 0))
    pieces = jax.ShapeDtypeStruct((PIECES, ROWS_D, D), BF16)
    return pl.pallas_call(
        attend_back_kernel,
        grid_spec=pltpu.PrefetchScalarGridSpec(
            num_scalar_prefetch=1,
            grid=(chunks,),
            in_specs=[
                tile, tile, tile, tile,
                pl.BlockSpec((1, D, CHUNK), lambda c, m: (c, 0, 0)),
                pl.BlockSpec((1, 16, CHUNK), lambda c, m: (c, 0, 0)),
                pl.BlockSpec((1, HEADS, CHUNK, CHUNK), lambda c, m: (m[META_KIND + c], 0, 0, 0)),
                full(rows, D),
                ANY, ANY,
            ],
            out_specs=[ANY] * 6,
            scratch_shapes=[
                pltpu.VMEM((D, CHUNK), F32),
                pltpu.VMEM((D, CHUNK), F32),
                pltpu.VMEM((2, HEADS, CHUNK, CHUNK), F32),
                pltpu.VMEM((2, rows, 3 * D // 2), BF16),
                pltpu.VMEM((2, BAND // ROWS_D, ROWS_D, D), BF16),
                pltpu.VMEM((2, BAND // ROWS_D, ROWS_D, D // 2), BF16),
                pltpu.SemaphoreType.DMA((6,)),
            ],
        ),
        out_shape=[
            jax.ShapeDtypeStruct((2, rows, 3 * D // 2), BF16),
            jax.ShapeDtypeStruct((2, HEADS, CHUNK, CHUNK), F32),
            *[pieces] * 4,
        ],
        input_output_aliases={9: 4, 10: 5},
        compiler_params=pltpu.CompilerParams(vmem_limit_bytes=VMEM_BIG),
        cost_estimate=pl.CostEstimate(
            flops=20 * 10**9, bytes_accessed=30 * rows * D, transcendentals=0
        ),
        name="attend_back",
    )(meta, query, key, value, do, turned, lse, bias, low, *before)


def last_kernel(
    meta, dqkv_ref, x_ref, dx_ref, vec_ref, a0, a1, b0, b1,
    out_ref, sums_ref, sums_p_ref, w_scr, sem,
):
    @pl.when(pl.program_id(0) == 0)
    def _():
        load = Load(meta, sem, w_scr)
        load.cols("a", a0, a1, 0, 0, D)
        load.cols("b", b0, b1, D, 0, D // 2)
        load.wait()
        sums_ref[...] = jnp.zeros_like(sums_ref)
        sums_p_ref[...] = jnp.zeros_like(sums_p_ref)

    dh = dot(dqkv_ref[0], w_scr[0], NT) + dot(dqkv_ref[1], w_scr[1], NT)
    for half in range(2):
        sums_p_ref[half : half + 1] += col_sum(dqkv_ref[half].astype(F32))
    scaled, spread = unit_rows(x_ref[...].astype(F32))
    sums_ref[0:1] += col_sum(dh * scaled)
    sums_ref[1:2] += col_sum(dh)
    out_ref[...] = (dx_ref[...] + unit_rows_back(dh * vec_ref[0:1], scaled, spread)).astype(BF16)


def last(meta, dqkv, tokens, dx, vec, w_in):
    rows = tokens.shape[0]
    tile = pl.BlockSpec((CHUNK, D), lambda c, m: (c, 0))
    return pl.pallas_call(
        last_kernel,
        grid_spec=pltpu.PrefetchScalarGridSpec(
            num_scalar_prefetch=1,
            grid=(rows // CHUNK,),
            in_specs=[
                pl.BlockSpec((2, CHUNK, 3 * D // 2), lambda c, m: (0, c, 0)),
                tile, tile,
                full(16, D),
                ANY, ANY, ANY, ANY,
            ],
            out_specs=[tile, full(8, D), full(2, 3 * D // 2)],
            scratch_shapes=[pltpu.VMEM((2, D, 3 * D // 2), BF16), pltpu.SemaphoreType.DMA],
        ),
        out_shape=[
            jax.ShapeDtypeStruct((rows, D), BF16),
            jax.ShapeDtypeStruct((8, D), F32),
            jax.ShapeDtypeStruct((2, 3 * D // 2), F32),
        ],
        compiler_params=pltpu.CompilerParams(vmem_limit_bytes=VMEM_BIG),
        cost_estimate=pl.CostEstimate(
            flops=2 * rows * D * 3 * D, bytes_accessed=16 * rows * D, transcendentals=0
        ),
        name="last",
    )(meta, dqkv, tokens, dx, vec, *w_in)


def swap(values, mask, count):
    return lax.ppermute(values, AXES, [(i, i ^ mask) for i in range(count)])


def tie(values, after):
    values, after = list(values), list(after)
    if not after:
        return values
    return list(lax.optimization_barrier(tuple(values + after))[: len(values)])


class Chain:
    def __init__(self, net, steps, finish):
        self.net, self.steps, self.finish = net, list(steps), finish
        self.got = [None] * len(self.steps)
        self.sends = [[] for _ in self.steps]
        self.results = [None] * len(self.steps)

    def go(self, *after):
        for i, step in enumerate(self.steps):
            if self.results[i] is not None:
                continue
            try:
                got = self.got[i] if self.got[i] is None else tie(self.got[i], after)
                sends = step.send(got)
                values = [v for v, _ in sends]
                if got is None:
                    values = tie(values, after)
                self.sends[i] = values
                self.got[i] = [self.net.swap(v, m) for v, (_, m) in zip(values, sends)]
            except StopIteration as end:
                self.results[i] = end.value
                self.sends[i] = []
        return self

    @property
    def sent(self):
        return [v for part in self.sends for v in part]

    @property
    def received(self):
        return [v for part in self.got for v in part or []]

    def done(self, *after):
        while any(r is None for r in self.results):
            self.go(*after)
            after = ()
        return self.finish(self.results)


class Ready:
    def __init__(self, value):
        self.value, self.sent, self.received = value, [], []

    def go(self, *after):
        return self

    def done(self, *after):
        return self.value


def add_kernel(*refs, sizes):
    outs = refs[sum(sizes) :]
    at = 0
    for size, out in zip(sizes, outs):
        total = refs[at][...].astype(F32)
        for ref in refs[at + 1 : at + size]:
            total += ref[...].astype(F32)
        out[...] = total.astype(BF16)
        at += size


def add_pieces(parts, count):
    rows = parts[0][0].shape[1]
    step = min(count, 4)
    return pl.pallas_call(
        functools.partial(add_kernel, sizes=[len(p) for p in parts]),
        grid=(count // step,),
        in_specs=[
            pl.BlockSpec((step, rows, D), lambda i: (count // step + i, 0, 0)) for p in parts for _ in p
        ],
        out_specs=[pl.BlockSpec((step, rows, D), lambda i: (i, 0, 0))] * len(parts),
        out_shape=[jax.ShapeDtypeStruct((count, rows, D), BF16)] * len(parts),
        compiler_params=pltpu.CompilerParams(vmem_limit_bytes=32 * 2**20),
        cost_estimate=pl.CostEstimate(
            flops=count * rows * D * 4, bytes_accessed=16 * count * rows * D, transcendentals=0
        ),
        name="add_pieces",
    )(*(a for p in parts for a in p))


def add_last_kernel(*refs, sizes):
    outs = refs[sum(sizes) :]
    rows = refs[0].shape[1]
    for z, out in enumerate(outs):
        at = 0
        for k, size in enumerate(sizes):
            total = refs[at][z].astype(F32)
            for ref in refs[at + 1 : at + size]:
                total += ref[z].astype(F32)
            out[k * rows : (k + 1) * rows] = total.astype(out.dtype)
            at += size


def add_last_pieces(parts):
    rows = parts[0][0].shape[1]
    shape = (len(parts) * rows, D)
    return pl.pallas_call(
        functools.partial(add_last_kernel, sizes=[len(p) for p in parts]),
        grid=(1,),
        in_specs=[pl.BlockSpec((4, rows, D), lambda i: (0, 0, 0)) for p in parts for _ in p],
        out_specs=[full(*shape)] * 4,
        out_shape=[jax.ShapeDtypeStruct(shape, F32)] + [jax.ShapeDtypeStruct(shape, BF16)] * 3,
        compiler_params=pltpu.CompilerParams(vmem_limit_bytes=32 * 2**20),
        cost_estimate=pl.CostEstimate(
            flops=rows * D * 24, bytes_accessed=80 * rows * D, transcendentals=0
        ),
        name="add_last_pieces",
    )(*(a for p in parts for a in p))


class Cube:
    SIDES = {"a": (2, 4), "b": (4, 2)}

    def __init__(self):
        self.me = lax.axis_index(AXES).astype(jnp.int32)

    def swap(self, values, mask):
        return swap(values, mask, 32)

    def masks(self, order):
        shift = self.SIDES[order]
        return np.array(
            [8 * (k & 3) + shift[0] * (k >> 2 & 1) + shift[1] * (k >> 3) for k in range(PIECES)]
        )

    def meta(self):
        chip = self.me >> 1
        place = jnp.arange(PIECES, dtype=jnp.int32)
        start = [chip ^ jnp.asarray(self.masks(o) >> 1, jnp.int32) for o in "ab"]
        mask = chip ^ place
        x, y = mask & 1, mask >> 1 & 1
        to = [(mask >> 2) + 4 * x + 8 * y, (mask >> 2) + 4 * y + 8 * x]
        return self.me & 1, start + to

    def spread(self, piece, parts):
        got = yield [(piece, 8 * z) for z in (1, 2, 3)]
        held = jnp.stack([piece] + got)
        ends = np.cumsum([0] + [w for _, w in parts])
        cuts = [held[..., a:b] for a, b in zip(ends[:-1], ends[1:])]
        for stage in (0, 1):
            got = yield [(c, self.SIDES[order][stage]) for c, (order, _) in zip(cuts, parts)]
            cuts = [jnp.concatenate(pair) for pair in zip(cuts, got)]
        got = yield [(c, 1) for c in cuts]
        return [v for pair in zip(cuts, got) for v in pair]

    def gather_cols(self, shards, parts):
        left, right = (
            jnp.concatenate([h[side] for h in (jnp.split(s, 2, axis=1) for s in shards)], axis=1)
            for side in (0, 1)
        )
        odd = (self.me & 1) == 1
        got = self.swap(jnp.where(odd, left, right), 1)
        mine = jnp.where(odd, right, left)
        block = jnp.where(odd, jnp.concatenate([got, mine]), jnp.concatenate([mine, got]))
        return Chain(self, [self.spread(block, parts)], lambda results: results[0])

    def gather_rows(self, shard, parts):
        return Chain(self, [self.spread(shard, parts)], lambda results: results[0])

    def gather_small(self, pack):
        every = jnp.broadcast_to(pack, (32, pack.shape[0]))
        return lax.all_to_all(every, AXES, 0, 0, tiled=True)

    def reduce_small(self, pack):
        return lax.all_to_all(pack, AXES, 0, 0, tiled=True)

    def gather_rows(self, shard, order):
        return Chain(self, [self.spread(shard, order)], lambda parts: parts[0])

    def collect(self, owns, others, orders):
        got = yield [(o, 1) for o in others]
        terms = [[a, b] for a, b in zip(owns, got)]
        count = PIECES
        for stage in (1, 0):
            count //= 2
            sends = add_pieces(terms, count)
            got = yield [(v, self.SIDES[o][stage]) for v, o in zip(sends, orders)]
            terms = [part + [g] for part, g in zip(terms, got)]
        mine, *sends = add_last_pieces(terms)
        got = yield [(v, 8 * z) for z, v in zip((1, 2, 3), sends)]
        return mine + sum(g.astype(F32) for g in got)

    def reduce_ff(self, others, owns):
        def finish(results):
            (total,) = results
            block = jnp.concatenate([total[:ROWS_D], total[ROWS_D : 2 * ROWS_D]], axis=1)
            return jnp.concatenate(self.join(block), axis=1), total[2 * ROWS_D :]

        return Chain(self, [self.collect(owns, others, "ab")], finish)

    def reduce_attn(self, others, owns):
        def finish(results):
            (total,) = results
            block = jnp.concatenate([total[:ROWS_D], total[ROWS_D:]], axis=1)
            sides = self.join(block)
            cut = 3 * D // 2
            return tuple(
                jnp.concatenate([s[:, part] for s in sides], axis=1)
                for part in (slice(0, cut), slice(cut, None))
            )

        return Chain(self, [self.collect(owns, others, "ab")], finish)

    def join(self, block):
        rows = block.shape[0] // 2
        low, high = block[:rows], block[rows:]
        odd = (self.me & 1) == 1
        got = self.swap(jnp.where(odd, low, high), 1)
        mine = jnp.where(odd, high, low)
        return jnp.where(odd, got, mine), jnp.where(odd, mine, got)


class Plain:
    def __init__(self, count):
        self.count = count
        self.me = lax.axis_index(AXES)

    def meta(self):
        place = jnp.arange(PIECES, dtype=jnp.int32)
        return jnp.int32(0), [place] * 4

    def gather_cols(self, shards, parts):
        whole = [lax.all_gather(s, AXES, axis=0, tiled=True) for s in shards]
        left, right = (
            jnp.concatenate([h[side] for h in (jnp.split(w, 2, axis=1) for w in whole)], axis=1)
            for side in (0, 1)
        )
        out, at = [], 0
        for _, width in parts:
            for half in (left, right):
                out.append(half[:, at : at + width].reshape(PIECES, -1, width))
            at += width
        return Ready(out)

    def gather_small(self, pack):
        return lax.all_gather(pack, AXES)

    def reduce_small(self, pack):
        return lax.psum_scatter(pack, AXES, scatter_dimension=0, tiled=True)

    def gather_rows(self, shard, parts):
        whole = lax.all_gather(shard, AXES, axis=0, tiled=True)
        whole = whole.reshape(PIECES, 2, -1, whole.shape[1])
        out, at = [], 0
        for _, width in parts:
            out += [whole[:, side, :, at : at + width] for side in (0, 1)]
            at += width
        return Ready(out)

    def scatter(self, whole):
        return lax.psum_scatter(whole.astype(F32), AXES, scatter_dimension=0, tiled=True)

    def reduce_ff(self, others, owns):
        runs = [
            a[:, row : row + ROWS_D].reshape(D, D)
            for a in (owns[0], others[0])
            for row in (0, ROWS_D)
        ]
        rows = jnp.stack([owns[1], others[1]], axis=1).reshape(FF, D)
        return Ready((self.scatter(jnp.concatenate(runs, axis=1)), self.scatter(rows)))

    def reduce_attn(self, others, owns):
        halves_in, halves_out = [], []
        for a, b in (owns, others):
            a, b = a.reshape(D, D), b.reshape(D, D)
            halves_in += [a, b[:, : D // 2]]
            halves_out.append(b[:, D // 2 :])
        return Ready(tuple(self.scatter(jnp.concatenate(h, axis=1)) for h in (halves_in, halves_out)))


PARTS_ATTN = (("a", D), ("b", D))
PARTS_HALVES = (("a", FF // 4), ("b", FF // 4))
PARTS_ROWS = (("a", D // 2), ("b", D // 2))


def body(
    tokens,
    cotangent,
    w_attn_in,
    w_attn_out,
    w_fc_in,
    w_fc_out,
    gains_d,
    biases_d,
    gains_ff,
    biases_ff,
    rel_table,
    head_scale,
    bucket,
    lengths,
    *,
    count,
    cube,
):
    net = Cube() if cube else Plain(count)
    rows = tokens.shape[0]
    chunks = rows // CHUNK

    gather_attn = net.gather_cols([w_attn_in, w_attn_out], PARTS_ATTN).go()
    small = tie((gains_d, biases_d, gains_ff[None], biases_ff, rel_table), gather_attn.sent)
    sizes = [v.size for v in small]
    ends = np.cumsum(sizes)
    width = -(-int(ends[-1] + 16) // 1024) * 1024
    pack = jnp.concatenate([v.reshape(-1) for v in small] + [jnp.zeros(width - ends[-1], BF16)])
    packs = net.gather_small(pack)

    bucket, lengths = tie([bucket, lengths], [pack])
    large = jnp.sum((bucket == 1).astype(jnp.int32), dtype=jnp.int32)
    kinds = (jnp.arange(chunks, dtype=jnp.int32) >= large).astype(jnp.int32)
    core, tables = net.meta()
    meta = jnp.concatenate(
        [core.astype(jnp.int32)[None], kinds, large[None], jnp.zeros(2, jnp.int32), *tables, lengths]
    )
    keys, keys_back, queries = (jnp.asarray(t) for t in pick_tables())
    gather_ff = net.gather_cols([w_fc_in], PARTS_HALVES)
    gather_down = net.gather_rows(w_fc_out, PARTS_ROWS)

    arrived = gather_attn.received
    gather_attn.go(meta)
    gather_ff.go(*arrived)
    gather_attn.go()
    (packs,) = tie([packs], gather_attn.sent + gather_ff.sent)
    vec, wide, lines = unpack(packs, head_scale[None], count)
    bias = build_bias(lines, keys, queries)
    gather_ff.go(bias)
    gather_attn.go(*gather_ff.sent)
    gather_down.go(*gather_ff.sent)
    attn_pieces = gather_attn.done()
    out_pieces = attn_pieces[2:]

    (tokens_in,) = tie([tokens], gather_ff.sent)
    low_in, query, key, value = project(meta, tokens_in, vec, attn_pieces)
    gather_ff.go(low_in)
    gather_down.go(low_in)
    (query_in,) = tie([query], gather_ff.sent + gather_down.sent)
    heads = attend(
        meta, query_in, key, value, bias, tokens, vec, out_pieces, 0, chunks // 2
    )
    gather_down.go(heads[2])
    gather_ff.go(heads[2])
    (query_in,) = tie([query], gather_down.sent + gather_ff.sent)
    mixed, turned, lse, mid, low_attn, low_mid = attend(
        meta, query_in, key, value, bias, tokens, vec, out_pieces, chunks // 2,
        chunks - chunks // 2, heads,
    )
    gather_down.go(lse)
    ff_pieces = gather_ff.done(lse)
    down_pieces = gather_down.done()
    out_tokens, sums_a, sums_ff, dz, *ff_grads = feed(
        meta, mid, low_mid, cotangent, vec, wide, ff_pieces, down_pieces
    )

    reduce_ff = net.reduce_ff(ff_grads[:2], ff_grads[2:]).go()
    (dz,) = tie([dz], reduce_ff.sent)
    dx, do, sums_b, *out_grads = middle(
        meta, dz, mid, mixed, cotangent, low_attn, vec, ff_pieces, out_pieces
    )
    reduce_ff.go(sums_b)
    (do,) = tie([do], reduce_ff.sent)
    dqkv, tiles, other_a, own_a, other_b, own_b = attend_back(
        meta, query, key, value, do, turned, lse, bias, low_in, out_grads
    )
    reduce_attn = net.reduce_attn((other_a, other_b), (own_a, own_b)).go()
    reduce_ff.go(tiles)
    (tiles,) = tie([tiles], reduce_ff.sent)
    (tiles,) = tie([tiles], reduce_attn.sent)
    grad_table = table_grads(tiles, keys_back, queries)
    reduce_attn.go(grad_table)
    reduce_ff.go(grad_table)
    (dqkv,) = tie([dqkv], reduce_attn.sent + reduce_ff.sent)
    grad_tokens, sums_c, sums_p = last(meta, dqkv, tokens, dx, vec, attn_pieces)
    reduce_attn.go(sums_c)
    terms = (sums_a, sums_b, sums_c, sums_p, sums_ff, grad_table)
    terms = pack_terms(*tie(terms, reduce_attn.sent + reduce_ff.received), count, width)
    reduce_attn.go(terms)
    mine = net.reduce_small(terms)
    grad_fc_in, grad_fc_out = reduce_ff.done(*reduce_attn.received)
    grad_attn_in, grad_attn_out = reduce_attn.done()

    grads = small_grads(mine, [v.shape for v in small] + [(1, HEADS)])
    return (
        out_tokens,
        grad_tokens,
        grad_attn_in,
        grad_attn_out,
        grad_fc_in,
        grad_fc_out,
        grads[0],
        grads[1],
        grads[2][0],
        grads[3],
        grads[4],
        grads[5][0],
    )


def solution(mesh):
    rows = P(AXES, None)
    columns = P(None, AXES)
    line = P(AXES)
    count = mesh.shape["wide"] * mesh.shape["narrow"]
    cube = (mesh.shape["wide"], mesh.shape["narrow"]) == (8, 4)
    return jax.shard_map(
        functools.partial(body, count=count, cube=cube),
        mesh=mesh,
        in_specs=(
            rows, rows, rows, rows, rows, rows,
            columns, columns, line, columns, columns, P(), line, line,
        ),
        out_specs=(
            rows, rows, rows, rows, rows, rows,
            columns, columns, line, columns, columns, P(),
        ),
        check_vma=False,
    )
```

```python
import functools

import jax
import jax.numpy as jnp
import numpy as np
from jax import lax
from jax.experimental import pallas as pl
from jax.experimental.pallas import tpu as pltpu
from jax.sharding import PartitionSpec as P

HEADS = 12
HEAD_DIM = 64
D = 768
FF = 3072
GRID_L = 15
GRID_S = 8
SLOT_L = 256
SLOT_S = 64
STRIDE = 32
RELS = 1024
CHUNK = 256
PAIR = 2 * CHUNK
PIECES = 16
ROWS_D = D // PIECES
ROWS_F = FF // (2 * PIECES)

NEG_FILL = -1e30
NORM_EPS = 1e-05
HALF_ROOT = 0.7071067811865476
DENSITY_SCALE = 0.3989422804014327
QUERY_SCALE = 0.125
AXES = ("wide", "narrow")
F32 = jnp.float32
BF16 = jnp.bfloat16
VMEM_BIG = 60 * 2**20
VMEM_ALL = 63 * 2**20

NN = (((1,), (0,)), ((), ()))
NT = (((1,), (1,)), ((), ()))
TN = (((0,), (0,)), ((), ()))


ANY = pl.BlockSpec(memory_space=pl.ANY)


def full(*shape):
    return pl.BlockSpec(shape, lambda *_: (0,) * len(shape))


def dot(left, right, dims=NN):
    return lax.dot_general(left, right, dims, preferred_element_type=F32)


def unit_rows(values):
    center = values - jnp.mean(values, axis=-1, keepdims=True)
    spread = lax.rsqrt(jnp.mean(center * center, axis=-1, keepdims=True) + NORM_EPS)
    return center * spread, spread


def unit_rows_back(inner, scaled, spread):
    return spread * (
        inner
        - jnp.mean(inner, axis=-1, keepdims=True)
        - scaled * jnp.mean(inner * scaled, axis=-1, keepdims=True)
    )


def col_sum(values):
    return jnp.sum(values, axis=0, keepdims=True)


def unit_position(kind):
    place = np.arange(CHUNK)
    if kind == 0:
        return np.minimum(place // GRID_L, GRID_L - 1), place % GRID_L
    inner = place % SLOT_S
    return inner // GRID_S, inner % GRID_S


def pick_tables():
    keys = np.zeros((2, CHUNK, 512), np.float32)
    keys_back = np.zeros((2, CHUNK, 512), np.float32)
    queries = np.zeros((2, CHUNK, CHUNK), np.float32)
    for kind in range(2):
        row, col = unit_position(kind)
        line = STRIDE * row + col
        keys[kind, np.arange(CHUNK), line] = 1
        keys_back[kind, np.arange(CHUNK), 511 - line] = 1
        queries[kind, 16 * row + col, np.arange(CHUNK)] = 1
    return keys.astype(BF16), keys_back.astype(BF16), queries.astype(BF16)


def owner_of_lane(lanes, each, last=None):
    lane = lax.broadcasted_iota(jnp.int32, lanes, 1)
    entry = lane if last is None else last - lane
    device = lax.broadcasted_iota(jnp.int32, lanes, 0)
    return ((entry >= device * each) & (entry < device * each + each)).astype(BF16)


def place_in_part(lanes, each, last=None):
    lane = lax.broadcasted_iota(jnp.int32, lanes, 1)
    entry = lane if last is None else last - lane
    row = lax.broadcasted_iota(jnp.int32, lanes, 0)
    return ((entry >= 0) & (lax.rem(entry + each, each) == row)).astype(F32)


def unpack_kernel(pack_ref, scale_ref, vec_ref, wide_ref, line_ref, *, count):
    each_d, each_f, each_t = D // count, FF // count, RELS // count
    pack = pack_ref[...]

    def rows(start, amount, each, lanes, last=None):
        owner = owner_of_lane((count, lanes), each, last)
        place = place_in_part((each, lanes), each, last)
        part = pack[:, start : start + amount * each]
        spread = dot(part, owner, TN)
        return [col_sum(spread[r * each : r * each + each] * place) for r in range(amount)]

    d_rows = rows(0, 10, each_d, D)
    ff_rows = rows(10 * each_d, 3, each_f, FF)
    lines = rows(10 * each_d + 3 * each_f, HEADS, each_t, RELS, 1006)
    lane = lax.broadcasted_iota(jnp.int32, (HEADS, D), 1)
    row = lax.broadcasted_iota(jnp.int32, (HEADS, D), 0)
    heads = dot(scale_ref[...], (lane // HEAD_DIM == row).astype(BF16))
    vec_ref[...] = jnp.concatenate(d_rows + [heads, jnp.zeros((5, D), F32)], axis=0)
    wide_ref[...] = jnp.concatenate(ff_rows + [jnp.zeros((5, FF), F32)], axis=0)
    for h in range(HEADS):
        line_ref[h] = jnp.broadcast_to(lines[h], (16, RELS))


def unpack(pack, scale, count):
    return pl.pallas_call(
        functools.partial(unpack_kernel, count=count),
        out_shape=[
            jax.ShapeDtypeStruct((16, D), F32),
            jax.ShapeDtypeStruct((8, FF), F32),
            jax.ShapeDtypeStruct((HEADS, 16, RELS), F32),
        ],
        compiler_params=pltpu.CompilerParams(vmem_limit_bytes=VMEM_BIG),
        cost_estimate=pl.CostEstimate(flops=2 * 10**9, bytes_accessed=4 * 10**6, transcendentals=0),
        name="unpack",
    )(pack, scale)


TURN = 4


def bias_kernel(line_ref, keys_ref, queries_ref, out_ref):
    left = lax.broadcasted_iota(jnp.int32, (CHUNK, CHUNK), 0) // SLOT_S
    right = lax.broadcasted_iota(jnp.int32, (CHUNK, CHUNK), 1) // SLOT_S
    spread_rows = []
    for h in range(TURN):
        base = pltpu.roll(line_ref[h], RELS - 511, 1, stride=1, stride_axis=0)
        turns = [base] + [pltpu.roll(base, STRIDE * m, 1) for m in (1, 2, 3)]
        twice = [jnp.concatenate([t, t[:, :512]], axis=1) for t in turns]
        groups = []
        for r in range(16):
            start = (RELS - 128 * (r // 4)) % RELS
            groups.append(twice[r % 4][:, start : start + 512])
        spread_rows.append(jnp.concatenate(groups, axis=0).astype(BF16))
    by_key = [
        (dot(keys_ref[0], g, NT).astype(BF16), dot(keys_ref[1, :SLOT_S], g, NT).astype(BF16))
        for g in spread_rows
    ]
    for h in range(TURN):
        out_ref[0, h] = dot(by_key[h][0], queries_ref[0]).astype(BF16)
        tile = dot(by_key[h][1], queries_ref[1])
        tile = jnp.concatenate([tile] * (CHUNK // SLOT_S), axis=0)
        out_ref[1, h] = jnp.where(left == right, tile, NEG_FILL).astype(BF16)


def build_bias(lines, keys, queries):
    return pl.pallas_call(
        bias_kernel,
        grid=(HEADS // TURN,),
        in_specs=[
            pl.BlockSpec((TURN, 16, RELS), lambda h: (h, 0, 0)),
            full(2, CHUNK, 512),
            full(2, CHUNK, CHUNK),
        ],
        out_specs=pl.BlockSpec((2, TURN, CHUNK, CHUNK), lambda h: (0, h, 0, 0)),
        out_shape=jax.ShapeDtypeStruct((2, HEADS, CHUNK, CHUNK), BF16),
        compiler_params=pltpu.CompilerParams(vmem_limit_bytes=VMEM_BIG),
        cost_estimate=pl.CostEstimate(flops=8 * 10**9, bytes_accessed=4 * 10**6, transcendentals=0),
        name="bias_tiles",
    )(lines, keys, queries)


def pack_kernel(a_ref, b_ref, c_ref, p_ref, ff_ref, table_ref, out_ref, *, count):
    each_d, each_f, each_t = D // count, FF // count, RELS // count

    def columns(rows, each, lanes):
        owner = owner_of_lane((count, lanes), each)
        place = place_in_part((each, lanes), each)
        parts = []
        for row in rows:
            high, rest = halves(row * place)
            parts.append(dot(high, owner, NT) + dot(rest, owner, NT))
        return jnp.concatenate(parts, axis=0)

    a, b, c = a_ref[...], b_ref[...], c_ref[...]
    p = p_ref[...]
    d_rows = [
        c[0:1], b[3:4], b[0:1],
        c[1:2], p[0:1, :D], p[1:2, D // 2 :], b[4:5], b[2:3], b[1:2], a[0:1],
    ]
    ff = ff_ref[...]
    lane = lax.broadcasted_iota(jnp.int32, (16, D), 1)
    row = lax.broadcasted_iota(jnp.int32, (16, D), 0)
    high, rest = halves(jnp.broadcast_to(b[5:6], (16, D)) * (lane // HEAD_DIM == row).astype(F32))
    ones = jnp.ones((count, D), BF16)
    out = [
        columns(d_rows, each_d, D),
        columns([ff[0:1], ff[2:3], ff[1:2]], each_f, FF),
        columns([table_ref[h, 0:1] for h in range(HEADS)], each_t, RELS),
        dot(high, ones, NT) + dot(rest, ones, NT),
    ]
    used = sum(o.shape[0] for o in out)
    out.append(jnp.zeros((out_ref.shape[1] - used, count), F32))
    out_ref[...] = jnp.concatenate(out, axis=0).T


def pack_terms(sums_a, sums_b, sums_c, sums_p, sums_ff, table, count, width):
    return pl.pallas_call(
        functools.partial(pack_kernel, count=count),
        out_shape=jax.ShapeDtypeStruct((count, width), F32),
        compiler_params=pltpu.CompilerParams(vmem_limit_bytes=VMEM_BIG),
        cost_estimate=pl.CostEstimate(flops=10**9, bytes_accessed=10**6, transcendentals=0),
        name="pack_terms",
    )(sums_a, sums_b, sums_c, sums_p, sums_ff, table)


def small_kernel(terms_ref, *out_refs):
    total = col_sum(terms_ref[...])
    at = 0
    for out_ref in out_refs:
        rows, width = out_ref.shape
        for r in range(rows):
            out_ref[r : r + 1] = total[:, at : at + width]
            at += width


def small_grads(terms, shapes):
    return pl.pallas_call(
        small_kernel,
        out_shape=[jax.ShapeDtypeStruct(s, F32) for s in shapes],
        cost_estimate=pl.CostEstimate(flops=10**6, bytes_accessed=4 * 10**5, transcendentals=0),
        name="small_grads",
    )(terms)


def halves(values):
    high = values.astype(BF16)
    return high, (values - high.astype(F32)).astype(BF16)


def table_kernel(tiles_ref, keys_ref, queries_ref, out_ref):
    by_query = []
    for h in range(TURN):
        small = tiles_ref[1, h, :SLOT_S]
        for part in range(1, CHUNK // SLOT_S):
            small = small + tiles_ref[1, h, part * SLOT_S : (part + 1) * SLOT_S]
        by_query.append(
            (
                dot(queries_ref[0], tiles_ref[0, h].astype(BF16), NT).astype(BF16),
                dot(queries_ref[1], small.astype(BF16), NT).astype(BF16),
            )
        )
    totals = [
        dot(large, keys_ref[0]) + dot(small, keys_ref[1, :SLOT_S]) for large, small in by_query
    ]
    for h, total in enumerate(totals):
        line = jnp.zeros((16, RELS), F32)
        for m in range(4):
            part = jnp.zeros((16, RELS), F32)
            for k in range(4):
                group = total[16 * (4 * k + m) : 16 * (4 * k + m) + 16]
                pieces = [group, jnp.zeros((16, 512 - 128 * k), F32)]
                if k:
                    pieces = [jnp.zeros((16, 128 * k), F32)] + pieces
                part += jnp.concatenate(pieces, axis=1)
            line += pltpu.roll(part, STRIDE * m, 1) if m else part
        line = pltpu.roll(line, 0, 1, stride=1, stride_axis=0)
        out_ref[h] = pltpu.roll(jnp.broadcast_to(col_sum(line), (8, RELS)), RELS - 16, 1)


def table_grads(tiles, keys_back, queries):
    return pl.pallas_call(
        table_kernel,
        grid=(HEADS // TURN,),
        in_specs=[
            pl.BlockSpec((2, TURN, CHUNK, CHUNK), lambda h: (0, h, 0, 0)),
            full(2, CHUNK, 512),
            full(2, CHUNK, CHUNK),
        ],
        out_specs=pl.BlockSpec((TURN, 8, RELS), lambda h: (h, 0, 0)),
        out_shape=jax.ShapeDtypeStruct((HEADS, 8, RELS), F32),
        compiler_params=pltpu.CompilerParams(vmem_limit_bytes=VMEM_BIG),
        cost_estimate=pl.CostEstimate(flops=8 * 10**9, bytes_accessed=6 * 10**6, transcendentals=0),
        name="table_grads",
    )(tiles, keys_back, queries)


META_KIND = 1
META_LARGE = 5
META_LENGTH = 72
META_FROM = {"a": 8, "b": 24}
META_TO = {"a": 40, "b": 56}


def live_rows(meta, chunk):
    place = lax.broadcasted_iota(jnp.int32, (CHUNK, 1), 0)
    large = meta[META_LARGE]
    first = large + (chunk - large) * (SLOT_L // SLOT_S)
    is_large = chunk < large
    end = jnp.zeros((CHUNK, 1), jnp.int32)
    for part in range(SLOT_L // SLOT_S):
        slot = jnp.where(is_large, chunk, first + part)
        start = jnp.where(is_large, 0, part * SLOT_S)
        end = jnp.where(place >= part * SLOT_S, start + meta[META_LENGTH + slot], end)
    return (place < end).astype(F32)


class Load:
    def __init__(self, meta, sem, scratch):
        self.meta, self.sem, self.scratch = meta, sem, scratch

    def cols(self, order, own, other, start, source_start, width):
        core, rows = self.meta[0], own.shape[1]
        for k in range(PIECES):
            place = pl.multiple_of(self.meta[META_FROM[order] + k] * rows, 16)
            for half, source in ((core, own), (1 - core, other)):
                pltpu.make_async_copy(
                    source.at[k, :, pl.ds(source_start, width)],
                    self.scratch.at[half, pl.ds(place, rows), pl.ds(start, width)],
                    self.sem,
                ).start()

    def rows(self, order, own, other, start):
        core, rows, width = self.meta[0], own.shape[1], own.shape[2]
        for k in range(PIECES):
            chip = self.meta[META_FROM[order] + k]
            for half, source in ((core, own), (1 - core, other)):
                place = pl.multiple_of((2 * chip + half) * rows, 16)
                pltpu.make_async_copy(
                    source.at[k],
                    self.scratch.at[pl.ds(place, rows), pl.ds(start, width)],
                    self.sem,
                ).start()

    def wait(self):
        pltpu.make_async_copy(self.scratch, self.scratch, self.sem).wait()


PARTS = (slice(0, CHUNK), slice(CHUNK, PAIR))


def project_kernel(meta, x_ref, vec_ref, a0, a1, b0, b1, low_ref, q_ref, k_ref, v_ref, w_scr, sem):
    @pl.when(pl.program_id(0) == 0)
    def _():
        load = Load(meta, sem, w_scr)
        load.cols("a", a0, a1, 0, 0, D)
        load.cols("b", b0, b1, D, 0, D // 2)
        load.wait()

    products = []
    for p in PARTS:
        scaled, _ = unit_rows(x_ref[p].astype(F32))
        low = (scaled * vec_ref[0:1] + vec_ref[3:4]).astype(BF16)
        low_ref[p] = low
        products.append((dot(low, w_scr[0]), dot(low, w_scr[1])))
    for p, (first, second) in zip(PARTS, products):
        q_ref[p] = ((first[:, :D] + vec_ref[4:5]) * QUERY_SCALE).astype(BF16)
        k_ref[p, : D // 2] = first[:, D:].astype(BF16)
        k_ref[p, D // 2 :] = second[:, : D // 2].astype(BF16)
        v_ref[p] = (second[:, D // 2 :] + vec_ref[5:6]).astype(BF16)


def project(meta, tokens, vec, pieces):
    rows = tokens.shape[0]
    tile = pl.BlockSpec((PAIR, D), lambda c, m: (c, 0))
    return pl.pallas_call(
        project_kernel,
        grid_spec=pltpu.PrefetchScalarGridSpec(
            num_scalar_prefetch=1,
            grid=(rows // PAIR,),
            in_specs=[tile, full(16, D), ANY, ANY, ANY, ANY],
            out_specs=[tile] * 4,
            scratch_shapes=[pltpu.VMEM((2, D, 3 * D // 2), BF16), pltpu.SemaphoreType.DMA],
        ),
        out_shape=[jax.ShapeDtypeStruct((rows, D), BF16)] * 4,
        compiler_params=pltpu.CompilerParams(vmem_limit_bytes=VMEM_BIG),
        cost_estimate=pl.CostEstimate(
            flops=2 * rows * D * 3 * D, bytes_accessed=16 * rows * D, transcendentals=0
        ),
        name="project",
    )(meta, tokens, vec, *pieces)


def attend_kernel(meta, q_ref, k_ref, v_ref, bias_ref, x_ref, vec_ref, o0, o1, *refs, first):
    mixed_ref, turned_ref, lse_ref, mid_ref, aln_ref, low_ref, wo_scr, sem = refs[-8:]

    @pl.when(pl.program_id(0) == 0)
    def _():
        Load(meta, sem, wo_scr).cols("b", o0, o1, 0, D // 2, D // 2)

    mask = (1.0 - live_rows(meta, pl.program_id(0) + first)) * NEG_FILL
    mask = jnp.broadcast_to(mask, (CHUNK, CHUNK))
    query_turned = q_ref[...].astype(F32).T.astype(BF16)
    value_turned = v_ref[...].astype(F32).T.astype(BF16)
    parts = [slice(h * HEAD_DIM, (h + 1) * HEAD_DIM) for h in range(HEADS)]
    sums = []

    def mix(h, exponent, largest, row_total):
        out = dot(value_turned[parts[h]], exponent)
        turned_ref[0, parts[h]] = out * (1.0 / row_total)
        sums.append(largest + jnp.log(row_total))

    product, before = dot(k_ref[:, parts[0]], query_turned[parts[0]]), None
    for h in range(HEADS):
        scores = product + bias_ref[0, h].astype(F32) + mask
        if h + 1 < HEADS:
            product = dot(k_ref[:, parts[h + 1]], query_turned[parts[h + 1]])
        largest = jnp.max(scores, axis=0, keepdims=True)
        exponent = jnp.exp(scores - largest)
        row_total = jnp.sum(exponent, axis=0, keepdims=True)
        if before:
            mix(*before)
        before = (h, exponent.astype(BF16), largest, row_total)
    mix(*before)
    lse_ref[0] = jnp.concatenate(sums + [jnp.zeros((16 - HEADS, CHUNK), F32)], axis=0)
    mixed = turned_ref[0].T
    mixed_ref[...] = mixed

    @pl.when(pl.program_id(0) == 0)
    def _():
        Load(meta, sem, wo_scr).wait()

    scaled, _ = unit_rows(mixed * vec_ref[10:11])
    aln = (scaled * vec_ref[1:2] + vec_ref[6:7]).astype(BF16)
    aln_ref[...] = aln
    branch = jnp.concatenate([dot(aln, wo_scr[0]), dot(aln, wo_scr[1])], axis=1)
    mid = x_ref[...].astype(F32) + branch + vec_ref[7:8]
    mid_ref[...] = mid
    scaled, _ = unit_rows(mid)
    low_ref[...] = (scaled * vec_ref[2:3] + vec_ref[8:9]).astype(BF16)


def attend(meta, query, key, value, bias, tokens, vec, w_out, first, chunks, before=()):
    rows = query.shape[0]
    tile = pl.BlockSpec((CHUNK, D), lambda c, m: (c + first, 0))
    return pl.pallas_call(
        functools.partial(attend_kernel, first=first),
        grid_spec=pltpu.PrefetchScalarGridSpec(
            num_scalar_prefetch=1,
            grid=(chunks,),
            in_specs=[
                tile, tile, tile,
                pl.BlockSpec(
                    (1, HEADS, CHUNK, CHUNK), lambda c, m: (m[META_KIND + c + first], 0, 0, 0)
                ),
                tile,
                full(16, D),
                ANY, ANY,
            ]
            + [ANY] * len(before),
            out_specs=[
                tile,
                pl.BlockSpec((1, D, CHUNK), lambda c, m: (c + first, 0, 0)),
                pl.BlockSpec((1, 16, CHUNK), lambda c, m: (c + first, 0, 0)),
                tile, tile, tile,
            ],
            scratch_shapes=[pltpu.VMEM((2, D, D // 2), BF16), pltpu.SemaphoreType.DMA],
        ),
        out_shape=[
            jax.ShapeDtypeStruct((rows, D), F32),
            jax.ShapeDtypeStruct((rows // CHUNK, D, CHUNK), F32),
            jax.ShapeDtypeStruct((rows // CHUNK, 16, CHUNK), F32),
            jax.ShapeDtypeStruct((rows, D), F32),
            jax.ShapeDtypeStruct((rows, D), BF16),
            jax.ShapeDtypeStruct((rows, D), BF16),
        ],
        input_output_aliases={9 + i: i for i in range(len(before))},
        compiler_params=pltpu.CompilerParams(vmem_limit_bytes=VMEM_BIG),
        cost_estimate=pl.CostEstimate(
            flops=10 * 10**9, bytes_accessed=16 * rows * D, transcendentals=0
        ),
        name="attend",
    )(meta, query, key, value, bias, tokens, vec, *w_out, *before)


CUT = 512
ROOT_PART = 0.3275911 * HALF_ROOT
TAIL = (0.127414796, -0.142248368, 0.7107068705, -0.7265760135, 0.5307027145)


def normal_parts(z):
    density = jnp.exp(-0.5 * z * z)
    t = 1.0 / (1.0 + ROOT_PART * jnp.abs(z))
    tail = TAIL[4] * t + TAIL[3]
    for c in (TAIL[2], TAIL[1], TAIL[0]):
        tail = tail * t + c
    tail = tail * t * density
    return jnp.where(z >= 0.0, 1.0 - tail, tail), z * (DENSITY_SCALE * density)


def lane_sum(values):
    return jnp.sum(values, axis=-1, keepdims=True)


def feed_kernel(
    meta, mid_ref, low_ref, cot_ref, vec_ref, wide_ref,
    i0, i1, i2, i3, f0, f1, f2, f3,
    out_ref, sums_ref, sums_ff_ref, dz_out, g0, g1, g2, g3,
    wi_scr, wf_scr, unit_scr, slope_scr, dm_scr,
    df_scr, low_scr, m_scr, dz_scr, cols_scr, rows_scr, sems, stage_sems,
):
    step = pl.program_id(0)
    mine = pl.ds(pl.multiple_of(step * CHUNK, CHUNK), CHUNK)

    def feed_loads():
        return [Load(meta, sems.at[i], s) for i, s in enumerate((wi_scr, wf_scr))]

    def arrived(which):
        @pl.when(step == 0)
        def _():
            feed_loads()[which].wait()

    @pl.when(step == 0)
    def _():
        loads = feed_loads()
        loads[0].cols("a", i0, i1, 0, 0, FF // 4)
        loads[0].cols("b", i2, i3, FF // 4, 0, FF // 4)
        loads[1].rows("a", f0, f1, 0)
        loads[1].rows("b", f2, f3, D // 2)
        sums_ref[...] = jnp.zeros_like(sums_ref)
        sums_ff_ref[...] = jnp.zeros_like(sums_ff_ref)

    live = live_rows(meta, step)
    df_full = cot_ref[...].astype(F32) * live
    df = df_full.astype(BF16)
    df_scr[mine] = df
    sums_ref[0:1] += col_sum(df_full)
    mid = mid_ref[...]
    low = low_ref[...]
    low_scr[mine] = low
    arrived(0)

    cuts = [slice(a, a + CUT) for a in range(0, FF, CUT)]
    inner = [(a * CUT // (FF // 2), slice(a * CUT % (FF // 2), a * CUT % (FF // 2) + CUT)) for a in range(FF // CUT)]
    total = jnp.zeros((CHUNK, 1), F32)
    for cut, (half, part) in zip(cuts, inner):
        z = dot(low, wi_scr[half, :, part]) + wide_ref[1:2, cut]
        cumulative, rest = normal_parts(z)
        act = z * cumulative
        unit_scr[:, cut] = act
        slope_scr[:, cut] = cumulative + rest
        total += lane_sum(act)
    mean = total * (1.0 / FF)
    square = jnp.zeros((CHUNK, 1), F32)
    arrived(1)
    for cut in cuts:
        dm_scr[:, cut] = dot(df, wf_scr[cut], NT)
        center = unit_scr[:, cut] - mean
        square += lane_sum(center * center)
    spread = lax.rsqrt(square * (1.0 / FF) + NORM_EPS)
    out = mid + vec_ref[9:10]
    first = jnp.zeros((CHUNK, 1), F32)
    second = jnp.zeros((CHUNK, 1), F32)
    for cut in cuts:
        unit = (unit_scr[:, cut] - mean) * spread
        unit_scr[:, cut] = unit
        m = (unit * wide_ref[0:1, cut] + wide_ref[2:3, cut]).astype(BF16)
        m_scr[mine, cut] = m
        out += dot(m, wf_scr[cut])
        dm = dm_scr[:, cut]
        sums_ff_ref[0:1, cut] += col_sum(dm * unit)
        sums_ff_ref[1:2, cut] += col_sum(dm)
        inside = dm * wide_ref[0:1, cut]
        first += lane_sum(inside)
        second += lane_sum(inside * unit)
    out_ref[...] = (out * live).astype(BF16)
    first = first * (1.0 / FF)
    second = second * (1.0 / FF)
    for cut, (half, part) in zip(cuts, inner):
        inside = dm_scr[:, cut] * wide_ref[0:1, cut]
        du = spread * (inside - first - unit_scr[:, cut] * second)
        dz_full = du * slope_scr[:, cut]
        sums_ff_ref[2:3, cut] += col_sum(dz_full)
        dz_scr[half, mine, part] = dz_full.astype(BF16)
    pltpu.make_async_copy(dz_scr.at[:, mine], dz_out.at[:, mine], sems.at[2]).start()

    @pl.when(step == pl.num_programs(0) - 1)
    def _():
        core = meta[0]
        stages = [Stage(cols_scr, stage_sems, 0), Stage(rows_scr, stage_sems, 2)]
        for side, out in ((1 - core, g0), (core, g2)):
            for b in range(D // BAND):
                band = dot(low_scr[:, b * BAND : (b + 1) * BAND], dz_scr[side], TN).astype(BF16)
                stage = stages[0].take()
                for i in range(BAND // ROWS_D):
                    rows = slice(i * ROWS_D, (i + 1) * ROWS_D)
                    stage[i, :ROWS_D] = band[rows, :D]
                    stage[i, ROWS_D:] = band[rows, D:]
                    piece = meta[META_TO["a"] + b * (BAND // ROWS_D) + i]
                    stages[0].send(stage.at[i], out.at[piece])
        for b in range(FF // BAND):
            band = dot(m_scr[:, b * BAND : (b + 1) * BAND], df_scr[...], TN).astype(BF16)
            stage = stages[1].take()
            for i in range(BAND // ROWS_F):
                stage[i] = band[i * ROWS_F : (i + 1) * ROWS_F]
            for parity in range(2):
                for own, out in ((True, g3), (False, g1)):

                    @pl.when((core == parity) == own)
                    def _():
                        for i in range(parity, BAND // ROWS_F, 2):
                            piece = meta[META_TO["b"] + (b * (BAND // ROWS_F) + i) // 2]
                            stages[1].send(stage.at[i], out.at[piece])

        for stage in stages:
            stage.end()
        pltpu.make_async_copy(dz_scr, dz_out, sems.at[2]).wait()


class Stage:
    def __init__(self, scratch, sems, first):
        self.scratch, self.sems, self.first, self.count = scratch, sems, first, 0

    def wait(self, slot):
        buffer = self.scratch.at[slot]
        pltpu.make_async_copy(buffer, buffer, self.sems.at[self.first + slot]).wait()

    def take(self):
        self.slot = self.count % 2
        if self.count >= 2:
            self.wait(self.slot)
        self.count += 1
        return self.scratch.at[self.slot]

    def send(self, source, target):
        pltpu.make_async_copy(source, target, self.sems.at[self.first + self.slot]).start()

    def end(self):
        for slot in range(min(2, self.count)):
            self.wait((self.count - 1 - slot) % 2)


BAND = 384


def feed(meta, mid, low, cot, vec, wide, w_in, w_down):
    rows = mid.shape[0]
    tile = pl.BlockSpec((CHUNK, D), lambda c, m: (c, 0))
    return pl.pallas_call(
        feed_kernel,
        grid_spec=pltpu.PrefetchScalarGridSpec(
            num_scalar_prefetch=1,
            grid=(rows // CHUNK,),
            in_specs=[
                tile, tile, tile,
                full(16, D), full(8, FF),
                *[ANY] * 8,
            ],
            out_specs=[tile, full(8, D), full(3, FF), *[ANY] * 5],
            scratch_shapes=[
                pltpu.VMEM((2, D, FF // 2), BF16),
                pltpu.VMEM((FF, D), BF16),
                pltpu.VMEM((CHUNK, FF), F32),
                pltpu.VMEM((CHUNK, FF), F32),
                pltpu.VMEM((CHUNK, FF), F32),
                pltpu.VMEM((rows, D), BF16),
                pltpu.VMEM((rows, D), BF16),
                pltpu.VMEM((rows, FF), BF16),
                pltpu.VMEM((2, rows, FF // 2), BF16),
                pltpu.VMEM((2, BAND // ROWS_D, 2 * ROWS_D, D), BF16),
                pltpu.VMEM((2, BAND // ROWS_F, ROWS_F, D), BF16),
                pltpu.SemaphoreType.DMA((4,)),
                pltpu.SemaphoreType.DMA((4,)),
            ],
        ),
        out_shape=[
            jax.ShapeDtypeStruct((rows, D), BF16),
            jax.ShapeDtypeStruct((8, D), F32),
            jax.ShapeDtypeStruct((3, FF), F32),
            jax.ShapeDtypeStruct((2, rows, FF // 2), BF16),
        ]
        + [jax.ShapeDtypeStruct((PIECES, ROWS_F, D), BF16)] * 4,
        compiler_params=pltpu.CompilerParams(vmem_limit_bytes=VMEM_ALL),
        cost_estimate=pl.CostEstimate(
            flops=2 * rows * D * 5 * FF, bytes_accessed=40 * rows * D, transcendentals=0
        ),
        name="feed",
    )(meta, mid, low, cot, vec, wide, *w_in, *w_down)


def middle_kernel(
    meta, dz_ref, mid_ref, mixed_ref, cot_ref, aln_ref, vec_ref, i0, i1, i2, i3, o0, o1,
    dx_ref, do_ref, sums_ref, other_out, own_out, wi_scr, wo_scr, da_scr, stage_scr, sems,
):
    step = pl.program_id(0)

    def loads():
        return [Load(meta, sems.at[i], s) for i, s in enumerate((wi_scr, wo_scr))]

    @pl.when(step == 0)
    def _():
        first, second = loads()
        first.cols("a", i0, i1, 0, 0, FF // 4)
        first.cols("b", i2, i3, FF // 4, 0, FF // 4)
        second.cols("b", o0, o1, 0, D // 2, D // 2)
        sums_ref[...] = jnp.zeros_like(sums_ref)
        first.wait()
        second.wait()

    dhs = [dot(dz_ref[0, p], wi_scr[0], NT) + dot(dz_ref[1, p], wi_scr[1], NT) for p in PARTS]
    dns = []
    for k, (p, dh) in enumerate(zip(PARTS, dhs)):
        scaled, spread = unit_rows(mid_ref[p])
        grad = cot_ref[p].astype(F32) * live_rows(meta, 2 * step + k)
        dx = grad + unit_rows_back(dh * vec_ref[2:3], scaled, spread)
        da = dx.astype(BF16)
        dns.append(dot(da[:, : D // 2], wo_scr[0], NT) + dot(da[:, D // 2 :], wo_scr[1], NT))
        mine = pl.ds(pl.multiple_of(step * PAIR + k * CHUNK, CHUNK), CHUNK)
        da_scr[0, mine] = da[:, : D // 2]
        da_scr[1, mine] = da[:, D // 2 :]
        dx_ref[p] = dx
        sums_ref[0:1] += col_sum(dh * scaled)
        sums_ref[1:2] += col_sum(dh)
        sums_ref[2:3] += col_sum(dx)
    for p, dn in zip(PARTS, dns):
        mixed = mixed_ref[p]
        scaled, spread = unit_rows(mixed * vec_ref[10:11])
        heads = unit_rows_back(dn * vec_ref[1:2], scaled, spread)
        do_ref[p] = (heads * vec_ref[10:11]).astype(BF16)
        sums_ref[3:4] += col_sum(dn * scaled)
        sums_ref[4:5] += col_sum(dn)
        sums_ref[5:6] += col_sum(heads * mixed)

    @pl.when(step == pl.num_programs(0) - 1)
    def _():
        core = meta[0]
        stages = Stage(stage_scr, sems, 2)
        for side, out in ((1 - core, other_out), (core, own_out)):
            band = dot(aln_ref[...], da_scr[side], TN).astype(BF16)
            stage = stages.take()
            for i in range(PIECES):
                stage[i] = band[i * ROWS_D : (i + 1) * ROWS_D]
                piece = meta[META_TO["b"] + i]
                stages.send(stage.at[i], out.at[piece, :, pl.ds(D // 2, D // 2)])
        stages.end()


def middle(meta, dz, mid, mixed, cot, aln, vec, w_in, w_out):
    rows = mid.shape[0]
    tile = pl.BlockSpec((PAIR, D), lambda c, m: (c, 0))
    return pl.pallas_call(
        middle_kernel,
        grid_spec=pltpu.PrefetchScalarGridSpec(
            num_scalar_prefetch=1,
            grid=(rows // PAIR,),
            in_specs=[
                pl.BlockSpec((2, PAIR, FF // 2), lambda c, m: (0, c, 0)),
                tile, tile, tile,
                full(rows, D),
                full(16, D),
                *[ANY] * 6,
            ],
            out_specs=[tile, tile, full(8, D), ANY, ANY],
            scratch_shapes=[
                pltpu.VMEM((2, D, FF // 2), BF16),
                pltpu.VMEM((2, D, D // 2), BF16),
                pltpu.VMEM((2, rows, D // 2), BF16),
                pltpu.VMEM((2, PIECES, ROWS_D, D // 2), BF16),
                pltpu.SemaphoreType.DMA((4,)),
            ],
        ),
        out_shape=[
            jax.ShapeDtypeStruct((rows, D), F32),
            jax.ShapeDtypeStruct((rows, D), BF16),
            jax.ShapeDtypeStruct((8, D), F32),
        ]
        + [jax.ShapeDtypeStruct((PIECES, ROWS_D, D), BF16)] * 2,
        compiler_params=pltpu.CompilerParams(vmem_limit_bytes=VMEM_BIG),
        cost_estimate=pl.CostEstimate(
            flops=2 * rows * D * (2 * D + FF), bytes_accessed=30 * rows * D, transcendentals=0
        ),
        name="middle",
    )(meta, dz, mid, mixed, cot, aln, vec, *w_in, *w_out)


def attend_back_kernel(
    meta, q_ref, k_ref, v_ref, do_ref, turned_ref, lse_ref, bias_ref, low_ref, before_0, before_1,
    dqkv_out, tiles_out, g0, g2, g1, g3, dq_scr, do_scr, tiles_ref, dqkv_scr, a_scr, b_scr, sems,
):
    step = pl.program_id(0)
    mine = pl.ds(pl.multiple_of(step * CHUNK, CHUNK), CHUNK)
    kind = meta[META_KIND + step]

    @pl.when(step == 0)
    def _():
        tiles_ref[...] = jnp.zeros_like(tiles_ref)

    query = q_ref[...]
    query_turned = query.astype(F32).T.astype(BF16)
    key_turned = k_ref[...].astype(F32).T.astype(BF16)
    do_scr[...] = do_ref[...].astype(F32).T
    mask = jnp.broadcast_to((1.0 - live_rows(meta, pl.program_id(0))) * NEG_FILL, (CHUNK, CHUNK))
    parts = [slice(h * HEAD_DIM, (h + 1) * HEAD_DIM) for h in range(HEADS)]
    dk, dv = [], []

    def products(h):
        part = parts[h]
        return (
            dot(k_ref[:, part], query_turned[part]),
            dot(v_ref[:, part], do_scr[part].astype(BF16)),
        )

    def finish(h, probs, ds):
        dv.append(dot(probs, do_ref[:, parts[h]]))
        dk.append(dot(ds, q_ref[:, parts[h]]))
        dq_scr[parts[h]] = dot(key_turned[parts[h]], ds)

    coming, before = products(0), None
    for h in range(HEADS):
        scores, dprobs = coming
        if h + 1 < HEADS:
            coming = products(h + 1)
        scores = scores + bias_ref[0, h].astype(F32) + mask
        probs = jnp.exp(scores - lse_ref[0, h : h + 1])
        centre = jnp.sum(do_scr[parts[h]] * turned_ref[0, parts[h]], axis=0, keepdims=True)
        ds = probs * (dprobs - centre)
        tiles_ref[kind, h] += ds
        if before:
            finish(*before)
        before = (h, probs.astype(BF16), ds.astype(BF16))
    finish(*before)
    dq = (dq_scr[...].T * QUERY_SCALE).astype(BF16)
    dk = jnp.concatenate(dk, axis=1).astype(BF16)
    dv = jnp.concatenate(dv, axis=1).astype(BF16)
    dqkv_scr[0, mine, :D] = dq
    dqkv_scr[0, mine, D:] = dk[:, : D // 2]
    dqkv_scr[1, mine, : D // 2] = dk[:, D // 2 :]
    dqkv_scr[1, mine, D // 2 :] = dv
    pltpu.make_async_copy(dqkv_scr.at[:, mine], dqkv_out.at[:, mine], sems.at[0]).start()

    @pl.when(step == pl.num_programs(0) - 1)
    def _():
        pltpu.make_async_copy(tiles_ref, tiles_out, sems.at[1]).start()
        core = meta[0]
        stages = [Stage(a_scr, sems, 2), Stage(b_scr, sems, 4)]
        for side, out_a, out_b in ((1 - core, g0, g1), (core, g2, g3)):
            for b in range(D // BAND):
                band = dot(low_ref[:, b * BAND : (b + 1) * BAND], dqkv_scr[side], TN).astype(BF16)
                stage_a, stage_b = (stage.take() for stage in stages)
                for i in range(BAND // ROWS_D):
                    rows = slice(i * ROWS_D, (i + 1) * ROWS_D)
                    stage_a[i] = band[rows, :D]
                    stage_b[i] = band[rows, D:]
                    piece = meta[META_TO["a"] + b * (BAND // ROWS_D) + i]
                    stages[0].send(stage_a.at[i], out_a.at[piece])
                    piece = meta[META_TO["b"] + b * (BAND // ROWS_D) + i]
                    stages[1].send(stage_b.at[i], out_b.at[piece, :, pl.ds(0, D // 2)])
        for stage in stages:
            stage.end()
        pltpu.make_async_copy(dqkv_scr, dqkv_out, sems.at[0]).wait()
        pltpu.make_async_copy(tiles_ref, tiles_out, sems.at[1]).wait()


def attend_back(meta, query, key, value, do, turned, lse, bias, low, before):
    rows = query.shape[0]
    chunks = rows // CHUNK
    tile = pl.BlockSpec((CHUNK, D), lambda c, m: (c, 0))
    pieces = jax.ShapeDtypeStruct((PIECES, ROWS_D, D), BF16)
    return pl.pallas_call(
        attend_back_kernel,
        grid_spec=pltpu.PrefetchScalarGridSpec(
            num_scalar_prefetch=1,
            grid=(chunks,),
            in_specs=[
                tile, tile, tile, tile,
                pl.BlockSpec((1, D, CHUNK), lambda c, m: (c, 0, 0)),
                pl.BlockSpec((1, 16, CHUNK), lambda c, m: (c, 0, 0)),
                pl.BlockSpec((1, HEADS, CHUNK, CHUNK), lambda c, m: (m[META_KIND + c], 0, 0, 0)),
                full(rows, D),
                ANY, ANY,
            ],
            out_specs=[ANY] * 6,
            scratch_shapes=[
                pltpu.VMEM((D, CHUNK), F32),
                pltpu.VMEM((D, CHUNK), F32),
                pltpu.VMEM((2, HEADS, CHUNK, CHUNK), F32),
                pltpu.VMEM((2, rows, 3 * D // 2), BF16),
                pltpu.VMEM((2, BAND // ROWS_D, ROWS_D, D), BF16),
                pltpu.VMEM((2, BAND // ROWS_D, ROWS_D, D // 2), BF16),
                pltpu.SemaphoreType.DMA((6,)),
            ],
        ),
        out_shape=[
            jax.ShapeDtypeStruct((2, rows, 3 * D // 2), BF16),
            jax.ShapeDtypeStruct((2, HEADS, CHUNK, CHUNK), F32),
            *[pieces] * 4,
        ],
        input_output_aliases={9: 4, 10: 5},
        compiler_params=pltpu.CompilerParams(vmem_limit_bytes=VMEM_BIG),
        cost_estimate=pl.CostEstimate(
            flops=20 * 10**9, bytes_accessed=30 * rows * D, transcendentals=0
        ),
        name="attend_back",
    )(meta, query, key, value, do, turned, lse, bias, low, *before)


def last_kernel(
    meta, dqkv_ref, x_ref, dx_ref, vec_ref, a0, a1, b0, b1,
    out_ref, sums_ref, sums_p_ref, w_scr, sem,
):
    @pl.when(pl.program_id(0) == 0)
    def _():
        load = Load(meta, sem, w_scr)
        load.cols("a", a0, a1, 0, 0, D)
        load.cols("b", b0, b1, D, 0, D // 2)
        load.wait()
        sums_ref[...] = jnp.zeros_like(sums_ref)
        sums_p_ref[...] = jnp.zeros_like(sums_p_ref)

    dh = dot(dqkv_ref[0], w_scr[0], NT) + dot(dqkv_ref[1], w_scr[1], NT)
    for half in range(2):
        sums_p_ref[half : half + 1] += col_sum(dqkv_ref[half].astype(F32))
    scaled, spread = unit_rows(x_ref[...].astype(F32))
    sums_ref[0:1] += col_sum(dh * scaled)
    sums_ref[1:2] += col_sum(dh)
    out_ref[...] = (dx_ref[...] + unit_rows_back(dh * vec_ref[0:1], scaled, spread)).astype(BF16)


def last(meta, dqkv, tokens, dx, vec, w_in):
    rows = tokens.shape[0]
    tile = pl.BlockSpec((CHUNK, D), lambda c, m: (c, 0))
    return pl.pallas_call(
        last_kernel,
        grid_spec=pltpu.PrefetchScalarGridSpec(
            num_scalar_prefetch=1,
            grid=(rows // CHUNK,),
            in_specs=[
                pl.BlockSpec((2, CHUNK, 3 * D // 2), lambda c, m: (0, c, 0)),
                tile, tile,
                full(16, D),
                ANY, ANY, ANY, ANY,
            ],
            out_specs=[tile, full(8, D), full(2, 3 * D // 2)],
            scratch_shapes=[pltpu.VMEM((2, D, 3 * D // 2), BF16), pltpu.SemaphoreType.DMA],
        ),
        out_shape=[
            jax.ShapeDtypeStruct((rows, D), BF16),
            jax.ShapeDtypeStruct((8, D), F32),
            jax.ShapeDtypeStruct((2, 3 * D // 2), F32),
        ],
        compiler_params=pltpu.CompilerParams(vmem_limit_bytes=VMEM_BIG),
        cost_estimate=pl.CostEstimate(
            flops=2 * rows * D * 3 * D, bytes_accessed=16 * rows * D, transcendentals=0
        ),
        name="last",
    )(meta, dqkv, tokens, dx, vec, *w_in)


def swap(values, mask, count):
    return lax.ppermute(values, AXES, [(i, i ^ mask) for i in range(count)])


def tie(values, after):
    values, after = list(values), list(after)
    if not after:
        return values
    return list(lax.optimization_barrier(tuple(values + after))[: len(values)])


class Chain:
    def __init__(self, net, steps, finish):
        self.net, self.steps, self.finish = net, list(steps), finish
        self.got = [None] * len(self.steps)
        self.sends = [[] for _ in self.steps]
        self.results = [None] * len(self.steps)

    def go(self, *after):
        for i, step in enumerate(self.steps):
            if self.results[i] is not None:
                continue
            try:
                got = self.got[i] if self.got[i] is None else tie(self.got[i], after)
                sends = step.send(got)
                values = [v for v, _ in sends]
                if got is None:
                    values = tie(values, after)
                self.sends[i] = values
                self.got[i] = [self.net.swap(v, m) for v, (_, m) in zip(values, sends)]
            except StopIteration as end:
                self.results[i] = end.value
                self.sends[i] = []
        return self

    @property
    def sent(self):
        return [v for part in self.sends for v in part]

    @property
    def received(self):
        return [v for part in self.got for v in part or []]

    def done(self, *after):
        while any(r is None for r in self.results):
            self.go(*after)
            after = ()
        return self.finish(self.results)


class Ready:
    def __init__(self, value):
        self.value, self.sent, self.received = value, [], []

    def go(self, *after):
        return self

    def done(self, *after):
        return self.value


def add_kernel(*refs, sizes):
    outs = refs[sum(sizes) :]
    at = 0
    for size, out in zip(sizes, outs):
        total = refs[at][...].astype(F32)
        for ref in refs[at + 1 : at + size]:
            total += ref[...].astype(F32)
        out[...] = total.astype(BF16)
        at += size


def add_pieces(parts, count):
    rows = parts[0][0].shape[1]
    step = min(count, 4)
    return pl.pallas_call(
        functools.partial(add_kernel, sizes=[len(p) for p in parts]),
        grid=(count // step,),
        in_specs=[
            pl.BlockSpec((step, rows, D), lambda i: (count // step + i, 0, 0)) for p in parts for _ in p
        ],
        out_specs=[pl.BlockSpec((step, rows, D), lambda i: (i, 0, 0))] * len(parts),
        out_shape=[jax.ShapeDtypeStruct((count, rows, D), BF16)] * len(parts),
        compiler_params=pltpu.CompilerParams(vmem_limit_bytes=32 * 2**20),
        cost_estimate=pl.CostEstimate(
            flops=count * rows * D * 4, bytes_accessed=16 * count * rows * D, transcendentals=0
        ),
        name="add_pieces",
    )(*(a for p in parts for a in p))


def add_last_kernel(*refs, sizes):
    outs = refs[sum(sizes) :]
    rows = refs[0].shape[1]
    for z, out in enumerate(outs):
        at = 0
        for k, size in enumerate(sizes):
            total = refs[at][z].astype(F32)
            for ref in refs[at + 1 : at + size]:
                total += ref[z].astype(F32)
            out[k * rows : (k + 1) * rows] = total.astype(out.dtype)
            at += size


def add_last_pieces(parts):
    rows = parts[0][0].shape[1]
    shape = (len(parts) * rows, D)
    return pl.pallas_call(
        functools.partial(add_last_kernel, sizes=[len(p) for p in parts]),
        grid=(1,),
        in_specs=[pl.BlockSpec((4, rows, D), lambda i: (0, 0, 0)) for p in parts for _ in p],
        out_specs=[full(*shape)] * 4,
        out_shape=[jax.ShapeDtypeStruct(shape, F32)] + [jax.ShapeDtypeStruct(shape, BF16)] * 3,
        compiler_params=pltpu.CompilerParams(vmem_limit_bytes=32 * 2**20),
        cost_estimate=pl.CostEstimate(
            flops=rows * D * 24, bytes_accessed=80 * rows * D, transcendentals=0
        ),
        name="add_last_pieces",
    )(*(a for p in parts for a in p))


class Cube:
    SIDES = {"a": (2, 4), "b": (4, 2)}

    def __init__(self):
        self.me = lax.axis_index(AXES).astype(jnp.int32)

    def swap(self, values, mask):
        return swap(values, mask, 32)

    def masks(self, order):
        shift = self.SIDES[order]
        return np.array(
            [8 * (k & 3) + shift[0] * (k >> 2 & 1) + shift[1] * (k >> 3) for k in range(PIECES)]
        )

    def meta(self):
        chip = self.me >> 1
        place = jnp.arange(PIECES, dtype=jnp.int32)
        start = [chip ^ jnp.asarray(self.masks(o) >> 1, jnp.int32) for o in "ab"]
        mask = chip ^ place
        x, y = mask & 1, mask >> 1 & 1
        to = [(mask >> 2) + 4 * x + 8 * y, (mask >> 2) + 4 * y + 8 * x]
        return self.me & 1, start + to

    def spread(self, piece, parts):
        got = yield [(piece, 8 * z) for z in (1, 2, 3)]
        held = jnp.stack([piece] + got)
        ends = np.cumsum([0] + [w for _, w in parts])
        cuts = [held[..., a:b] for a, b in zip(ends[:-1], ends[1:])]
        for stage in (0, 1):
            got = yield [(c, self.SIDES[order][stage]) for c, (order, _) in zip(cuts, parts)]
            cuts = [jnp.concatenate(pair) for pair in zip(cuts, got)]
        got = yield [(c, 1) for c in cuts]
        return [v for pair in zip(cuts, got) for v in pair]

    def gather_cols(self, shards, parts):
        left, right = (
            jnp.concatenate([h[side] for h in (jnp.split(s, 2, axis=1) for s in shards)], axis=1)
            for side in (0, 1)
        )
        odd = (self.me & 1) == 1
        got = self.swap(jnp.where(odd, left, right), 1)
        mine = jnp.where(odd, right, left)
        block = jnp.where(odd, jnp.concatenate([got, mine]), jnp.concatenate([mine, got]))
        return Chain(self, [self.spread(block, parts)], lambda results: results[0])

    def gather_rows(self, shard, parts):
        return Chain(self, [self.spread(shard, parts)], lambda results: results[0])

    def gather_small(self, pack):
        every = jnp.broadcast_to(pack, (32, pack.shape[0]))
        return lax.all_to_all(every, AXES, 0, 0, tiled=True)

    def reduce_small(self, pack):
        return lax.all_to_all(pack, AXES, 0, 0, tiled=True)

    def gather_rows(self, shard, order):
        return Chain(self, [self.spread(shard, order)], lambda parts: parts[0])

    def collect(self, owns, others, orders):
        got = yield [(o, 1) for o in others]
        terms = [[a, b] for a, b in zip(owns, got)]
        count = PIECES
        for stage in (1, 0):
            count //= 2
            sends = add_pieces(terms, count)
            got = yield [(v, self.SIDES[o][stage]) for v, o in zip(sends, orders)]
            terms = [part + [g] for part, g in zip(terms, got)]
        mine, *sends = add_last_pieces(terms)
        got = yield [(v, 8 * z) for z, v in zip((1, 2, 3), sends)]
        return mine + sum(g.astype(F32) for g in got)

    def reduce_ff(self, others, owns):
        def finish(results):
            (total,) = results
            block = jnp.concatenate([total[:ROWS_D], total[ROWS_D : 2 * ROWS_D]], axis=1)
            return jnp.concatenate(self.join(block), axis=1), total[2 * ROWS_D :]

        return Chain(self, [self.collect(owns, others, "ab")], finish)

    def reduce_attn(self, others, owns):
        def finish(results):
            (total,) = results
            block = jnp.concatenate([total[:ROWS_D], total[ROWS_D:]], axis=1)
            sides = self.join(block)
            cut = 3 * D // 2
            return tuple(
                jnp.concatenate([s[:, part] for s in sides], axis=1)
                for part in (slice(0, cut), slice(cut, None))
            )

        return Chain(self, [self.collect(owns, others, "ab")], finish)

    def join(self, block):
        rows = block.shape[0] // 2
        low, high = block[:rows], block[rows:]
        odd = (self.me & 1) == 1
        got = self.swap(jnp.where(odd, low, high), 1)
        mine = jnp.where(odd, high, low)
        return jnp.where(odd, got, mine), jnp.where(odd, mine, got)


class Plain:
    def __init__(self, count):
        self.count = count
        self.me = lax.axis_index(AXES)

    def meta(self):
        place = jnp.arange(PIECES, dtype=jnp.int32)
        return jnp.int32(0), [place] * 4

    def gather_cols(self, shards, parts):
        whole = [lax.all_gather(s, AXES, axis=0, tiled=True) for s in shards]
        left, right = (
            jnp.concatenate([h[side] for h in (jnp.split(w, 2, axis=1) for w in whole)], axis=1)
            for side in (0, 1)
        )
        out, at = [], 0
        for _, width in parts:
            for half in (left, right):
                out.append(half[:, at : at + width].reshape(PIECES, -1, width))
            at += width
        return Ready(out)

    def gather_small(self, pack):
        return lax.all_gather(pack, AXES)

    def reduce_small(self, pack):
        return lax.psum_scatter(pack, AXES, scatter_dimension=0, tiled=True)

    def gather_rows(self, shard, parts):
        whole = lax.all_gather(shard, AXES, axis=0, tiled=True)
        whole = whole.reshape(PIECES, 2, -1, whole.shape[1])
        out, at = [], 0
        for _, width in parts:
            out += [whole[:, side, :, at : at + width] for side in (0, 1)]
            at += width
        return Ready(out)

    def scatter(self, whole):
        return lax.psum_scatter(whole.astype(F32), AXES, scatter_dimension=0, tiled=True)

    def reduce_ff(self, others, owns):
        runs = [
            a[:, row : row + ROWS_D].reshape(D, D)
            for a in (owns[0], others[0])
            for row in (0, ROWS_D)
        ]
        rows = jnp.stack([owns[1], others[1]], axis=1).reshape(FF, D)
        return Ready((self.scatter(jnp.concatenate(runs, axis=1)), self.scatter(rows)))

    def reduce_attn(self, others, owns):
        halves_in, halves_out = [], []
        for a, b in (owns, others):
            a, b = a.reshape(D, D), b.reshape(D, D)
            halves_in += [a, b[:, : D // 2]]
            halves_out.append(b[:, D // 2 :])
        return Ready(tuple(self.scatter(jnp.concatenate(h, axis=1)) for h in (halves_in, halves_out)))


PARTS_ATTN = (("a", D), ("b", D))
PARTS_HALVES = (("a", FF // 4), ("b", FF // 4))
PARTS_ROWS = (("a", D // 2), ("b", D // 2))


def body(
    tokens,
    cotangent,
    w_attn_in,
    w_attn_out,
    w_fc_in,
    w_fc_out,
    gains_d,
    biases_d,
    gains_ff,
    biases_ff,
    rel_table,
    head_scale,
    bucket,
    lengths,
    *,
    count,
    cube,
):
    net = Cube() if cube else Plain(count)
    rows = tokens.shape[0]
    chunks = rows // CHUNK

    gather_attn = net.gather_cols([w_attn_in, w_attn_out], PARTS_ATTN).go()
    small = tie((gains_d, biases_d, gains_ff[None], biases_ff, rel_table), gather_attn.sent)
    sizes = [v.size for v in small]
    ends = np.cumsum(sizes)
    width = -(-int(ends[-1] + 16) // 1024) * 1024
    pack = jnp.concatenate([v.reshape(-1) for v in small] + [jnp.zeros(width - ends[-1], BF16)])
    packs = net.gather_small(pack)

    bucket, lengths = tie([bucket, lengths], [pack])
    large = jnp.sum((bucket == 1).astype(jnp.int32), dtype=jnp.int32)
    kinds = (jnp.arange(chunks, dtype=jnp.int32) >= large).astype(jnp.int32)
    core, tables = net.meta()
    meta = jnp.concatenate(
        [core.astype(jnp.int32)[None], kinds, large[None], jnp.zeros(2, jnp.int32), *tables, lengths]
    )
    keys, keys_back, queries = (jnp.asarray(t) for t in pick_tables())
    gather_ff = net.gather_cols([w_fc_in], PARTS_HALVES)
    gather_down = net.gather_rows(w_fc_out, PARTS_ROWS)

    arrived = gather_attn.received
    gather_attn.go(meta)
    gather_ff.go(*arrived)
    gather_attn.go()
    (packs,) = tie([packs], gather_attn.sent + gather_ff.sent)
    vec, wide, lines = unpack(packs, head_scale[None], count)
    bias = build_bias(lines, keys, queries)
    gather_ff.go(bias)
    gather_attn.go(*gather_ff.sent)
    gather_down.go(*gather_ff.sent)
    attn_pieces = gather_attn.done()
    out_pieces = attn_pieces[2:]

    (tokens_in,) = tie([tokens], gather_ff.sent)
    low_in, query, key, value = project(meta, tokens_in, vec, attn_pieces)
    gather_ff.go(low_in)
    gather_down.go(low_in)
    (query_in,) = tie([query], gather_ff.sent + gather_down.sent)
    heads = attend(
        meta, query_in, key, value, bias, tokens, vec, out_pieces, 0, chunks // 2
    )
    gather_down.go(heads[2])
    (query_in,) = tie([query], gather_down.sent)
    mixed, turned, lse, mid, low_attn, low_mid = attend(
        meta, query_in, key, value, bias, tokens, vec, out_pieces, chunks // 2,
        chunks - chunks // 2, heads,
    )
    gather_ff.go(lse)
    gather_down.go(*gather_ff.sent)
    ff_pieces = gather_ff.done()
    down_pieces = gather_down.done()
    out_tokens, sums_a, sums_ff, dz, *ff_grads = feed(
        meta, mid, low_mid, cotangent, vec, wide, ff_pieces, down_pieces
    )

    reduce_ff = net.reduce_ff(ff_grads[:2], ff_grads[2:]).go()
    (dz,) = tie([dz], reduce_ff.sent)
    dx, do, sums_b, *out_grads = middle(
        meta, dz, mid, mixed, cotangent, low_attn, vec, ff_pieces, out_pieces
    )
    reduce_ff.go(sums_b)
    (do,) = tie([do], reduce_ff.sent)
    dqkv, tiles, other_a, own_a, other_b, own_b = attend_back(
        meta, query, key, value, do, turned, lse, bias, low_in, out_grads
    )
    reduce_attn = net.reduce_attn((other_a, other_b), (own_a, own_b)).go()
    reduce_ff.go(tiles)
    (tiles,) = tie([tiles], reduce_ff.sent)
    (tiles,) = tie([tiles], reduce_attn.sent)
    grad_table = table_grads(tiles, keys_back, queries)
    reduce_attn.go(grad_table)
    reduce_ff.go(grad_table)
    (dqkv,) = tie([dqkv], reduce_attn.sent + reduce_ff.sent)
    grad_tokens, sums_c, sums_p = last(meta, dqkv, tokens, dx, vec, attn_pieces)
    reduce_attn.go(sums_c)
    terms = (sums_a, sums_b, sums_c, sums_p, sums_ff, grad_table)
    terms = pack_terms(*tie(terms, reduce_attn.sent + reduce_ff.received), count, width)
    reduce_attn.go(terms)
    mine = net.reduce_small(terms)
    grad_fc_in, grad_fc_out = reduce_ff.done(*reduce_attn.received)
    grad_attn_in, grad_attn_out = reduce_attn.done()

    grads = small_grads(mine, [v.shape for v in small] + [(1, HEADS)])
    return (
        out_tokens,
        grad_tokens,
        grad_attn_in,
        grad_attn_out,
        grad_fc_in,
        grad_fc_out,
        grads[0],
        grads[1],
        grads[2][0],
        grads[3],
        grads[4],
        grads[5][0],
    )


def solution(mesh):
    rows = P(AXES, None)
    columns = P(None, AXES)
    line = P(AXES)
    count = mesh.shape["wide"] * mesh.shape["narrow"]
    cube = (mesh.shape["wide"], mesh.shape["narrow"]) == (8, 4)
    return jax.shard_map(
        functools.partial(body, count=count, cube=cube),
        mesh=mesh,
        in_specs=(
            rows, rows, rows, rows, rows, rows,
            columns, columns, line, columns, columns, P(), line, line,
        ),
        out_specs=(
            rows, rows, rows, rows, rows, rows,
            columns, columns, line, columns, columns, P(),
        ),
        check_vma=False,
    )
```
